32 devices in a mesh: tm: 4 (over y, x), sx: 2 (over core), sy: 4 (over z).
Axes of the slice: x: 2, y: 2, z: 4, core: 2. Of those that a mesh axis runs over, the one named last changes fastest.
Arguments:
- frames: bfloat16 [8, 64, 64, 512], P('tm', 'sx', 'sy'), may hold values from -6 to 6
- input_weight: bfloat16 [3, 3, 512, 512], replicated, may hold values from -0.09375 to 0.09375
- output_weight: bfloat16 [3, 3, 512, 512], replicated, may hold values from -0.09375 to 0.09375
- pole_index: int32 [512], replicated, may hold values from 0 to 15
- gelu_scale: float32 [512], replicated, may hold values from 0.15 to 0.6
- start_state: float32 [64, 64, 512], P('sx', 'sy'), may hold values from -12 to 12
Outputs:
- result: bfloat16 [8, 64, 64, 512], P('tm', 'sx', 'sy')
The draws below stay inside these ranges and needn't reach their ends.
All inputs are finite; a program needn't handle non-finite values.
Results may differ from the reference program's by a relative error of at most 0.0049.
Values may be sent and summed in bfloat16 or wider, within the bound.
No kernel may reach another device: no remote copies, remote signals or barrier semaphores. Data moves between devices by JAX's collectives and lax.ppermute only.
A program may use at most 128 MiB of HBM per device.

```python
import math
import jax
import jax.numpy as jnp
from jax import lax

C = 512
NPOLES = 16
TF = 8
H = 64
W = 64


def touch_ends(array, rng, least, high):
    longest = array.shape.index(max(array.shape))
    spots = []
    for shift in (0, 1):
        where = [jax.random.randint(jax.random.fold_in(rng, axis), (), 0, length) for axis, length in enumerate(array.shape)]
        where[longest] = (where[longest] + shift) % array.shape[longest]
        spots.append(tuple(where))
    return array.at[spots[0]].set(least).at[spots[1]].set(high)


def shard_levels(key, shape, cuts, low, largest):
    gain, own = 1.0, jax.random.fold_in(key, 6)
    for position, blocks in cuts:
        draws = jnp.exp(jax.random.uniform(jax.random.fold_in(own, position), (blocks,), jnp.float32, low / len(cuts), largest / len(cuts)))
        gain = gain * jnp.repeat(draws, shape[position] // blocks).reshape([-1 if axis == position else 1 for axis in range(len(shape))])
    return gain


def scatter_about(key, extent, deviation, limit, cuts=(), held_as=jnp.bfloat16):
    entries = jax.random.normal(key, extent, jnp.float32) * deviation
    if len(cuts) > 0:
        entries = shard_levels(key, extent, cuts, -0.22, 0.18) * entries
    return jnp.clip(entries, min=-limit, max=limit).astype(held_as)


def setup_inputs(seed: int = 0) -> dict:
    key_list = jax.random.split(jax.random.key(seed), 7)
    frames = scatter_about(key_list[0], (TF, H, W, C), 1.0, 6.0, ((0, 4), (1, 2), (2, 4)))
    input_weight = scatter_about(key_list[1], (3, 3, C, C), (9 * C) ** -0.5, 0.09375)
    output_weight = scatter_about(key_list[2], (3, 3, C, C), (9 * C) ** -0.5, 0.09375)
    pole_index = touch_ends(jax.random.randint(key_list[3], (C,), 0, NPOLES), jax.random.fold_in(key_list[3], 1), 0, NPOLES - 1).astype(jnp.int32)
    gelu_scale = jnp.clip(jnp.exp(jax.random.uniform(key_list[4], (C,), jnp.float32, math.log(0.15), math.log(0.6))), 0.15, 0.6)
    start_state = scatter_about(key_list[5], (H, W, C), 2.0, 12.0, ((0, 2), (1, 4)), jnp.float32)
    return {"frames": frames, "input_weight": input_weight, "output_weight": output_weight, "pole_index": pole_index, "gelu_scale": gelu_scale, "start_state": start_state}


def convolve(frame, weight):
    rows, cols, channels = frame.shape
    padded = jnp.pad(frame, ((1, 1), (1, 1), (0, 0)))
    total = jnp.zeros((rows * cols, channels), jnp.float32)
    for row_shift in range(3):
        for col_shift in range(3):
            window = padded[row_shift:row_shift + rows, col_shift:col_shift + cols, :].reshape(-1, channels)
            total = total + jnp.dot(window, weight[row_shift, col_shift], preferred_element_type=jnp.float32)
    return total.reshape(rows, cols, channels)


def reference(frames, input_weight, output_weight, pole_index, gelu_scale, start_state):
    decay = jnp.exp(-0.001 * jnp.exp(pole_index.astype(jnp.float32) * (math.log(300.0) / (NPOLES - 1))))

    def advance(state, frame):
        drive = convolve(frame, input_weight)
        state = decay * state + drive
        mixed = jax.nn.gelu(gelu_scale * state).astype(jnp.bfloat16)
        return state, convolve(mixed, output_weight).astype(jnp.bfloat16)

    final_state, outputs = lax.scan(advance, start_state, frames)
    return outputs
```

```python
import math

import jax
import jax.numpy as jnp
from jax import lax
from jax.sharding import PartitionSpec as P

NPOLES = 16


def from_neighbours(before, after, axis):
    count = lax.axis_size(axis)
    if count == 2:
        first = lax.axis_index(axis) == 0
        got = lax.ppermute(jnp.where(first, before, after), axis, [(0, 1), (1, 0)])
        zero = jnp.zeros_like(got)
        return jnp.where(first, zero, got), jnp.where(first, got, zero)
    return (
        lax.ppermute(before, axis, [(i, i + 1) for i in range(count - 1)]),
        lax.ppermute(after, axis, [(i + 1, i) for i in range(count - 1)]),
    )


def pack(parts):
    return jnp.concatenate([part.reshape(-1, part.shape[-1]) for part in parts], axis=0)


def unpack(packed, parts):
    out, at = [], 0
    for part in parts:
        size = math.prod(part.shape[:-1])
        out.append(packed[at : at + size].reshape(part.shape))
        at += size
    return out


def extended(cells, start, axis, dim):
    def ends(width, array, where):
        size = array.shape[where]
        return (
            lax.slice_in_dim(array, size - width, size, axis=where),
            lax.slice_in_dim(array, 0, width, axis=where),
        )

    tail, head = ends(2, cells, dim + 1)
    start_tail, start_head = ends(1, start, dim)
    before = [tail, start_tail.astype(jnp.bfloat16)]
    after = [head, start_head.astype(jnp.bfloat16)]
    low, high = from_neighbours(pack(before), pack(after), axis)
    low, high = unpack(low, before), unpack(high, after)
    cells = jnp.concatenate([low[0], cells, high[0]], axis=dim + 1)
    start = jnp.concatenate(
        [low[1].astype(jnp.float32), start, high[1].astype(jnp.float32)], axis=dim
    )
    return cells, start


def convolve(cells, weight):
    return lax.conv_general_dilated(
        cells,
        weight,
        (1, 1),
        "VALID",
        dimension_numbers=("NHWC", "HWIO", "NHWC"),
        preferred_element_type=jnp.float32,
    )


def on_device(frames, input_weight, output_weight, pole_index, gelu_scale, start_state):
    count, rows, cols, channels = frames.shape
    groups = lax.axis_size("tm")
    position = lax.axis_index("tm")
    rate = -0.001 * jnp.exp(pole_index.astype(jnp.float32) * (math.log(300.0) / (NPOLES - 1)))
    decay = jnp.exp(rate)

    cells, start = extended(frames, start_state, "sx", 0)
    cells, start = extended(cells, start, "sy", 1)
    drive = convolve(cells, input_weight)
    state = drive[0]
    partial_states = [state]
    for step in range(1, count):
        state = decay * state + drive[step]
        partial_states.append(state)

    flat = state.reshape(-1, channels).astype(jnp.bfloat16)
    used = flat.shape[0]
    block = -(-used // (groups * 16)) * 16
    flat = jnp.pad(flat, ((0, groups * block - used), (0, 0)))
    ends = lax.all_to_all(flat.reshape(groups, block, channels), "tm", 0, 0)
    carried = jnp.exp(count * rate)
    entry = jnp.zeros((block, channels), jnp.float32)
    entries = [entry]
    for index in range(groups - 1):
        entry = carried * entry + ends[index].astype(jnp.float32)
        entries.append(entry)
    entries = lax.all_to_all(jnp.stack(entries).astype(jnp.bfloat16), "tm", 0, 0)
    entry = entries.reshape(-1, channels)[:used].reshape(state.shape).astype(jnp.float32)
    incoming = jnp.exp((count * position).astype(jnp.float32) * rate) * start + entry

    row = lax.axis_index("sx") * rows + jnp.arange(-1, rows + 1)
    col = lax.axis_index("sy") * cols + jnp.arange(-1, cols + 1)
    row_in = (row >= 0) & (row < lax.axis_size("sx") * rows)
    col_in = (col >= 0) & (col < lax.axis_size("sy") * cols)
    inside = (row_in[:, None] & col_in[None, :])[:, :, None]
    activated = []
    for step in range(count):
        full_state = jnp.exp((step + 1) * rate) * incoming + partial_states[step]
        mixed = jax.nn.gelu(gelu_scale * full_state)
        activated.append(jnp.where(inside, mixed, 0.0).astype(jnp.bfloat16))
    return convolve(jnp.stack(activated, axis=0), output_weight).astype(jnp.bfloat16)


def solution(mesh):
    return jax.shard_map(
        on_device,
        mesh=mesh,
        in_specs=(P("tm", "sx", "sy", None), P(), P(), P(), P(), P("sx", "sy", None)),
        out_specs=P("tm", "sx", "sy", None),
        check_vma=False,
    )
```

```python
import math

import jax
import jax.numpy as jnp
from jax import lax
from jax.experimental import pallas as pl
from jax.experimental.pallas import tpu as pltpu
from jax.sharding import PartitionSpec as P

NPOLES = 16
VMEM_LIMIT = 48 * 1024 * 1024
WHOLE = pl.BlockSpec(memory_space=pltpu.VMEM)


def from_neighbours(before, after, axis):
    count = lax.axis_size(axis)
    if count == 2:
        first = lax.axis_index(axis) == 0
        got = lax.ppermute(jnp.where(first, before, after), axis, [(0, 1), (1, 0)])
        zero = jnp.zeros_like(got)
        return jnp.where(first, zero, got), jnp.where(first, got, zero)
    return (
        lax.ppermute(before, axis, [(i, i + 1) for i in range(count - 1)]),
        lax.ppermute(after, axis, [(i + 1, i) for i in range(count - 1)]),
    )


def halos(cells):
    top, bottom = from_neighbours(cells[:, -1:], cells[:, :1], "sx")

    def column(at):
        return jnp.concatenate([top[:, :, at], cells[:, :, at], bottom[:, :, at]], axis=1)

    left, right = from_neighbours(column(-1), column(0), "sy")
    return top, bottom, left, right


def shifted(product, step):
    if step == 0:
        return product
    cols = product.shape[1]
    col = lax.broadcasted_iota(jnp.int32, product.shape, 1)
    if step == 1:
        return jnp.where(col == cols - 1, 0.0, pltpu.roll(product, cols - 1, 1))
    return jnp.where(col == 0, 0.0, pltpu.roll(product, 1, 1))


def tile_kernel(cells_ref, top_ref, bottom_ref, weight_ref, out_ref, held_ref):
    count, rows, cols, channels = cells_ref.shape
    step = pl.program_id(0)
    block = 16

    @pl.when(step == 0)
    def _():
        held_ref[:, :1] = top_ref[...]
        held_ref[:, 1 : rows + 1] = cells_ref[...]
        held_ref[:, rows + 1 :] = bottom_ref[...]

    for which in range(3):

        @pl.when(step == which)
        def _():
            for frame in range(count):
                for row in range(0, rows, block):
                    taps = [
                        held_ref[frame, row + tap : row + tap + block].reshape(-1, channels)
                        for tap in range(3)
                    ]
                    product = jnp.dot(
                        jnp.concatenate(taps, axis=1),
                        weight_ref[...].reshape(3 * channels, -1),
                        preferred_element_type=jnp.float32,
                    ).reshape(block, cols, -1)
                    product = shifted(product, which)
                    here = (frame, slice(row, row + block))
                    if which == 0:
                        out_ref[here] = product
                    else:
                        out_ref[here] += product


def conv_tile(cells, top, bottom, weight):
    count, rows, cols, channels = cells.shape
    outs = weight.shape[-1]
    return pl.pallas_call(
        tile_kernel,
        grid=(3,),
        in_specs=[
            WHOLE,
            WHOLE,
            WHOLE,
            pl.BlockSpec((3, 1, channels, outs), lambda step: (0, (step + 1) % 3, 0, 0)),
        ],
        out_specs=pl.BlockSpec((count, rows, cols, outs), lambda step: (0, 0, 0, 0)),
        out_shape=jax.ShapeDtypeStruct((count, rows, cols, outs), jnp.float32),
        scratch_shapes=[pltpu.VMEM((count, rows + 2, cols, channels), cells.dtype)],
        compiler_params=pltpu.CompilerParams(vmem_limit_bytes=VMEM_LIMIT),
        cost_estimate=pl.CostEstimate(
            flops=18 * count * rows * cols * channels * outs,
            bytes_accessed=2 * weight.size + 6 * cells.size,
            transcendentals=0,
        ),
    )(cells, top, bottom, weight)


def add_column(total_ref, side_ref, weight_ref, out_ref):
    count, rows, cols, _ = total_ref.shape
    part = jnp.dot(
        side_ref[0],
        weight_ref[...].reshape(side_ref.shape[2], -1),
        preferred_element_type=jnp.float32,
    )
    part = part.reshape(count, rows, 1, -1)

    @pl.when(pl.program_id(0) == 0)
    def _():
        out_ref[...] = total_ref[...]
        out_ref[:, :, :1] += part

    @pl.when(pl.program_id(0) == 1)
    def _():
        out_ref[:, :, cols - 1 :] += part


def drive_kernel(total_ref, side_ref, weight_ref, decay_ref, out_ref, end_ref):
    add_column(total_ref, side_ref, weight_ref, out_ref)

    @pl.when(pl.program_id(0) == 1)
    def _():
        state = out_ref[0]
        for frame in range(1, out_ref.shape[0]):
            state = decay_ref[...] * state + out_ref[frame]
        end_ref[...] = state.astype(end_ref.dtype)


def result_kernel(total_ref, side_ref, weight_ref, out_ref, sum_ref):
    add_column(total_ref, side_ref, weight_ref, sum_ref)

    @pl.when(pl.program_id(0) == 1)
    def _():
        out_ref[...] = sum_ref[...].astype(out_ref.dtype)


def taps_of(left, right, rows):
    sides = jnp.stack([left, right])
    taps = [sides[:, :, tap : tap + rows] for tap in range(3)]
    taps = jnp.concatenate(taps, axis=-1)
    return taps.reshape(2, -1, taps.shape[-1])


def side_specs(total, sides, weight):
    return [
        WHOLE,
        pl.BlockSpec((1, *sides.shape[1:]), lambda step: (step, 0, 0)),
        pl.BlockSpec((3, 1, *weight.shape[2:]), lambda step: (0, 2 * step, 0, 0)),
    ]


def params():
    return pltpu.CompilerParams(vmem_limit_bytes=VMEM_LIMIT)


def finish_drive(total, sides, weight, decay):
    return pl.pallas_call(
        drive_kernel,
        grid=(2,),
        in_specs=[*side_specs(total, sides, weight), WHOLE],
        out_specs=[
            pl.BlockSpec(total.shape, lambda step: (0, 0, 0, 0)),
            pl.BlockSpec(total.shape[1:], lambda step: (0, 0, 0)),
        ],
        out_shape=[
            jax.ShapeDtypeStruct(total.shape, jnp.float32),
            jax.ShapeDtypeStruct(total.shape[1:], jnp.bfloat16),
        ],
        compiler_params=params(),
    )(total, sides, weight, decay)


def finish_result(total, sides, weight):
    return pl.pallas_call(
        result_kernel,
        grid=(2,),
        in_specs=side_specs(total, sides, weight),
        out_specs=pl.BlockSpec(total.shape, lambda step: (0, 0, 0, 0)),
        out_shape=jax.ShapeDtypeStruct(total.shape, jnp.bfloat16),
        scratch_shapes=[pltpu.VMEM(total.shape, jnp.float32)],
        compiler_params=params(),
    )(total, sides, weight)


def entry_kernel(ends_ref, carried_ref, out_ref):
    entry = jnp.zeros(ends_ref.shape[1:], jnp.float32)
    out_ref[0] = entry.astype(out_ref.dtype)
    for index in range(ends_ref.shape[0] - 1):
        entry = carried_ref[...] * entry + ends_ref[index].astype(jnp.float32)
        out_ref[index + 1] = entry.astype(out_ref.dtype)


def mixed_kernel(drive_ref, entry_ref, start_ref, reach_ref, decay_ref, scale_ref, out_ref):
    state = reach_ref[...] * start_ref[...] + entry_ref[...].astype(jnp.float32)
    for frame in range(drive_ref.shape[0]):
        state = decay_ref[...] * state + drive_ref[frame]
        out_ref[frame] = jax.nn.gelu(scale_ref[...] * state).astype(out_ref.dtype)


def mix(drive, entry, start, reach, decay, scale):
    count, rows, cols, channels = drive.shape
    block = 8
    lane = pl.BlockSpec((1, channels), lambda step: (0, 0))
    tile = pl.BlockSpec((block, cols, channels), lambda step: (step, 0, 0))
    tiles = pl.BlockSpec((count, block, cols, channels), lambda step: (0, step, 0, 0))
    return pl.pallas_call(
        mixed_kernel,
        grid=(rows // block,),
        in_specs=[tiles, tile, tile, lane, lane, lane],
        out_specs=tiles,
        out_shape=jax.ShapeDtypeStruct(drive.shape, jnp.bfloat16),
        compiler_params=params(),
    )(drive, entry, start, reach, decay, scale)


def on_device(frames, input_weight, output_weight, pole_index, gelu_scale, start_state):
    count, rows, cols, channels = frames.shape
    groups = lax.axis_size("tm")
    position = lax.axis_index("tm")
    rate = -0.001 * jnp.exp(pole_index.astype(jnp.float32) * (math.log(300.0) / (NPOLES - 1)))
    rate = rate[None]
    decay = jnp.exp(rate)

    top, bottom, left, right = halos(frames)
    total = conv_tile(frames, top, bottom, input_weight)
    drive, end = finish_drive(total, taps_of(left, right, rows), input_weight, decay)

    ends = lax.all_to_all(end.reshape(groups, -1, channels), "tm", 0, 0)
    entries = pl.pallas_call(
        entry_kernel,
        in_specs=[WHOLE, WHOLE],
        out_specs=WHOLE,
        out_shape=jax.ShapeDtypeStruct(ends.shape, ends.dtype),
        compiler_params=params(),
    )(ends, jnp.exp(count * rate))
    entry = lax.all_to_all(entries, "tm", 0, 0).reshape(rows, cols, channels)

    reach = jnp.exp((count * position).astype(jnp.float32) * rate)
    mixed = mix(drive, entry, start_state, reach, decay, gelu_scale[None])

    top, bottom, left, right = halos(mixed)
    total = conv_tile(mixed, top, bottom, output_weight)
    return finish_result(total, taps_of(left, right, rows), output_weight)


def solution(mesh):
    return jax.shard_map(
        on_device,
        mesh=mesh,
        in_specs=(P("tm", "sx", "sy", None), P(), P(), P(), P(), P("sx", "sy", None)),
        out_specs=P("tm", "sx", "sy", None),
        check_vma=False,
    )
```

```python
import math

import jax
import jax.numpy as jnp
from jax import lax
from jax.experimental import pallas as pl
from jax.experimental.pallas import tpu as pltpu
from jax.sharding import PartitionSpec as P

NPOLES = 16
VMEM_LIMIT = 24 * 1024 * 1024
WHOLE = pl.BlockSpec(memory_space=pltpu.VMEM)
LANES = 256


def call(kernel, out_shape, *args, scratch=(), flops=0):
    outs = jax.tree.leaves(out_shape)
    moved = sum(leaf.size * leaf.dtype.itemsize for leaf in (*args, *outs))
    return pl.pallas_call(
        kernel,
        in_specs=[WHOLE] * len(args),
        out_specs=jax.tree.map(lambda _: WHOLE, out_shape),
        out_shape=out_shape,
        scratch_shapes=scratch,
        compiler_params=pltpu.CompilerParams(vmem_limit_bytes=VMEM_LIMIT),
        cost_estimate=pl.CostEstimate(flops=flops, bytes_accessed=moved, transcendentals=0),
    )(*args)


def is_core(which):
    return (lax.axis_index("sx") == which).astype(jnp.float32)


def rate_of(pole_ref):
    pole = pole_ref[...].astype(jnp.float32)
    return -0.001 * jnp.exp(pole * (math.log(300.0) / (NPOLES - 1)))


def put_edges(frame, tile, give_ref, keep_ref):
    rows, cols, _ = tile.shape
    zero, one = is_core(0), is_core(1)
    left, right = tile[:, 0, :], tile[:, cols - 1, :]
    give_ref[frame, :cols] = (zero * tile[rows - 1] + one * tile[0]).astype(give_ref.dtype)
    give_ref[frame, cols:] = (zero * right + one * left).astype(give_ref.dtype)
    keep_ref[frame] = (zero * left + one * right).astype(keep_ref.dtype)


def edges_kernel(cells_ref, give_ref, keep_ref):
    for frame in range(cells_ref.shape[0]):
        put_edges(frame, cells_ref[frame].astype(jnp.float32), give_ref, keep_ref)


def edge_shapes(cells):
    count, rows, cols, channels = cells.shape
    return (
        jax.ShapeDtypeStruct((count, cols + rows, channels), jnp.bfloat16),
        jax.ShapeDtypeStruct((count, rows, channels), jnp.bfloat16),
    )


def swap_cores(array):
    return lax.ppermute(array, "sx", [(0, 1), (1, 0)])


def trade_columns(give, keep, cols):
    chips = lax.axis_size("sy")
    got = swap_cores(give)
    pairs = [(chip, chips + chip - 1) for chip in range(1, chips)]
    pairs += [(after, before) for before, after in pairs]
    column = jnp.concatenate([keep, got[:, cols:]], axis=1)
    return got, lax.ppermute(column, ("sx", "sy"), pairs)


def fill(lhs_ref, frame, at, cells_ref, got_ref):
    _, rows, cols, channels = cells_ref.shape
    size = rows * cols
    row = got_ref[frame, :cols].astype(jnp.float32)
    above = (is_core(1) * row).astype(lhs_ref.dtype)
    below = (is_core(0) * row).astype(lhs_ref.dtype)
    cells = cells_ref[frame].reshape(size, channels)
    mid, low = slice(channels, 2 * channels), slice(2 * channels, 3 * channels)
    lhs_ref[frame, at : at + cols, :channels] = above
    lhs_ref[frame, at + cols : at + size, :channels] = cells[: size - cols]
    lhs_ref[frame, at : at + size, mid] = cells
    lhs_ref[frame, at : at + size - cols, low] = cells[cols:]
    lhs_ref[frame, at + size - cols : at + size, low] = below


def centre_kernel(cells_ref, got_ref, weight_ref, total_ref, lhs_ref):
    count, rows, cols, channels = cells_ref.shape
    for frame in range(count):
        fill(lhs_ref, frame, 0, cells_ref, got_ref)
    for lane in range(0, weight_ref.shape[-1], LANES):
        lanes = slice(lane, lane + LANES)
        weight = weight_ref[:, 1, :, lanes].reshape(3 * channels, LANES)
        for frame in range(count):
            total = jnp.dot(lhs_ref[frame], weight, preferred_element_type=jnp.float32)
            total_ref[frame, :, :, lanes] = total.reshape(rows, cols, LANES)


def centre(cells, got, weight):
    count, rows, cols, channels = cells.shape
    outs = weight.shape[-1]
    return call(
        centre_kernel,
        jax.ShapeDtypeStruct((count, rows, cols, outs), jnp.float32),
        cells,
        got,
        weight,
        scratch=[pltpu.VMEM((count, rows * cols, 3 * channels), cells.dtype)],
        flops=6 * count * rows * cols * channels * outs,
    )


def row_taps(mid, above, below):
    rows = mid.shape[0]
    row = lax.broadcasted_iota(jnp.int32, mid.shape, 0)
    up = jnp.where(row == 0, above, pltpu.roll(mid, 1, 0))
    down = jnp.where(row == rows - 1, below, pltpu.roll(mid, rows - 1, 0))
    return jnp.concatenate([up, mid, down], axis=1)


def fill_sides(lhs_ref, frame, rows, mine_ref, theirs_ref):
    zero, one = is_core(0), is_core(1)
    mine = mine_ref[frame].astype(jnp.float32)
    theirs = theirs_ref[frame].astype(jnp.float32)
    mine = row_taps(mine[rows:], one * mine[rows - 1 : rows], zero * mine[:1])
    theirs = row_taps(
        theirs[:rows], one * theirs[2 * rows - 1 :], zero * theirs[rows : rows + 1]
    )
    lhs_ref[frame, :rows] = (zero * mine + one * theirs).astype(lhs_ref.dtype)
    lhs_ref[frame, lhs_ref.shape[1] - rows :] = (zero * theirs + one * mine).astype(lhs_ref.dtype)


def outer_taps(cells_ref, got_ref, mine_ref, theirs_ref, weight_ref, total_ref, lhs_ref, finish):
    count, rows, cols, channels = cells_ref.shape
    size = rows * cols
    for frame in range(count):
        fill(lhs_ref, frame, rows, cells_ref, got_ref)
        fill_sides(lhs_ref, frame, rows, mine_ref, theirs_ref)
    col = lax.broadcasted_iota(jnp.int32, (rows, cols, LANES), 1)
    for lane in range(0, weight_ref.shape[-1], LANES):
        lanes = slice(lane, lane + LANES)
        first = weight_ref[:, 0, :, lanes].reshape(3 * channels, LANES)
        last = weight_ref[:, 2, :, lanes].reshape(3 * channels, LANES)
        totals = []
        for frame in range(count):
            before = jnp.dot(
                lhs_ref[frame, : rows + size], first, preferred_element_type=jnp.float32
            )
            after = jnp.dot(lhs_ref[frame, rows:], last, preferred_element_type=jnp.float32)
            side, before = before[:rows], before[rows:].reshape(rows, cols, LANES)
            total = total_ref[frame, :, :, lanes]
            total += jnp.where(col == 0, side.reshape(rows, 1, LANES), pltpu.roll(before, 1, 1))
            side, after = after[size:], after[:size].reshape(rows, cols, LANES)
            total += jnp.where(
                col == cols - 1, side.reshape(rows, 1, LANES), pltpu.roll(after, cols - 1, 1)
            )
            totals.append(total)
        finish(lanes, totals)


def drive_kernel(
    cells_ref, got_ref, mine_ref, theirs_ref, weight_ref, total_ref, pole_ref, out_ref, end_ref, lhs_ref
):
    decay = jnp.exp(rate_of(pole_ref))

    def finish(lanes, totals):
        state = None
        for frame, total in enumerate(totals):
            out_ref[frame, :, :, lanes] = total
            state = total if state is None else decay[:, lanes] * state + total
        end_ref[:, :, lanes] = state.astype(end_ref.dtype)

    outer_taps(cells_ref, got_ref, mine_ref, theirs_ref, weight_ref, total_ref, lhs_ref, finish)


def result_kernel(
    cells_ref, got_ref, mine_ref, theirs_ref, weight_ref, total_ref, out_ref, lhs_ref
):
    def finish(lanes, totals):
        for frame, total in enumerate(totals):
            out_ref[frame, :, :, lanes] = total.astype(out_ref.dtype)

    outer_taps(cells_ref, got_ref, mine_ref, theirs_ref, weight_ref, total_ref, lhs_ref, finish)


def convolve(cells, give, keep, weight, kernel, out_shape, *more):
    count, rows, cols, channels = cells.shape
    got, mine = trade_columns(give, keep, cols)
    mine, total = lax.optimization_barrier((mine, centre(cells, got, weight)))
    return call(
        kernel,
        out_shape,
        cells,
        got,
        mine,
        swap_cores(mine),
        weight,
        total,
        *more,
        scratch=[pltpu.VMEM((count, rows * (cols + 2), 3 * channels), cells.dtype)],
        flops=12 * cells.size * weight.shape[-1],
    )


def entry_kernel(frames, ends_ref, pole_ref, out_ref):
    carried = jnp.exp(frames * rate_of(pole_ref))
    entry = jnp.zeros(ends_ref.shape[1:], jnp.float32)
    out_ref[0] = entry.astype(out_ref.dtype)
    for index in range(ends_ref.shape[0] - 1):
        entry = carried * entry + ends_ref[index].astype(jnp.float32)
        out_ref[index + 1] = entry.astype(out_ref.dtype)


def mixed_kernel(
    drive_ref, entry_ref, start_ref, pole_ref, scale_ref, out_ref, give_ref, keep_ref
):
    rate = rate_of(pole_ref)
    decay = jnp.exp(rate)
    count = drive_ref.shape[0]
    reach = jnp.exp((count * lax.axis_index("tm")).astype(jnp.float32) * rate)
    state = reach * start_ref[...] + entry_ref[...].astype(jnp.float32)
    for frame in range(count):
        state = decay * state + drive_ref[frame]
        mixed = jax.nn.gelu(scale_ref[...] * state)
        out_ref[frame] = mixed.astype(out_ref.dtype)
        put_edges(frame, mixed, give_ref, keep_ref)


def on_device(frames, input_weight, output_weight, pole_index, gelu_scale, start_state):
    count, rows, cols, channels = frames.shape
    groups = lax.axis_size("tm")
    assert lax.axis_size("sx") == 2
    pole = pole_index[None]

    give, keep = call(edges_kernel, edge_shapes(frames), frames)
    drive, end = convolve(
        frames,
        give,
        keep,
        input_weight,
        drive_kernel,
        (
            jax.ShapeDtypeStruct((count, rows, cols, channels), jnp.float32),
            jax.ShapeDtypeStruct((rows, cols, channels), jnp.bfloat16),
        ),
        pole,
    )

    ends = lax.all_to_all(end.reshape(groups, -1, channels), "tm", 0, 0)
    entries = call(
        lambda *refs: entry_kernel(count, *refs),
        jax.ShapeDtypeStruct(ends.shape, ends.dtype),
        ends,
        pole,
    )
    entry = lax.all_to_all(entries, "tm", 0, 0).reshape(rows, cols, channels)

    mixed, give, keep = call(
        mixed_kernel,
        (jax.ShapeDtypeStruct(frames.shape, jnp.bfloat16), *edge_shapes(frames)),
        drive,
        entry,
        start_state,
        pole,
        gelu_scale[None],
    )
    return convolve(
        mixed,
        give,
        keep,
        output_weight,
        result_kernel,
        jax.ShapeDtypeStruct(frames.shape, jnp.bfloat16),
    )


def solution(mesh):
    return jax.shard_map(
        on_device,
        mesh=mesh,
        in_specs=(P("tm", "sx", "sy", None), P(), P(), P(), P(), P("sx", "sy", None)),
        out_specs=P("tm", "sx", "sy", None),
        check_vma=False,
    )
```

```python
import math

import jax
import jax.numpy as jnp
from jax import lax
from jax.experimental import pallas as pl
from jax.experimental.pallas import tpu as pltpu
from jax.sharding import PartitionSpec as P

NPOLES = 16
VMEM_LIMIT = 24 * 1024 * 1024
WHOLE = pl.BlockSpec(memory_space=pltpu.VMEM)
HBM = pl.BlockSpec(memory_space=pltpu.HBM)
LANES = 256


def call(kernel, out_shape, *args, scratch=(), flops=0, out_specs=None, aliases=None):
    outs = jax.tree.leaves(out_shape)
    moved = sum(leaf.size * leaf.dtype.itemsize for leaf in (*args, *outs))
    return pl.pallas_call(
        kernel,
        in_specs=[WHOLE] * len(args),
        out_specs=out_specs or jax.tree.map(lambda _: WHOLE, out_shape),
        out_shape=out_shape,
        scratch_shapes=scratch,
        input_output_aliases=aliases or {},
        compiler_params=pltpu.CompilerParams(vmem_limit_bytes=VMEM_LIMIT),
        cost_estimate=pl.CostEstimate(flops=flops, bytes_accessed=moved, transcendentals=0),
    )(*args)


def is_core(which):
    return (lax.axis_index("sx") == which).astype(jnp.float32)


def rate_of(pole_ref):
    pole = pole_ref[...].astype(jnp.float32)
    return -0.001 * jnp.exp(pole * (math.log(300.0) / (NPOLES - 1)))


def put_edges(frame, row, left, right, give_ref, keep_ref):
    cols = row.shape[0]
    zero, one = is_core(0), is_core(1)
    give_ref[frame, :cols] = row.astype(give_ref.dtype)
    give_ref[frame, cols:] = (zero * right + one * left).astype(give_ref.dtype)
    keep_ref[frame] = (zero * left + one * right).astype(keep_ref.dtype)


def inner_row(rows):
    return jnp.where(lax.axis_index("sx") == 0, rows - 1, 0)


def edge_shapes(cells):
    count, rows, cols, channels = cells.shape
    return (
        jax.ShapeDtypeStruct((count, cols + rows, channels), jnp.bfloat16),
        jax.ShapeDtypeStruct((count, rows, channels), jnp.bfloat16),
    )


def edges_kernel(cells_ref, give_ref, keep_ref):
    count, rows, cols, _ = cells_ref.shape
    for frame in range(count):
        tile = cells_ref[frame].astype(jnp.float32)
        row = cells_ref[frame, inner_row(rows)]
        put_edges(frame, row, tile[:, 0, :], tile[:, cols - 1, :], give_ref, keep_ref)


def swap_cores(array):
    return lax.ppermute(array, "sx", [(0, 1), (1, 0)])


def trade_columns(give, keep, cols):
    chips = lax.axis_size("sy")
    got = swap_cores(give)
    pairs = [(chip, chips + chip - 1) for chip in range(1, chips)]
    pairs += [(after, before) for before, after in pairs]
    column = jnp.concatenate([keep, got[:, cols:]], axis=1)
    return got, lax.ppermute(column, ("sx", "sy"), pairs)


def centre_kernel(cells_ref, got_ref, weight_ref, total_ref, lhs_ref):
    count, rows, cols, channels = cells_ref.shape
    size = rows * cols
    room = count * rows
    tap = weight_ref.shape[1] // 2
    mid, low = slice(channels, 2 * channels), slice(2 * channels, 3 * channels)
    for frame in range(count):
        at = room + frame * size
        row = got_ref[frame, :cols].astype(jnp.float32)
        cells = cells_ref[frame].reshape(size, channels)
        lhs_ref[at : at + cols, :channels] = (is_core(1) * row).astype(lhs_ref.dtype)
        lhs_ref[at + cols : at + size, :channels] = cells[: size - cols]
        lhs_ref[at : at + size, mid] = cells
        lhs_ref[at : at + size - cols, low] = cells[cols:]
        lhs_ref[at + size - cols : at + size, low] = (is_core(0) * row).astype(lhs_ref.dtype)
    for lane in range(0, weight_ref.shape[-1], LANES):
        lanes = slice(lane, lane + LANES)
        weight = weight_ref[:, tap, :, lanes].reshape(3 * channels, LANES)
        total = jnp.dot(lhs_ref[room:], weight, preferred_element_type=jnp.float32)
        total_ref[:, :, :, lanes] = total.reshape(count, rows, cols, LANES)


def centre(cells, got, weight):
    count, rows, cols, channels = cells.shape
    outs = weight.shape[-1]
    return call(
        centre_kernel,
        (
            jax.ShapeDtypeStruct((count, rows, cols, outs), jnp.float32),
            jax.ShapeDtypeStruct((count * rows * (cols + 1), 3 * channels), cells.dtype),
        ),
        cells,
        got,
        weight,
        flops=6 * count * rows * cols * channels * outs,
    )


def outer_taps(mine, halo_ref, weight_ref, total_ref, lhs_ref, finish):
    count, rows, cols, _ = total_ref.shape
    room = count * rows
    zero, one = is_core(0), is_core(1)
    row = lax.broadcasted_iota(jnp.int32, (rows, halo_ref.shape[2]), 0)
    for frame in range(count):
        halo = halo_ref[frame].astype(jnp.float32)
        if mine:
            mid, above, below = halo[rows:], halo[rows - 1 : rows], halo[:1]
        else:
            mid, above, below = halo[:rows], halo[2 * rows - 1 :], halo[rows : rows + 1]
        up = jnp.where(row == 0, one * above, pltpu.roll(mid, 1, 0))
        down = jnp.where(row == rows - 1, zero * below, pltpu.roll(mid, rows - 1, 0))
        taps = jnp.concatenate([up, mid, down], axis=1)
        lhs_ref[frame * rows : (frame + 1) * rows] = taps.astype(lhs_ref.dtype)

    def side(column, shift, edge):
        col = lax.broadcasted_iota(jnp.int32, (count, rows, cols, LANES), 2)
        for lane in range(0, weight_ref.shape[-1], LANES):
            lanes = slice(lane, lane + LANES)
            weight = weight_ref[:, column, :, lanes].reshape(-1, LANES)
            product = jnp.dot(lhs_ref[...], weight, preferred_element_type=jnp.float32)
            halo = product[:room].reshape(count, rows, 1, LANES)
            product = pltpu.roll(product[room:].reshape(count, rows, cols, LANES), shift, 2)
            finish(lanes, total_ref[:, :, :, lanes] + jnp.where(col == edge, halo, product))

    pl.when(lax.axis_index("sx") == (0 if mine else 1))(lambda: side(0, 1, 0))
    pl.when(lax.axis_index("sx") == (1 if mine else 0))(
        lambda: side(weight_ref.shape[1] - 1, cols - 1, cols - 1)
    )


def own_kernel(halo_ref, weight_ref, total_ref, _, out_ref, lhs_ref):
    def finish(lanes, total):
        out_ref[:, :, :, lanes] = total

    outer_taps(True, halo_ref, weight_ref, total_ref, lhs_ref, finish)


def drive_kernel(halo_ref, weight_ref, total_ref, _, pole_ref, out_ref, end_ref, lhs_ref):
    decay = jnp.exp(rate_of(pole_ref))

    def finish(lanes, total):
        out_ref[:, :, :, lanes] = total
        state = total[0]
        for frame in range(1, total.shape[0]):
            state = decay[:, lanes] * state + total[frame]
        end_ref[:, :, lanes] = state.astype(end_ref.dtype)

    outer_taps(False, halo_ref, weight_ref, total_ref, lhs_ref, finish)


def result_kernel(halo_ref, weight_ref, total_ref, _, out_ref, lhs_ref, held_ref, sems):
    def store(lanes):
        return pltpu.make_async_copy(
            held_ref.at[:, :, :, lanes],
            out_ref.at[:, :, :, lanes],
            sems.at[lanes.start // LANES],
        )

    def finish(lanes, total):
        held_ref[:, :, :, lanes] = total.astype(held_ref.dtype)
        store(lanes).start()

    outer_taps(False, halo_ref, weight_ref, total_ref, lhs_ref, finish)
    for lane in range(0, held_ref.shape[-1], LANES):
        store(slice(lane, lane + LANES)).wait()


def convolve(cells, give, keep, weight, middle, kernel, out_shape, *more, out_specs, scratch=()):
    got, mine = trade_columns(give, keep, cells.shape[2])
    mine, (total, lhs) = lax.optimization_barrier((mine, centre(cells, got, middle)))
    theirs = swap_cores(mine)
    flops = 6 * cells.size * weight.shape[-1]
    held = jax.ShapeDtypeStruct(lhs.shape, lhs.dtype)
    total, lhs = call(
        own_kernel,
        (jax.ShapeDtypeStruct(total.shape, total.dtype), held),
        mine,
        weight,
        total,
        lhs,
        flops=flops,
        aliases={3: 1},
    )
    *outs, _ = call(
        kernel,
        (*out_shape, held),
        theirs,
        weight,
        total,
        lhs,
        *more,
        flops=flops,
        out_specs=(*out_specs, WHOLE),
        aliases={3: len(out_shape)},
        scratch=scratch,
    )
    return outs


def entry_kernel(frames, ends_ref, pole_ref, out_ref):
    carried = jnp.exp(frames * rate_of(pole_ref))
    entry = jnp.zeros(ends_ref.shape[1:], jnp.float32)
    out_ref[0] = entry.astype(out_ref.dtype)
    for index in range(ends_ref.shape[0] - 1):
        entry = carried * entry + ends_ref[index].astype(jnp.float32)
        out_ref[index + 1] = entry.astype(out_ref.dtype)


def activated(drives, entry, start, pole_ref, scale_ref):
    rate = rate_of(pole_ref)
    decay = jnp.exp(rate)
    reach = jnp.exp((len(drives) * lax.axis_index("tm")).astype(jnp.float32) * rate)
    state = reach * start + entry.astype(jnp.float32)
    for drive in drives:
        state = decay * state + drive
        yield jax.nn.gelu(scale_ref[...] * state)


def mixed_edges_kernel(
    drive_ref, entry_ref, start_ref, pole_ref, scale_ref, give_ref, keep_ref
):
    count, rows, cols, _ = drive_ref.shape
    inner = inner_row(rows)
    entry = entry_ref[...].astype(jnp.float32)

    def column(col):
        drives = [drive_ref[frame][:, col, :] for frame in range(count)]
        return activated(drives, entry[:, col, :], start_ref[...][:, col, :], pole_ref, scale_ref)

    drives = [drive_ref[frame, inner] for frame in range(count)]
    row = activated(drives, entry_ref[inner], start_ref[inner], pole_ref, scale_ref)
    edges = (row, column(0), column(cols - 1))
    for frame, (row, left, right) in enumerate(zip(*edges)):
        put_edges(frame, row, left, right, give_ref, keep_ref)


def mixed_kernel(drive_ref, entry_ref, start_ref, pole_ref, scale_ref, out_ref):
    count, rows, _, _ = drive_ref.shape
    block = 8
    for row in range(0, rows, block):
        here = slice(row, row + block)
        drives = [drive_ref[frame, here] for frame in range(count)]
        mixed = activated(drives, entry_ref[here], start_ref[here], pole_ref, scale_ref)
        for frame, tile in enumerate(mixed):
            out_ref[frame, here] = tile.astype(out_ref.dtype)


def on_device(frames, input_weight, output_weight, pole_index, gelu_scale, start_state):
    count, rows, cols, channels = frames.shape
    groups = lax.axis_size("tm")
    assert lax.axis_size("sx") == 2
    pole = pole_index[None]

    give, keep = call(edges_kernel, edge_shapes(frames), frames)
    middle = input_weight[:, 1:2]
    drive, end = convolve(
        frames,
        give,
        keep,
        input_weight,
        middle,
        drive_kernel,
        (
            jax.ShapeDtypeStruct((count, rows, cols, channels), jnp.float32),
            jax.ShapeDtypeStruct((rows, cols, channels), jnp.bfloat16),
        ),
        pole,
        out_specs=(WHOLE, WHOLE),
    )

    ends = lax.all_to_all(end.reshape(groups, -1, channels), "tm", 0, 0)
    entries = call(
        lambda *refs: entry_kernel(count, *refs),
        jax.ShapeDtypeStruct(ends.shape, ends.dtype),
        ends,
        pole,
    )
    entry = lax.all_to_all(entries, "tm", 0, 0).reshape(rows, cols, channels)

    states = (drive, entry, start_state, pole, gelu_scale[None])
    shape = jax.ShapeDtypeStruct(frames.shape, jnp.bfloat16)
    give, keep = call(mixed_edges_kernel, edge_shapes(frames), *states)
    mixed = call(mixed_kernel, shape, *states)
    (result,) = convolve(
        mixed,
        give,
        keep,
        output_weight,
        output_weight,
        result_kernel,
        (shape,),
        out_specs=(HBM,),
        scratch=[
            pltpu.VMEM(frames.shape, jnp.bfloat16),
            pltpu.SemaphoreType.DMA((channels // LANES,)),
        ],
    )
    return result


def solution(mesh):
    return jax.shard_map(
        on_device,
        mesh=mesh,
        in_specs=(P("tm", "sx", "sy", None), P(), P(), P(), P(), P("sx", "sy", None)),
        out_specs=P("tm", "sx", "sy", None),
        check_vma=False,
    )
```

```python
import math

import jax
import jax.numpy as jnp
from jax import lax
from jax.experimental import pallas as pl
from jax.experimental.pallas import tpu as pltpu
from jax.sharding import PartitionSpec as P

NPOLES = 16
VMEM_LIMIT = 24 * 1024 * 1024
WHOLE = pl.BlockSpec(memory_space=pltpu.VMEM)
HBM = pl.BlockSpec(memory_space=pltpu.HBM)
LANES = 256


def call(kernel, out_shape, *args, scratch=(), flops=0, out_specs=None, aliases=None):
    outs = jax.tree.leaves(out_shape)
    moved = sum(leaf.size * leaf.dtype.itemsize for leaf in (*args, *outs))
    return pl.pallas_call(
        kernel,
        in_specs=[WHOLE] * len(args),
        out_specs=out_specs or jax.tree.map(lambda _: WHOLE, out_shape),
        out_shape=out_shape,
        scratch_shapes=scratch,
        input_output_aliases=aliases or {},
        compiler_params=pltpu.CompilerParams(vmem_limit_bytes=VMEM_LIMIT),
        cost_estimate=pl.CostEstimate(flops=flops, bytes_accessed=moved, transcendentals=0),
    )(*args)


def of(shape, dtype):
    return jax.ShapeDtypeStruct(shape, dtype)


def is_core(which):
    return (lax.axis_index("sx") == which).astype(jnp.float32)


def rate_of(pole_ref):
    pole = pole_ref[...].astype(jnp.float32)
    return -0.001 * jnp.exp(pole * (math.log(300.0) / (NPOLES - 1)))


def inner_row(rows):
    return jnp.where(lax.axis_index("sx") == 0, rows - 1, 0)


def swap_cores(array):
    return lax.ppermute(array, "sx", [(0, 1), (1, 0)])


def put_columns(index, left, right, give_ref, keep_ref):
    zero, one = is_core(0), is_core(1)
    count, rows, _ = keep_ref.shape
    at = give_ref.shape[0] - (count - index) * rows
    give_ref[at : at + rows] = (zero * right + one * left).astype(give_ref.dtype)
    keep_ref[index] = (zero * left + one * right).astype(keep_ref.dtype)


def edges_kernel(cells_ref, give_ref, keep_ref):
    count, rows, cols, _ = cells_ref.shape
    for frame in range(count):
        give_ref[frame * cols : (frame + 1) * cols] = cells_ref[frame, inner_row(rows)]
        tile = cells_ref[frame].astype(jnp.float32)
        for depth in range(2):
            left, right = tile[:, depth, :], tile[:, cols - 1 - depth, :]
            put_columns(2 * frame + depth, left, right, give_ref, keep_ref)


def start_edges_kernel(start_ref, _, __, give_ref, keep_ref):
    cols = start_ref.shape[1]
    tile = start_ref[...]
    index = keep_ref.shape[0] - 1
    put_columns(index, tile[:, 0, :], tile[:, cols - 1, :], give_ref, keep_ref)


def trade_columns(give, keep, at):
    chips = lax.axis_size("sy")
    got = swap_cores(give)
    pairs = [(chip, chips + chip - 1) for chip in range(1, chips)]
    pairs += [(after, before) for before, after in pairs]
    columns = jnp.concatenate([keep, got[at:].reshape(keep.shape)], axis=1)
    return got, lax.ppermute(columns, ("sx", "sy"), pairs)


def fill(lhs_ref, at, cells_ref, frame, row):
    _, rows, cols, channels = cells_ref.shape
    size = rows * cols
    row = row.astype(jnp.float32)
    cells = cells_ref[frame].reshape(size, channels)
    mid, low = slice(channels, 2 * channels), slice(2 * channels, 3 * channels)
    lhs_ref[at : at + cols, :channels] = (is_core(1) * row).astype(lhs_ref.dtype)
    lhs_ref[at + cols : at + size, :channels] = cells[: size - cols]
    lhs_ref[at : at + size, mid] = cells
    lhs_ref[at : at + size - cols, low] = cells[cols:]
    lhs_ref[at + size - cols : at + size, low] = (is_core(0) * row).astype(lhs_ref.dtype)


def row_taps(column, above, below):
    rows = column.shape[0]
    row = lax.broadcasted_iota(jnp.int32, column.shape, 0)
    up = jnp.where(row == 0, is_core(1) * above, pltpu.roll(column, 1, 0))
    down = jnp.where(row == rows - 1, is_core(0) * below, pltpu.roll(column, rows - 1, 0))
    return jnp.concatenate([up, column, down], axis=1)


def dot(lhs, weight_ref, column, lanes):
    weight = weight_ref[:, column, :, lanes].reshape(lhs.shape[1], -1)
    return jnp.dot(lhs, weight, preferred_element_type=jnp.float32)


def main_kernel(cells_ref, got_ref, weight_ref, total_ref, spill_ref, lhs_ref):
    count, rows, cols, _ = cells_ref.shape
    size = rows * cols
    for frame in range(count):
        fill(lhs_ref, frame * size, cells_ref, frame, got_ref[frame * cols : (frame + 1) * cols])
    tile = (count, rows, cols, LANES)
    col = lax.broadcasted_iota(jnp.int32, tile, 2)
    for lane in range(0, weight_ref.shape[-1], LANES):
        lanes = slice(lane, lane + LANES)
        total = dot(lhs_ref[...], weight_ref, 1, lanes).reshape(tile)
        first = dot(lhs_ref[...], weight_ref, 0, lanes).reshape(tile)
        spill_ref[1, :, lanes] = first[:, :, cols - 1, :].reshape(count * rows, LANES)
        total += jnp.where(col == 0, 0.0, pltpu.roll(first, 1, 2))
        last = dot(lhs_ref[...], weight_ref, 2, lanes).reshape(tile)
        spill_ref[0, :, lanes] = last[:, :, 0, :].reshape(count * rows, LANES)
        total_ref[:, :, :, lanes] = total + jnp.where(
            col == cols - 1, 0.0, pltpu.roll(last, cols - 1, 2)
        )


def drive_kernel(
    mine_ref, theirs_ref, weight_ref, total_ref, spill_ref, pole_ref,
    drive_ref, beside_ref, end_ref, start_ref, lhs_ref,
):
    count, rows, cols, _ = total_ref.shape
    room = count * rows
    zero, one = is_core(0), is_core(1)
    core = lax.axis_index("sx")
    slots = ((1, 0), (2, 3))
    for frame in range(count):
        for depth in range(2):
            own = mine_ref[2 * frame + depth].astype(jnp.float32)
            other = theirs_ref[2 * frame + depth].astype(jnp.float32)
            own = row_taps(own[rows:], own[rows - 1 : rows], own[:1])
            other = row_taps(other[:rows], other[2 * rows - 1 :], other[rows : rows + 1])
            for swapped, taps in enumerate((own, other)):
                slot = jnp.where(core == swapped, slots[0][depth], slots[1][depth])
                at = pl.multiple_of(slot * room + frame * rows, rows)
                lhs_ref[pl.ds(at, rows)] = taps.astype(lhs_ref.dtype)
    own = mine_ref[2 * count, rows:].astype(jnp.float32)
    other = theirs_ref[2 * count, :rows].astype(jnp.float32)
    start_ref[:rows] = zero * own + one * other
    start_ref[rows:] = zero * other + one * own

    decay = jnp.exp(rate_of(pole_ref))
    tile = (count, rows, cols, LANES)
    col = lax.broadcasted_iota(jnp.int32, tile, 2)
    for lane in range(0, weight_ref.shape[-1], LANES):
        lanes = slice(lane, lane + LANES)
        first = dot(lhs_ref[: 2 * room], weight_ref, 0, lanes)
        middle = dot(lhs_ref[room : 3 * room], weight_ref, 1, lanes)
        last = dot(lhs_ref[2 * room :], weight_ref, 2, lanes)
        left = (spill_ref[0, :, lanes] + first[:room] + middle[:room]).reshape(count, rows, LANES)
        right = (spill_ref[1, :, lanes] + middle[room:] + last[room:]).reshape(count, rows, LANES)
        near = first[room:].reshape(count, rows, 1, LANES)
        total = total_ref[:, :, :, lanes] + jnp.where(col == 0, near, 0.0)
        near = last[:room].reshape(count, rows, 1, LANES)
        total += jnp.where(col == cols - 1, near, 0.0)
        drive_ref[:, :, :, lanes] = total
        beside_ref[:, :rows, lanes] = left
        beside_ref[:, rows:, lanes] = right
        state, left_state, right_state = total[0], left[0], right[0]
        for frame in range(1, count):
            state = decay[:, lanes] * state + total[frame]
            left_state = decay[:, lanes] * left_state + left[frame]
            right_state = decay[:, lanes] * right_state + right[frame]
        size = rows * cols
        end_ref[:size, lanes] = state.reshape(size, LANES).astype(end_ref.dtype)
        end_ref[size : size + rows, lanes] = left_state.astype(end_ref.dtype)
        end_ref[size + rows :, lanes] = right_state.astype(end_ref.dtype)


def entry_kernel(frames, ends_ref, pole_ref, out_ref):
    carried = jnp.exp(frames * rate_of(pole_ref))
    entry = jnp.zeros(ends_ref.shape[1:], jnp.float32)
    out_ref[0] = entry.astype(out_ref.dtype)
    for index in range(ends_ref.shape[0] - 1):
        entry = carried * entry + ends_ref[index].astype(jnp.float32)
        out_ref[index + 1] = entry.astype(out_ref.dtype)


def activated(drives, entry, start, pole_ref, scale_ref):
    rate = rate_of(pole_ref)
    decay = jnp.exp(rate)
    reach = jnp.exp((len(drives) * lax.axis_index("tm")).astype(jnp.float32) * rate)
    state = reach * start + entry.astype(jnp.float32)
    for drive in drives:
        state = decay * state + drive
        yield jax.nn.gelu(scale_ref[...] * state)


def beside_kernel(
    drive_ref, beside_ref, entry_ref, start_ref, sides_ref, pole_ref, scale_ref, give_ref, out_ref
):
    count, rows, cols, channels = drive_ref.shape
    size = rows * cols
    inner = inner_row(rows)
    at = pl.multiple_of(inner * cols, cols)
    chip, chips = lax.axis_index("sy"), lax.axis_size("sy")
    row = lax.broadcasted_iota(jnp.int32, (2 * rows, channels), 0)
    side = jnp.where(row < rows, (chip > 0).astype(jnp.float32), (chip < chips - 1).astype(jnp.float32))
    beside = activated(
        [beside_ref[frame] for frame in range(count)],
        entry_ref[size:],
        sides_ref[...],
        pole_ref,
        scale_ref,
    )
    tile = activated(
        [drive_ref[frame, inner] for frame in range(count)],
        entry_ref[pl.ds(at, cols)],
        start_ref[inner],
        pole_ref,
        scale_ref,
    )
    zero, one = is_core(0), is_core(1)
    for frame, (cells, mixed) in enumerate(zip(tile, beside)):
        mixed = side * mixed
        out_ref[frame] = mixed.astype(out_ref.dtype)
        give_ref[frame, :cols] = cells.astype(give_ref.dtype)
        left = zero * mixed[rows - 1 : rows] + one * mixed[:1]
        right = zero * mixed[2 * rows - 1 :] + one * mixed[rows : rows + 1]
        which = lax.broadcasted_iota(jnp.int32, (cols, channels), 0)
        ends = jnp.where(which == 0, left, right)
        give_ref[frame, cols:] = ends.astype(give_ref.dtype)


def mixed_kernel(drive_ref, entry_ref, start_ref, pole_ref, scale_ref, out_ref):
    count, rows, cols, channels = drive_ref.shape
    block = 8
    for row in range(0, rows, block):
        here = slice(row, row + block)
        drives = [drive_ref[frame, here] for frame in range(count)]
        entry = entry_ref[row * cols : (row + block) * cols].reshape(block, cols, channels)
        mixed = activated(drives, entry, start_ref[here], pole_ref, scale_ref)
        for frame, tile in enumerate(mixed):
            out_ref[frame, here] = tile.astype(out_ref.dtype)


def result_kernel(cells_ref, got_ref, beside_ref, weight_ref, out_ref, lhs_ref, held_ref, sems):
    count, rows, cols, _ = cells_ref.shape
    size, room = rows * cols, count * rows
    for frame in range(count):
        fill(lhs_ref, room + frame * size, cells_ref, frame, got_ref[frame, :cols])
        ends = got_ref[frame, cols:].astype(jnp.float32)
        beside = beside_ref[frame].astype(jnp.float32)
        for side, at in enumerate((0, room + count * size)):
            column, end = beside[side * rows : (side + 1) * rows], ends[side : side + 1]
            here = slice(at + frame * rows, at + (frame + 1) * rows)
            lhs_ref[here] = row_taps(column, end, end).astype(lhs_ref.dtype)

    def store(lanes):
        return pltpu.make_async_copy(
            held_ref.at[:, :, :, lanes],
            out_ref.at[:, :, :, lanes],
            sems.at[lanes.start // LANES],
        )

    inner = count * size
    tile = (count, rows, cols, LANES)
    col = lax.broadcasted_iota(jnp.int32, tile, 2)
    for lane in range(0, weight_ref.shape[-1], LANES):
        lanes = slice(lane, lane + LANES)
        total = dot(lhs_ref[room : room + inner], weight_ref, 1, lanes).reshape(tile)
        first = dot(lhs_ref[: room + inner], weight_ref, 0, lanes)
        halo = first[:room].reshape(count, rows, 1, LANES)
        total += jnp.where(col == 0, halo, pltpu.roll(first[room:].reshape(tile), 1, 2))
        last = dot(lhs_ref[room:], weight_ref, 2, lanes)
        halo = last[inner:].reshape(count, rows, 1, LANES)
        total += jnp.where(
            col == cols - 1, halo, pltpu.roll(last[:inner].reshape(tile), cols - 1, 2)
        )
        held_ref[:, :, :, lanes] = total.astype(held_ref.dtype)
        store(lanes).start()
    for lane in range(0, weight_ref.shape[-1], LANES):
        store(slice(lane, lane + LANES)).wait()


def on_device(frames, input_weight, output_weight, pole_index, gelu_scale, start_state):
    count, rows, cols, channels = frames.shape
    size, room = rows * cols, count * rows
    wide = 3 * channels
    groups = lax.axis_size("tm")
    assert lax.axis_size("sx") == 2
    narrow = frames.dtype
    pole, scale = pole_index[None], gelu_scale[None]

    shapes = (
        of((count * cols + (2 * count + 1) * rows, channels), narrow),
        of((2 * count + 1, rows, channels), narrow),
    )
    edges = call(edges_kernel, shapes, frames, flops=2000000000)
    give, keep = call(start_edges_kernel, shapes, start_state, *edges, aliases={1: 0, 2: 1})
    got, mine = trade_columns(give, keep, count * cols)
    main = call(
        main_kernel,
        (of(frames.shape, jnp.float32), of((2, room, channels), jnp.float32)),
        frames,
        got,
        input_weight,
        scratch=[pltpu.VMEM((count * size, wide), narrow)],
        flops=18 * frames.size * channels,
    )
    mine, (total, spill) = lax.optimization_barrier((mine, main))
    drive, beside, end, sides = call(
        drive_kernel,
        (
            of(frames.shape, jnp.float32),
            of((count, 2 * rows, channels), jnp.float32),
            of((size + 2 * rows, channels), narrow),
            of((2 * rows, channels), jnp.float32),
        ),
        mine,
        swap_cores(mine),
        input_weight,
        total,
        spill,
        pole,
        scratch=[pltpu.VMEM((4 * room, wide), narrow)],
        flops=36 * room * channels * channels,
    )

    ends = lax.all_to_all(end.reshape(groups, -1, channels), "tm", 0, 0)
    entries = call(
        lambda *refs: entry_kernel(count, *refs), of(ends.shape, narrow), ends, pole
    )
    entry = lax.all_to_all(entries, "tm", 0, 0).reshape(end.shape)

    give, beside = call(
        beside_kernel,
        (of((count, 2 * cols, channels), narrow), of(beside.shape, narrow)),
        drive,
        beside,
        entry,
        start_state,
        sides,
        pole,
        scale,
    )
    got = swap_cores(give)
    mixed = call(mixed_kernel, of(frames.shape, narrow), drive, entry, start_state, pole, scale)
    return call(
        result_kernel,
        of(frames.shape, narrow),
        mixed,
        got,
        beside,
        output_weight,
        out_specs=HBM,
        scratch=[
            pltpu.VMEM((count * size + 2 * room, wide), narrow),
            pltpu.VMEM(frames.shape, narrow),
            pltpu.SemaphoreType.DMA((channels // LANES,)),
        ],
        flops=18 * frames.size * channels,
    )


def solution(mesh):
    return jax.shard_map(
        on_device,
        mesh=mesh,
        in_specs=(P("tm", "sx", "sy", None), P(), P(), P(), P(), P("sx", "sy", None)),
        out_specs=P("tm", "sx", "sy", None),
        check_vma=False,
    )
```

```python
import functools
import math

import jax
import jax.numpy as jnp
from jax import lax
from jax.experimental import pallas as pl
from jax.experimental.pallas import tpu as pltpu
from jax.sharding import PartitionSpec as P

NPOLES = 16
VMEM_LIMIT = 24 * 1024 * 1024
WHOLE = pl.BlockSpec(memory_space=pltpu.VMEM)
HBM = pl.BlockSpec(memory_space=pltpu.HBM)
LANES = 256
EDGES_COST = 2_000_000_000


def call(kernel, out_shape, *args, scratch=(), flops=0, out_specs=None, aliases=None):
    outs = jax.tree.leaves(out_shape)
    moved = sum(leaf.size * leaf.dtype.itemsize for leaf in (*args, *outs))
    return pl.pallas_call(
        kernel,
        in_specs=[WHOLE] * len(args),
        out_specs=out_specs or jax.tree.map(lambda _: WHOLE, out_shape),
        out_shape=out_shape,
        scratch_shapes=scratch,
        input_output_aliases=aliases or {},
        compiler_params=pltpu.CompilerParams(vmem_limit_bytes=VMEM_LIMIT),
        cost_estimate=pl.CostEstimate(flops=flops, bytes_accessed=moved, transcendentals=0),
    )(*args)


def of(shape, dtype):
    return jax.ShapeDtypeStruct(shape, dtype)


def is_core(which):
    return (lax.axis_index("sx") == which).astype(jnp.float32)


def rate_of(pole_ref):
    pole = pole_ref[...].astype(jnp.float32)
    return -0.001 * jnp.exp(pole * (math.log(300.0) / (NPOLES - 1)))


def inner_row(rows):
    return jnp.where(lax.axis_index("sx") == 0, rows - 1, 0)


def swap_cores(array):
    return lax.ppermute(array, "sx", [(0, 1), (1, 0)])


def put_columns(index, left, right, give_ref, keep_ref):
    zero, one = is_core(0), is_core(1)
    count, rows, _ = keep_ref.shape
    at = give_ref.shape[0] - (count - index) * rows
    give_ref[at : at + rows] = (zero * right + one * left).astype(give_ref.dtype)
    keep_ref[index] = (zero * left + one * right).astype(keep_ref.dtype)


def edges_kernel(cells_ref, give_ref, keep_ref, wide_ref):
    count, rows, cols, channels = cells_ref.shape
    for frame in range(count):
        give_ref[frame * cols : (frame + 1) * cols] = cells_ref[frame, inner_row(rows)]
        tile = cells_ref[frame].reshape(rows * cols, channels).astype(jnp.float32)
        lanes = wide_ref.shape[-1]
        for part in range(channels // lanes):
            wide_ref[frame, part] = tile[:, part * lanes : (part + 1) * lanes]

        def column(col):
            parts = [
                wide_ref[frame, part, pl.ds(col, rows, stride=cols), :]
                for part in range(channels // lanes)
            ]
            return jnp.concatenate(parts, axis=1)

        for depth in range(2):
            left, right = column(depth), column(cols - 1 - depth)
            put_columns(2 * frame + depth, left, right, give_ref, keep_ref)


def start_edges_kernel(start_ref, _, __, give_ref, keep_ref):
    tile, cols = start_ref[...], start_ref.shape[1]
    index = keep_ref.shape[0] - 1
    put_columns(index, tile[:, 0, :], tile[:, cols - 1, :], give_ref, keep_ref)


def trade_columns(give, keep, at):
    chips = lax.axis_size("sy")
    got = swap_cores(give)
    pairs = [(chip, chips + chip - 1) for chip in range(1, chips)]
    pairs += [(after, before) for before, after in pairs]
    columns = jnp.concatenate([keep, got[at:].reshape(keep.shape)], axis=1)
    return got, lax.ppermute(columns, ("sx", "sy"), pairs)


def fill(lhs_ref, at, cells_ref, frame, row):
    _, rows, cols, channels = cells_ref.shape
    size = rows * cols
    row = row.astype(jnp.float32)
    cells = cells_ref[frame].reshape(size, channels)
    mid, low = slice(channels, 2 * channels), slice(2 * channels, 3 * channels)
    lhs_ref[at : at + cols, :channels] = (is_core(1) * row).astype(lhs_ref.dtype)
    lhs_ref[at + cols : at + size, :channels] = cells[: size - cols]
    lhs_ref[at : at + size, mid] = cells
    lhs_ref[at : at + size - cols, low] = cells[cols:]
    lhs_ref[at + size - cols : at + size, low] = (is_core(0) * row).astype(lhs_ref.dtype)


def row_taps(column, above, below):
    rows = column.shape[0]
    row = lax.broadcasted_iota(jnp.int32, column.shape, 0)
    up = jnp.where(row == 0, is_core(1) * above, pltpu.roll(column, 1, 0))
    down = jnp.where(row == rows - 1, is_core(0) * below, pltpu.roll(column, rows - 1, 0))
    return jnp.concatenate([up, column, down], axis=1)


def dot(lhs, weight_ref, column, lanes):
    weight = weight_ref[:, column, :, lanes].reshape(lhs.shape[1], -1)
    return jnp.dot(lhs, weight, preferred_element_type=jnp.float32)


def main_kernel(cells_ref, got_ref, weight_ref, total_ref, spill_ref, lhs_ref):
    count, rows, cols, _ = cells_ref.shape
    size = rows * cols
    for frame in range(count):
        fill(lhs_ref, frame * size, cells_ref, frame, got_ref[frame * cols : (frame + 1) * cols])
    tile = (count, rows, cols, LANES)
    col = lax.broadcasted_iota(jnp.int32, tile, 2)
    for lane in range(0, weight_ref.shape[-1], LANES):
        lanes = slice(lane, lane + LANES)
        total = dot(lhs_ref[...], weight_ref, 1, lanes).reshape(tile)
        first = dot(lhs_ref[...], weight_ref, 0, lanes).reshape(tile)
        spill_ref[1, :, lanes] = first[:, :, cols - 1, :].reshape(count * rows, LANES)
        total += jnp.where(col == 0, 0.0, pltpu.roll(first, 1, 2))
        last = dot(lhs_ref[...], weight_ref, 2, lanes).reshape(tile)
        spill_ref[0, :, lanes] = last[:, :, 0, :].reshape(count * rows, LANES)
        total_ref[:, :, :, lanes] = total + jnp.where(
            col == cols - 1, 0.0, pltpu.roll(last, cols - 1, 2)
        )


def drive_kernel(
    mine_ref, theirs_ref, weight_ref, total_ref, spill_ref, pole_ref,
    drive_ref, beside_ref, start_ref, *more_refs,
):
    count, rows, cols, _ = total_ref.shape
    room = count * rows
    *end_refs, lhs_ref = more_refs
    zero, one = is_core(0), is_core(1)
    core = lax.axis_index("sx")
    slots = ((1, 0), (2, 3))
    for frame in range(count):
        for depth in range(2):
            own = mine_ref[2 * frame + depth].astype(jnp.float32)
            other = theirs_ref[2 * frame + depth].astype(jnp.float32)
            own = row_taps(own[rows:], own[rows - 1 : rows], own[:1])
            other = row_taps(other[:rows], other[2 * rows - 1 :], other[rows : rows + 1])
            for swapped, taps in enumerate((own, other)):
                slot = jnp.where(core == swapped, slots[0][depth], slots[1][depth])
                at = pl.multiple_of(slot * room + frame * rows, rows)
                lhs_ref[pl.ds(at, rows)] = taps.astype(lhs_ref.dtype)
    own = mine_ref[2 * count, rows:].astype(jnp.float32)
    other = theirs_ref[2 * count, :rows].astype(jnp.float32)
    start_ref[:rows] = zero * own + one * other
    start_ref[rows:] = zero * other + one * own

    decay = jnp.exp(rate_of(pole_ref))
    tile = (count, rows, cols, LANES)
    col = lax.broadcasted_iota(jnp.int32, tile, 2)
    for lane in range(0, weight_ref.shape[-1], LANES):
        lanes = slice(lane, lane + LANES)
        first = dot(lhs_ref[: 2 * room], weight_ref, 0, lanes)
        middle = dot(lhs_ref[room : 3 * room], weight_ref, 1, lanes)
        last = dot(lhs_ref[2 * room :], weight_ref, 2, lanes)
        left = (spill_ref[0, :, lanes] + first[:room] + middle[:room]).reshape(count, rows, LANES)
        right = (spill_ref[1, :, lanes] + middle[room:] + last[room:]).reshape(count, rows, LANES)
        near = first[room:].reshape(count, rows, 1, LANES)
        total = total_ref[:, :, :, lanes] + jnp.where(col == 0, near, 0.0)
        near = last[:room].reshape(count, rows, 1, LANES)
        total += jnp.where(col == cols - 1, near, 0.0)
        drive_ref[:, :, :, lanes] = total
        beside_ref[:, :rows, lanes] = left
        beside_ref[:, rows:, lanes] = right
        state, left_state, right_state = total[0], left[0], right[0]
        for frame in range(1, count):
            state = decay[:, lanes] * state + total[frame]
            left_state = decay[:, lanes] * left_state + left[frame]
            right_state = decay[:, lanes] * right_state + right[frame]
        size = rows * cols
        end_ref = end_refs[lane // LANES]
        end_ref[:size] = state.reshape(size, LANES).astype(end_ref.dtype)
        end_ref[size : size + rows] = left_state.astype(end_ref.dtype)
        end_ref[size + rows :] = right_state.astype(end_ref.dtype)


def entry_kernel(frames, ends_ref, pole_ref, out_ref):
    carried = jnp.exp(frames * rate_of(pole_ref))
    entry = jnp.zeros(ends_ref.shape[1:], jnp.float32)
    out_ref[0] = entry.astype(out_ref.dtype)
    for index in range(ends_ref.shape[0] - 1):
        entry = carried * entry + ends_ref[index].astype(jnp.float32)
        out_ref[index + 1] = entry.astype(out_ref.dtype)


def exchange(ends, pole, frames):
    groups = lax.axis_size("tm")
    end = jnp.concatenate(ends, axis=1)
    shares = lax.all_to_all(end.reshape(groups, -1, end.shape[1]), "tm", 0, 0)
    entries = call(
        functools.partial(entry_kernel, frames), of(shares.shape, end.dtype), shares, pole
    )
    return lax.all_to_all(entries, "tm", 0, 0).reshape(end.shape)


def pick(values):
    group = lax.axis_index("tm")
    picked = values[-1]
    for index, value in enumerate(values[:-1]):
        picked = jnp.where(group == index, value, picked)
    return picked


def on_core(first, second):
    return jnp.where(lax.axis_index("sx") == 0, first, second)


def weigh(one, by_one, other, by_other):
    return by_one * one[...].astype(jnp.float32) + by_other * other[...].astype(jnp.float32)


def relay_kernel(frames, part, end_ref, got_ref, pole_ref, out_ref):
    rate = rate_of(pole_ref)[:, part * LANES : (part + 1) * LANES]
    carried, twice = jnp.exp(frames * rate), jnp.exp(2 * frames * rate)
    none, same = jnp.zeros_like(rate), jnp.ones_like(rate)
    own = on_core(pick([carried, same, same, same]), pick([same, same, same, none]))
    got = on_core(pick([same, carried, carried, carried]), pick([none, none, twice, same]))
    out_ref[...] = weigh(end_ref, own, got_ref, got).astype(out_ref.dtype)


def arrived_kernel(frames, parts, *refs):
    *got_refs, pole_ref, out_ref = refs
    rate = rate_of(pole_ref)
    carried = jnp.exp(frames * rate)
    none, same = jnp.zeros_like(rate), jnp.ones_like(rate)
    early = on_core(pick([none, same, none, same]), pick([none, none, carried, carried]))
    late = on_core(pick([none, none, same, carried]), pick([none, same, same, same]))
    for part in range(parts):
        lanes = slice(part * LANES, (part + 1) * LANES)
        first, second = got_refs[part], got_refs[parts + part]
        out_ref[:, lanes] = weigh(first, early[:, lanes], second, late[:, lanes])


def exchange_four(ends, pole, frames):
    def along(pairs, core):
        return [(2 * source + core, 2 * target + core) for source, target in pairs]

    axes = ("tm", "sx")
    down = [(0, 2), (1, 3)]
    first_round = along([(0, 1), (1, 0), (2, 3)], 0) + along(down, 1)
    second_round = along(down, 0) + along([(0, 1), (2, 3), (3, 2)], 1)
    got = [lax.ppermute(end, axes, first_round) for end in ends]
    relayed = [
        call(
            functools.partial(relay_kernel, frames, part),
            of(end.shape, end.dtype),
            end,
            here,
            pole,
        )
        for part, (end, here) in enumerate(zip(ends, got))
    ]
    last = [lax.ppermute(end, axes, second_round) for end in relayed]
    return call(
        functools.partial(arrived_kernel, frames, len(ends)),
        of((ends[0].shape[0], pole.shape[1]), jnp.float32),
        *got,
        *last,
        pole,
    )


def activated(drives, entry, start, pole_ref, scale_ref):
    rate = rate_of(pole_ref)
    decay = jnp.exp(rate)
    reach = jnp.exp((len(drives) * lax.axis_index("tm")).astype(jnp.float32) * rate)
    state = reach * start + entry.astype(jnp.float32)
    for drive in drives:
        state = decay * state + drive
        yield jax.nn.gelu(scale_ref[...] * state)


def beside_kernel(
    drive_ref, beside_ref, entry_ref, start_ref, sides_ref, pole_ref, scale_ref, give_ref, out_ref
):
    count, rows, cols, channels = drive_ref.shape
    size = rows * cols
    inner = inner_row(rows)
    at = pl.multiple_of(inner * cols, cols)
    chip, chips = lax.axis_index("sy"), lax.axis_size("sy")
    row = lax.broadcasted_iota(jnp.int32, (2 * rows, channels), 0)
    side = jnp.where(row < rows, (chip > 0).astype(jnp.float32), (chip < chips - 1).astype(jnp.float32))
    beside = activated(
        [beside_ref[frame] for frame in range(count)],
        entry_ref[size:],
        sides_ref[...],
        pole_ref,
        scale_ref,
    )
    tile = activated(
        [drive_ref[frame, inner] for frame in range(count)],
        entry_ref[pl.ds(at, cols)],
        start_ref[inner],
        pole_ref,
        scale_ref,
    )
    zero, one = is_core(0), is_core(1)
    for frame, (cells, mixed) in enumerate(zip(tile, beside)):
        mixed = side * mixed
        out_ref[frame] = mixed.astype(out_ref.dtype)
        give_ref[frame, :cols] = cells.astype(give_ref.dtype)
        left = zero * mixed[rows - 1 : rows] + one * mixed[:1]
        right = zero * mixed[2 * rows - 1 :] + one * mixed[rows : rows + 1]
        which = lax.broadcasted_iota(jnp.int32, (cols, channels), 0)
        ends = jnp.where(which == 0, left, right)
        give_ref[frame, cols:] = ends.astype(give_ref.dtype)


def mixed_kernel(drive_ref, entry_ref, start_ref, pole_ref, scale_ref, out_ref):
    count, rows, cols, channels = drive_ref.shape
    block = 8
    for row in range(0, rows, block):
        here = slice(row, row + block)
        drives = [drive_ref[frame, here] for frame in range(count)]
        entry = entry_ref[row * cols : (row + block) * cols].reshape(block, cols, channels)
        mixed = activated(drives, entry, start_ref[here], pole_ref, scale_ref)
        for frame, tile in enumerate(mixed):
            out_ref[frame, here] = tile.astype(out_ref.dtype)


def result_kernel(cells_ref, got_ref, beside_ref, weight_ref, out_ref, lhs_ref, held_ref, sems):
    count, rows, cols, _ = cells_ref.shape
    size, room = rows * cols, count * rows
    for frame in range(count):
        fill(lhs_ref, room + frame * size, cells_ref, frame, got_ref[frame, :cols])
        ends = got_ref[frame, cols:].astype(jnp.float32)
        beside = beside_ref[frame].astype(jnp.float32)
        for side, at in enumerate((0, room + count * size)):
            column, end = beside[side * rows : (side + 1) * rows], ends[side : side + 1]
            here = slice(at + frame * rows, at + (frame + 1) * rows)
            lhs_ref[here] = row_taps(column, end, end).astype(lhs_ref.dtype)

    def store(frame, lanes):
        return pltpu.make_async_copy(
            held_ref.at[frame, :, :, lanes],
            out_ref.at[frame, :, :, lanes],
            sems.at[frame, lanes.start // LANES],
        )

    inner = count * size
    tile = (count, rows, cols, LANES)
    col = lax.broadcasted_iota(jnp.int32, tile, 2)
    for lane in range(0, weight_ref.shape[-1], LANES):
        lanes = slice(lane, lane + LANES)
        total = dot(lhs_ref[room : room + inner], weight_ref, 1, lanes).reshape(tile)
        first = dot(lhs_ref[: room + inner], weight_ref, 0, lanes)
        halo = first[:room].reshape(count, rows, 1, LANES)
        total += jnp.where(col == 0, halo, pltpu.roll(first[room:].reshape(tile), 1, 2))
        last = dot(lhs_ref[room:], weight_ref, 2, lanes)
        halo = last[inner:].reshape(count, rows, 1, LANES)
        total += jnp.where(
            col == cols - 1, halo, pltpu.roll(last[:inner].reshape(tile), cols - 1, 2)
        )
        for frame in range(count):
            held_ref[frame, :, :, lanes] = total[frame].astype(held_ref.dtype)
            store(frame, lanes).start()
    for lane in range(0, weight_ref.shape[-1], LANES):
        for frame in range(count):
            store(frame, slice(lane, lane + LANES)).wait()


def on_device(frames, input_weight, output_weight, pole_index, gelu_scale, start_state):
    count, rows, cols, channels = frames.shape
    size, room = rows * cols, count * rows
    wide = 3 * channels
    assert lax.axis_size("sx") == 2
    narrow = frames.dtype
    pole, scale = pole_index[None], gelu_scale[None]

    shapes = (
        of((count * cols + (2 * count + 1) * rows, channels), narrow),
        of((2 * count + 1, rows, channels), narrow),
    )
    edges = call(
        edges_kernel,
        shapes,
        frames,
        scratch=[pltpu.VMEM((count, channels // 128, size, 128), jnp.float32)],
        flops=EDGES_COST,
    )
    give, keep = call(
        start_edges_kernel,
        shapes,
        start_state,
        *edges,
        aliases={1: 0, 2: 1},
    )
    got, mine = trade_columns(give, keep, count * cols)
    main = call(
        main_kernel,
        (of(frames.shape, jnp.float32), of((2, room, channels), jnp.float32)),
        frames,
        got,
        input_weight,
        scratch=[pltpu.VMEM((count * size, wide), narrow)],
        flops=18 * frames.size * channels,
    )
    mine, (total, spill) = lax.optimization_barrier((mine, main))
    parts = channels // LANES
    drive, beside, sides, *ends = call(
        drive_kernel,
        (
            of(frames.shape, jnp.float32),
            of((count, 2 * rows, channels), jnp.float32),
            of((2 * rows, channels), jnp.float32),
            *[of((size + 2 * rows, LANES), narrow)] * parts,
        ),
        mine,
        swap_cores(mine),
        input_weight,
        total,
        spill,
        pole,
        scratch=[pltpu.VMEM((4 * room, wide), narrow)],
        flops=36 * room * channels * channels,
    )
    entry = (exchange_four if lax.axis_size("tm") == 4 else exchange)(ends, pole, count)

    give, beside = call(
        beside_kernel,
        (of((count, 2 * cols, channels), narrow), of(beside.shape, narrow)),
        drive,
        beside,
        entry,
        start_state,
        sides,
        pole,
        scale,
    )
    got = swap_cores(give)
    mixed = call(mixed_kernel, of(frames.shape, narrow), drive, entry, start_state, pole, scale)
    return call(
        result_kernel,
        of(frames.shape, narrow),
        mixed,
        got,
        beside,
        output_weight,
        out_specs=HBM,
        scratch=[
            pltpu.VMEM((count * size + 2 * room, wide), narrow),
            pltpu.VMEM(frames.shape, narrow),
            pltpu.SemaphoreType.DMA((count, parts)),
        ],
        flops=18 * frames.size * channels,
    )


def solution(mesh):
    return jax.shard_map(
        on_device,
        mesh=mesh,
        in_specs=(P("tm", "sx", "sy", None), P(), P(), P(), P(), P("sx", "sy", None)),
        out_specs=P("tm", "sx", "sy", None),
        check_vma=False,
    )
```

```python
import functools
import math

import jax
import jax.numpy as jnp
from jax import lax
from jax.experimental import pallas as pl
from jax.experimental.pallas import tpu as pltpu
from jax.sharding import PartitionSpec as P

NPOLES = 16
VMEM_LIMIT = 24 * 1024 * 1024
WHOLE = pl.BlockSpec(memory_space=pltpu.VMEM)
HBM = pl.BlockSpec(memory_space=pltpu.HBM)
LANES = 256
EDGES_COST = 2_000_000_000


def call(kernel, out_shape, *args, scratch=(), flops=0, out_specs=None, aliases=None):
    outs = jax.tree.leaves(out_shape)
    moved = sum(leaf.size * leaf.dtype.itemsize for leaf in (*args, *outs))
    return pl.pallas_call(
        kernel,
        in_specs=[WHOLE] * len(args),
        out_specs=out_specs or jax.tree.map(lambda _: WHOLE, out_shape),
        out_shape=out_shape,
        scratch_shapes=scratch,
        input_output_aliases=aliases or {},
        compiler_params=pltpu.CompilerParams(vmem_limit_bytes=VMEM_LIMIT),
        cost_estimate=pl.CostEstimate(flops=flops, bytes_accessed=moved, transcendentals=0),
    )(*args)


def of(shape, dtype):
    return jax.ShapeDtypeStruct(shape, dtype)


def is_core(which):
    return (lax.axis_index("sx") == which).astype(jnp.float32)


def rate_of(pole_ref):
    pole = pole_ref[...].astype(jnp.float32)
    return -0.001 * jnp.exp(pole * (math.log(300.0) / (NPOLES - 1)))


def inner_row(rows):
    return jnp.where(lax.axis_index("sx") == 0, rows - 1, 0)


def swap_cores(array):
    return lax.ppermute(array, "sx", [(0, 1), (1, 0)])


def put_columns(index, left, right, give_ref, keep_ref):
    zero, one = is_core(0), is_core(1)
    count, rows, _ = keep_ref.shape
    at = give_ref.shape[0] - (count - index) * rows
    give_ref[at : at + rows] = (zero * right + one * left).astype(give_ref.dtype)
    keep_ref[index] = (zero * left + one * right).astype(keep_ref.dtype)


def edges_kernel(cells_ref, give_ref, keep_ref, wide_ref):
    count, rows, cols, channels = cells_ref.shape
    for frame in range(count):
        give_ref[frame * cols : (frame + 1) * cols] = cells_ref[frame, inner_row(rows)]
        tile = cells_ref[frame].reshape(rows * cols, channels).astype(jnp.float32)
        lanes = wide_ref.shape[-1]
        for part in range(channels // lanes):
            wide_ref[frame, part] = tile[:, part * lanes : (part + 1) * lanes]

        def column(col):
            parts = [
                wide_ref[frame, part, pl.ds(col, rows, stride=cols), :]
                for part in range(channels // lanes)
            ]
            return jnp.concatenate(parts, axis=1)

        for depth in range(2):
            left, right = column(depth), column(cols - 1 - depth)
            put_columns(2 * frame + depth, left, right, give_ref, keep_ref)


def start_edges_kernel(start_ref, _, __, give_ref, keep_ref):
    tile, cols = start_ref[...], start_ref.shape[1]
    index = keep_ref.shape[0] - 1
    put_columns(index, tile[:, 0, :], tile[:, cols - 1, :], give_ref, keep_ref)


def trade_columns(give, keep, at):
    chips = lax.axis_size("sy")
    got = swap_cores(give)
    pairs = [(chip, chips + chip - 1) for chip in range(1, chips)]
    pairs += [(after, before) for before, after in pairs]
    columns = jnp.concatenate([keep, got[at:].reshape(keep.shape)], axis=1)
    return got, lax.ppermute(columns, ("sx", "sy"), pairs)


def fill(lhs_ref, at, cells_ref, frame, row):
    _, rows, cols, channels = cells_ref.shape
    size = rows * cols
    row = row.astype(jnp.float32)
    cells = cells_ref[frame].reshape(size, channels)
    mid, low = slice(channels, 2 * channels), slice(2 * channels, 3 * channels)
    lhs_ref[at : at + cols, :channels] = (is_core(1) * row).astype(lhs_ref.dtype)
    lhs_ref[at + cols : at + size, :channels] = cells[: size - cols]
    lhs_ref[at : at + size, mid] = cells
    lhs_ref[at : at + size - cols, low] = cells[cols:]
    lhs_ref[at + size - cols : at + size, low] = (is_core(0) * row).astype(lhs_ref.dtype)


def row_taps(column, above, below):
    rows = column.shape[0]
    row = lax.broadcasted_iota(jnp.int32, column.shape, 0)
    up = jnp.where(row == 0, is_core(1) * above, pltpu.roll(column, 1, 0))
    down = jnp.where(row == rows - 1, is_core(0) * below, pltpu.roll(column, rows - 1, 0))
    return jnp.concatenate([up, column, down], axis=1)


def dot(lhs, weight_ref, column, lanes, inputs=slice(None)):
    weight = weight_ref[:, column, inputs, lanes].reshape(lhs.shape[1], -1)
    return jnp.dot(lhs, weight, preferred_element_type=jnp.float32)


def main_kernel(cells_ref, got_ref, weight_ref, total_ref, spill_ref, lhs_ref):
    count, rows, cols, _ = cells_ref.shape
    size = rows * cols
    for frame in range(count):
        fill(lhs_ref, frame * size, cells_ref, frame, got_ref[frame * cols : (frame + 1) * cols])
    tile = (count, rows, cols, LANES)
    col = lax.broadcasted_iota(jnp.int32, tile, 2)
    for lane in range(0, weight_ref.shape[-1], LANES):
        lanes = slice(lane, lane + LANES)
        total = dot(lhs_ref[...], weight_ref, 1, lanes).reshape(tile)
        first = dot(lhs_ref[...], weight_ref, 0, lanes).reshape(tile)
        spill_ref[1, :, lanes] = first[:, :, cols - 1, :].reshape(count * rows, LANES)
        total += jnp.where(col == 0, 0.0, pltpu.roll(first, 1, 2))
        last = dot(lhs_ref[...], weight_ref, 2, lanes).reshape(tile)
        spill_ref[0, :, lanes] = last[:, :, 0, :].reshape(count * rows, LANES)
        total_ref[:, :, :, lanes] = total + jnp.where(
            col == cols - 1, 0.0, pltpu.roll(last, cols - 1, 2)
        )


def halo_kernel(mine_ref, theirs_ref, lhs_ref, start_ref):
    rows = mine_ref.shape[1] // 2
    count = mine_ref.shape[0] // 2
    room = count * rows
    zero, one = is_core(0), is_core(1)
    core = lax.axis_index("sx")
    slots = ((1, 0), (2, 3))
    for frame in range(count):
        for depth in range(2):
            own = mine_ref[2 * frame + depth].astype(jnp.float32)
            other = theirs_ref[2 * frame + depth].astype(jnp.float32)
            own = row_taps(own[rows:], own[rows - 1 : rows], own[:1])
            other = row_taps(other[:rows], other[2 * rows - 1 :], other[rows : rows + 1])
            for swapped, taps in enumerate((own, other)):
                slot = jnp.where(core == swapped, slots[0][depth], slots[1][depth])
                at = pl.multiple_of(slot * room + frame * rows, rows)
                lhs_ref[pl.ds(at, rows)] = taps.astype(lhs_ref.dtype)
    own = mine_ref[2 * count, rows:].astype(jnp.float32)
    other = theirs_ref[2 * count, :rows].astype(jnp.float32)
    start_ref[:rows] = zero * own + one * other
    start_ref[rows:] = zero * other + one * own


def drive_kernel(
    lanes, lhs_ref, weight_ref, total_ref, spill_ref, pole_ref, drive_ref, beside_ref, end_ref
):
    count, rows, cols, wide = drive_ref.shape
    room, size = count * rows, rows * cols
    decay = jnp.exp(rate_of(pole_ref))[:, lanes]
    col = lax.broadcasted_iota(jnp.int32, drive_ref.shape, 2)
    first = dot(lhs_ref[: 2 * room], weight_ref, 0, lanes)
    middle = dot(lhs_ref[room : 3 * room], weight_ref, 1, lanes)
    last = dot(lhs_ref[2 * room :], weight_ref, 2, lanes)
    left = (spill_ref[0, :, lanes] + first[:room] + middle[:room]).reshape(count, rows, wide)
    right = (spill_ref[1, :, lanes] + middle[room:] + last[room:]).reshape(count, rows, wide)
    near = first[room:].reshape(count, rows, 1, wide)
    total = total_ref[:, :, :, lanes] + jnp.where(col == 0, near, 0.0)
    near = last[:room].reshape(count, rows, 1, wide)
    total += jnp.where(col == cols - 1, near, 0.0)
    drive_ref[...] = total
    beside_ref[:, :rows] = left
    beside_ref[:, rows:] = right
    state, left_state, right_state = total[0], left[0], right[0]
    for frame in range(1, count):
        state = decay * state + total[frame]
        left_state = decay * left_state + left[frame]
        right_state = decay * right_state + right[frame]
    end_ref[:size] = state.reshape(size, wide).astype(end_ref.dtype)
    end_ref[size : size + rows] = left_state.astype(end_ref.dtype)
    end_ref[size + rows :] = right_state.astype(end_ref.dtype)


def entry_kernel(frames, ends_ref, pole_ref, out_ref):
    carried = jnp.exp(frames * rate_of(pole_ref))
    entry = jnp.zeros(ends_ref.shape[1:], jnp.float32)
    out_ref[0] = entry.astype(out_ref.dtype)
    for index in range(ends_ref.shape[0] - 1):
        entry = carried * entry + ends_ref[index].astype(jnp.float32)
        out_ref[index + 1] = entry.astype(out_ref.dtype)


def exchange(ends, pole, frames):
    groups = lax.axis_size("tm")
    end = jnp.concatenate(ends, axis=1)
    shares = lax.all_to_all(end.reshape(groups, -1, end.shape[1]), "tm", 0, 0)
    entries = call(
        functools.partial(entry_kernel, frames), of(shares.shape, end.dtype), shares, pole
    )
    entry = lax.all_to_all(entries, "tm", 0, 0).reshape(end.shape)
    return [(part,) for part in jnp.split(entry, len(ends), axis=1)]


def pick(values):
    group = lax.axis_index("tm")
    picked = values[-1]
    for index, value in enumerate(values[:-1]):
        picked = jnp.where(group == index, value, picked)
    return picked


def on_core(first, second):
    return jnp.where(lax.axis_index("sx") == 0, first, second)


def weigh(one, by_one, other, by_other):
    return by_one * one[...].astype(jnp.float32) + by_other * other[...].astype(jnp.float32)


def relay_kernel(frames, part, end_ref, got_ref, pole_ref, out_ref):
    rate = rate_of(pole_ref)[:, part * LANES : (part + 1) * LANES]
    carried, twice = jnp.exp(frames * rate), jnp.exp(2 * frames * rate)
    none, same = jnp.zeros_like(rate), jnp.ones_like(rate)
    own = on_core(pick([carried, same, same, same]), pick([same, same, same, none]))
    got = on_core(pick([same, carried, carried, carried]), pick([none, none, twice, same]))
    out_ref[...] = weigh(end_ref, own, got_ref, got).astype(out_ref.dtype)


def exchange_four(ends, pole, frames):
    def along(pairs, core):
        return [(2 * source + core, 2 * target + core) for source, target in pairs]

    axes = ("tm", "sx")
    down = [(0, 2), (1, 3)]
    first_round = along([(0, 1), (1, 0), (2, 3)], 0) + along(down, 1)
    second_round = along(down, 0) + along([(0, 1), (2, 3), (3, 2)], 1)
    got = [lax.ppermute(end, axes, first_round) for end in ends]
    relayed = [
        call(
            functools.partial(relay_kernel, frames, part),
            of(end.shape, end.dtype),
            end,
            here,
            pole,
        )
        for part, (end, here) in enumerate(zip(ends, got))
    ]
    return [(here, lax.ppermute(end, axes, second_round)) for here, end in zip(got, relayed)]


class Mix:
    def __init__(self, lanes, count, arrived_refs, pole_ref, scale_ref):
        self.rate = rate_of(pole_ref)[:, lanes]
        self.scale = scale_ref[:, lanes]
        self.count = count
        self.arrived_refs = arrived_refs

    def entry(self, rows):
        parts = [ref[rows].astype(jnp.float32) for ref in self.arrived_refs]
        if len(parts) == 1:
            return parts[0]
        carried = jnp.exp(self.count * self.rate)
        none, same = jnp.zeros_like(self.rate), jnp.ones_like(self.rate)
        early = on_core(pick([none, same, none, same]), pick([none, none, carried, carried]))
        late = on_core(pick([none, none, same, carried]), pick([none, same, same, same]))
        return early * parts[0] + late * parts[1]

    def __call__(self, drives, rows, start):
        decay = jnp.exp(self.rate)
        reach = jnp.exp((self.count * lax.axis_index("tm")).astype(jnp.float32) * self.rate)
        state = reach * start + self.entry(rows).reshape(start.shape)
        for drive in drives:
            state = decay * state + drive
            yield jax.nn.gelu(self.scale * state)


def beside_kernel(lanes, *refs):
    drive_ref, beside_ref, start_ref, sides_ref, pole_ref, scale_ref, *arrived_refs = refs[:-2]
    give_ref, out_ref = refs[-2:]
    count, rows, cols, wide = drive_ref.shape
    size = rows * cols
    inner = inner_row(rows)
    mix = Mix(lanes, count, arrived_refs, pole_ref, scale_ref)
    chip, chips = lax.axis_index("sy"), lax.axis_size("sy")
    row = lax.broadcasted_iota(jnp.int32, (2 * rows, wide), 0)
    side = jnp.where(row < rows, (chip > 0).astype(jnp.float32), (chip < chips - 1).astype(jnp.float32))
    beside = mix(
        [beside_ref[frame] for frame in range(count)], slice(size, None), sides_ref[:, lanes]
    )
    here = pl.ds(pl.multiple_of(inner * cols, cols), cols)
    tile = mix(
        [drive_ref[frame, inner] for frame in range(count)], here, start_ref[inner, :, lanes]
    )
    zero, one = is_core(0), is_core(1)
    for frame, (cells, mixed) in enumerate(zip(tile, beside)):
        mixed = side * mixed
        out_ref[frame] = mixed.astype(out_ref.dtype)
        give_ref[frame, :cols] = cells.astype(give_ref.dtype)
        left = zero * mixed[rows - 1 : rows] + one * mixed[:1]
        right = zero * mixed[2 * rows - 1 :] + one * mixed[rows : rows + 1]
        which = lax.broadcasted_iota(jnp.int32, (cols, wide), 0)
        ends = jnp.where(which == 0, left, right)
        give_ref[frame, cols:] = ends.astype(give_ref.dtype)


def mixed_kernel(lanes, *refs):
    drive_ref, start_ref, pole_ref, scale_ref, *arrived_refs, out_ref = refs
    count, rows, cols, _ = drive_ref.shape
    mix = Mix(lanes, count, arrived_refs, pole_ref, scale_ref)
    block = 8
    for row in range(0, rows, block):
        here = slice(row, row + block)
        drives = [drive_ref[frame, here] for frame in range(count)]
        cells = slice(row * cols, (row + block) * cols)
        for frame, tile in enumerate(mix(drives, cells, start_ref[here, :, lanes])):
            out_ref[frame, here] = tile.astype(out_ref.dtype)


def fill_tile(lhs_ref, cells_ref, got_ref, beside_ref):
    count, rows, cols, _ = cells_ref.shape
    size, room = rows * cols, count * rows
    for frame in range(count):
        fill(lhs_ref, room + frame * size, cells_ref, frame, got_ref[frame, :cols])
        ends = got_ref[frame, cols:].astype(jnp.float32)
        beside = beside_ref[frame].astype(jnp.float32)
        for side, at in enumerate((0, room + count * size)):
            column, end = beside[side * rows : (side + 1) * rows], ends[side : side + 1]
            here = slice(at + frame * rows, at + (frame + 1) * rows)
            lhs_ref[here] = row_taps(column, end, end).astype(lhs_ref.dtype)


def tile_sum(tile, inputs, lanes, lhs_ref, weight_ref, before_ref):
    count, rows, cols, _ = tile
    inner, room = count * rows * cols, count * rows
    col = lax.broadcasted_iota(jnp.int32, tile, 2)
    total = dot(lhs_ref[room : room + inner], weight_ref, 1, lanes, inputs).reshape(tile)
    if before_ref is not None:
        total += before_ref[...]
    first = dot(lhs_ref[: room + inner], weight_ref, 0, lanes, inputs)
    halo = first[:room].reshape(count, rows, 1, LANES)
    total += jnp.where(col == 0, halo, pltpu.roll(first[room:].reshape(tile), 1, 2))
    last = dot(lhs_ref[room:], weight_ref, 2, lanes, inputs)
    halo = last[inner:].reshape(count, rows, 1, LANES)
    return total + jnp.where(
        col == cols - 1, halo, pltpu.roll(last[:inner].reshape(tile), cols - 1, 2)
    )


def opening_kernel(inputs, lanes, has_before, cells_ref, got_ref, beside_ref, weight_ref, *refs):
    *before_refs, out_ref, lhs_ref = refs
    fill_tile(lhs_ref, cells_ref, got_ref, beside_ref)
    before_ref = before_refs[0] if has_before else None
    out_ref[...] = tile_sum(out_ref.shape, inputs, lanes, lhs_ref, weight_ref, before_ref)


def further_kernel(inputs, lanes, has_before, lhs_ref, weight_ref, *refs):
    *before_refs, out_ref = refs
    before_ref = before_refs[0] if has_before else None
    out_ref[...] = tile_sum(out_ref.shape, inputs, lanes, lhs_ref, weight_ref, before_ref)


def result_kernel(inputs, outputs, cells_ref, got_ref, beside_ref, weight_ref, *refs):
    *before_refs, out_ref, lhs_ref, held_ref, sems = refs
    count, rows, cols, _ = cells_ref.shape
    fill_tile(lhs_ref, cells_ref, got_ref, beside_ref)

    def store(frame, part):
        here = (frame, slice(None), slice(None), outputs[part])
        return pltpu.make_async_copy(held_ref.at[here], out_ref.at[here], sems.at[frame, part])

    for part, lanes in enumerate(outputs):
        before_ref = before_refs[part] if before_refs else None
        tile = (count, rows, cols, LANES)
        total = tile_sum(tile, inputs, lanes, lhs_ref, weight_ref, before_ref)
        for frame in range(count):
            held_ref[frame, :, :, lanes] = total[frame].astype(held_ref.dtype)
            store(frame, part).start()
    for part in range(len(outputs)):
        for frame in range(count):
            store(frame, part).wait()


def on_device(frames, input_weight, output_weight, pole_index, gelu_scale, start_state):
    count, rows, cols, channels = frames.shape
    size, room = rows * cols, count * rows
    wide = 3 * channels
    assert lax.axis_size("sx") == 2
    narrow = frames.dtype
    pole, scale = pole_index[None], gelu_scale[None]

    shapes = (
        of((count * cols + (2 * count + 1) * rows, channels), narrow),
        of((2 * count + 1, rows, channels), narrow),
    )
    edges = call(
        edges_kernel,
        shapes,
        frames,
        scratch=[pltpu.VMEM((count, channels // 128, size, 128), jnp.float32)],
        flops=EDGES_COST,
    )
    give, keep = call(
        start_edges_kernel,
        shapes,
        start_state,
        *edges,
        aliases={1: 0, 2: 1},
    )
    got, mine = trade_columns(give, keep, count * cols)
    main = call(
        main_kernel,
        (of(frames.shape, jnp.float32), of((2, room, channels), jnp.float32)),
        frames,
        got,
        input_weight,
        scratch=[pltpu.VMEM((count * size, wide), narrow)],
        flops=18 * frames.size * channels,
    )
    mine, (total, spill) = lax.optimization_barrier((mine, main))
    halo, sides = call(
        halo_kernel,
        (of((4 * room, wide), narrow), of((2 * rows, channels), jnp.float32)),
        mine,
        swap_cores(mine),
    )
    parts = [slice(lane, lane + LANES) for lane in range(0, channels, LANES)]
    drives, besides, ends = zip(
        *(
            call(
                functools.partial(drive_kernel, lanes),
                (
                    of((count, rows, cols, LANES), jnp.float32),
                    of((count, 2 * rows, LANES), jnp.float32),
                    of((size + 2 * rows, LANES), narrow),
                ),
                halo,
                input_weight,
                total,
                spill,
                pole,
                flops=36 * room * channels * LANES,
            )
            for lanes in parts
        )
    )
    arrivals = (exchange_four if lax.axis_size("tm") == 4 else exchange)(ends, pole, count)

    sums, lhs = [None] * len(parts), None
    inner = of((count, rows, cols, LANES), jnp.float32)
    taps = (count * size + 2 * room, 3 * LANES)
    for lanes, drive, beside, arrived in zip(parts, drives, besides, arrivals):
        if lhs is not None:
            *arrived, sums[0] = lax.optimization_barrier((*arrived, sums[0]))
        give, edge = call(
            functools.partial(beside_kernel, lanes),
            (of((count, 2 * cols, LANES), narrow), of(beside.shape, narrow)),
            drive,
            beside,
            start_state,
            sides,
            pole,
            scale,
            *arrived,
        )
        if lhs is not None:
            give, lhs = lax.optimization_barrier((give, lhs))
            for index in range(1, len(parts)):
                sums[index] = call(
                    functools.partial(further_kernel, before, parts[index], sums[index] is not None),
                    inner,
                    lhs,
                    output_weight,
                    *([] if sums[index] is None else [sums[index]]),
                    flops=18 * drive.size * LANES,
                )
        got = swap_cores(give)
        mixed = call(
            functools.partial(mixed_kernel, lanes),
            of(drive.shape, narrow),
            drive,
            start_state,
            pole,
            scale,
            *arrived,
        )
        if lanes != parts[-1]:
            sums[0], lhs = call(
                functools.partial(opening_kernel, lanes, parts[0], sums[0] is not None),
                (inner, of(taps, narrow)),
                mixed,
                got,
                edge,
                output_weight,
                *([] if sums[0] is None else [sums[0]]),
                flops=18 * drive.size * LANES,
            )
            before = lanes
    return call(
        functools.partial(result_kernel, parts[-1], parts),
        of(frames.shape, narrow),
        mixed,
        got,
        edge,
        output_weight,
        *([] if sums[0] is None else sums),
        out_specs=HBM,
        scratch=[
            pltpu.VMEM(taps, narrow),
            pltpu.VMEM(frames.shape, narrow),
            pltpu.SemaphoreType.DMA((count, len(parts))),
        ],
        flops=18 * mixed.size * channels,
    )


def solution(mesh):
    return jax.shard_map(
        on_device,
        mesh=mesh,
        in_specs=(P("tm", "sx", "sy", None), P(), P(), P(), P(), P("sx", "sy", None)),
        out_specs=P("tm", "sx", "sy", None),
        check_vma=False,
    )
```

```python
import functools
import math

import jax
import jax.numpy as jnp
from jax import lax
from jax.experimental import pallas as pl
from jax.experimental.pallas import tpu as pltpu
from jax.sharding import PartitionSpec as P

NPOLES = 16
VMEM_LIMIT = 24 * 1024 * 1024
WHOLE = pl.BlockSpec(memory_space=pltpu.VMEM)
HBM = pl.BlockSpec(memory_space=pltpu.HBM)
LANES = 256
EDGES_COST = 2_000_000_000
RELAY_COST = 3_000_000_000


def call(kernel, out_shape, *args, scratch=(), flops=0, out_specs=None, aliases=None):
    outs = jax.tree.leaves(out_shape)
    moved = sum(leaf.size * leaf.dtype.itemsize for leaf in (*args, *outs))
    return pl.pallas_call(
        kernel,
        in_specs=[WHOLE] * len(args),
        out_specs=out_specs or jax.tree.map(lambda _: WHOLE, out_shape),
        out_shape=out_shape,
        scratch_shapes=scratch,
        input_output_aliases=aliases or {},
        compiler_params=pltpu.CompilerParams(vmem_limit_bytes=VMEM_LIMIT),
        cost_estimate=pl.CostEstimate(flops=flops, bytes_accessed=moved, transcendentals=0),
    )(*args)


def of(shape, dtype):
    return jax.ShapeDtypeStruct(shape, dtype)


def is_core(which):
    return (lax.axis_index("sx") == which).astype(jnp.float32)


def rate_of(pole_ref):
    pole = pole_ref[...].astype(jnp.float32)
    return -0.001 * jnp.exp(pole * (math.log(300.0) / (NPOLES - 1)))


def inner_row(rows):
    return jnp.where(lax.axis_index("sx") == 0, rows - 1, 0)


def swap_cores(array):
    return lax.ppermute(array, "sx", [(0, 1), (1, 0)])


def put_columns(index, left, right, give_ref, keep_ref):
    zero, one = is_core(0), is_core(1)
    count, rows, _ = keep_ref.shape
    at = give_ref.shape[0] - (count - index) * rows
    give_ref[at : at + rows] = (zero * right + one * left).astype(give_ref.dtype)
    keep_ref[index] = (zero * left + one * right).astype(keep_ref.dtype)


def edges_kernel(cells_ref, give_ref, keep_ref, wide_ref):
    count, rows, cols, channels = cells_ref.shape
    for frame in range(count):
        give_ref[frame * cols : (frame + 1) * cols] = cells_ref[frame, inner_row(rows)]
        tile = cells_ref[frame].reshape(rows * cols, channels).astype(jnp.float32)
        lanes = wide_ref.shape[-1]
        for part in range(channels // lanes):
            wide_ref[frame, part] = tile[:, part * lanes : (part + 1) * lanes]

        def column(col):
            parts = [
                wide_ref[frame, part, pl.ds(col, rows, stride=cols), :]
                for part in range(channels // lanes)
            ]
            return jnp.concatenate(parts, axis=1)

        for depth in range(2):
            left, right = column(depth), column(cols - 1 - depth)
            put_columns(2 * frame + depth, left, right, give_ref, keep_ref)


def start_edges_kernel(start_ref, _, __, give_ref, keep_ref):
    tile, cols = start_ref[...], start_ref.shape[1]
    index = keep_ref.shape[0] - 1
    put_columns(index, tile[:, 0, :], tile[:, cols - 1, :], give_ref, keep_ref)


def trade_columns(give, keep, at):
    chips = lax.axis_size("sy")
    got = swap_cores(give)
    pairs = [(chip, chips + chip - 1) for chip in range(1, chips)]
    pairs += [(after, before) for before, after in pairs]
    columns = jnp.concatenate([keep, got[at:].reshape(keep.shape)], axis=1)
    return got, lax.ppermute(columns, ("sx", "sy"), pairs)


def fill(lhs_ref, at, cells_ref, frame, row):
    _, rows, cols, channels = cells_ref.shape
    size = rows * cols
    row = row.astype(jnp.float32)
    cells = cells_ref[frame].reshape(size, channels)
    mid, low = slice(channels, 2 * channels), slice(2 * channels, 3 * channels)
    lhs_ref[at : at + cols, :channels] = (is_core(1) * row).astype(lhs_ref.dtype)
    lhs_ref[at + cols : at + size, :channels] = cells[: size - cols]
    lhs_ref[at : at + size, mid] = cells
    lhs_ref[at : at + size - cols, low] = cells[cols:]
    lhs_ref[at + size - cols : at + size, low] = (is_core(0) * row).astype(lhs_ref.dtype)


def row_taps(column, above, below):
    rows = column.shape[0]
    row = lax.broadcasted_iota(jnp.int32, column.shape, 0)
    up = jnp.where(row == 0, is_core(1) * above, pltpu.roll(column, 1, 0))
    down = jnp.where(row == rows - 1, is_core(0) * below, pltpu.roll(column, rows - 1, 0))
    return jnp.concatenate([up, column, down], axis=1)


def dot(lhs, weight_ref, column, lanes, inputs=slice(None)):
    weight = weight_ref[:, column, inputs, lanes].reshape(lhs.shape[1], -1)
    return jnp.dot(lhs, weight, preferred_element_type=jnp.float32)


def main_kernel(cells_ref, got_ref, weight_ref, total_ref, spill_ref, lhs_ref):
    count, rows, cols, _ = cells_ref.shape
    size = rows * cols
    for frame in range(count):
        fill(lhs_ref, frame * size, cells_ref, frame, got_ref[frame * cols : (frame + 1) * cols])
    tile = (count, rows, cols, LANES)
    col = lax.broadcasted_iota(jnp.int32, tile, 2)
    for lane in range(0, weight_ref.shape[-1], LANES):
        lanes = slice(lane, lane + LANES)
        total = dot(lhs_ref[...], weight_ref, 1, lanes).reshape(tile)
        first = dot(lhs_ref[...], weight_ref, 0, lanes).reshape(tile)
        spill_ref[1, :, lanes] = first[:, :, cols - 1, :].reshape(count * rows, LANES)
        total += jnp.where(col == 0, 0.0, pltpu.roll(first, 1, 2))
        last = dot(lhs_ref[...], weight_ref, 2, lanes).reshape(tile)
        spill_ref[0, :, lanes] = last[:, :, 0, :].reshape(count * rows, LANES)
        total_ref[:, :, :, lanes] = total + jnp.where(
            col == cols - 1, 0.0, pltpu.roll(last, cols - 1, 2)
        )


def halo_kernel(mine_ref, theirs_ref, lhs_ref, start_ref):
    rows = mine_ref.shape[1] // 2
    count = mine_ref.shape[0] // 2
    room = count * rows
    zero, one = is_core(0), is_core(1)
    core = lax.axis_index("sx")
    slots = ((1, 0), (2, 3))
    for frame in range(count):
        for depth in range(2):
            own = mine_ref[2 * frame + depth].astype(jnp.float32)
            other = theirs_ref[2 * frame + depth].astype(jnp.float32)
            own = row_taps(own[rows:], own[rows - 1 : rows], own[:1])
            other = row_taps(other[:rows], other[2 * rows - 1 :], other[rows : rows + 1])
            for swapped, taps in enumerate((own, other)):
                slot = jnp.where(core == swapped, slots[0][depth], slots[1][depth])
                at = pl.multiple_of(slot * room + frame * rows, rows)
                lhs_ref[pl.ds(at, rows)] = taps.astype(lhs_ref.dtype)
    own = mine_ref[2 * count, rows:].astype(jnp.float32)
    other = theirs_ref[2 * count, :rows].astype(jnp.float32)
    start_ref[:rows] = zero * own + one * other
    start_ref[rows:] = zero * other + one * own


def drive_kernel(
    lanes, lhs_ref, weight_ref, total_ref, spill_ref, pole_ref, drive_ref, beside_ref, *end_refs
):
    count, rows, cols, wide = drive_ref.shape
    room, size = count * rows, rows * cols
    decay = jnp.exp(rate_of(pole_ref))[:, lanes]
    col = lax.broadcasted_iota(jnp.int32, drive_ref.shape, 2)
    first = dot(lhs_ref[: 2 * room], weight_ref, 0, lanes)
    middle = dot(lhs_ref[room : 3 * room], weight_ref, 1, lanes)
    last = dot(lhs_ref[2 * room :], weight_ref, 2, lanes)
    left = (spill_ref[0, :, lanes] + first[:room] + middle[:room]).reshape(count, rows, wide)
    right = (spill_ref[1, :, lanes] + middle[room:] + last[room:]).reshape(count, rows, wide)
    near = first[room:].reshape(count, rows, 1, wide)
    total = total_ref[:, :, :, lanes] + jnp.where(col == 0, near, 0.0)
    near = last[:room].reshape(count, rows, 1, wide)
    total += jnp.where(col == cols - 1, near, 0.0)
    drive_ref[...] = total
    beside_ref[:, :rows] = left
    beside_ref[:, rows:] = right
    state, left_state, right_state = total[0], left[0], right[0]
    for frame in range(1, count):
        state = decay * state + total[frame]
        left_state = decay * left_state + left[frame]
        right_state = decay * right_state + right[frame]
    at = 0
    for end_ref in end_refs:
        piece = slice(at, at + end_ref.shape[1])
        at = piece.stop
        end_ref[:size] = state.reshape(size, wide)[:, piece].astype(end_ref.dtype)
        end_ref[size : size + rows] = left_state[:, piece].astype(end_ref.dtype)
        end_ref[size + rows :] = right_state[:, piece].astype(end_ref.dtype)


def entry_kernel(frames, ends_ref, pole_ref, out_ref):
    carried = jnp.exp(frames * rate_of(pole_ref))
    entry = jnp.zeros(ends_ref.shape[1:], jnp.float32)
    out_ref[0] = entry.astype(out_ref.dtype)
    for index in range(ends_ref.shape[0] - 1):
        entry = carried * entry + ends_ref[index].astype(jnp.float32)
        out_ref[index + 1] = entry.astype(out_ref.dtype)


def exchange(ends, pole, frames):
    groups = lax.axis_size("tm")
    end = jnp.concatenate(ends, axis=1)
    shares = lax.all_to_all(end.reshape(groups, -1, end.shape[1]), "tm", 0, 0)
    entries = call(
        functools.partial(entry_kernel, frames), of(shares.shape, end.dtype), shares, pole
    )
    entry = lax.all_to_all(entries, "tm", 0, 0).reshape(end.shape)
    return [(part,) for part in jnp.split(entry, pieces_at(ends), axis=1)]


def pieces_at(ends):
    at = [0]
    for end in ends:
        at.append(at[-1] + end.shape[1])
    return at[1:-1]


def pick(values):
    group = lax.axis_index("tm")
    picked = values[-1]
    for index, value in enumerate(values[:-1]):
        picked = jnp.where(group == index, value, picked)
    return picked


def on_core(first, second):
    return jnp.where(lax.axis_index("sx") == 0, first, second)


def weigh(one, by_one, other, by_other):
    return by_one * one[...].astype(jnp.float32) + by_other * other[...].astype(jnp.float32)


def relay_kernel(frames, lanes, end_ref, got_ref, pole_ref, out_ref):
    rate = rate_of(pole_ref)[:, lanes]
    carried, twice = jnp.exp(frames * rate), jnp.exp(2 * frames * rate)
    none, same = jnp.zeros_like(rate), jnp.ones_like(rate)
    own = on_core(pick([carried, same, same, same]), pick([same, same, same, none]))
    got = on_core(pick([same, carried, carried, carried]), pick([none, none, twice, same]))
    out_ref[...] = weigh(end_ref, own, got_ref, got).astype(out_ref.dtype)


def exchange_four(ends, pole, frames):
    def along(pairs, core):
        return [(2 * source + core, 2 * target + core) for source, target in pairs]

    axes = ("tm", "sx")
    down = [(0, 2), (1, 3)]
    first_round = along([(0, 1), (1, 0), (2, 3)], 0) + along(down, 1)
    second_round = along(down, 0) + along([(0, 1), (2, 3), (3, 2)], 1)
    got = [lax.ppermute(end, axes, first_round) for end in ends]
    relayed = [
        call(
            functools.partial(relay_kernel, frames, slice(at, at + end.shape[1])),
            of(end.shape, end.dtype),
            end,
            here,
            pole,
            flops=RELAY_COST,
        )
        for at, end, here in zip([0, *pieces_at(ends)], ends, got)
    ]
    return [(here, lax.ppermute(end, axes, second_round)) for here, end in zip(got, relayed)]


class Mix:
    def __init__(self, lanes, rounds, count, arrived_refs, pole_ref, scale_ref):
        self.rounds = rounds
        self.rate = rate_of(pole_ref)[:, lanes]
        self.scale = scale_ref[:, lanes]
        self.count = count
        self.arrived_refs = arrived_refs

    def entry(self, rows):
        parts = [
            jnp.concatenate(
                [ref[rows].astype(jnp.float32) for ref in self.arrived_refs[start :: self.rounds]],
                axis=1,
            )
            for start in range(self.rounds)
        ]
        if self.rounds == 1:
            return parts[0]
        carried = jnp.exp(self.count * self.rate)
        none, same = jnp.zeros_like(self.rate), jnp.ones_like(self.rate)
        early = on_core(pick([none, same, none, same]), pick([none, none, carried, carried]))
        late = on_core(pick([none, none, same, carried]), pick([none, same, same, same]))
        return early * parts[0] + late * parts[1]

    def __call__(self, drives, rows, start):
        decay = jnp.exp(self.rate)
        reach = jnp.exp((self.count * lax.axis_index("tm")).astype(jnp.float32) * self.rate)
        state = reach * start + self.entry(rows).reshape(start.shape)
        for drive in drives:
            state = decay * state + drive
            yield jax.nn.gelu(self.scale * state)


def beside_kernel(lanes, rounds, *refs):
    drive_ref, beside_ref, start_ref, sides_ref, pole_ref, scale_ref, *arrived_refs = refs[:-2]
    give_ref, out_ref = refs[-2:]
    count, rows, cols, wide = drive_ref.shape
    size = rows * cols
    inner = inner_row(rows)
    mix = Mix(lanes, rounds, count, arrived_refs, pole_ref, scale_ref)
    chip, chips = lax.axis_index("sy"), lax.axis_size("sy")
    row = lax.broadcasted_iota(jnp.int32, (2 * rows, wide), 0)
    side = jnp.where(row < rows, (chip > 0).astype(jnp.float32), (chip < chips - 1).astype(jnp.float32))
    beside = mix(
        [beside_ref[frame] for frame in range(count)], slice(size, None), sides_ref[:, lanes]
    )
    here = pl.ds(pl.multiple_of(inner * cols, cols), cols)
    tile = mix(
        [drive_ref[frame, inner] for frame in range(count)], here, start_ref[inner, :, lanes]
    )
    zero, one = is_core(0), is_core(1)
    for frame, (cells, mixed) in enumerate(zip(tile, beside)):
        mixed = side * mixed
        out_ref[frame] = mixed.astype(out_ref.dtype)
        give_ref[frame, :cols] = cells.astype(give_ref.dtype)
        left = zero * mixed[rows - 1 : rows] + one * mixed[:1]
        right = zero * mixed[2 * rows - 1 :] + one * mixed[rows : rows + 1]
        which = lax.broadcasted_iota(jnp.int32, (cols, wide), 0)
        ends = jnp.where(which == 0, left, right)
        give_ref[frame, cols:] = ends.astype(give_ref.dtype)


def mixed_kernel(lanes, rounds, *refs):
    drive_ref, start_ref, pole_ref, scale_ref, *arrived_refs, out_ref = refs
    count, rows, cols, _ = drive_ref.shape
    mix = Mix(lanes, rounds, count, arrived_refs, pole_ref, scale_ref)
    block = 8
    for row in range(0, rows, block):
        here = slice(row, row + block)
        drives = [drive_ref[frame, here] for frame in range(count)]
        cells = slice(row * cols, (row + block) * cols)
        for frame, tile in enumerate(mix(drives, cells, start_ref[here, :, lanes])):
            out_ref[frame, here] = tile.astype(out_ref.dtype)


def fill_tile(lhs_ref, cells_ref, got_ref, beside_ref):
    count, rows, cols, _ = cells_ref.shape
    size, room = rows * cols, count * rows
    for frame in range(count):
        fill(lhs_ref, room + frame * size, cells_ref, frame, got_ref[frame, :cols])
        ends = got_ref[frame, cols:].astype(jnp.float32)
        beside = beside_ref[frame].astype(jnp.float32)
        for side, at in enumerate((0, room + count * size)):
            column, end = beside[side * rows : (side + 1) * rows], ends[side : side + 1]
            here = slice(at + frame * rows, at + (frame + 1) * rows)
            lhs_ref[here] = row_taps(column, end, end).astype(lhs_ref.dtype)


def tile_sum(tile, inputs, lanes, lhs_ref, weight_ref, before_ref):
    count, rows, cols, _ = tile
    inner, room = count * rows * cols, count * rows
    col = lax.broadcasted_iota(jnp.int32, tile, 2)
    total = dot(lhs_ref[room : room + inner], weight_ref, 1, lanes, inputs).reshape(tile)
    if before_ref is not None:
        total += before_ref[...]
    first = dot(lhs_ref[: room + inner], weight_ref, 0, lanes, inputs)
    halo = first[:room].reshape(count, rows, 1, LANES)
    total += jnp.where(col == 0, halo, pltpu.roll(first[room:].reshape(tile), 1, 2))
    last = dot(lhs_ref[room:], weight_ref, 2, lanes, inputs)
    halo = last[inner:].reshape(count, rows, 1, LANES)
    return total + jnp.where(
        col == cols - 1, halo, pltpu.roll(last[:inner].reshape(tile), cols - 1, 2)
    )


def opening_kernel(inputs, lanes, has_before, cells_ref, got_ref, beside_ref, weight_ref, *refs):
    *before_refs, out_ref, lhs_ref = refs
    fill_tile(lhs_ref, cells_ref, got_ref, beside_ref)
    before_ref = before_refs[0] if has_before else None
    out_ref[...] = tile_sum(out_ref.shape, inputs, lanes, lhs_ref, weight_ref, before_ref)


def further_kernel(inputs, lanes, has_before, lhs_ref, weight_ref, *refs):
    *before_refs, out_ref = refs
    before_ref = before_refs[0] if has_before else None
    out_ref[...] = tile_sum(out_ref.shape, inputs, lanes, lhs_ref, weight_ref, before_ref)


def result_kernel(inputs, outputs, cells_ref, got_ref, beside_ref, weight_ref, *refs):
    *before_refs, out_ref, lhs_ref, held_ref, sems = refs
    count, rows, cols, _ = cells_ref.shape
    fill_tile(lhs_ref, cells_ref, got_ref, beside_ref)

    def store(frame, part):
        here = (frame, slice(None), slice(None), outputs[part])
        return pltpu.make_async_copy(held_ref.at[here], out_ref.at[here], sems.at[frame, part])

    for part, lanes in enumerate(outputs):
        before_ref = before_refs[part] if before_refs else None
        tile = (count, rows, cols, LANES)
        total = tile_sum(tile, inputs, lanes, lhs_ref, weight_ref, before_ref)
        for frame in range(count):
            held_ref[frame, :, :, lanes] = total[frame].astype(held_ref.dtype)
            store(frame, part).start()
    for part in range(len(outputs)):
        for frame in range(count):
            store(frame, part).wait()


def on_device(frames, input_weight, output_weight, pole_index, gelu_scale, start_state):
    count, rows, cols, channels = frames.shape
    size, room = rows * cols, count * rows
    wide = 3 * channels
    assert lax.axis_size("sx") == 2
    narrow = frames.dtype
    pole, scale = pole_index[None], gelu_scale[None]

    shapes = (
        of((count * cols + (2 * count + 1) * rows, channels), narrow),
        of((2 * count + 1, rows, channels), narrow),
    )
    edges = call(
        edges_kernel,
        shapes,
        frames,
        scratch=[pltpu.VMEM((count, channels // 128, size, 128), jnp.float32)],
        flops=EDGES_COST,
    )
    give, keep = call(
        start_edges_kernel,
        shapes,
        start_state,
        *edges,
        aliases={1: 0, 2: 1},
    )
    got, mine = trade_columns(give, keep, count * cols)
    main = call(
        main_kernel,
        (of(frames.shape, jnp.float32), of((2, room, channels), jnp.float32)),
        frames,
        got,
        input_weight,
        scratch=[pltpu.VMEM((count * size, wide), narrow)],
        flops=18 * frames.size * channels,
    )
    mine, (total, spill) = lax.optimization_barrier((mine, main))
    halo, sides = call(
        halo_kernel,
        (of((4 * room, wide), narrow), of((2 * rows, channels), jnp.float32)),
        mine,
        swap_cores(mine),
    )
    parts = [slice(lane, lane + LANES) for lane in range(0, channels, LANES)]
    pieces = [[LANES // 2] * 2, *[[LANES]] * (len(parts) - 1)]
    drives, besides, ends = [], [], []
    for lanes, widths in zip(parts, pieces):
        drive, beside, *end = call(
            functools.partial(drive_kernel, lanes),
            (
                of((count, rows, cols, LANES), jnp.float32),
                of((count, 2 * rows, LANES), jnp.float32),
                *[of((size + 2 * rows, width), narrow) for width in widths],
            ),
            halo,
            input_weight,
            total,
            spill,
            pole,
            flops=36 * room * channels * LANES,
        )
        drives.append(drive)
        besides.append(beside)
        ends += end
    pairs = (exchange_four if lax.axis_size("tm") == 4 else exchange)(ends, pole, count)
    rounds = len(pairs[0])
    pairs = iter(pairs)
    arrivals = [[each for _ in widths for each in next(pairs)] for widths in pieces]

    sums, lhs = [None] * len(parts), None
    inner = of((count, rows, cols, LANES), jnp.float32)
    taps = (count * size + 2 * room, 3 * LANES)
    for lanes, drive, beside, arrived in zip(parts, drives, besides, arrivals):
        if lhs is not None:
            *arrived, sums[0] = lax.optimization_barrier((*arrived, sums[0]))
        give, edge = call(
            functools.partial(beside_kernel, lanes, rounds),
            (of((count, 2 * cols, LANES), narrow), of(beside.shape, narrow)),
            drive,
            beside,
            start_state,
            sides,
            pole,
            scale,
            *arrived,
        )
        if lhs is not None:
            give, lhs = lax.optimization_barrier((give, lhs))
            for index in range(1, len(parts)):
                sums[index] = call(
                    functools.partial(further_kernel, before, parts[index], sums[index] is not None),
                    inner,
                    lhs,
                    output_weight,
                    *([] if sums[index] is None else [sums[index]]),
                    flops=18 * drive.size * LANES,
                )
        got = swap_cores(give)
        mixed = call(
            functools.partial(mixed_kernel, lanes, rounds),
            of(drive.shape, narrow),
            drive,
            start_state,
            pole,
            scale,
            *arrived,
        )
        if lanes != parts[-1]:
            sums[0], lhs = call(
                functools.partial(opening_kernel, lanes, parts[0], sums[0] is not None),
                (inner, of(taps, narrow)),
                mixed,
                got,
                edge,
                output_weight,
                *([] if sums[0] is None else [sums[0]]),
                flops=36 * drive.size * LANES,
            )
            before = lanes
    return call(
        functools.partial(result_kernel, parts[-1], parts),
        of(frames.shape, narrow),
        mixed,
        got,
        edge,
        output_weight,
        *([] if sums[0] is None else sums),
        out_specs=HBM,
        scratch=[
            pltpu.VMEM(taps, narrow),
            pltpu.VMEM(frames.shape, narrow),
            pltpu.SemaphoreType.DMA((count, len(parts))),
        ],
        flops=18 * mixed.size * channels,
    )


def solution(mesh):
    return jax.shard_map(
        on_device,
        mesh=mesh,
        in_specs=(P("tm", "sx", "sy", None), P(), P(), P(), P(), P("sx", "sy", None)),
        out_specs=P("tm", "sx", "sy", None),
        check_vma=False,
    )
```

```python
import functools
import math

import jax
import jax.numpy as jnp
from jax import lax
from jax.experimental import pallas as pl
from jax.experimental.pallas import tpu as pltpu
from jax.sharding import PartitionSpec as P

NPOLES = 16
VMEM_LIMIT = 24 * 1024 * 1024
WHOLE = pl.BlockSpec(memory_space=pltpu.VMEM)
HBM = pl.BlockSpec(memory_space=pltpu.HBM)
LANES = 256
EDGES_COST = 2_000_000_000


def call(kernel, out_shape, *args, scratch=(), flops=0, out_specs=None, aliases=None):
    outs = jax.tree.leaves(out_shape)
    moved = sum(leaf.size * leaf.dtype.itemsize for leaf in (*args, *outs))
    return pl.pallas_call(
        kernel,
        in_specs=[WHOLE] * len(args),
        out_specs=out_specs or jax.tree.map(lambda _: WHOLE, out_shape),
        out_shape=out_shape,
        scratch_shapes=scratch,
        input_output_aliases=aliases or {},
        compiler_params=pltpu.CompilerParams(vmem_limit_bytes=VMEM_LIMIT),
        cost_estimate=pl.CostEstimate(flops=flops, bytes_accessed=moved, transcendentals=0),
    )(*args)


def of(shape, dtype):
    return jax.ShapeDtypeStruct(shape, dtype)


def is_core(which):
    return (lax.axis_index("sx") == which).astype(jnp.float32)


def rate_of(pole_ref):
    pole = pole_ref[...].astype(jnp.float32)
    return -0.001 * jnp.exp(pole * (math.log(300.0) / (NPOLES - 1)))


def inner_row(rows):
    return jnp.where(lax.axis_index("sx") == 0, rows - 1, 0)


def swap_cores(array):
    return lax.ppermute(array, "sx", [(0, 1), (1, 0)])


def put_columns(index, left, right, give_ref, keep_ref):
    zero, one = is_core(0), is_core(1)
    count, rows, _ = keep_ref.shape
    at = give_ref.shape[0] - (count - index) * rows
    give_ref[at : at + rows] = (zero * right + one * left).astype(give_ref.dtype)
    keep_ref[index] = (zero * left + one * right).astype(keep_ref.dtype)


def edges_kernel(cells_ref, give_ref, keep_ref, wide_ref):
    count, rows, cols, channels = cells_ref.shape
    for frame in range(count):
        give_ref[frame * cols : (frame + 1) * cols] = cells_ref[frame, inner_row(rows)]
        tile = cells_ref[frame].reshape(rows * cols, channels).astype(jnp.float32)
        lanes = wide_ref.shape[-1]
        for part in range(channels // lanes):
            wide_ref[frame, part] = tile[:, part * lanes : (part + 1) * lanes]

        def column(col):
            parts = [
                wide_ref[frame, part, pl.ds(col, rows, stride=cols), :]
                for part in range(channels // lanes)
            ]
            return jnp.concatenate(parts, axis=1)

        for depth in range(2):
            left, right = column(depth), column(cols - 1 - depth)
            put_columns(2 * frame + depth, left, right, give_ref, keep_ref)


def start_edges_kernel(start_ref, _, __, give_ref, keep_ref):
    tile, cols = start_ref[...], start_ref.shape[1]
    index = keep_ref.shape[0] - 1
    put_columns(index, tile[:, 0, :], tile[:, cols - 1, :], give_ref, keep_ref)


def trade_columns(give, keep, at):
    chips = lax.axis_size("sy")
    got = swap_cores(give)
    pairs = [(chip, chips + chip - 1) for chip in range(1, chips)]
    pairs += [(after, before) for before, after in pairs]
    columns = jnp.concatenate([keep, got[at:].reshape(keep.shape)], axis=1)
    return got, lax.ppermute(columns, ("sx", "sy"), pairs)


def put_cells(lhs_ref, at, size, cols, first, cells):
    count, channels = cells.shape
    upper, lower = min(count, size - cols - first), max(0, cols - first)
    here = at + first
    lhs_ref[here : here + count, channels : 2 * channels] = cells
    lhs_ref[here + cols : here + cols + upper, :channels] = cells[:upper]
    lhs_ref[here + lower - cols : here + count - cols, 2 * channels :] = cells[lower:]


def put_row(lhs_ref, at, size, row):
    cols, channels = row.shape
    row = row.astype(jnp.float32)
    last = slice(at + size - cols, at + size)
    lhs_ref[at : at + cols, :channels] = (is_core(1) * row).astype(lhs_ref.dtype)
    lhs_ref[last, 2 * channels :] = (is_core(0) * row).astype(lhs_ref.dtype)


def taps_kernel(cells_ref, lhs_ref):
    count, rows, cols, channels = cells_ref.shape
    size = rows * cols
    for frame in range(count):
        put_cells(lhs_ref, frame * size, size, cols, 0, cells_ref[frame].reshape(size, channels))


def row_taps(column, above, below):
    rows = column.shape[0]
    row = lax.broadcasted_iota(jnp.int32, column.shape, 0)
    up = jnp.where(row == 0, is_core(1) * above, pltpu.roll(column, 1, 0))
    down = jnp.where(row == rows - 1, is_core(0) * below, pltpu.roll(column, rows - 1, 0))
    return jnp.concatenate([up, column, down], axis=1)


def dot(lhs, weight_ref, column, lanes, inputs=slice(None)):
    weight = weight_ref[:, column, inputs, lanes].reshape(lhs.shape[1], -1)
    return jnp.dot(lhs, weight, preferred_element_type=jnp.float32)


def main_kernel(_, got_ref, weight_ref, total_ref, spill_ref, lhs_ref):
    count, rows, cols, _ = total_ref.shape
    size = rows * cols
    for frame in range(count):
        put_row(lhs_ref, frame * size, size, got_ref[frame * cols : (frame + 1) * cols])
    tile = (count, rows, cols, LANES)
    col = lax.broadcasted_iota(jnp.int32, tile, 2)
    for lane in range(0, weight_ref.shape[-1], LANES):
        lanes = slice(lane, lane + LANES)
        total = dot(lhs_ref[...], weight_ref, 1, lanes).reshape(tile)
        first = dot(lhs_ref[...], weight_ref, 0, lanes).reshape(tile)
        spill_ref[1, :, lanes] = first[:, :, cols - 1, :].reshape(count * rows, LANES)
        total += jnp.where(col == 0, 0.0, pltpu.roll(first, 1, 2))
        last = dot(lhs_ref[...], weight_ref, 2, lanes).reshape(tile)
        spill_ref[0, :, lanes] = last[:, :, 0, :].reshape(count * rows, LANES)
        total_ref[:, :, :, lanes] = total + jnp.where(
            col == cols - 1, 0.0, pltpu.roll(last, cols - 1, 2)
        )


def halo_kernel(mine_ref, theirs_ref, lhs_ref, start_ref):
    rows = mine_ref.shape[1] // 2
    count = mine_ref.shape[0] // 2
    room = count * rows
    zero, one = is_core(0), is_core(1)
    core = lax.axis_index("sx")
    slots = ((1, 0), (2, 3))
    for frame in range(count):
        for depth in range(2):
            own = mine_ref[2 * frame + depth].astype(jnp.float32)
            other = theirs_ref[2 * frame + depth].astype(jnp.float32)
            own = row_taps(own[rows:], own[rows - 1 : rows], own[:1])
            other = row_taps(other[:rows], other[2 * rows - 1 :], other[rows : rows + 1])
            for swapped, taps in enumerate((own, other)):
                slot = jnp.where(core == swapped, slots[0][depth], slots[1][depth])
                at = pl.multiple_of(slot * room + frame * rows, rows)
                lhs_ref[pl.ds(at, rows)] = taps.astype(lhs_ref.dtype)
    own = mine_ref[2 * count, rows:].astype(jnp.float32)
    other = theirs_ref[2 * count, :rows].astype(jnp.float32)
    start_ref[:rows] = zero * own + one * other
    start_ref[rows:] = zero * other + one * own


def drive_kernel(
    lanes, lhs_ref, weight_ref, total_ref, spill_ref, pole_ref, drive_ref, beside_ref, end_ref
):
    count, rows, cols, wide = drive_ref.shape
    room, size = count * rows, rows * cols
    decay = jnp.exp(rate_of(pole_ref))[:, lanes]
    col = lax.broadcasted_iota(jnp.int32, drive_ref.shape, 2)
    first = dot(lhs_ref[: 2 * room], weight_ref, 0, lanes)
    middle = dot(lhs_ref[room : 3 * room], weight_ref, 1, lanes)
    last = dot(lhs_ref[2 * room :], weight_ref, 2, lanes)
    left = (spill_ref[0, :, lanes] + first[:room] + middle[:room]).reshape(count, rows, wide)
    right = (spill_ref[1, :, lanes] + middle[room:] + last[room:]).reshape(count, rows, wide)
    near = first[room:].reshape(count, rows, 1, wide)
    total = total_ref[:, :, :, lanes] + jnp.where(col == 0, near, 0.0)
    near = last[:room].reshape(count, rows, 1, wide)
    total += jnp.where(col == cols - 1, near, 0.0)
    drive_ref[...] = total
    beside_ref[:, :rows] = left
    beside_ref[:, rows:] = right
    state, left_state, right_state = total[0], left[0], right[0]
    for frame in range(1, count):
        state = decay * state + total[frame]
        left_state = decay * left_state + left[frame]
        right_state = decay * right_state + right[frame]
    end_ref[:size] = state.reshape(size, wide).astype(end_ref.dtype)
    end_ref[size : size + rows] = left_state.astype(end_ref.dtype)
    end_ref[size + rows :] = right_state.astype(end_ref.dtype)


def entry_kernel(frames, ends_ref, pole_ref, out_ref):
    carried = jnp.exp(frames * rate_of(pole_ref))
    entry = jnp.zeros(ends_ref.shape[1:], jnp.float32)
    out_ref[0] = entry.astype(out_ref.dtype)
    for index in range(ends_ref.shape[0] - 1):
        entry = carried * entry + ends_ref[index].astype(jnp.float32)
        out_ref[index + 1] = entry.astype(out_ref.dtype)


def exchange(ends, pole, frames):
    groups = lax.axis_size("tm")
    end = jnp.concatenate(ends, axis=1)
    shares = lax.all_to_all(end.reshape(groups, -1, end.shape[1]), "tm", 0, 0)
    entries = call(
        functools.partial(entry_kernel, frames), of(shares.shape, end.dtype), shares, pole
    )
    entry = lax.all_to_all(entries, "tm", 0, 0).reshape(end.shape)
    return [(part,) for part in jnp.split(entry, len(ends), axis=1)]


def pick(values):
    group = lax.axis_index("tm")
    picked = values[-1]
    for index, value in enumerate(values[:-1]):
        picked = jnp.where(group == index, value, picked)
    return picked


def on_core(first, second):
    return jnp.where(lax.axis_index("sx") == 0, first, second)


def weigh(one, by_one, other, by_other):
    return by_one * one[...].astype(jnp.float32) + by_other * other[...].astype(jnp.float32)


def relay_kernel(frames, part, end_ref, got_ref, pole_ref, out_ref):
    rate = rate_of(pole_ref)[:, part * LANES : (part + 1) * LANES]
    carried, twice = jnp.exp(frames * rate), jnp.exp(2 * frames * rate)
    none, same = jnp.zeros_like(rate), jnp.ones_like(rate)
    own = on_core(pick([carried, same, same, same]), pick([same, same, same, none]))
    got = on_core(pick([same, carried, carried, carried]), pick([none, none, twice, same]))
    out_ref[...] = weigh(end_ref, own, got_ref, got).astype(out_ref.dtype)


def exchange_four(ends, pole, frames):
    def along(pairs, core):
        return [(2 * source + core, 2 * target + core) for source, target in pairs]

    axes = ("tm", "sx")
    down = [(0, 2), (1, 3)]
    first_round = along([(0, 1), (1, 0), (2, 3)], 0) + along(down, 1)
    second_round = along(down, 0) + along([(0, 1), (2, 3), (3, 2)], 1)
    got = [lax.ppermute(end, axes, first_round) for end in ends]
    relayed = [
        call(
            functools.partial(relay_kernel, frames, part),
            of(end.shape, end.dtype),
            end,
            here,
            pole,
        )
        for part, (end, here) in enumerate(zip(ends, got))
    ]
    return [(here, lax.ppermute(end, axes, second_round)) for here, end in zip(got, relayed)]


class Mix:
    def __init__(self, lanes, count, arrived_refs, pole_ref, scale_ref):
        self.rate = rate_of(pole_ref)[:, lanes]
        self.scale = scale_ref[:, lanes]
        self.count = count
        self.arrived_refs = arrived_refs

    def entry(self, rows):
        parts = [ref[rows].astype(jnp.float32) for ref in self.arrived_refs]
        if len(parts) == 1:
            return parts[0]
        carried = jnp.exp(self.count * self.rate)
        none, same = jnp.zeros_like(self.rate), jnp.ones_like(self.rate)
        early = on_core(pick([none, same, none, same]), pick([none, none, carried, carried]))
        late = on_core(pick([none, none, same, carried]), pick([none, same, same, same]))
        return early * parts[0] + late * parts[1]

    def __call__(self, drives, rows, start):
        decay = jnp.exp(self.rate)
        reach = jnp.exp((self.count * lax.axis_index("tm")).astype(jnp.float32) * self.rate)
        state = reach * start + self.entry(rows).reshape(start.shape)
        for drive in drives:
            state = decay * state + drive
            yield jax.nn.gelu(self.scale * state)


def beside_kernel(lanes, *refs):
    drive_ref, beside_ref, start_ref, sides_ref, pole_ref, scale_ref, *arrived_refs = refs[:-2]
    give_ref, out_ref = refs[-2:]
    count, rows, cols, wide = drive_ref.shape
    size = rows * cols
    inner = inner_row(rows)
    mix = Mix(lanes, count, arrived_refs, pole_ref, scale_ref)
    chip, chips = lax.axis_index("sy"), lax.axis_size("sy")
    row = lax.broadcasted_iota(jnp.int32, (2 * rows, wide), 0)
    side = jnp.where(row < rows, (chip > 0).astype(jnp.float32), (chip < chips - 1).astype(jnp.float32))
    beside = mix(
        [beside_ref[frame] for frame in range(count)], slice(size, None), sides_ref[:, lanes]
    )
    here = pl.ds(pl.multiple_of(inner * cols, cols), cols)
    tile = mix(
        [drive_ref[frame, inner] for frame in range(count)], here, start_ref[inner, :, lanes]
    )
    zero, one = is_core(0), is_core(1)
    for frame, (cells, mixed) in enumerate(zip(tile, beside)):
        mixed = side * mixed
        out_ref[frame] = mixed.astype(out_ref.dtype)
        give_ref[frame, :cols] = cells.astype(give_ref.dtype)
        left = zero * mixed[rows - 1 : rows] + one * mixed[:1]
        right = zero * mixed[2 * rows - 1 :] + one * mixed[rows : rows + 1]
        which = lax.broadcasted_iota(jnp.int32, (cols, wide), 0)
        ends = jnp.where(which == 0, left, right)
        give_ref[frame, cols:] = ends.astype(give_ref.dtype)


def mixed_kernel(lanes, *refs):
    drive_ref, start_ref, pole_ref, scale_ref, *arrived_refs, lhs_ref = refs
    count, rows, cols, wide = drive_ref.shape
    size, room = rows * cols, count * rows
    mix = Mix(lanes, count, arrived_refs, pole_ref, scale_ref)
    block = 8
    for row in range(0, rows, block):
        here = slice(row, row + block)
        drives = [drive_ref[frame, here] for frame in range(count)]
        cells = slice(row * cols, (row + block) * cols)
        for frame, tile in enumerate(mix(drives, cells, start_ref[here, :, lanes])):
            tile = tile.reshape(block * cols, wide).astype(lhs_ref.dtype)
            put_cells(lhs_ref, room + frame * size, size, cols, row * cols, tile)


def put_edges(lhs_ref, tile, got_ref, beside_ref):
    count, rows, cols, _ = tile
    size, room = rows * cols, count * rows
    for frame in range(count):
        put_row(lhs_ref, room + frame * size, size, got_ref[frame, :cols])
        ends = got_ref[frame, cols:].astype(jnp.float32)
        beside = beside_ref[frame].astype(jnp.float32)
        for side, at in enumerate((0, room + count * size)):
            column, end = beside[side * rows : (side + 1) * rows], ends[side : side + 1]
            here = slice(at + frame * rows, at + (frame + 1) * rows)
            lhs_ref[here] = row_taps(column, end, end).astype(lhs_ref.dtype)


def tile_sum(tile, inputs, lanes, lhs_ref, weight_ref, before_ref):
    count, rows, cols, _ = tile
    inner, room = count * rows * cols, count * rows
    col = lax.broadcasted_iota(jnp.int32, tile, 2)
    total = dot(lhs_ref[room : room + inner], weight_ref, 1, lanes, inputs).reshape(tile)
    if before_ref is not None:
        total += before_ref[...]
    first = dot(lhs_ref[: room + inner], weight_ref, 0, lanes, inputs)
    halo = first[:room].reshape(count, rows, 1, LANES)
    total += jnp.where(col == 0, halo, pltpu.roll(first[room:].reshape(tile), 1, 2))
    last = dot(lhs_ref[room:], weight_ref, 2, lanes, inputs)
    halo = last[inner:].reshape(count, rows, 1, LANES)
    return total + jnp.where(
        col == cols - 1, halo, pltpu.roll(last[:inner].reshape(tile), cols - 1, 2)
    )


def opening_kernel(inputs, lanes, has_before, _, got_ref, beside_ref, weight_ref, *refs):
    *before_refs, out_ref, lhs_ref = refs
    put_edges(lhs_ref, out_ref.shape, got_ref, beside_ref)
    before_ref = before_refs[0] if has_before else None
    out_ref[...] = tile_sum(out_ref.shape, inputs, lanes, lhs_ref, weight_ref, before_ref)


def further_kernel(inputs, lanes, has_before, lhs_ref, weight_ref, *refs):
    *before_refs, out_ref = refs
    before_ref = before_refs[0] if has_before else None
    out_ref[...] = tile_sum(out_ref.shape, inputs, lanes, lhs_ref, weight_ref, before_ref)


def result_kernel(inputs, outputs, _, got_ref, beside_ref, weight_ref, *refs):
    *before_refs, out_ref, lhs_ref, held_ref, sems = refs
    count, rows, cols, _ = held_ref.shape
    put_edges(lhs_ref, held_ref.shape, got_ref, beside_ref)

    def store(frame, part):
        here = (frame, slice(None), slice(None), outputs[part])
        return pltpu.make_async_copy(held_ref.at[here], out_ref.at[here], sems.at[frame, part])

    for part, lanes in enumerate(outputs):
        before_ref = before_refs[part] if before_refs else None
        tile = (count, rows, cols, LANES)
        total = tile_sum(tile, inputs, lanes, lhs_ref, weight_ref, before_ref)
        for frame in range(count):
            held_ref[frame, :, :, lanes] = total[frame].astype(held_ref.dtype)
            store(frame, part).start()
    for part in range(len(outputs)):
        for frame in range(count):
            store(frame, part).wait()


def on_device(frames, input_weight, output_weight, pole_index, gelu_scale, start_state):
    count, rows, cols, channels = frames.shape
    size, room = rows * cols, count * rows
    wide = 3 * channels
    assert lax.axis_size("sx") == 2
    narrow = frames.dtype
    pole, scale = pole_index[None], gelu_scale[None]

    shapes = (
        of((count * cols + (2 * count + 1) * rows, channels), narrow),
        of((2 * count + 1, rows, channels), narrow),
    )
    edges = call(
        edges_kernel,
        shapes,
        frames,
        scratch=[pltpu.VMEM((count, channels // 128, size, 128), jnp.float32)],
        flops=EDGES_COST,
    )
    give, keep = call(
        start_edges_kernel,
        shapes,
        start_state,
        *edges,
        aliases={1: 0, 2: 1},
    )
    got, mine = trade_columns(give, keep, count * cols)
    taps = of((count * size, wide), narrow)
    *main, _ = call(
        main_kernel,
        (of(frames.shape, jnp.float32), of((2, room, channels), jnp.float32), taps),
        call(taps_kernel, taps, frames),
        got,
        input_weight,
        aliases={0: 2},
        flops=18 * frames.size * channels,
    )
    mine, total, spill = lax.optimization_barrier((mine, *main))
    halo, sides = call(
        halo_kernel,
        (of((4 * room, wide), narrow), of((2 * rows, channels), jnp.float32)),
        mine,
        swap_cores(mine),
    )
    parts = [slice(lane, lane + LANES) for lane in range(0, channels, LANES)]
    drives, besides, ends = zip(
        *(
            call(
                functools.partial(drive_kernel, lanes),
                (
                    of((count, rows, cols, LANES), jnp.float32),
                    of((count, 2 * rows, LANES), jnp.float32),
                    of((size + 2 * rows, LANES), narrow),
                ),
                halo,
                input_weight,
                total,
                spill,
                pole,
                flops=36 * room * channels * LANES,
            )
            for lanes in parts
        )
    )
    arrivals = (exchange_four if lax.axis_size("tm") == 4 else exchange)(ends, pole, count)

    sums, lhs = [None] * len(parts), None
    inner = of((count, rows, cols, LANES), jnp.float32)
    taps = of((count * size + 2 * room, 3 * LANES), narrow)
    for lanes, drive, beside, arrived in zip(parts, drives, besides, arrivals):
        if lhs is not None:
            *arrived, sums[0] = lax.optimization_barrier((*arrived, sums[0]))
        give, edge = call(
            functools.partial(beside_kernel, lanes),
            (of((count, 2 * cols, LANES), narrow), of(beside.shape, narrow)),
            drive,
            beside,
            start_state,
            sides,
            pole,
            scale,
            *arrived,
        )
        if lhs is not None:
            give, lhs = lax.optimization_barrier((give, lhs))
            for index in range(1, len(parts)):
                sums[index] = call(
                    functools.partial(further_kernel, before, parts[index], sums[index] is not None),
                    inner,
                    lhs,
                    output_weight,
                    *([] if sums[index] is None else [sums[index]]),
                    flops=18 * drive.size * LANES,
                )
        got = swap_cores(give)
        mixed = call(
            functools.partial(mixed_kernel, lanes),
            taps,
            drive,
            start_state,
            pole,
            scale,
            *arrived,
        )
        if lanes != parts[-1]:
            sums[0], lhs = call(
                functools.partial(opening_kernel, lanes, parts[0], sums[0] is not None),
                (inner, taps),
                mixed,
                got,
                edge,
                output_weight,
                *([] if sums[0] is None else [sums[0]]),
                aliases={0: 1},
                flops=18 * drive.size * LANES,
            )
            before = lanes
    result, _ = call(
        functools.partial(result_kernel, parts[-1], parts),
        (of(frames.shape, narrow), taps),
        mixed,
        got,
        edge,
        output_weight,
        *([] if sums[0] is None else sums),
        out_specs=(HBM, WHOLE),
        aliases={0: 1},
        scratch=[
            pltpu.VMEM(frames.shape, narrow),
            pltpu.SemaphoreType.DMA((count, len(parts))),
        ],
        flops=18 * drive.size * channels,
    )
    return result


def solution(mesh):
    return jax.shard_map(
        on_device,
        mesh=mesh,
        in_specs=(P("tm", "sx", "sy", None), P(), P(), P(), P(), P("sx", "sy", None)),
        out_specs=P("tm", "sx", "sy", None),
        check_vma=False,
    )
```

```python
import functools
import math

import jax
import jax.numpy as jnp
from jax import lax
from jax.experimental import pallas as pl
from jax.experimental.pallas import tpu as pltpu
from jax.sharding import PartitionSpec as P

NPOLES = 16
VMEM_LIMIT = 24 * 1024 * 1024
WHOLE = pl.BlockSpec(memory_space=pltpu.VMEM)
HBM = pl.BlockSpec(memory_space=pltpu.HBM)
EDGES_COST = 2_000_000_000


def call(kernel, out_shape, *args, scratch=(), flops=0, out_specs=None, aliases=None):
    outs = jax.tree.leaves(out_shape)
    moved = sum(leaf.size * leaf.dtype.itemsize for leaf in (*args, *outs))
    return pl.pallas_call(
        kernel,
        in_specs=[WHOLE] * len(args),
        out_specs=out_specs or jax.tree.map(lambda _: WHOLE, out_shape),
        out_shape=out_shape,
        scratch_shapes=scratch,
        input_output_aliases=aliases or {},
        compiler_params=pltpu.CompilerParams(vmem_limit_bytes=VMEM_LIMIT),
        cost_estimate=pl.CostEstimate(flops=flops, bytes_accessed=moved, transcendentals=0),
    )(*args)


def of(shape, dtype):
    return jax.ShapeDtypeStruct(shape, dtype)


def is_core(which):
    return (lax.axis_index("sx") == which).astype(jnp.float32)


def rate_of(pole_ref):
    pole = pole_ref[...].astype(jnp.float32)
    return -0.001 * jnp.exp(pole * (math.log(300.0) / (NPOLES - 1)))


def inner_row(rows):
    return jnp.where(lax.axis_index("sx") == 0, rows - 1, 0)


def swap_cores(array):
    return lax.ppermute(array, "sx", [(0, 1), (1, 0)])


def put_columns(index, left, right, give_ref, keep_ref):
    zero, one = is_core(0), is_core(1)
    count, rows, _ = keep_ref.shape
    at = give_ref.shape[0] - (count - index) * rows
    give_ref[at : at + rows] = (zero * right + one * left).astype(give_ref.dtype)
    keep_ref[index] = (zero * left + one * right).astype(keep_ref.dtype)


def edges_kernel(cells_ref, give_ref, keep_ref, wide_ref):
    count, rows, cols, channels = cells_ref.shape
    for frame in range(count):
        give_ref[frame * cols : (frame + 1) * cols] = cells_ref[frame, inner_row(rows)]
        tile = cells_ref[frame].reshape(rows * cols, channels).astype(jnp.float32)
        lanes = wide_ref.shape[-1]
        for part in range(channels // lanes):
            wide_ref[frame, part] = tile[:, part * lanes : (part + 1) * lanes]

        def column(col):
            parts = [
                wide_ref[frame, part, pl.ds(col, rows, stride=cols), :]
                for part in range(channels // lanes)
            ]
            return jnp.concatenate(parts, axis=1)

        for depth in range(2):
            left, right = column(depth), column(cols - 1 - depth)
            put_columns(2 * frame + depth, left, right, give_ref, keep_ref)


def start_edges_kernel(start_ref, _, __, give_ref, keep_ref):
    tile, cols = start_ref[...], start_ref.shape[1]
    index = keep_ref.shape[0] - 1
    put_columns(index, tile[:, 0, :], tile[:, cols - 1, :], give_ref, keep_ref)


def trade_columns(give, keep, at):
    chips = lax.axis_size("sy")
    got = swap_cores(give)
    pairs = [(chip, chips + chip - 1) for chip in range(1, chips)]
    pairs += [(after, before) for before, after in pairs]
    columns = jnp.concatenate([keep, got[at:].reshape(keep.shape)], axis=1)
    return got, lax.ppermute(columns, ("sx", "sy"), pairs)


def put_cells(lhs_ref, at, size, cols, first, cells):
    count, channels = cells.shape
    upper, lower = min(count, size - cols - first), max(0, cols - first)
    here = at + first
    lhs_ref[here : here + count, channels : 2 * channels] = cells
    lhs_ref[here + cols : here + cols + upper, :channels] = cells[:upper]
    lhs_ref[here + lower - cols : here + count - cols, 2 * channels :] = cells[lower:]


def put_row(lhs_ref, at, size, row):
    cols, channels = row.shape
    row = row.astype(jnp.float32)
    last = slice(at + size - cols, at + size)
    lhs_ref[at : at + cols, :channels] = (is_core(1) * row).astype(lhs_ref.dtype)
    lhs_ref[last, 2 * channels :] = (is_core(0) * row).astype(lhs_ref.dtype)


def taps_kernel(cells_ref, lhs_ref):
    count, rows, cols, channels = cells_ref.shape
    size = rows * cols
    for frame in range(count):
        put_cells(lhs_ref, frame * size, size, cols, 0, cells_ref[frame].reshape(size, channels))


def row_taps(column, above, below):
    rows = column.shape[0]
    row = lax.broadcasted_iota(jnp.int32, column.shape, 0)
    up = jnp.where(row == 0, is_core(1) * above, pltpu.roll(column, 1, 0))
    down = jnp.where(row == rows - 1, is_core(0) * below, pltpu.roll(column, rows - 1, 0))
    return jnp.concatenate([up, column, down], axis=1)


def halves(channels):
    return slice(0, channels // 2), slice(channels // 2, channels)


def end_state(frames, pole_ref, lanes):
    decay = jnp.exp(rate_of(pole_ref))[:, lanes]
    state = frames[0]
    for frame in frames[1:]:
        state = decay * state + frame
    return state


def dot(lhs, weight_ref, column, lanes, inputs=slice(None)):
    weight = weight_ref[:, column, inputs, lanes].reshape(lhs.shape[1], -1)
    return jnp.dot(lhs, weight, preferred_element_type=jnp.float32)


def main_kernel(_, got_ref, weight_ref, pole_ref, total_ref, spill_ref, end_ref, lhs_ref):
    count, rows, cols, _ = total_ref.shape
    size = rows * cols
    for frame in range(count):
        put_row(lhs_ref, frame * size, size, got_ref[frame * cols : (frame + 1) * cols])
    for lanes in halves(weight_ref.shape[-1]):
        tile = (count, rows, cols, lanes.stop - lanes.start)
        col = lax.broadcasted_iota(jnp.int32, tile, 2)
        total = dot(lhs_ref[...], weight_ref, 1, lanes).reshape(tile)
        first = dot(lhs_ref[...], weight_ref, 0, lanes).reshape(tile)
        spill_ref[1, :, lanes] = first[:, :, cols - 1, :].reshape(count * rows, -1)
        total += jnp.where(col == 0, 0.0, pltpu.roll(first, 1, 2))
        last = dot(lhs_ref[...], weight_ref, 2, lanes).reshape(tile)
        spill_ref[0, :, lanes] = last[:, :, 0, :].reshape(count * rows, -1)
        total += jnp.where(col == cols - 1, 0.0, pltpu.roll(last, cols - 1, 2))
        total_ref[:, :, :, lanes] = total
        if lanes.start == 0:
            state = end_state([total[frame] for frame in range(count)], pole_ref, lanes)
            end_ref[...] = state.reshape(end_ref.shape).astype(end_ref.dtype)


def halo_kernel(mine_ref, theirs_ref, lhs_ref, start_ref):
    rows = mine_ref.shape[1] // 2
    count = mine_ref.shape[0] // 2
    room = count * rows
    zero, one = is_core(0), is_core(1)
    core = lax.axis_index("sx")
    slots = ((1, 0), (2, 3))
    for frame in range(count):
        for depth in range(2):
            own = mine_ref[2 * frame + depth].astype(jnp.float32)
            other = theirs_ref[2 * frame + depth].astype(jnp.float32)
            own = row_taps(own[rows:], own[rows - 1 : rows], own[:1])
            other = row_taps(other[:rows], other[2 * rows - 1 :], other[rows : rows + 1])
            for swapped, taps in enumerate((own, other)):
                slot = jnp.where(core == swapped, slots[0][depth], slots[1][depth])
                at = pl.multiple_of(slot * room + frame * rows, rows)
                lhs_ref[pl.ds(at, rows)] = taps.astype(lhs_ref.dtype)
    own = mine_ref[2 * count, rows:].astype(jnp.float32)
    other = theirs_ref[2 * count, :rows].astype(jnp.float32)
    start_ref[:rows] = zero * own + one * other
    start_ref[rows:] = zero * other + one * own


def drive_kernel(
    lhs_ref, weight_ref, total_ref, spill_ref, pole_ref, drive_ref, beside_ref, strips_ref, end_ref
):
    count, rows, cols, wide = drive_ref.shape
    room, size = count * rows, rows * cols
    at = size + 2 * rows
    for lanes in halves(weight_ref.shape[-1]):
        first = dot(lhs_ref[: 2 * room], weight_ref, 0, lanes)
        middle = dot(lhs_ref[room : 3 * room], weight_ref, 1, lanes)
        last = dot(lhs_ref[2 * room :], weight_ref, 2, lanes)
        left = (spill_ref[0, :, lanes] + first[:room] + middle[:room]).reshape(count, rows, wide)
        right = (spill_ref[1, :, lanes] + middle[room:] + last[room:]).reshape(count, rows, wide)
        total = total_ref[:, :, :, lanes]
        if lanes.start == 0:
            near = total[:, :, 0, :] + first[room:].reshape(count, rows, wide)
            far = total[:, :, cols - 1, :] + last[:room].reshape(count, rows, wide)
            strips = jnp.concatenate([left, near, far, right], axis=1)
            strips_ref[...] = strips
            state = end_state([strips[frame] for frame in range(count)], pole_ref, lanes)
            end_ref[at:] = state.astype(end_ref.dtype)
            continue
        col = lax.broadcasted_iota(jnp.int32, drive_ref.shape, 2)
        total += jnp.where(col == 0, first[room:].reshape(count, rows, 1, wide), 0.0)
        total += jnp.where(col == cols - 1, last[:room].reshape(count, rows, 1, wide), 0.0)
        drive_ref[...] = total
        state = end_state([total[frame] for frame in range(count)], pole_ref, lanes)
        end_ref[:size] = state.reshape(size, wide).astype(end_ref.dtype)
        beside = jnp.concatenate([left, right], axis=1)
        beside_ref[...] = beside
        state = end_state([beside[frame] for frame in range(count)], pole_ref, lanes)
        end_ref[size:at] = state.astype(end_ref.dtype)


def entry_kernel(frames, ends_ref, pole_ref, out_ref):
    carried = jnp.exp(frames * rate_of(pole_ref))
    entry = jnp.zeros(ends_ref.shape[1:], jnp.float32)
    out_ref[0] = entry.astype(out_ref.dtype)
    for index in range(ends_ref.shape[0] - 1):
        entry = carried * entry + ends_ref[index].astype(jnp.float32)
        out_ref[index + 1] = entry.astype(out_ref.dtype)


def exchange(pieces, pole, frames):
    groups = lax.axis_size("tm")
    arrivals = []
    for end, blocks in pieces:
        entries = []
        for rows, lanes in blocks:
            shares = end[rows].reshape(groups, -1, end.shape[1])
            shares = lax.all_to_all(shares, "tm", 0, 0)
            kernel = functools.partial(entry_kernel, frames)
            entry = call(kernel, of(shares.shape, end.dtype), shares, pole[:, lanes])
            entries.append(lax.all_to_all(entry, "tm", 0, 0).reshape(-1, end.shape[1]))
        arrivals.append((jnp.concatenate(entries, axis=0),))
    return arrivals


def pick(values):
    group = lax.axis_index("tm")
    picked = values[-1]
    for index, value in enumerate(values[:-1]):
        picked = jnp.where(group == index, value, picked)
    return picked


def on_core(first, second):
    return jnp.where(lax.axis_index("sx") == 0, first, second)


def weigh(one, by_one, other, by_other):
    return by_one * one.astype(jnp.float32) + by_other * other.astype(jnp.float32)


def relay_kernel(frames, blocks, end_ref, got_ref, pole_ref, out_ref):
    for rows, lanes in blocks:
        rate = rate_of(pole_ref)[:, lanes]
        carried, twice = jnp.exp(frames * rate), jnp.exp(2 * frames * rate)
        none, same = jnp.zeros_like(rate), jnp.ones_like(rate)
        own = on_core(pick([carried, same, same, same]), pick([same, same, same, none]))
        got = on_core(pick([same, carried, carried, carried]), pick([none, none, twice, same]))
        out_ref[rows] = weigh(end_ref[rows], own, got_ref[rows], got).astype(out_ref.dtype)


def exchange_four(pieces, pole, frames):
    def along(pairs, core):
        return [(2 * source + core, 2 * target + core) for source, target in pairs]

    axes = ("tm", "sx")
    down = [(0, 2), (1, 3)]
    first_round = along([(0, 1), (1, 0), (2, 3)], 0) + along(down, 1)
    second_round = along(down, 0) + along([(0, 1), (2, 3), (3, 2)], 1)
    arrivals = []
    for end, blocks in pieces:
        got = lax.ppermute(end, axes, first_round)
        kernel = functools.partial(relay_kernel, frames, blocks)
        relayed = call(kernel, of(end.shape, end.dtype), end, got, pole)
        arrivals.append((got, lax.ppermute(relayed, axes, second_round)))
    return arrivals


class Mix:
    def __init__(self, lanes, count, arrived_refs, pole_ref, scale_ref):
        self.rate = rate_of(pole_ref)[:, lanes]
        self.scale = scale_ref[:, lanes]
        self.count = count
        self.arrived_refs = arrived_refs

    def entry(self, rows):
        parts = [ref[rows] for ref in self.arrived_refs]
        if len(parts) == 1:
            return parts[0].astype(jnp.float32)
        carried = jnp.exp(self.count * self.rate)
        none, same = jnp.zeros_like(self.rate), jnp.ones_like(self.rate)
        early = on_core(pick([none, same, none, same]), pick([none, none, carried, carried]))
        late = on_core(pick([none, none, same, carried]), pick([none, same, same, same]))
        return weigh(parts[0], early, parts[1], late)

    def __call__(self, drives, rows, start):
        decay = jnp.exp(self.rate)
        reach = jnp.exp((self.count * lax.axis_index("tm")).astype(jnp.float32) * self.rate)
        state = reach * start + self.entry(rows).reshape(start.shape)
        for drive in drives:
            state = decay * state + drive
            yield jax.nn.gelu(self.scale * state)


def middle_kernel(lanes, *refs):
    total_ref, start_ref, pole_ref, scale_ref, *arrived_refs, give_ref = refs
    count, rows, cols, _ = total_ref.shape
    mix = Mix(lanes, count, arrived_refs, pole_ref, scale_ref)
    inner = inner_row(rows)
    drives = [total_ref[frame, inner, :, lanes] for frame in range(count)]
    here = pl.ds(pl.multiple_of(inner * cols, cols), cols)
    col = lax.broadcasted_iota(jnp.int32, give_ref.shape[1:], 0)
    for frame, cells in enumerate(mix(drives, here, start_ref[inner, :, lanes])):
        cells = jnp.where((col == 0) | (col == cols - 1), 0.0, cells)
        give_ref[frame] = cells.astype(give_ref.dtype)


def mixed_kernel(lanes, inner_only, *refs):
    drive_ref, start_ref, pole_ref, scale_ref, *arrived_refs, lhs_ref = refs
    count, rows, cols, _ = drive_ref.shape
    wide = lanes.stop - lanes.start
    size = rows * cols
    room = (lhs_ref.shape[0] - count * size) // 2
    mix = Mix(lanes, count, arrived_refs, pole_ref, scale_ref)
    held = lanes if inner_only else slice(None)
    block = 8
    col = lax.broadcasted_iota(jnp.int32, (block, cols, wide), 1)
    for row in range(0, rows, block):
        here = slice(row, row + block)
        drives = [drive_ref[frame, here, :, held] for frame in range(count)]
        cells = slice(row * cols, (row + block) * cols)
        for frame, tile in enumerate(mix(drives, cells, start_ref[here, :, lanes])):
            if inner_only:
                tile = jnp.where((col == 0) | (col == cols - 1), 0.0, tile)
            tile = tile.reshape(block * cols, wide).astype(lhs_ref.dtype)
            put_cells(lhs_ref, room + frame * size, size, cols, row * cols, tile)


def strip_start_kernel(start_ref, sides_ref, out_ref):
    rows, cols, _ = start_ref.shape
    start = start_ref[...]
    out_ref[:rows] = sides_ref[:rows]
    out_ref[rows : 2 * rows] = start[:, 0, :]
    out_ref[2 * rows : 3 * rows] = start[:, cols - 1, :]
    out_ref[3 * rows :] = sides_ref[rows:]


def late_kernel(parts, *refs):
    drive_ref, beside_ref, strips_ref, start_ref, strip_start_ref, pole_ref, scale_ref, *refs = refs
    *arrived_refs, give_ref, beside_out_ref, strips_out_ref = refs
    count, rows, cols, wide = drive_ref.shape
    size = rows * cols
    inner = inner_row(rows)
    zero, one = is_core(0), is_core(1)
    chip, chips = lax.axis_index("sy"), lax.axis_size("sy")
    inside = [(chip > 0).astype(jnp.float32), (chip < chips - 1).astype(jnp.float32)]
    early, late = (Mix(lanes, count, arrived_refs, pole_ref, scale_ref) for lanes in parts)

    def columns_of(cells, count):
        return [cells[index * rows : (index + 1) * rows] for index in range(count)]

    starts = columns_of(strip_start_ref, 4)
    starts = jnp.concatenate([starts[0][:, parts[1]], starts[3][:, parts[1]]], axis=0)
    at = size + 2 * rows
    beside = late([beside_ref[frame] for frame in range(count)], slice(size, at), starts)
    strips = early(
        [strips_ref[frame] for frame in range(count)],
        slice(at, at + 4 * rows),
        strip_start_ref[:, parts[0]],
    )
    here = pl.ds(pl.multiple_of(inner * cols, cols), cols)
    drives = [drive_ref[frame, inner] for frame in range(count)]
    tile = late(drives, here, start_ref[inner, :, parts[1]])
    which = lax.broadcasted_iota(jnp.int32, (cols, wide), 0)
    for frame, (cells, sides, strip) in enumerate(zip(tile, beside, strips)):
        sides, strip = columns_of(sides, 2), columns_of(strip, 4)
        sides = [sides[0] * inside[0], sides[1] * inside[1]]
        strip = [strip[0] * inside[0], strip[1], strip[2], strip[3] * inside[1]]
        give_ref[frame, :cols] = cells.astype(give_ref.dtype)
        ends = jnp.zeros(which.shape, jnp.float32)
        for index, column in enumerate((*sides, *strip)):
            end = zero * column[rows - 1 :] + one * column[:1]
            ends = jnp.where(which == index, end, ends)
        give_ref[frame, cols:] = ends.astype(give_ref.dtype)
        beside_out_ref[frame] = jnp.concatenate(sides, axis=0).astype(give_ref.dtype)
        strips_out_ref[frame] = jnp.concatenate(strip, axis=0).astype(give_ref.dtype)


def put_columns_taps(lhs_ref, slots, frame, count, columns, ends):
    rows = columns.shape[0] // len(slots)
    columns, ends = columns.astype(jnp.float32), ends.astype(jnp.float32)
    for index, slot in enumerate(slots):
        column, end = columns[index * rows : (index + 1) * rows], ends[index : index + 1]
        at = slot + frame * rows
        lhs_ref[at : at + rows] = row_taps(column, end, end).astype(lhs_ref.dtype)


def tile_sum(tile, inputs, lanes, room, lhs_ref, weight_ref):
    count, rows, cols, wide = tile
    inner = count * rows * cols
    col = lax.broadcasted_iota(jnp.int32, tile, 2)

    def beside(cells):
        return cells.reshape(count, rows, 1, wide) if room else 0.0

    total = dot(lhs_ref[room : room + inner], weight_ref, 1, lanes, inputs).reshape(tile)
    first = dot(lhs_ref[: room + inner], weight_ref, 0, lanes, inputs)
    halo = beside(first[:room])
    total += jnp.where(col == 0, halo, pltpu.roll(first[room:].reshape(tile), 1, 2))
    last = dot(lhs_ref[room:], weight_ref, 2, lanes, inputs)
    halo = beside(last[inner:])
    return total + jnp.where(
        col == cols - 1, halo, pltpu.roll(last[:inner].reshape(tile), cols - 1, 2)
    )


def strip_sum(tile, inputs, lanes, lhs_ref, weight_ref):
    count, rows, cols, wide = tile
    room = count * rows
    col = lax.broadcasted_iota(jnp.int32, tile, 2)
    first = dot(lhs_ref[: 2 * room], weight_ref, 0, lanes, inputs)
    middle = dot(lhs_ref[room : 3 * room], weight_ref, 1, lanes, inputs)
    last = dot(lhs_ref[2 * room :], weight_ref, 2, lanes, inputs)
    total = 0.0
    for at, cells in (
        (0, first[:room] + middle[:room]),
        (1, first[room:]),
        (cols - 2, last[:room]),
        (cols - 1, middle[room:] + last[room:]),
    ):
        total = jnp.where(col == at, cells.reshape(count, rows, 1, wide), total)
    return total


def opening_kernel(inputs, lanes, _, got_ref, weight_ref, out_ref, lhs_ref):
    count, rows, cols, _ = out_ref.shape
    size = rows * cols
    for frame in range(count):
        put_row(lhs_ref, frame * size, size, got_ref[frame])
    out_ref[...] = tile_sum(out_ref.shape, inputs, lanes, 0, lhs_ref, weight_ref)


def further_kernel(inputs, lanes, lhs_ref, weight_ref, out_ref):
    out_ref[...] = tile_sum(out_ref.shape, inputs, lanes, 0, lhs_ref, weight_ref)


def result_kernel(
    parts, _, got_ref, beside_ref, strips_ref, weight_ref, *refs
):
    *before_refs, out_ref, lhs_ref, held_ref, strip_lhs_ref, sems = refs
    count, rows, cols, _ = held_ref.shape
    size, room = rows * cols, count * rows
    for frame in range(count):
        put_row(lhs_ref, room + frame * size, size, got_ref[frame, :cols])
        ends = got_ref[frame, cols:]
        put_columns_taps(
            lhs_ref, (0, room + count * size), frame, count, beside_ref[frame], ends
        )
        slots = [slot * room for slot in range(4)]
        put_columns_taps(
            strip_lhs_ref, slots, frame, count, strips_ref[frame], ends.astype(jnp.float32)[2:]
        )

    def store(frame, part):
        here = (frame, slice(None), slice(None), parts[part])
        return pltpu.make_async_copy(held_ref.at[here], out_ref.at[here], sems.at[frame, part])

    for part, lanes in enumerate(parts):
        tile = (count, rows, cols, lanes.stop - lanes.start)
        total = before_refs[part][...]
        total += strip_sum(tile, parts[0], lanes, strip_lhs_ref, weight_ref)
        total += tile_sum(tile, parts[1], lanes, room, lhs_ref, weight_ref)
        for frame in range(count):
            held_ref[frame, :, :, lanes] = total[frame].astype(held_ref.dtype)
            store(frame, part).start()
    for part in range(len(parts)):
        for frame in range(count):
            store(frame, part).wait()


def on_device(frames, input_weight, output_weight, pole_index, gelu_scale, start_state):
    count, rows, cols, channels = frames.shape
    size, room = rows * cols, count * rows
    wide = 3 * channels
    assert lax.axis_size("sx") == 2
    narrow = frames.dtype
    pole, scale = pole_index[None], gelu_scale[None]

    shapes = (
        of((count * cols + (2 * count + 1) * rows, channels), narrow),
        of((2 * count + 1, rows, channels), narrow),
    )
    edges = call(
        edges_kernel,
        shapes,
        frames,
        scratch=[pltpu.VMEM((count, channels // 128, size, 128), jnp.float32)],
        flops=EDGES_COST,
    )
    give, keep = call(
        start_edges_kernel,
        shapes,
        start_state,
        *edges,
        aliases={1: 0, 2: 1},
    )
    got, mine = trade_columns(give, keep, count * cols)
    taps = of((count * size, wide), narrow)
    parts = halves(channels)
    half = channels // 2
    inner = of((count, rows, cols, half), jnp.float32)
    *main, early, _ = call(
        main_kernel,
        (
            of(frames.shape, jnp.float32),
            of((2, room, channels), jnp.float32),
            of((size, half), narrow),
            taps,
        ),
        call(taps_kernel, taps, frames),
        got,
        input_weight,
        pole,
        aliases={0: 3},
        flops=18 * frames.size * channels,
    )
    mine, total, spill = lax.optimization_barrier((mine, *main))
    halo, sides = call(
        halo_kernel,
        (of((4 * room, wide), narrow), of((2 * rows, channels), jnp.float32)),
        mine,
        swap_cores(mine),
    )
    drive, beside, strips, late = call(
        drive_kernel,
        (
            inner,
            of((count, 2 * rows, half), jnp.float32),
            of((count, 4 * rows, half), jnp.float32),
            of((size + 6 * rows, half), narrow),
        ),
        halo,
        input_weight,
        total,
        spill,
        pole,
        flops=36 * room * channels * channels,
    )
    at = size + 2 * rows
    pieces = [
        (early, [(slice(0, size), parts[0])]),
        (late, [(slice(0, at), parts[1]), (slice(at, at + 4 * rows), parts[0])]),
    ]
    exchanged = (exchange_four if lax.axis_size("tm") == 4 else exchange)(pieces, pole, count)
    early, late = exchanged

    mixing = (start_state, pole, scale)
    give = call(
        functools.partial(middle_kernel, parts[0]),
        of((count, cols, half), narrow),
        total,
        *mixing,
        *early,
    )
    taps = of((count * size, 3 * half), narrow)
    lhs = call(
        functools.partial(mixed_kernel, parts[0], True), taps, total, *mixing, *early
    )
    strip_start = call(strip_start_kernel, of((4 * rows, channels), jnp.float32), start_state, sides)
    flops = 18 * inner.size * half
    first_sum, lhs = call(
        functools.partial(opening_kernel, parts[0], parts[0]),
        (inner, taps),
        lhs,
        swap_cores(give),
        output_weight,
        aliases={0: 1},
        flops=flops,
    )
    second_sum = call(
        functools.partial(further_kernel, parts[0], parts[1]),
        inner,
        lhs,
        output_weight,
        flops=flops,
    )
    *late, first_sum, second_sum = lax.optimization_barrier((*late, first_sum, second_sum))
    give, beside, strips = call(
        functools.partial(late_kernel, parts),
        (
            of((count, 2 * cols, half), narrow),
            of(beside.shape, narrow),
            of(strips.shape, narrow),
        ),
        drive,
        beside,
        strips,
        start_state,
        strip_start,
        pole,
        scale,
        *late,
    )
    taps = of((count * size + 2 * room, 3 * half), narrow)
    lhs = call(functools.partial(mixed_kernel, parts[1], False), taps, drive, *mixing, *late)
    result, _ = call(
        functools.partial(result_kernel, parts),
        (of(frames.shape, narrow), taps),
        lhs,
        swap_cores(give),
        beside,
        strips,
        output_weight,
        first_sum,
        second_sum,
        out_specs=(HBM, WHOLE),
        aliases={0: 1},
        scratch=[
            pltpu.VMEM(frames.shape, narrow),
            pltpu.VMEM((4 * room, 3 * half), narrow),
            pltpu.SemaphoreType.DMA((count, len(parts))),
        ],
        flops=2 * flops,
    )
    return result


def solution(mesh):
    return jax.shard_map(
        on_device,
        mesh=mesh,
        in_specs=(P("tm", "sx", "sy", None), P(), P(), P(), P(), P("sx", "sy", None)),
        out_specs=P("tm", "sx", "sy", None),
        check_vma=False,
    )
```

```python
import functools
import math

import jax
import jax.numpy as jnp
from jax import lax
from jax.experimental import pallas as pl
from jax.experimental.pallas import tpu as pltpu
from jax.sharding import PartitionSpec as P

NPOLES = 16
VMEM_LIMIT = 24 * 1024 * 1024
WHOLE = pl.BlockSpec(memory_space=pltpu.VMEM)
HBM = pl.BlockSpec(memory_space=pltpu.HBM)
EDGES_COST = 2_000_000_000


def call(kernel, out_shape, *args, scratch=(), flops=0, out_specs=None, aliases=None):
    outs = jax.tree.leaves(out_shape)
    moved = sum(leaf.size * leaf.dtype.itemsize for leaf in (*args, *outs))
    return pl.pallas_call(
        kernel,
        in_specs=[WHOLE] * len(args),
        out_specs=out_specs or jax.tree.map(lambda _: WHOLE, out_shape),
        out_shape=out_shape,
        scratch_shapes=scratch,
        input_output_aliases=aliases or {},
        compiler_params=pltpu.CompilerParams(vmem_limit_bytes=VMEM_LIMIT),
        cost_estimate=pl.CostEstimate(flops=flops, bytes_accessed=moved, transcendentals=0),
    )(*args)


def of(shape, dtype):
    return jax.ShapeDtypeStruct(shape, dtype)


def is_core(which):
    return (lax.axis_index("sx") == which).astype(jnp.float32)


def rate_of(pole_ref):
    pole = pole_ref[...].astype(jnp.float32)
    return -0.001 * jnp.exp(pole * (math.log(300.0) / (NPOLES - 1)))


def inner_row(rows):
    return jnp.where(lax.axis_index("sx") == 0, rows - 1, 0)


def swap_cores(array):
    return lax.ppermute(array, "sx", [(0, 1), (1, 0)])


def put_columns(index, left, right, give_ref, keep_ref):
    zero, one = is_core(0), is_core(1)
    count, rows, _ = keep_ref.shape
    at = give_ref.shape[0] - (count - index) * rows
    give_ref[at : at + rows] = (zero * left + one * right).astype(give_ref.dtype)
    keep_ref[index] = (zero * right + one * left).astype(keep_ref.dtype)


def edges_kernel(cells_ref, give_ref, keep_ref, wide_ref):
    count, rows, cols, channels = cells_ref.shape
    for frame in range(count):
        give_ref[frame * cols : (frame + 1) * cols] = cells_ref[frame, inner_row(rows)]
        tile = cells_ref[frame].reshape(rows * cols, channels).astype(jnp.float32)
        lanes = wide_ref.shape[-1]
        for part in range(channels // lanes):
            wide_ref[frame, part] = tile[:, part * lanes : (part + 1) * lanes]

        def column(col):
            parts = [
                wide_ref[frame, part, pl.ds(col, rows, stride=cols), :]
                for part in range(channels // lanes)
            ]
            return jnp.concatenate(parts, axis=1)

        for depth in range(2):
            left, right = column(depth), column(cols - 1 - depth)
            put_columns(2 * frame + depth, left, right, give_ref, keep_ref)


def start_edges_kernel(start_ref, _, __, give_ref, keep_ref):
    tile, cols = start_ref[...], start_ref.shape[1]
    index = keep_ref.shape[0] - 1
    put_columns(index, tile[:, 0, :], tile[:, cols - 1, :], give_ref, keep_ref)


def trade_columns(give, keep, at):
    chips = lax.axis_size("sy")
    got = swap_cores(give)
    pairs = [(chip, chips + chip + 1) for chip in range(chips - 1)]
    pairs += [(after, before) for before, after in pairs]
    columns = jnp.concatenate([keep, got[at:].reshape(keep.shape)], axis=1)
    return got, lax.ppermute(columns, ("sx", "sy"), pairs)


def put_cells(lhs_ref, at, size, cols, first, cells):
    count, channels = cells.shape
    upper, lower = min(count, size - cols - first), max(0, cols - first)
    here = at + first
    lhs_ref[here : here + count, channels : 2 * channels] = cells
    lhs_ref[here + cols : here + cols + upper, :channels] = cells[:upper]
    lhs_ref[here + lower - cols : here + count - cols, 2 * channels :] = cells[lower:]


def put_row(lhs_ref, at, size, row):
    cols, channels = row.shape
    row = row.astype(jnp.float32)
    last = slice(at + size - cols, at + size)
    lhs_ref[at : at + cols, :channels] = (is_core(1) * row).astype(lhs_ref.dtype)
    lhs_ref[last, 2 * channels :] = (is_core(0) * row).astype(lhs_ref.dtype)


def taps_kernel(cells_ref, lhs_ref):
    count, rows, cols, channels = cells_ref.shape
    size = rows * cols
    for frame in range(count):
        put_cells(lhs_ref, frame * size, size, cols, 0, cells_ref[frame].reshape(size, channels))


def row_taps(column, above, below):
    rows = column.shape[0]
    row = lax.broadcasted_iota(jnp.int32, column.shape, 0)
    up = jnp.where(row == 0, is_core(1) * above, pltpu.roll(column, 1, 0))
    down = jnp.where(row == rows - 1, is_core(0) * below, pltpu.roll(column, rows - 1, 0))
    return jnp.concatenate([up, column, down], axis=1)


def halves(channels):
    return slice(0, channels // 2), slice(channels // 2, channels)


def end_state(frames, pole_ref, lanes):
    decay = jnp.exp(rate_of(pole_ref))[:, lanes]
    state = frames[0]
    for frame in frames[1:]:
        state = decay * state + frame
    return state


def dot(lhs, weight_ref, column, lanes, inputs=slice(None)):
    weight = weight_ref[:, column, inputs, lanes].reshape(lhs.shape[1], -1)
    return jnp.dot(lhs, weight, preferred_element_type=jnp.float32)


def main_kernel(_, got_ref, weight_ref, pole_ref, total_ref, spill_ref, end_ref, lhs_ref):
    count, rows, cols, _ = total_ref.shape
    size = rows * cols
    for frame in range(count):
        put_row(lhs_ref, frame * size, size, got_ref[frame * cols : (frame + 1) * cols])
    for lanes in halves(weight_ref.shape[-1]):
        tile = (count, rows, cols, lanes.stop - lanes.start)
        col = lax.broadcasted_iota(jnp.int32, tile, 2)
        total = dot(lhs_ref[...], weight_ref, 1, lanes).reshape(tile)
        first = dot(lhs_ref[...], weight_ref, 0, lanes).reshape(tile)
        spill_ref[1, :, lanes] = first[:, :, cols - 1, :].reshape(count * rows, -1)
        total += jnp.where(col == 0, 0.0, pltpu.roll(first, 1, 2))
        last = dot(lhs_ref[...], weight_ref, 2, lanes).reshape(tile)
        spill_ref[0, :, lanes] = last[:, :, 0, :].reshape(count * rows, -1)
        total += jnp.where(col == cols - 1, 0.0, pltpu.roll(last, cols - 1, 2))
        total_ref[:, :, :, lanes] = total
        if lanes.start == 0:
            state = end_state([total[frame] for frame in range(count)], pole_ref, lanes)
            end_ref[...] = state.reshape(end_ref.shape).astype(end_ref.dtype)


def halo_kernel(mine_ref, theirs_ref, lhs_ref, start_ref):
    rows = mine_ref.shape[1] // 2
    count = mine_ref.shape[0] // 2
    room = count * rows
    zero, one = is_core(0), is_core(1)
    core = lax.axis_index("sx")
    slots = ((1, 0), (2, 3))
    for frame in range(count):
        for depth in range(2):
            own = mine_ref[2 * frame + depth].astype(jnp.float32)
            other = theirs_ref[2 * frame + depth].astype(jnp.float32)
            own = row_taps(own[rows:], own[rows - 1 : rows], own[:1])
            other = row_taps(other[:rows], other[2 * rows - 1 :], other[rows : rows + 1])
            for swapped, taps in enumerate((own, other)):
                slot = jnp.where(core == swapped, slots[1][depth], slots[0][depth])
                at = pl.multiple_of(slot * room + frame * rows, rows)
                lhs_ref[pl.ds(at, rows)] = taps.astype(lhs_ref.dtype)
    own = mine_ref[2 * count, rows:].astype(jnp.float32)
    other = theirs_ref[2 * count, :rows].astype(jnp.float32)
    start_ref[:rows] = zero * other + one * own
    start_ref[rows:] = zero * own + one * other


def drive_kernel(
    lhs_ref, weight_ref, total_ref, spill_ref, pole_ref, drive_ref, beside_ref, strips_ref, end_ref
):
    count, rows, cols, wide = drive_ref.shape
    room, size = count * rows, rows * cols
    at = size + 2 * rows
    for lanes in halves(weight_ref.shape[-1]):
        first = dot(lhs_ref[: 2 * room], weight_ref, 0, lanes)
        middle = dot(lhs_ref[room : 3 * room], weight_ref, 1, lanes)
        last = dot(lhs_ref[2 * room :], weight_ref, 2, lanes)
        left = (spill_ref[0, :, lanes] + first[:room] + middle[:room]).reshape(count, rows, wide)
        right = (spill_ref[1, :, lanes] + middle[room:] + last[room:]).reshape(count, rows, wide)
        total = total_ref[:, :, :, lanes]
        if lanes.start == 0:
            near = total[:, :, 0, :] + first[room:].reshape(count, rows, wide)
            far = total[:, :, cols - 1, :] + last[:room].reshape(count, rows, wide)
            strips = jnp.concatenate([left, near, far, right], axis=1)
            strips_ref[...] = strips
            state = end_state([strips[frame] for frame in range(count)], pole_ref, lanes)
            end_ref[at:] = state.astype(end_ref.dtype)
            continue
        col = lax.broadcasted_iota(jnp.int32, drive_ref.shape, 2)
        total += jnp.where(col == 0, first[room:].reshape(count, rows, 1, wide), 0.0)
        total += jnp.where(col == cols - 1, last[:room].reshape(count, rows, 1, wide), 0.0)
        drive_ref[...] = total
        state = end_state([total[frame] for frame in range(count)], pole_ref, lanes)
        end_ref[:size] = state.reshape(size, wide).astype(end_ref.dtype)
        beside = jnp.concatenate([left, right], axis=1)
        beside_ref[...] = beside
        state = end_state([beside[frame] for frame in range(count)], pole_ref, lanes)
        end_ref[size:at] = state.astype(end_ref.dtype)


def entry_kernel(frames, ends_ref, pole_ref, out_ref):
    carried = jnp.exp(frames * rate_of(pole_ref))
    entry = jnp.zeros(ends_ref.shape[1:], jnp.float32)
    out_ref[0] = entry.astype(out_ref.dtype)
    for index in range(ends_ref.shape[0] - 1):
        entry = carried * entry + ends_ref[index].astype(jnp.float32)
        out_ref[index + 1] = entry.astype(out_ref.dtype)


def exchange(pieces, pole, frames):
    groups = lax.axis_size("tm")
    arrivals = []
    for end, blocks in pieces:
        entries = []
        for rows, lanes in blocks:
            shares = end[rows].reshape(groups, -1, end.shape[1])
            shares = lax.all_to_all(shares, "tm", 0, 0)
            kernel = functools.partial(entry_kernel, frames)
            entry = call(kernel, of(shares.shape, end.dtype), shares, pole[:, lanes])
            entries.append(lax.all_to_all(entry, "tm", 0, 0).reshape(-1, end.shape[1]))
        arrivals.append((jnp.concatenate(entries, axis=0),))
    return arrivals


def pick(values):
    group = lax.axis_index("tm")
    picked = values[-1]
    for index, value in enumerate(values[:-1]):
        picked = jnp.where(group == index, value, picked)
    return picked


def on_core(first, second):
    return jnp.where(lax.axis_index("sx") == 0, first, second)


def weigh(one, by_one, other, by_other):
    return by_one * one.astype(jnp.float32) + by_other * other.astype(jnp.float32)


def relay_kernel(frames, blocks, end_ref, got_ref, pole_ref, out_ref):
    for rows, lanes in blocks:
        rate = rate_of(pole_ref)[:, lanes]
        carried, twice = jnp.exp(frames * rate), jnp.exp(2 * frames * rate)
        none, same = jnp.zeros_like(rate), jnp.ones_like(rate)
        own = on_core(pick([carried, same, same, same]), pick([same, same, same, none]))
        got = on_core(pick([same, carried, carried, carried]), pick([none, none, twice, same]))
        out_ref[rows] = weigh(end_ref[rows], own, got_ref[rows], got).astype(out_ref.dtype)


def exchange_four(pieces, pole, frames):
    def along(pairs, core):
        return [(2 * source + core, 2 * target + core) for source, target in pairs]

    axes = ("tm", "sx")
    down = [(0, 2), (1, 3)]
    first_round = along([(0, 1), (1, 0), (2, 3)], 0) + along(down, 1)
    second_round = along(down, 0) + along([(0, 1), (2, 3), (3, 2)], 1)
    arrivals = []
    for end, blocks in pieces:
        got = lax.ppermute(end, axes, first_round)
        kernel = functools.partial(relay_kernel, frames, blocks)
        relayed = call(kernel, of(end.shape, end.dtype), end, got, pole)
        arrivals.append((got, lax.ppermute(relayed, axes, second_round)))
    return arrivals


class Mix:
    def __init__(self, lanes, count, arrived_refs, pole_ref, scale_ref):
        self.rate = rate_of(pole_ref)[:, lanes]
        self.scale = scale_ref[:, lanes]
        self.count = count
        self.arrived_refs = arrived_refs

    def entry(self, rows):
        parts = [ref[rows] for ref in self.arrived_refs]
        if len(parts) == 1:
            return parts[0].astype(jnp.float32)
        carried = jnp.exp(self.count * self.rate)
        none, same = jnp.zeros_like(self.rate), jnp.ones_like(self.rate)
        early = on_core(pick([none, same, none, same]), pick([none, none, carried, carried]))
        late = on_core(pick([none, none, same, carried]), pick([none, same, same, same]))
        return weigh(parts[0], early, parts[1], late)

    def __call__(self, drives, rows, start):
        decay = jnp.exp(self.rate)
        reach = jnp.exp((self.count * lax.axis_index("tm")).astype(jnp.float32) * self.rate)
        state = reach * start + self.entry(rows).reshape(start.shape)
        for drive in drives:
            state = decay * state + drive
            yield jax.nn.gelu(self.scale * state)


def middle_kernel(lanes, *refs):
    total_ref, start_ref, pole_ref, scale_ref, *arrived_refs, give_ref = refs
    count, rows, cols, _ = total_ref.shape
    mix = Mix(lanes, count, arrived_refs, pole_ref, scale_ref)
    inner = inner_row(rows)
    drives = [total_ref[frame, inner, :, lanes] for frame in range(count)]
    here = pl.ds(pl.multiple_of(inner * cols, cols), cols)
    col = lax.broadcasted_iota(jnp.int32, give_ref.shape[1:], 0)
    for frame, cells in enumerate(mix(drives, here, start_ref[inner, :, lanes])):
        cells = jnp.where((col == 0) | (col == cols - 1), 0.0, cells)
        give_ref[frame] = cells.astype(give_ref.dtype)


def mixed_kernel(lanes, inner_only, *refs):
    drive_ref, start_ref, pole_ref, scale_ref, *arrived_refs, lhs_ref = refs
    count, rows, cols, _ = drive_ref.shape
    wide = lanes.stop - lanes.start
    size = rows * cols
    room = (lhs_ref.shape[0] - count * size) // 2
    mix = Mix(lanes, count, arrived_refs, pole_ref, scale_ref)
    held = lanes if inner_only else slice(None)
    block = 8
    col = lax.broadcasted_iota(jnp.int32, (block, cols, wide), 1)
    for row in range(0, rows, block):
        here = slice(row, row + block)
        drives = [drive_ref[frame, here, :, held] for frame in range(count)]
        cells = slice(row * cols, (row + block) * cols)
        for frame, tile in enumerate(mix(drives, cells, start_ref[here, :, lanes])):
            if inner_only:
                tile = jnp.where((col == 0) | (col == cols - 1), 0.0, tile)
            tile = tile.reshape(block * cols, wide).astype(lhs_ref.dtype)
            put_cells(lhs_ref, room + frame * size, size, cols, row * cols, tile)


def strip_start_kernel(start_ref, sides_ref, out_ref):
    rows, cols, _ = start_ref.shape
    start = start_ref[...]
    out_ref[:rows] = sides_ref[:rows]
    out_ref[rows : 2 * rows] = start[:, 0, :]
    out_ref[2 * rows : 3 * rows] = start[:, cols - 1, :]
    out_ref[3 * rows :] = sides_ref[rows:]


def late_kernel(parts, *refs):
    drive_ref, beside_ref, strips_ref, start_ref, strip_start_ref, pole_ref, scale_ref, *refs = refs
    *arrived_refs, give_ref, beside_out_ref, strips_out_ref = refs
    count, rows, cols, wide = drive_ref.shape
    size = rows * cols
    inner = inner_row(rows)
    zero, one = is_core(0), is_core(1)
    chip, chips = lax.axis_index("sy"), lax.axis_size("sy")
    inside = [(chip > 0).astype(jnp.float32), (chip < chips - 1).astype(jnp.float32)]
    early, late = (Mix(lanes, count, arrived_refs, pole_ref, scale_ref) for lanes in parts)

    def columns_of(cells, count):
        return [cells[index * rows : (index + 1) * rows] for index in range(count)]

    starts = columns_of(strip_start_ref, 4)
    starts = jnp.concatenate([starts[0][:, parts[1]], starts[3][:, parts[1]]], axis=0)
    at = size + 2 * rows
    beside = late([beside_ref[frame] for frame in range(count)], slice(size, at), starts)
    strips = early(
        [strips_ref[frame] for frame in range(count)],
        slice(at, at + 4 * rows),
        strip_start_ref[:, parts[0]],
    )
    here = pl.ds(pl.multiple_of(inner * cols, cols), cols)
    drives = [drive_ref[frame, inner] for frame in range(count)]
    tile = late(drives, here, start_ref[inner, :, parts[1]])
    which = lax.broadcasted_iota(jnp.int32, (cols, wide), 0)
    for frame, (cells, sides, strip) in enumerate(zip(tile, beside, strips)):
        sides, strip = columns_of(sides, 2), columns_of(strip, 4)
        sides = [sides[0] * inside[0], sides[1] * inside[1]]
        strip = [strip[0] * inside[0], strip[1], strip[2], strip[3] * inside[1]]
        give_ref[frame, :cols] = cells.astype(give_ref.dtype)
        ends = jnp.zeros(which.shape, jnp.float32)
        for index, column in enumerate((*sides, *strip)):
            end = zero * column[rows - 1 :] + one * column[:1]
            ends = jnp.where(which == index, end, ends)
        give_ref[frame, cols:] = ends.astype(give_ref.dtype)
        beside_out_ref[frame] = jnp.concatenate(sides, axis=0).astype(give_ref.dtype)
        strips_out_ref[frame] = jnp.concatenate(strip, axis=0).astype(give_ref.dtype)


def put_columns_taps(lhs_ref, slots, frame, count, columns, ends):
    rows = columns.shape[0] // len(slots)
    columns, ends = columns.astype(jnp.float32), ends.astype(jnp.float32)
    for index, slot in enumerate(slots):
        column, end = columns[index * rows : (index + 1) * rows], ends[index : index + 1]
        at = slot + frame * rows
        lhs_ref[at : at + rows] = row_taps(column, end, end).astype(lhs_ref.dtype)


def tile_sum(tile, inputs, lanes, room, lhs_ref, weight_ref):
    count, rows, cols, wide = tile
    inner = count * rows * cols
    col = lax.broadcasted_iota(jnp.int32, tile, 2)

    def beside(cells):
        return cells.reshape(count, rows, 1, wide) if room else 0.0

    total = dot(lhs_ref[room : room + inner], weight_ref, 1, lanes, inputs).reshape(tile)
    first = dot(lhs_ref[: room + inner], weight_ref, 0, lanes, inputs)
    halo = beside(first[:room])
    total += jnp.where(col == 0, halo, pltpu.roll(first[room:].reshape(tile), 1, 2))
    last = dot(lhs_ref[room:], weight_ref, 2, lanes, inputs)
    halo = beside(last[inner:])
    return total + jnp.where(
        col == cols - 1, halo, pltpu.roll(last[:inner].reshape(tile), cols - 1, 2)
    )


def strip_sum(tile, inputs, lanes, lhs_ref, weight_ref):
    count, rows, cols, wide = tile
    room = count * rows
    col = lax.broadcasted_iota(jnp.int32, tile, 2)
    first = dot(lhs_ref[: 2 * room], weight_ref, 0, lanes, inputs)
    middle = dot(lhs_ref[room : 3 * room], weight_ref, 1, lanes, inputs)
    last = dot(lhs_ref[2 * room :], weight_ref, 2, lanes, inputs)
    total = 0.0
    for at, cells in (
        (0, first[:room] + middle[:room]),
        (1, first[room:]),
        (cols - 2, last[:room]),
        (cols - 1, middle[room:] + last[room:]),
    ):
        total = jnp.where(col == at, cells.reshape(count, rows, 1, wide), total)
    return total


def opening_kernel(inputs, lanes, _, got_ref, weight_ref, out_ref, lhs_ref):
    count, rows, cols, _ = out_ref.shape
    size = rows * cols
    for frame in range(count):
        put_row(lhs_ref, frame * size, size, got_ref[frame])
    out_ref[...] = tile_sum(out_ref.shape, inputs, lanes, 0, lhs_ref, weight_ref)


def further_kernel(inputs, lanes, lhs_ref, weight_ref, out_ref):
    out_ref[...] = tile_sum(out_ref.shape, inputs, lanes, 0, lhs_ref, weight_ref)


def result_kernel(
    parts, _, got_ref, beside_ref, strips_ref, weight_ref, *refs
):
    *before_refs, out_ref, lhs_ref, held_ref, strip_lhs_ref, sems = refs
    count, rows, cols, _ = held_ref.shape
    size, room = rows * cols, count * rows
    for frame in range(count):
        put_row(lhs_ref, room + frame * size, size, got_ref[frame, :cols])
        ends = got_ref[frame, cols:]
        put_columns_taps(
            lhs_ref, (0, room + count * size), frame, count, beside_ref[frame], ends
        )
        slots = [slot * room for slot in range(4)]
        put_columns_taps(
            strip_lhs_ref, slots, frame, count, strips_ref[frame], ends.astype(jnp.float32)[2:]
        )

    def store(frame, part):
        here = (frame, slice(None), slice(None), parts[part])
        return pltpu.make_async_copy(held_ref.at[here], out_ref.at[here], sems.at[frame, part])

    for part, lanes in enumerate(parts):
        tile = (count, rows, cols, lanes.stop - lanes.start)
        total = before_refs[part][...]
        total += strip_sum(tile, parts[0], lanes, strip_lhs_ref, weight_ref)
        total += tile_sum(tile, parts[1], lanes, room, lhs_ref, weight_ref)
        for frame in range(count):
            held_ref[frame, :, :, lanes] = total[frame].astype(held_ref.dtype)
            store(frame, part).start()
    for part in range(len(parts)):
        for frame in range(count):
            store(frame, part).wait()


def on_device(frames, input_weight, output_weight, pole_index, gelu_scale, start_state):
    count, rows, cols, channels = frames.shape
    size, room = rows * cols, count * rows
    wide = 3 * channels
    assert lax.axis_size("sx") == 2
    narrow = frames.dtype
    pole, scale = pole_index[None], gelu_scale[None]

    shapes = (
        of((count * cols + (2 * count + 1) * rows, channels), narrow),
        of((2 * count + 1, rows, channels), narrow),
    )
    edges = call(
        edges_kernel,
        shapes,
        frames,
        scratch=[pltpu.VMEM((count, channels // 128, size, 128), jnp.float32)],
        flops=EDGES_COST,
    )
    give, keep = call(
        start_edges_kernel,
        shapes,
        start_state,
        *edges,
        aliases={1: 0, 2: 1},
    )
    got, mine = trade_columns(give, keep, count * cols)
    taps = of((count * size, wide), narrow)
    parts = halves(channels)
    half = channels // 2
    inner = of((count, rows, cols, half), jnp.float32)
    *main, early, _ = call(
        main_kernel,
        (
            of(frames.shape, jnp.float32),
            of((2, room, channels), jnp.float32),
            of((size, half), narrow),
            taps,
        ),
        call(taps_kernel, taps, frames),
        got,
        input_weight,
        pole,
        aliases={0: 3},
        flops=18 * frames.size * channels,
    )
    mine, total, spill = lax.optimization_barrier((mine, *main))
    halo, sides = call(
        halo_kernel,
        (of((4 * room, wide), narrow), of((2 * rows, channels), jnp.float32)),
        mine,
        swap_cores(mine),
    )
    drive, beside, strips, late = call(
        drive_kernel,
        (
            inner,
            of((count, 2 * rows, half), jnp.float32),
            of((count, 4 * rows, half), jnp.float32),
            of((size + 6 * rows, half), narrow),
        ),
        halo,
        input_weight,
        total,
        spill,
        pole,
        flops=36 * room * channels * channels,
    )
    at = size + 2 * rows
    pieces = [
        (early, [(slice(0, size), parts[0])]),
        (late, [(slice(0, at), parts[1]), (slice(at, at + 4 * rows), parts[0])]),
    ]
    exchanged = (exchange_four if lax.axis_size("tm") == 4 else exchange)(pieces, pole, count)
    early, late = exchanged

    mixing = (start_state, pole, scale)
    give = call(
        functools.partial(middle_kernel, parts[0]),
        of((count, cols, half), narrow),
        total,
        *mixing,
        *early,
    )
    taps = of((count * size, 3 * half), narrow)
    lhs = call(
        functools.partial(mixed_kernel, parts[0], True), taps, total, *mixing, *early
    )
    strip_start = call(strip_start_kernel, of((4 * rows, channels), jnp.float32), start_state, sides)
    flops = 18 * inner.size * half
    first_sum, lhs = call(
        functools.partial(opening_kernel, parts[0], parts[0]),
        (inner, taps),
        lhs,
        swap_cores(give),
        output_weight,
        aliases={0: 1},
        flops=flops,
    )
    second_sum = call(
        functools.partial(further_kernel, parts[0], parts[1]),
        inner,
        lhs,
        output_weight,
        flops=flops,
    )
    *late, first_sum, second_sum = lax.optimization_barrier((*late, first_sum, second_sum))
    give, beside, strips = call(
        functools.partial(late_kernel, parts),
        (
            of((count, 2 * cols, half), narrow),
            of(beside.shape, narrow),
            of(strips.shape, narrow),
        ),
        drive,
        beside,
        strips,
        start_state,
        strip_start,
        pole,
        scale,
        *late,
    )
    taps = of((count * size + 2 * room, 3 * half), narrow)
    lhs = call(functools.partial(mixed_kernel, parts[1], False), taps, drive, *mixing, *late)
    result, _ = call(
        functools.partial(result_kernel, parts),
        (of(frames.shape, narrow), taps),
        lhs,
        swap_cores(give),
        beside,
        strips,
        output_weight,
        first_sum,
        second_sum,
        out_specs=(HBM, WHOLE),
        aliases={0: 1},
        scratch=[
            pltpu.VMEM(frames.shape, narrow),
            pltpu.VMEM((4 * room, 3 * half), narrow),
            pltpu.SemaphoreType.DMA((count, len(parts))),
        ],
        flops=2 * flops,
    )
    return result


def solution(mesh):
    return jax.shard_map(
        on_device,
        mesh=mesh,
        in_specs=(P("tm", "sx", "sy", None), P(), P(), P(), P(), P("sx", "sy", None)),
        out_specs=P("tm", "sx", "sy", None),
        check_vma=False,
    )
```

```python
import functools
import math

import jax
import jax.numpy as jnp
from jax import lax
from jax.experimental import pallas as pl
from jax.experimental.pallas import tpu as pltpu
from jax.sharding import PartitionSpec as P

NPOLES = 16
VMEM_LIMIT = 24 * 1024 * 1024
WHOLE = pl.BlockSpec(memory_space=pltpu.VMEM)
HBM = pl.BlockSpec(memory_space=pltpu.HBM)
EDGES_COST = 2_000_000_000


def call(kernel, out_shape, *args, scratch=(), flops=0, out_specs=None, aliases=None):
    outs = jax.tree.leaves(out_shape)
    moved = sum(leaf.size * leaf.dtype.itemsize for leaf in (*args, *outs))
    return pl.pallas_call(
        kernel,
        in_specs=[WHOLE] * len(args),
        out_specs=out_specs or jax.tree.map(lambda _: WHOLE, out_shape),
        out_shape=out_shape,
        scratch_shapes=scratch,
        input_output_aliases=aliases or {},
        compiler_params=pltpu.CompilerParams(vmem_limit_bytes=VMEM_LIMIT),
        cost_estimate=pl.CostEstimate(flops=flops, bytes_accessed=moved, transcendentals=0),
    )(*args)


def of(shape, dtype):
    return jax.ShapeDtypeStruct(shape, dtype)


def is_core(which):
    return (lax.axis_index("sx") == which).astype(jnp.float32)


def rate_of(pole_ref):
    pole = pole_ref[...].astype(jnp.float32)
    return -0.001 * jnp.exp(pole * (math.log(300.0) / (NPOLES - 1)))


def inner_row(rows):
    return jnp.where(lax.axis_index("sx") == 0, rows - 1, 0)


def swap_cores(array):
    return lax.ppermute(array, "sx", [(0, 1), (1, 0)])


def put_columns(index, left, right, give_ref, keep_ref):
    zero, one = is_core(0), is_core(1)
    count, rows, _ = keep_ref.shape
    at = give_ref.shape[0] - (count - index) * rows
    give_ref[at : at + rows] = (zero * left + one * right).astype(give_ref.dtype)
    keep_ref[index] = (zero * right + one * left).astype(keep_ref.dtype)


def edges_kernel(cells_ref, give_ref, keep_ref, wide_ref):
    count, rows, cols, channels = cells_ref.shape
    for frame in range(count):
        give_ref[frame * cols : (frame + 1) * cols] = cells_ref[frame, inner_row(rows)]
        tile = cells_ref[frame].reshape(rows * cols, channels).astype(jnp.float32)
        lanes = wide_ref.shape[-1]
        for part in range(channels // lanes):
            wide_ref[frame, part] = tile[:, part * lanes : (part + 1) * lanes]

        def column(col):
            parts = [
                wide_ref[frame, part, pl.ds(col, rows, stride=cols), :]
                for part in range(channels // lanes)
            ]
            return jnp.concatenate(parts, axis=1)

        for depth in range(2):
            left, right = column(depth), column(cols - 1 - depth)
            put_columns(2 * frame + depth, left, right, give_ref, keep_ref)


def start_edges_kernel(start_ref, _, __, give_ref, keep_ref):
    tile, cols = start_ref[...], start_ref.shape[1]
    index = keep_ref.shape[0] - 1
    put_columns(index, tile[:, 0, :], tile[:, cols - 1, :], give_ref, keep_ref)


def trade_columns(give, keep, at):
    chips = lax.axis_size("sy")
    got = swap_cores(give)
    pairs = [(chip, chips + chip + 1) for chip in range(chips - 1)]
    pairs += [(after, before) for before, after in pairs]
    columns = jnp.concatenate([keep, got[at:].reshape(keep.shape)], axis=1)
    return got, lax.ppermute(columns, ("sx", "sy"), pairs)


def put_cells(lhs_ref, at, size, cols, first, cells):
    count, channels = cells.shape
    upper, lower = min(count, size - cols - first), max(0, cols - first)
    here = at + first
    lhs_ref[here : here + count, channels : 2 * channels] = cells
    lhs_ref[here + cols : here + cols + upper, :channels] = cells[:upper]
    lhs_ref[here + lower - cols : here + count - cols, 2 * channels :] = cells[lower:]


def put_row(lhs_ref, at, size, row):
    cols, channels = row.shape
    row = row.astype(jnp.float32)
    last = slice(at + size - cols, at + size)
    lhs_ref[at : at + cols, :channels] = (is_core(1) * row).astype(lhs_ref.dtype)
    lhs_ref[last, 2 * channels :] = (is_core(0) * row).astype(lhs_ref.dtype)


def taps_kernel(cells_ref, lhs_ref):
    count, rows, cols, channels = cells_ref.shape
    size = rows * cols
    for frame in range(count):
        put_cells(lhs_ref, frame * size, size, cols, 0, cells_ref[frame].reshape(size, channels))


def row_taps(column, above, below):
    rows = column.shape[0]
    row = lax.broadcasted_iota(jnp.int32, column.shape, 0)
    up = jnp.where(row == 0, is_core(1) * above, pltpu.roll(column, 1, 0))
    down = jnp.where(row == rows - 1, is_core(0) * below, pltpu.roll(column, rows - 1, 0))
    return jnp.concatenate([up, column, down], axis=1)


def halves(channels):
    return slice(0, channels // 2), slice(channels // 2, channels)


def end_state(frames, pole_ref, lanes):
    decay = jnp.exp(rate_of(pole_ref))[:, lanes]
    state = frames[0]
    for frame in frames[1:]:
        state = decay * state + frame
    return state


def dot(lhs, weight_ref, column, lanes, inputs=slice(None)):
    weight = weight_ref[:, column, inputs, lanes].reshape(lhs.shape[1], -1)
    return jnp.dot(lhs, weight, preferred_element_type=jnp.float32)


def first_rows(rows):
    return rows // 4


def main_kernel(
    _, got_ref, weight_ref, pole_ref, total_ref, spill_ref, early_ref, late_ref, lhs_ref
):
    count, rows, cols, _ = total_ref.shape
    size = rows * cols
    for frame in range(count):
        put_row(lhs_ref, frame * size, size, got_ref[frame * cols : (frame + 1) * cols])
    for lanes in halves(weight_ref.shape[-1]):
        tile = (count, rows, cols, lanes.stop - lanes.start)
        col = lax.broadcasted_iota(jnp.int32, tile, 2)
        total = dot(lhs_ref[...], weight_ref, 1, lanes).reshape(tile)
        first = dot(lhs_ref[...], weight_ref, 0, lanes).reshape(tile)
        spill_ref[1, :, lanes] = first[:, :, cols - 1, :].reshape(count * rows, -1)
        total += jnp.where(col == 0, 0.0, pltpu.roll(first, 1, 2))
        last = dot(lhs_ref[...], weight_ref, 2, lanes).reshape(tile)
        spill_ref[0, :, lanes] = last[:, :, 0, :].reshape(count * rows, -1)
        total += jnp.where(col == cols - 1, 0.0, pltpu.roll(last, cols - 1, 2))
        total_ref[:, :, :, lanes] = total
        state = end_state([total[frame] for frame in range(count)], pole_ref, lanes)
        state = state.reshape(size, -1).astype(early_ref.dtype)
        if lanes.start == 0:
            early_ref[:size] = state
        else:
            cut = first_rows(rows) * cols
            early_ref[size:] = state[:cut]
            late_ref[: size - cut] = state[cut:]


def halo_kernel(mine_ref, theirs_ref, lhs_ref, start_ref):
    rows = mine_ref.shape[1] // 2
    count = mine_ref.shape[0] // 2
    room = count * rows
    zero, one = is_core(0), is_core(1)
    core = lax.axis_index("sx")
    slots = ((1, 0), (2, 3))
    for frame in range(count):
        for depth in range(2):
            own = mine_ref[2 * frame + depth].astype(jnp.float32)
            other = theirs_ref[2 * frame + depth].astype(jnp.float32)
            own = row_taps(own[rows:], own[rows - 1 : rows], own[:1])
            other = row_taps(other[:rows], other[2 * rows - 1 :], other[rows : rows + 1])
            for swapped, taps in enumerate((own, other)):
                slot = jnp.where(core == swapped, slots[1][depth], slots[0][depth])
                at = pl.multiple_of(slot * room + frame * rows, rows)
                lhs_ref[pl.ds(at, rows)] = taps.astype(lhs_ref.dtype)
    own = mine_ref[2 * count, rows:].astype(jnp.float32)
    other = theirs_ref[2 * count, :rows].astype(jnp.float32)
    start_ref[:rows] = zero * other + one * own
    start_ref[rows:] = zero * own + one * other


def strips_kernel(
    lhs_ref, weight_ref, total_ref, spill_ref, pole_ref, _, strips_ref, late_ref
):
    count, rows, cols, channels = total_ref.shape
    room = count * rows
    at = late_ref.shape[0] - 8 * rows
    for lanes in halves(channels):
        wide = lanes.stop - lanes.start
        first = dot(lhs_ref[: 2 * room], weight_ref, 0, lanes)
        middle = dot(lhs_ref[room : 3 * room], weight_ref, 1, lanes)
        last = dot(lhs_ref[2 * room :], weight_ref, 2, lanes)
        total = total_ref[:, :, :, lanes]
        strips = [
            (spill_ref[0, :, lanes] + first[:room] + middle[:room]).reshape(count, rows, wide),
            total[:, :, 0, :] + first[room:].reshape(count, rows, wide),
            total[:, :, cols - 1, :] + last[:room].reshape(count, rows, wide),
            (spill_ref[1, :, lanes] + middle[room:] + last[room:]).reshape(count, rows, wide),
        ]
        strips = jnp.concatenate(strips, axis=1)
        strips_ref[:, :, lanes] = strips
        state = end_state([strips[frame] for frame in range(count)], pole_ref, lanes)
        late_ref[at : at + 4 * rows] = state.astype(late_ref.dtype)
        at += 4 * rows


def entry_kernel(frames, ends_ref, pole_ref, out_ref):
    carried = jnp.exp(frames * rate_of(pole_ref))
    entry = jnp.zeros(ends_ref.shape[1:], jnp.float32)
    out_ref[0] = entry.astype(out_ref.dtype)
    for index in range(ends_ref.shape[0] - 1):
        entry = carried * entry + ends_ref[index].astype(jnp.float32)
        out_ref[index + 1] = entry.astype(out_ref.dtype)


def exchange(pieces, pole, frames):
    groups = lax.axis_size("tm")
    arrivals = []
    for end, blocks in pieces:
        entries = []
        for rows, lanes in blocks:
            shares = end[rows].reshape(groups, -1, end.shape[1])
            shares = lax.all_to_all(shares, "tm", 0, 0)
            kernel = functools.partial(entry_kernel, frames)
            entry = call(kernel, of(shares.shape, end.dtype), shares, pole[:, lanes])
            entries.append(lax.all_to_all(entry, "tm", 0, 0).reshape(-1, end.shape[1]))
        arrivals.append((jnp.concatenate(entries, axis=0),))
    return arrivals


def pick(values):
    group = lax.axis_index("tm")
    picked = values[-1]
    for index, value in enumerate(values[:-1]):
        picked = jnp.where(group == index, value, picked)
    return picked


def on_core(first, second):
    return jnp.where(lax.axis_index("sx") == 0, first, second)


def weigh(one, by_one, other, by_other):
    return by_one * one.astype(jnp.float32) + by_other * other.astype(jnp.float32)


def relay_kernel(frames, blocks, end_ref, got_ref, pole_ref, out_ref):
    for rows, lanes in blocks:
        rate = rate_of(pole_ref)[:, lanes]
        carried, twice = jnp.exp(frames * rate), jnp.exp(2 * frames * rate)
        none, same = jnp.zeros_like(rate), jnp.ones_like(rate)
        own = on_core(pick([carried, same, same, same]), pick([same, same, same, none]))
        got = on_core(pick([same, carried, carried, carried]), pick([none, none, twice, same]))
        out_ref[rows] = weigh(end_ref[rows], own, got_ref[rows], got).astype(out_ref.dtype)


def exchange_four(pieces, pole, frames):
    def along(pairs, core):
        return [(2 * source + core, 2 * target + core) for source, target in pairs]

    axes = ("tm", "sx")
    down = [(0, 2), (1, 3)]
    first_round = along([(0, 1), (1, 0), (2, 3)], 0) + along(down, 1)
    second_round = along(down, 0) + along([(0, 1), (2, 3), (3, 2)], 1)
    arrivals = []
    for end, blocks in pieces:
        got = lax.ppermute(end, axes, first_round)
        kernel = functools.partial(relay_kernel, frames, blocks)
        relayed = call(kernel, of(end.shape, end.dtype), end, got, pole)
        arrivals.append((got, lax.ppermute(relayed, axes, second_round)))
    return arrivals


class Mix:
    def __init__(self, lanes, count, pole_ref, scale_ref):
        self.rate = rate_of(pole_ref)[:, lanes]
        self.scale = scale_ref[:, lanes]
        self.count = count

    def entry(self, arrived_refs, rows):
        parts = [ref[rows] for ref in arrived_refs]
        if len(parts) == 1:
            return parts[0].astype(jnp.float32)
        carried = jnp.exp(self.count * self.rate)
        none, same = jnp.zeros_like(self.rate), jnp.ones_like(self.rate)
        early = on_core(pick([none, same, none, same]), pick([none, none, carried, carried]))
        late = on_core(pick([none, none, same, carried]), pick([none, same, same, same]))
        return weigh(parts[0], early, parts[1], late)

    def __call__(self, drives, entry, start):
        decay = jnp.exp(self.rate)
        reach = jnp.exp((self.count * lax.axis_index("tm")).astype(jnp.float32) * self.rate)
        state = reach * start + entry.reshape(start.shape)
        for drive in drives:
            state = decay * state + drive
            yield jax.nn.gelu(self.scale * state)


def no_border(cells, axis):
    col = lax.broadcasted_iota(jnp.int32, cells.shape, axis)
    return jnp.where((col == 0) | (col == cells.shape[axis] - 1), 0.0, cells)


def mixed_kernel(lanes, rounds, *refs):
    total_ref, start_ref, pole_ref, scale_ref, *arrived_refs, lhs_ref = refs
    count, rows, cols, _ = total_ref.shape
    size = rows * cols
    early_refs, late_refs = arrived_refs[:rounds], arrived_refs[rounds:]
    mix = Mix(lanes, count, pole_ref, scale_ref)
    block = first_rows(rows)
    for row in range(0, rows, block):
        here = slice(row, row + block)
        if lanes.start == 0:
            source, at = early_refs, row * cols
        elif row < block:
            source, at = early_refs, size
        else:
            source, at = late_refs, (row - block) * cols
        entry = mix.entry(source, slice(at, at + block * cols))
        drives = [total_ref[frame, here, :, lanes] for frame in range(count)]
        for frame, tile in enumerate(mix(drives, entry, start_ref[here, :, lanes])):
            tile = no_border(tile, 1).reshape(block * cols, -1).astype(lhs_ref.dtype)
            put_cells(lhs_ref, frame * size, size, cols, row * cols, tile)


def strip_start_kernel(start_ref, sides_ref, out_ref):
    rows, cols, _ = start_ref.shape
    start = start_ref[...]
    out_ref[:rows] = sides_ref[:rows]
    out_ref[rows : 2 * rows] = start[:, 0, :]
    out_ref[2 * rows : 3 * rows] = start[:, cols - 1, :]
    out_ref[3 * rows :] = sides_ref[rows:]


def late_kernel(rounds, *refs):
    total_ref, strips_ref, start_ref, strip_start_ref, pole_ref, scale_ref, *refs = refs
    *arrived_refs, give_ref, out_ref = refs
    early_refs, late_refs = arrived_refs[:rounds], arrived_refs[rounds:]
    count, rows, cols, channels = total_ref.shape
    size = rows * cols
    inner = inner_row(rows)
    zero, one = is_core(0), is_core(1)
    chip, chips = lax.axis_index("sy"), lax.axis_size("sy")
    inside = [(chip > 0).astype(jnp.float32), 1.0, 1.0, (chip < chips - 1).astype(jnp.float32)]
    cut = size - first_rows(rows) * cols
    for index, lanes in enumerate(halves(channels)):
        mix = Mix(lanes, count, pole_ref, scale_ref)
        here = slice(cut + 4 * rows * index, cut + 4 * rows * (index + 1))
        drives = [strips_ref[frame, :, lanes] for frame in range(count)]
        strips = mix(drives, mix.entry(late_refs, here), strip_start_ref[:, lanes])
        if index == 0:
            here = pl.ds(pl.multiple_of(inner * cols, cols), cols)
            entry = mix.entry(early_refs, here)
        else:
            entry = zero * mix.entry(late_refs, slice(cut - cols, cut))
            entry += one * mix.entry(early_refs, slice(size, size + cols))
        drives = [total_ref[frame, inner, :, lanes] for frame in range(count)]
        tile = mix(drives, entry, start_ref[inner, :, lanes])
        for frame, (cells, strip) in enumerate(zip(tile, strips)):
            give_ref[frame, :cols, lanes] = no_border(cells, 0).astype(give_ref.dtype)
            which = lax.broadcasted_iota(jnp.int32, cells.shape, 0)
            ends = jnp.zeros(cells.shape, jnp.float32)
            columns = []
            for slot, factor in enumerate(inside):
                column = factor * strip[slot * rows : (slot + 1) * rows]
                end = zero * column[rows - 1 :] + one * column[:1]
                ends = jnp.where(which == slot, end, ends)
                columns.append(column)
            give_ref[frame, cols:, lanes] = ends.astype(give_ref.dtype)
            out_ref[frame, :, lanes] = jnp.concatenate(columns, axis=0).astype(out_ref.dtype)


def put_columns_taps(lhs_ref, slots, frame, columns, ends):
    rows = columns.shape[0] // len(slots)
    columns, ends = columns.astype(jnp.float32), ends.astype(jnp.float32)
    for index, slot in enumerate(slots):
        column, end = columns[index * rows : (index + 1) * rows], ends[index : index + 1]
        at = slot + frame * rows
        lhs_ref[at : at + rows] = row_taps(column, end, end).astype(lhs_ref.dtype)


def tile_sum(tile, inputs, lanes, lhs_ref, weight_ref):
    cols = tile[2]
    col = lax.broadcasted_iota(jnp.int32, tile, 2)
    total = dot(lhs_ref[...], weight_ref, 1, lanes, inputs).reshape(tile)
    first = dot(lhs_ref[...], weight_ref, 0, lanes, inputs).reshape(tile)
    total += jnp.where(col == 0, 0.0, pltpu.roll(first, 1, 2))
    last = dot(lhs_ref[...], weight_ref, 2, lanes, inputs).reshape(tile)
    return total + jnp.where(col == cols - 1, 0.0, pltpu.roll(last, cols - 1, 2))


def strip_sum(tile, lanes, lhs_ref, weight_ref):
    count, rows, cols, wide = tile
    room = count * rows
    col = lax.broadcasted_iota(jnp.int32, tile, 2)
    first = dot(lhs_ref[: 2 * room], weight_ref, 0, lanes)
    middle = dot(lhs_ref[room : 3 * room], weight_ref, 1, lanes)
    last = dot(lhs_ref[2 * room :], weight_ref, 2, lanes)
    total = 0.0
    for at, cells in (
        (0, first[:room] + middle[:room]),
        (1, first[room:]),
        (cols - 2, last[:room]),
        (cols - 1, middle[room:] + last[room:]),
    ):
        total = jnp.where(col == at, cells.reshape(count, rows, 1, wide), total)
    return total


def row_sum(tile, inputs, lanes, got_ref, weight_ref):
    count, rows, cols, wide = tile
    given = jnp.concatenate([got_ref[frame, :cols, inputs] for frame in range(count)], axis=0)
    tap = jnp.where(lax.axis_index("sx") == 0, weight_ref.shape[0] - 1, 0)
    col = lax.broadcasted_iota(jnp.int32, (count, cols, wide), 1)

    def product(column):
        weight = weight_ref[pl.ds(tap, 1), column, inputs, lanes].reshape(given.shape[1], wide)
        total = jnp.dot(given, weight, preferred_element_type=jnp.float32)
        return total.reshape(count, cols, wide)

    total = product(1)
    total += jnp.where(col == 0, 0.0, pltpu.roll(product(0), 1, 1))
    total += jnp.where(col == cols - 1, 0.0, pltpu.roll(product(2), cols - 1, 1))
    row = lax.broadcasted_iota(jnp.int32, tile, 1)
    return jnp.where(row == inner_row(rows), total.reshape(count, 1, cols, wide), 0.0)


def opening_kernel(inputs, lanes, lhs_ref, weight_ref, out_ref):
    out_ref[...] = tile_sum(out_ref.shape, inputs, lanes, lhs_ref, weight_ref)


def result_kernel(parts, _, got_ref, strips_ref, weight_ref, *refs):
    *before_refs, out_ref, lhs_ref, held_ref, strip_lhs_ref, sems = refs
    count, rows, cols, _ = held_ref.shape
    size, room = rows * cols, count * rows
    slots = [slot * room for slot in range(4)]
    for frame in range(count):
        put_row(lhs_ref, frame * size, size, got_ref[frame, :cols, parts[1]])
        put_columns_taps(strip_lhs_ref, slots, frame, strips_ref[frame], got_ref[frame, cols:])

    def store(frame, part):
        here = (frame, slice(None), slice(None), parts[part])
        return pltpu.make_async_copy(held_ref.at[here], out_ref.at[here], sems.at[frame, part])

    for part, lanes in enumerate(parts):
        tile = (count, rows, cols, lanes.stop - lanes.start)
        total = before_refs[part][...]
        total += row_sum(tile, parts[0], lanes, got_ref, weight_ref)
        total += strip_sum(tile, lanes, strip_lhs_ref, weight_ref)
        total += tile_sum(tile, parts[1], lanes, lhs_ref, weight_ref)
        for frame in range(count):
            held_ref[frame, :, :, lanes] = total[frame].astype(held_ref.dtype)
            store(frame, part).start()
    for part in range(len(parts)):
        for frame in range(count):
            store(frame, part).wait()


def on_device(frames, input_weight, output_weight, pole_index, gelu_scale, start_state):
    count, rows, cols, channels = frames.shape
    size, room = rows * cols, count * rows
    wide = 3 * channels
    assert lax.axis_size("sx") == 2
    narrow = frames.dtype
    pole, scale = pole_index[None], gelu_scale[None]

    shapes = (
        of((count * cols + (2 * count + 1) * rows, channels), narrow),
        of((2 * count + 1, rows, channels), narrow),
    )
    edges = call(
        edges_kernel,
        shapes,
        frames,
        scratch=[pltpu.VMEM((count, channels // 128, size, 128), jnp.float32)],
        flops=EDGES_COST,
    )
    give, keep = call(
        start_edges_kernel,
        shapes,
        start_state,
        *edges,
        aliases={1: 0, 2: 1},
    )
    got, mine = trade_columns(give, keep, count * cols)
    taps = of((count * size, wide), narrow)
    parts = halves(channels)
    half = channels // 2
    inner = of((count, rows, cols, half), jnp.float32)
    cut = first_rows(rows) * cols
    *main, early, late, _ = call(
        main_kernel,
        (
            of(frames.shape, jnp.float32),
            of((2, room, channels), jnp.float32),
            of((size + cut, half), narrow),
            of((size - cut + 8 * rows, half), narrow),
            taps,
        ),
        call(taps_kernel, taps, frames),
        got,
        input_weight,
        pole,
        aliases={0: 4},
        flops=18 * frames.size * channels,
    )
    mine, total, spill, late = lax.optimization_barrier((mine, *main, late))
    halo, sides = call(
        halo_kernel,
        (of((4 * room, wide), narrow), of((2 * rows, channels), jnp.float32)),
        mine,
        swap_cores(mine),
    )
    strips, late = call(
        strips_kernel,
        (of((count, 4 * rows, channels), jnp.float32), of(late.shape, narrow)),
        halo,
        input_weight,
        total,
        spill,
        pole,
        late,
        aliases={5: 1},
        flops=36 * room * channels * channels,
    )
    at = size - cut
    pieces = [
        (early, [(slice(0, size), parts[0]), (slice(size, size + cut), parts[1])]),
        (
            late,
            [
                (slice(0, at), parts[1]),
                (slice(at, at + 4 * rows), parts[0]),
                (slice(at + 4 * rows, at + 8 * rows), parts[1]),
            ],
        ),
    ]
    early, late = (exchange_four if lax.axis_size("tm") == 4 else exchange)(pieces, pole, count)
    rounds = len(early)

    mixing = (start_state, pole, scale)
    taps = of((count * size, 3 * half), narrow)
    lhs = call(
        functools.partial(mixed_kernel, parts[0], rounds), taps, total, *mixing, *early
    )
    strip_start = call(strip_start_kernel, of((4 * rows, channels), jnp.float32), start_state, sides)
    flops = 18 * inner.size * half
    first_sum = call(
        functools.partial(opening_kernel, parts[0], parts[0]),
        inner,
        lhs,
        output_weight,
        flops=flops,
    )
    *late, first_sum = lax.optimization_barrier((*late, first_sum))
    give, strips = call(
        functools.partial(late_kernel, rounds),
        (of((count, 2 * cols, channels), narrow), of(strips.shape, narrow)),
        total,
        strips,
        start_state,
        strip_start,
        pole,
        scale,
        *early,
        *late,
    )
    give, lhs = lax.optimization_barrier((give, lhs))
    second_sum = call(
        functools.partial(opening_kernel, parts[0], parts[1]),
        inner,
        lhs,
        output_weight,
        flops=flops,
    )
    lhs = call(
        functools.partial(mixed_kernel, parts[1], rounds), taps, total, *mixing, *early, *late
    )
    result, _ = call(
        functools.partial(result_kernel, parts),
        (of(frames.shape, narrow), taps),
        lhs,
        swap_cores(give),
        strips,
        output_weight,
        first_sum,
        second_sum,
        out_specs=(HBM, WHOLE),
        aliases={0: 1},
        scratch=[
            pltpu.VMEM(frames.shape, narrow),
            pltpu.VMEM((4 * room, wide), narrow),
            pltpu.SemaphoreType.DMA((count, len(parts))),
        ],
        flops=2 * flops,
    )
    return result


def solution(mesh):
    return jax.shard_map(
        on_device,
        mesh=mesh,
        in_specs=(P("tm", "sx", "sy", None), P(), P(), P(), P(), P("sx", "sy", None)),
        out_specs=P("tm", "sx", "sy", None),
        check_vma=False,
    )
```

```python
import functools
import math

import jax
import jax.numpy as jnp
from jax import lax
from jax.experimental import pallas as pl
from jax.experimental.pallas import tpu as pltpu
from jax.sharding import PartitionSpec as P

NPOLES = 16
VMEM_LIMIT = 24 * 1024 * 1024
WHOLE = pl.BlockSpec(memory_space=pltpu.VMEM)
HBM = pl.BlockSpec(memory_space=pltpu.HBM)
EDGES_COST = 2_000_000_000


def call(kernel, out_shape, *args, scratch=(), flops=0, out_specs=None, aliases=None):
    outs = jax.tree.leaves(out_shape)
    moved = sum(leaf.size * leaf.dtype.itemsize for leaf in (*args, *outs))
    return pl.pallas_call(
        kernel,
        in_specs=[WHOLE] * len(args),
        out_specs=out_specs or jax.tree.map(lambda _: WHOLE, out_shape),
        out_shape=out_shape,
        scratch_shapes=scratch,
        input_output_aliases=aliases or {},
        compiler_params=pltpu.CompilerParams(vmem_limit_bytes=VMEM_LIMIT),
        cost_estimate=pl.CostEstimate(flops=flops, bytes_accessed=moved, transcendentals=0),
    )(*args)


def of(shape, dtype):
    return jax.ShapeDtypeStruct(shape, dtype)


def is_core(which):
    return (lax.axis_index("sx") == which).astype(jnp.float32)


def rate_of(pole_ref):
    pole = pole_ref[...].astype(jnp.float32)
    return -0.001 * jnp.exp(pole * (math.log(300.0) / (NPOLES - 1)))


def inner_row(rows):
    return jnp.where(lax.axis_index("sx") == 0, rows - 1, 0)


def swap_cores(array):
    return lax.ppermute(array, "sx", [(0, 1), (1, 0)])


def put_columns(index, left, right, give_ref, keep_ref):
    zero, one = is_core(0), is_core(1)
    count, rows, _ = keep_ref.shape
    at = give_ref.shape[0] - (count - index) * rows
    give_ref[at : at + rows] = (zero * left + one * right).astype(give_ref.dtype)
    keep_ref[index] = (zero * right + one * left).astype(keep_ref.dtype)


def edges_kernel(cells_ref, give_ref, keep_ref, wide_ref):
    count, rows, cols, channels = cells_ref.shape
    for frame in range(count):
        give_ref[frame * cols : (frame + 1) * cols] = cells_ref[frame, inner_row(rows)]
        tile = cells_ref[frame].reshape(rows * cols, channels).astype(jnp.float32)
        lanes = wide_ref.shape[-1]
        for part in range(channels // lanes):
            wide_ref[frame, part] = tile[:, part * lanes : (part + 1) * lanes]

        def column(col):
            parts = [
                wide_ref[frame, part, pl.ds(col, rows, stride=cols), :]
                for part in range(channels // lanes)
            ]
            return jnp.concatenate(parts, axis=1)

        for depth in range(2):
            left, right = column(depth), column(cols - 1 - depth)
            put_columns(2 * frame + depth, left, right, give_ref, keep_ref)


def start_edges_kernel(start_ref, _, __, give_ref, keep_ref):
    tile, cols = start_ref[...], start_ref.shape[1]
    index = keep_ref.shape[0] - 1
    put_columns(index, tile[:, 0, :], tile[:, cols - 1, :], give_ref, keep_ref)


def trade_columns(give, keep, at):
    chips = lax.axis_size("sy")
    got = swap_cores(give)
    pairs = [(chip, chips + chip + 1) for chip in range(chips - 1)]
    pairs += [(after, before) for before, after in pairs]
    columns = jnp.concatenate([keep, got[at:].reshape(keep.shape)], axis=1)
    return got, lax.ppermute(columns, ("sx", "sy"), pairs)


def put_cells(lhs_ref, at, size, cols, first, cells):
    count, channels = cells.shape
    upper, lower = min(count, size - cols - first), max(0, cols - first)
    here = at + first
    lhs_ref[here : here + count, channels : 2 * channels] = cells
    lhs_ref[here + cols : here + cols + upper, :channels] = cells[:upper]
    lhs_ref[here + lower - cols : here + count - cols, 2 * channels :] = cells[lower:]


def put_row(lhs_ref, at, size, row):
    cols, channels = row.shape
    row = row.astype(jnp.float32)
    last = slice(at + size - cols, at + size)
    lhs_ref[at : at + cols, :channels] = (is_core(1) * row).astype(lhs_ref.dtype)
    lhs_ref[last, 2 * channels :] = (is_core(0) * row).astype(lhs_ref.dtype)


def taps_kernel(cells_ref, lhs_ref):
    count, rows, cols, channels = cells_ref.shape
    size = rows * cols
    for frame in range(count):
        put_cells(lhs_ref, frame * size, size, cols, 0, cells_ref[frame].reshape(size, channels))


def row_taps(column, above, below):
    rows = column.shape[0]
    row = lax.broadcasted_iota(jnp.int32, column.shape, 0)
    up = jnp.where(row == 0, is_core(1) * above, pltpu.roll(column, 1, 0))
    down = jnp.where(row == rows - 1, is_core(0) * below, pltpu.roll(column, rows - 1, 0))
    return jnp.concatenate([up, column, down], axis=1)


def halves(channels):
    return slice(0, channels // 2), slice(channels // 2, channels)


def end_state(frames, pole_ref, lanes):
    decay = jnp.exp(rate_of(pole_ref))[:, lanes]
    state = frames[0]
    for frame in frames[1:]:
        state = decay * state + frame
    return state


def dot(lhs, weight_ref, column, lanes, inputs=slice(None)):
    weight = weight_ref[:, column, inputs, lanes].reshape(lhs.shape[1], -1)
    return jnp.dot(lhs, weight, preferred_element_type=jnp.float32)


def main_kernel(_, got_ref, weight_ref, pole_ref, total_ref, spill_ref, end_ref, lhs_ref):
    count, rows, cols, _ = total_ref.shape
    size = rows * cols
    for frame in range(count):
        put_row(lhs_ref, frame * size, size, got_ref[frame * cols : (frame + 1) * cols])
    for lanes in halves(weight_ref.shape[-1]):
        tile = (rows, cols, lanes.stop - lanes.start)
        col = lax.broadcasted_iota(jnp.int32, tile, 1)
        totals = []
        for frame in range(count):
            cells = lhs_ref[frame * size : (frame + 1) * size]
            here = slice(frame * rows, (frame + 1) * rows)
            total = dot(cells, weight_ref, 1, lanes).reshape(tile)
            first = dot(cells, weight_ref, 0, lanes).reshape(tile)
            spill_ref[1, here, lanes] = first[:, cols - 1, :]
            total += jnp.where(col == 0, 0.0, pltpu.roll(first, 1, 1))
            last = dot(cells, weight_ref, 2, lanes).reshape(tile)
            spill_ref[0, here, lanes] = last[:, 0, :]
            total += jnp.where(col == cols - 1, 0.0, pltpu.roll(last, cols - 1, 1))
            total_ref[frame, :, :, lanes] = total
            totals.append(total)
        if lanes.start == 0:
            state = end_state(totals, pole_ref, lanes)
            end_ref[...] = state.reshape(end_ref.shape).astype(end_ref.dtype)


def halo_kernel(mine_ref, theirs_ref, lhs_ref, start_ref):
    rows = mine_ref.shape[1] // 2
    count = mine_ref.shape[0] // 2
    room = count * rows
    zero, one = is_core(0), is_core(1)
    core = lax.axis_index("sx")
    slots = ((1, 0), (2, 3))
    for frame in range(count):
        for depth in range(2):
            own = mine_ref[2 * frame + depth].astype(jnp.float32)
            other = theirs_ref[2 * frame + depth].astype(jnp.float32)
            own = row_taps(own[rows:], own[rows - 1 : rows], own[:1])
            other = row_taps(other[:rows], other[2 * rows - 1 :], other[rows : rows + 1])
            for swapped, taps in enumerate((own, other)):
                slot = jnp.where(core == swapped, slots[1][depth], slots[0][depth])
                at = pl.multiple_of(slot * room + frame * rows, rows)
                lhs_ref[pl.ds(at, rows)] = taps.astype(lhs_ref.dtype)
    own = mine_ref[2 * count, rows:].astype(jnp.float32)
    other = theirs_ref[2 * count, :rows].astype(jnp.float32)
    start_ref[:rows] = zero * other + one * own
    start_ref[rows:] = zero * own + one * other


def drive_kernel(
    lhs_ref, weight_ref, total_ref, spill_ref, pole_ref, drive_ref, beside_ref, strips_ref, end_ref
):
    count, rows, cols, wide = drive_ref.shape
    room, size = count * rows, rows * cols
    at = size + 2 * rows
    for lanes in halves(weight_ref.shape[-1]):
        first = dot(lhs_ref[: 2 * room], weight_ref, 0, lanes)
        middle = dot(lhs_ref[room : 3 * room], weight_ref, 1, lanes)
        last = dot(lhs_ref[2 * room :], weight_ref, 2, lanes)
        left = (spill_ref[0, :, lanes] + first[:room] + middle[:room]).reshape(count, rows, wide)
        right = (spill_ref[1, :, lanes] + middle[room:] + last[room:]).reshape(count, rows, wide)
        total = total_ref[:, :, :, lanes]
        if lanes.start == 0:
            near = total[:, :, 0, :] + first[room:].reshape(count, rows, wide)
            far = total[:, :, cols - 1, :] + last[:room].reshape(count, rows, wide)
            strips = jnp.concatenate([left, near, far, right], axis=1)
            strips_ref[...] = strips
            state = end_state([strips[frame] for frame in range(count)], pole_ref, lanes)
            end_ref[at:] = state.astype(end_ref.dtype)
            continue
        col = lax.broadcasted_iota(jnp.int32, drive_ref.shape, 2)
        total += jnp.where(col == 0, first[room:].reshape(count, rows, 1, wide), 0.0)
        total += jnp.where(col == cols - 1, last[:room].reshape(count, rows, 1, wide), 0.0)
        drive_ref[...] = total
        state = end_state([total[frame] for frame in range(count)], pole_ref, lanes)
        end_ref[:size] = state.reshape(size, wide).astype(end_ref.dtype)
        beside = jnp.concatenate([left, right], axis=1)
        beside_ref[...] = beside
        state = end_state([beside[frame] for frame in range(count)], pole_ref, lanes)
        end_ref[size:at] = state.astype(end_ref.dtype)


def entry_kernel(frames, ends_ref, pole_ref, out_ref):
    carried = jnp.exp(frames * rate_of(pole_ref))
    entry = jnp.zeros(ends_ref.shape[1:], jnp.float32)
    out_ref[0] = entry.astype(out_ref.dtype)
    for index in range(ends_ref.shape[0] - 1):
        entry = carried * entry + ends_ref[index].astype(jnp.float32)
        out_ref[index + 1] = entry.astype(out_ref.dtype)


def exchange(pieces, pole, frames):
    groups = lax.axis_size("tm")
    arrivals = []
    for end, blocks in pieces:
        entries = []
        for rows, lanes in blocks:
            shares = end[rows].reshape(groups, -1, end.shape[1])
            shares = lax.all_to_all(shares, "tm", 0, 0)
            kernel = functools.partial(entry_kernel, frames)
            entry = call(kernel, of(shares.shape, end.dtype), shares, pole[:, lanes])
            entries.append(lax.all_to_all(entry, "tm", 0, 0).reshape(-1, end.shape[1]))
        arrivals.append((jnp.concatenate(entries, axis=0),))
    return arrivals


def pick(values):
    group = lax.axis_index("tm")
    picked = values[-1]
    for index, value in enumerate(values[:-1]):
        picked = jnp.where(group == index, value, picked)
    return picked


def on_core(first, second):
    return jnp.where(lax.axis_index("sx") == 0, first, second)


def weigh(one, by_one, other, by_other):
    return by_one * one.astype(jnp.float32) + by_other * other.astype(jnp.float32)


def relay_kernel(frames, blocks, end_ref, got_ref, pole_ref, out_ref):
    for rows, lanes in blocks:
        rate = rate_of(pole_ref)[:, lanes]
        carried, twice = jnp.exp(frames * rate), jnp.exp(2 * frames * rate)
        none, same = jnp.zeros_like(rate), jnp.ones_like(rate)
        own = on_core(pick([carried, same, same, same]), pick([same, same, same, none]))
        got = on_core(pick([same, carried, carried, carried]), pick([none, none, twice, same]))
        out_ref[rows] = weigh(end_ref[rows], own, got_ref[rows], got).astype(out_ref.dtype)


def exchange_four(pieces, pole, frames):
    def along(pairs, core):
        return [(2 * source + core, 2 * target + core) for source, target in pairs]

    axes = ("tm", "sx")
    down = [(0, 2), (1, 3)]
    first_round = along([(0, 1), (1, 0), (2, 3)], 0) + along(down, 1)
    second_round = along(down, 0) + along([(0, 1), (2, 3), (3, 2)], 1)
    arrivals = []
    for end, blocks in pieces:
        got = lax.ppermute(end, axes, first_round)
        kernel = functools.partial(relay_kernel, frames, blocks)
        relayed = call(kernel, of(end.shape, end.dtype), end, got, pole)
        arrivals.append((got, lax.ppermute(relayed, axes, second_round)))
    return arrivals


class Mix:
    def __init__(self, lanes, count, arrived_refs, pole_ref, scale_ref):
        self.rate = rate_of(pole_ref)[:, lanes]
        self.scale = scale_ref[:, lanes]
        self.count = count
        self.arrived_refs = arrived_refs

    def entry(self, rows):
        parts = [ref[rows] for ref in self.arrived_refs]
        if len(parts) == 1:
            return parts[0].astype(jnp.float32)
        carried = jnp.exp(self.count * self.rate)
        none, same = jnp.zeros_like(self.rate), jnp.ones_like(self.rate)
        early = on_core(pick([none, same, none, same]), pick([none, none, carried, carried]))
        late = on_core(pick([none, none, same, carried]), pick([none, same, same, same]))
        return weigh(parts[0], early, parts[1], late)

    def __call__(self, drives, rows, start):
        decay = jnp.exp(self.rate)
        reach = jnp.exp((self.count * lax.axis_index("tm")).astype(jnp.float32) * self.rate)
        state = reach * start + self.entry(rows).reshape(start.shape)
        for drive in drives:
            state = decay * state + drive
            yield jax.nn.gelu(self.scale * state)


def middle_kernel(lanes, *refs):
    total_ref, start_ref, pole_ref, scale_ref, *arrived_refs, give_ref = refs
    count, rows, cols, _ = total_ref.shape
    mix = Mix(lanes, count, arrived_refs, pole_ref, scale_ref)
    inner = inner_row(rows)
    drives = [total_ref[frame, inner, :, lanes] for frame in range(count)]
    here = pl.ds(pl.multiple_of(inner * cols, cols), cols)
    col = lax.broadcasted_iota(jnp.int32, give_ref.shape[1:], 0)
    for frame, cells in enumerate(mix(drives, here, start_ref[inner, :, lanes])):
        cells = jnp.where((col == 0) | (col == cols - 1), 0.0, cells)
        give_ref[frame] = cells.astype(give_ref.dtype)


def mixed_kernel(lanes, inner_only, *refs):
    drive_ref, start_ref, pole_ref, scale_ref, *arrived_refs, lhs_ref = refs
    count, rows, cols, _ = drive_ref.shape
    wide = lanes.stop - lanes.start
    size = rows * cols
    stride = lhs_ref.shape[0] // count
    room = (stride - size) // 2
    mix = Mix(lanes, count, arrived_refs, pole_ref, scale_ref)
    held = lanes if inner_only else slice(None)
    block = 8
    col = lax.broadcasted_iota(jnp.int32, (block, cols, wide), 1)
    for row in range(0, rows, block):
        here = slice(row, row + block)
        drives = [drive_ref[frame, here, :, held] for frame in range(count)]
        cells = slice(row * cols, (row + block) * cols)
        for frame, tile in enumerate(mix(drives, cells, start_ref[here, :, lanes])):
            if inner_only:
                tile = jnp.where((col == 0) | (col == cols - 1), 0.0, tile)
            tile = tile.reshape(block * cols, wide).astype(lhs_ref.dtype)
            put_cells(lhs_ref, frame * stride + room, size, cols, row * cols, tile)


def strip_start_kernel(start_ref, sides_ref, out_ref):
    rows, cols, _ = start_ref.shape
    start = start_ref[...]
    out_ref[:rows] = sides_ref[:rows]
    out_ref[rows : 2 * rows] = start[:, 0, :]
    out_ref[2 * rows : 3 * rows] = start[:, cols - 1, :]
    out_ref[3 * rows :] = sides_ref[rows:]


def late_kernel(parts, *refs):
    drive_ref, beside_ref, strips_ref, start_ref, strip_start_ref, pole_ref, scale_ref, *refs = refs
    *arrived_refs, give_ref, beside_out_ref, strips_out_ref = refs
    count, rows, cols, wide = drive_ref.shape
    size = rows * cols
    inner = inner_row(rows)
    zero, one = is_core(0), is_core(1)
    chip, chips = lax.axis_index("sy"), lax.axis_size("sy")
    inside = [(chip > 0).astype(jnp.float32), (chip < chips - 1).astype(jnp.float32)]
    early, late = (Mix(lanes, count, arrived_refs, pole_ref, scale_ref) for lanes in parts)

    def columns_of(cells, count):
        return [cells[index * rows : (index + 1) * rows] for index in range(count)]

    starts = columns_of(strip_start_ref, 4)
    starts = jnp.concatenate([starts[0][:, parts[1]], starts[3][:, parts[1]]], axis=0)
    at = size + 2 * rows
    beside = late([beside_ref[frame] for frame in range(count)], slice(size, at), starts)
    strips = early(
        [strips_ref[frame] for frame in range(count)],
        slice(at, at + 4 * rows),
        strip_start_ref[:, parts[0]],
    )
    here = pl.ds(pl.multiple_of(inner * cols, cols), cols)
    drives = [drive_ref[frame, inner] for frame in range(count)]
    tile = late(drives, here, start_ref[inner, :, parts[1]])
    which = lax.broadcasted_iota(jnp.int32, (cols, wide), 0)
    for frame, (cells, sides, strip) in enumerate(zip(tile, beside, strips)):
        sides, strip = columns_of(sides, 2), columns_of(strip, 4)
        sides = [sides[0] * inside[0], sides[1] * inside[1]]
        strip = [strip[0] * inside[0], strip[1], strip[2], strip[3] * inside[1]]
        give_ref[frame, :cols] = cells.astype(give_ref.dtype)
        ends = jnp.zeros(which.shape, jnp.float32)
        for index, column in enumerate((*sides, *strip)):
            end = zero * column[rows - 1 :] + one * column[:1]
            ends = jnp.where(which == index, end, ends)
        give_ref[frame, cols:] = ends.astype(give_ref.dtype)
        beside_out_ref[frame] = jnp.concatenate(sides, axis=0).astype(give_ref.dtype)
        strips_out_ref[frame] = jnp.concatenate(strip, axis=0).astype(give_ref.dtype)


def put_columns_taps(lhs_ref, slots, columns, ends):
    rows = columns.shape[0] // len(slots)
    columns, ends = columns.astype(jnp.float32), ends.astype(jnp.float32)
    for index, at in enumerate(slots):
        column, end = columns[index * rows : (index + 1) * rows], ends[index : index + 1]
        lhs_ref[at : at + rows] = row_taps(column, end, end).astype(lhs_ref.dtype)


def tile_sum(tile, inputs, lanes, room, lhs_ref, weight_ref):
    count, rows, cols, wide = tile
    size = rows * cols
    col = lax.broadcasted_iota(jnp.int32, tile[1:], 1)

    def beside(cells):
        return cells.reshape(rows, 1, wide) if room else 0.0

    for frame in range(count):
        at = frame * (size + 2 * room)
        end = at + room + size
        total = dot(lhs_ref[at + room : end], weight_ref, 1, lanes, inputs).reshape(tile[1:])
        first = dot(lhs_ref[at:end], weight_ref, 0, lanes, inputs)
        shifted = pltpu.roll(first[room:].reshape(tile[1:]), 1, 1)
        total += jnp.where(col == 0, beside(first[:room]), shifted)
        last = dot(lhs_ref[at + room : end + room], weight_ref, 2, lanes, inputs)
        shifted = pltpu.roll(last[:size].reshape(tile[1:]), cols - 1, 1)
        yield total + jnp.where(col == cols - 1, beside(last[size:]), shifted)


def strip_sum(tile, inputs, lanes, lhs_ref, weight_ref):
    count, rows, cols, wide = tile
    room = count * rows
    col = lax.broadcasted_iota(jnp.int32, tile, 2)
    first = dot(lhs_ref[: 2 * room], weight_ref, 0, lanes, inputs)
    middle = dot(lhs_ref[room : 3 * room], weight_ref, 1, lanes, inputs)
    last = dot(lhs_ref[2 * room :], weight_ref, 2, lanes, inputs)
    total = 0.0
    for at, cells in (
        (0, first[:room] + middle[:room]),
        (1, first[room:]),
        (cols - 2, last[:room]),
        (cols - 1, middle[room:] + last[room:]),
    ):
        total = jnp.where(col == at, cells.reshape(count, rows, 1, wide), total)
    return total


def opening_kernel(inputs, lanes, _, got_ref, weight_ref, out_ref, lhs_ref):
    count, rows, cols, _ = out_ref.shape
    size = rows * cols
    for frame in range(count):
        put_row(lhs_ref, frame * size, size, got_ref[frame])
    further_kernel(inputs, lanes, lhs_ref, weight_ref, out_ref)


def further_kernel(inputs, lanes, lhs_ref, weight_ref, out_ref):
    tiles = tile_sum(out_ref.shape, inputs, lanes, 0, lhs_ref, weight_ref)
    for frame, total in enumerate(tiles):
        out_ref[frame] = total


def result_kernel(
    parts, _, got_ref, beside_ref, strips_ref, weight_ref, *refs
):
    *before_refs, out_ref, lhs_ref, held_ref, strip_lhs_ref, sems = refs
    count, rows, cols, _ = held_ref.shape
    size, room = rows * cols, count * rows
    stride = size + 2 * rows
    for frame in range(count):
        at = frame * stride
        put_row(lhs_ref, at + rows, size, got_ref[frame, :cols])
        ends = got_ref[frame, cols:]
        put_columns_taps(lhs_ref, (at, at + rows + size), beside_ref[frame], ends)
        slots = [slot * room + frame * rows for slot in range(4)]
        put_columns_taps(strip_lhs_ref, slots, strips_ref[frame], ends.astype(jnp.float32)[2:])

    def store(frame, part):
        here = (frame, slice(None), slice(None), parts[part])
        return pltpu.make_async_copy(held_ref.at[here], out_ref.at[here], sems.at[frame, part])

    for part, lanes in enumerate(parts):
        tile = (count, rows, cols, lanes.stop - lanes.start)
        strips = strip_sum(tile, parts[0], lanes, strip_lhs_ref, weight_ref)
        tiles = tile_sum(tile, parts[1], lanes, rows, lhs_ref, weight_ref)
        for frame, total in enumerate(tiles):
            total += before_refs[part][frame] + strips[frame]
            held_ref[frame, :, :, lanes] = total.astype(held_ref.dtype)
            store(frame, part).start()
    for part in range(len(parts)):
        for frame in range(count):
            store(frame, part).wait()


def on_device(frames, input_weight, output_weight, pole_index, gelu_scale, start_state):
    count, rows, cols, channels = frames.shape
    size, room = rows * cols, count * rows
    wide = 3 * channels
    assert lax.axis_size("sx") == 2
    narrow = frames.dtype
    pole, scale = pole_index[None], gelu_scale[None]

    shapes = (
        of((count * cols + (2 * count + 1) * rows, channels), narrow),
        of((2 * count + 1, rows, channels), narrow),
    )
    edges = call(
        edges_kernel,
        shapes,
        frames,
        scratch=[pltpu.VMEM((count, channels // 128, size, 128), jnp.float32)],
        flops=EDGES_COST,
    )
    give, keep = call(
        start_edges_kernel,
        shapes,
        start_state,
        *edges,
        aliases={1: 0, 2: 1},
    )
    got, mine = trade_columns(give, keep, count * cols)
    taps = of((count * size, wide), narrow)
    parts = halves(channels)
    half = channels // 2
    inner = of((count, rows, cols, half), jnp.float32)
    *main, early, _ = call(
        main_kernel,
        (
            of(frames.shape, jnp.float32),
            of((2, room, channels), jnp.float32),
            of((size, half), narrow),
            taps,
        ),
        call(taps_kernel, taps, frames),
        got,
        input_weight,
        pole,
        aliases={0: 3},
        flops=18 * frames.size * channels,
    )
    mine, total, spill = lax.optimization_barrier((mine, *main))
    halo, sides = call(
        halo_kernel,
        (of((4 * room, wide), narrow), of((2 * rows, channels), jnp.float32)),
        mine,
        swap_cores(mine),
    )
    drive, beside, strips, late = call(
        drive_kernel,
        (
            inner,
            of((count, 2 * rows, half), jnp.float32),
            of((count, 4 * rows, half), jnp.float32),
            of((size + 6 * rows, half), narrow),
        ),
        halo,
        input_weight,
        total,
        spill,
        pole,
        flops=36 * room * channels * channels,
    )
    at = size + 2 * rows
    pieces = [
        (early, [(slice(0, size), parts[0])]),
        (late, [(slice(0, at), parts[1]), (slice(at, at + 4 * rows), parts[0])]),
    ]
    exchanged = (exchange_four if lax.axis_size("tm") == 4 else exchange)(pieces, pole, count)
    early, late = exchanged

    mixing = (start_state, pole, scale)
    give = call(
        functools.partial(middle_kernel, parts[0]),
        of((count, cols, half), narrow),
        total,
        *mixing,
        *early,
    )
    taps = of((count * size, 3 * half), narrow)
    lhs = call(
        functools.partial(mixed_kernel, parts[0], True), taps, total, *mixing, *early
    )
    strip_start = call(strip_start_kernel, of((4 * rows, channels), jnp.float32), start_state, sides)
    flops = 18 * inner.size * half
    first_sum, lhs = call(
        functools.partial(opening_kernel, parts[0], parts[0]),
        (inner, taps),
        lhs,
        swap_cores(give),
        output_weight,
        aliases={0: 1},
        flops=flops,
    )
    second_sum = call(
        functools.partial(further_kernel, parts[0], parts[1]),
        inner,
        lhs,
        output_weight,
        flops=flops,
    )
    *late, first_sum, second_sum = lax.optimization_barrier((*late, first_sum, second_sum))
    give, beside, strips = call(
        functools.partial(late_kernel, parts),
        (
            of((count, 2 * cols, half), narrow),
            of(beside.shape, narrow),
            of(strips.shape, narrow),
        ),
        drive,
        beside,
        strips,
        start_state,
        strip_start,
        pole,
        scale,
        *late,
    )
    taps = of((count * size + 2 * room, 3 * half), narrow)
    lhs = call(functools.partial(mixed_kernel, parts[1], False), taps, drive, *mixing, *late)
    result, _ = call(
        functools.partial(result_kernel, parts),
        (of(frames.shape, narrow), taps),
        lhs,
        swap_cores(give),
        beside,
        strips,
        output_weight,
        first_sum,
        second_sum,
        out_specs=(HBM, WHOLE),
        aliases={0: 1},
        scratch=[
            pltpu.VMEM(frames.shape, narrow),
            pltpu.VMEM((4 * room, 3 * half), narrow),
            pltpu.SemaphoreType.DMA((count, len(parts))),
        ],
        flops=2 * flops,
    )
    return result


def solution(mesh):
    return jax.shard_map(
        on_device,
        mesh=mesh,
        in_specs=(P("tm", "sx", "sy", None), P(), P(), P(), P(), P("sx", "sy", None)),
        out_specs=P("tm", "sx", "sy", None),
        check_vma=False,
    )
```

```python
import functools
import math

import jax
import jax.numpy as jnp
from jax import lax
from jax.experimental import pallas as pl
from jax.experimental.pallas import tpu as pltpu
from jax.sharding import PartitionSpec as P

NPOLES = 16
VMEM_LIMIT = 24 * 1024 * 1024
WHOLE = pl.BlockSpec(memory_space=pltpu.VMEM)
HBM = pl.BlockSpec(memory_space=pltpu.HBM)
EDGES_COST = 2_000_000_000


def call(kernel, out_shape, *args, scratch=(), flops=0, out_specs=None, aliases=None):
    outs = jax.tree.leaves(out_shape)
    moved = sum(leaf.size * leaf.dtype.itemsize for leaf in (*args, *outs))
    return pl.pallas_call(
        kernel,
        in_specs=[WHOLE] * len(args),
        out_specs=out_specs or jax.tree.map(lambda _: WHOLE, out_shape),
        out_shape=out_shape,
        scratch_shapes=scratch,
        input_output_aliases=aliases or {},
        compiler_params=pltpu.CompilerParams(vmem_limit_bytes=VMEM_LIMIT),
        cost_estimate=pl.CostEstimate(flops=flops, bytes_accessed=moved, transcendentals=0),
    )(*args)


def of(shape, dtype):
    return jax.ShapeDtypeStruct(shape, dtype)


def is_core(which):
    return (lax.axis_index("sx") == which).astype(jnp.float32)


def rate_of(pole_ref):
    pole = pole_ref[...].astype(jnp.float32)
    return -0.001 * jnp.exp(pole * (math.log(300.0) / (NPOLES - 1)))


def inner_row(rows):
    return jnp.where(lax.axis_index("sx") == 0, rows - 1, 0)


def swap_cores(array):
    return lax.ppermute(array, "sx", [(0, 1), (1, 0)])


def put_columns(index, left, right, give_ref, keep_ref):
    zero, one = is_core(0), is_core(1)
    count, rows, _ = keep_ref.shape
    at = give_ref.shape[0] - (count - index) * rows
    give_ref[at : at + rows] = (zero * left + one * right).astype(give_ref.dtype)
    keep_ref[index] = (zero * right + one * left).astype(keep_ref.dtype)


def edges_kernel(cells_ref, give_ref, keep_ref, wide_ref):
    count, rows, cols, channels = cells_ref.shape
    for frame in range(count):
        give_ref[frame * cols : (frame + 1) * cols] = cells_ref[frame, inner_row(rows)]
        tile = cells_ref[frame].reshape(rows * cols, channels).astype(jnp.float32)
        lanes = wide_ref.shape[-1]
        for part in range(channels // lanes):
            wide_ref[frame, part] = tile[:, part * lanes : (part + 1) * lanes]

        def column(col):
            parts = [
                wide_ref[frame, part, pl.ds(col, rows, stride=cols), :]
                for part in range(channels // lanes)
            ]
            return jnp.concatenate(parts, axis=1)

        for depth in range(2):
            left, right = column(depth), column(cols - 1 - depth)
            put_columns(2 * frame + depth, left, right, give_ref, keep_ref)


def start_edges_kernel(start_ref, _, __, give_ref, keep_ref):
    tile, cols = start_ref[...], start_ref.shape[1]
    index = keep_ref.shape[0] - 1
    put_columns(index, tile[:, 0, :], tile[:, cols - 1, :], give_ref, keep_ref)


def trade_columns(give, keep, at):
    chips = lax.axis_size("sy")
    got = swap_cores(give)
    pairs = [(chip, chips + chip + 1) for chip in range(chips - 1)]
    pairs += [(after, before) for before, after in pairs]
    columns = jnp.concatenate([keep, got[at:].reshape(keep.shape)], axis=1)
    return got, lax.ppermute(columns, ("sx", "sy"), pairs)


def put_cells(lhs_ref, at, size, cols, first, cells):
    count, channels = cells.shape
    upper, lower = min(count, size - cols - first), max(0, cols - first)
    here = at + first
    lhs_ref[here : here + count, channels : 2 * channels] = cells
    lhs_ref[here + cols : here + cols + upper, :channels] = cells[:upper]
    lhs_ref[here + lower - cols : here + count - cols, 2 * channels :] = cells[lower:]


def put_row(lhs_ref, at, size, row):
    cols, channels = row.shape
    row = row.astype(jnp.float32)
    last = slice(at + size - cols, at + size)
    lhs_ref[at : at + cols, :channels] = (is_core(1) * row).astype(lhs_ref.dtype)
    lhs_ref[last, 2 * channels :] = (is_core(0) * row).astype(lhs_ref.dtype)


def taps_kernel(cells_ref, lhs_ref):
    count, rows, cols, channels = cells_ref.shape
    size = rows * cols
    for frame in range(count):
        put_cells(lhs_ref, frame * size, size, cols, 0, cells_ref[frame].reshape(size, channels))


def row_taps(column, above, below):
    rows = column.shape[0]
    row = lax.broadcasted_iota(jnp.int32, column.shape, 0)
    up = jnp.where(row == 0, is_core(1) * above, pltpu.roll(column, 1, 0))
    down = jnp.where(row == rows - 1, is_core(0) * below, pltpu.roll(column, rows - 1, 0))
    return jnp.concatenate([up, column, down], axis=1)


def halves(channels):
    return slice(0, channels // 2), slice(channels // 2, channels)


def end_state(frames, pole_ref, lanes):
    decay = jnp.exp(rate_of(pole_ref))[:, lanes]
    state = frames[0]
    for frame in frames[1:]:
        state = decay * state + frame
    return state


def dot(lhs, weight_ref, column, lanes, inputs=slice(None)):
    weight = weight_ref[:, column, inputs, lanes].reshape(lhs.shape[1], -1)
    return jnp.dot(lhs, weight, preferred_element_type=jnp.float32)


def main_kernel(_, got_ref, weight_ref, pole_ref, total_ref, spill_ref, end_ref, lhs_ref):
    count, rows, cols, _ = total_ref.shape
    size = rows * cols
    for frame in range(count):
        put_row(lhs_ref, frame * size, size, got_ref[frame * cols : (frame + 1) * cols])
    states = []
    for lanes in halves(weight_ref.shape[-1]):
        tile = (rows, cols, lanes.stop - lanes.start)
        col = lax.broadcasted_iota(jnp.int32, tile, 1)
        totals = []
        for frame in range(count):
            cells = lhs_ref[frame * size : (frame + 1) * size]
            here = slice(frame * rows, (frame + 1) * rows)
            total = dot(cells, weight_ref, 1, lanes).reshape(tile)
            first = dot(cells, weight_ref, 0, lanes).reshape(tile)
            spill_ref[1, here, lanes] = first[:, cols - 1, :]
            total += jnp.where(col == 0, 0.0, pltpu.roll(first, 1, 1))
            last = dot(cells, weight_ref, 2, lanes).reshape(tile)
            spill_ref[0, here, lanes] = last[:, 0, :]
            total += jnp.where(col == cols - 1, 0.0, pltpu.roll(last, cols - 1, 1))
            total_ref[frame, :, :, lanes] = total
            totals.append(total)
        states.append(end_state(totals, pole_ref, lanes))
    state = jnp.where(col == 0, pltpu.roll(states[1], cols - 1, 1), states[0])
    state = jnp.where(col == cols - 1, pltpu.roll(states[1], 1, 1), state)
    end_ref[...] = state.reshape(end_ref.shape).astype(end_ref.dtype)


def halo_kernel(mine_ref, theirs_ref, lhs_ref, start_ref):
    rows = mine_ref.shape[1] // 2
    count = mine_ref.shape[0] // 2
    room = count * rows
    zero, one = is_core(0), is_core(1)
    core = lax.axis_index("sx")
    slots = ((1, 0), (2, 3))
    for frame in range(count):
        for depth in range(2):
            own = mine_ref[2 * frame + depth].astype(jnp.float32)
            other = theirs_ref[2 * frame + depth].astype(jnp.float32)
            own = row_taps(own[rows:], own[rows - 1 : rows], own[:1])
            other = row_taps(other[:rows], other[2 * rows - 1 :], other[rows : rows + 1])
            for swapped, taps in enumerate((own, other)):
                slot = jnp.where(core == swapped, slots[1][depth], slots[0][depth])
                at = pl.multiple_of(slot * room + frame * rows, rows)
                lhs_ref[pl.ds(at, rows)] = taps.astype(lhs_ref.dtype)
    own = mine_ref[2 * count, rows:].astype(jnp.float32)
    other = theirs_ref[2 * count, :rows].astype(jnp.float32)
    start_ref[:rows] = zero * other + one * own
    start_ref[rows:] = zero * own + one * other


def drive_kernel(
    lhs_ref, weight_ref, total_ref, spill_ref, pole_ref, drive_ref, beside_ref, strips_ref, end_ref
):
    count, rows, cols, wide = drive_ref.shape
    room, size = count * rows, rows * cols
    at = size + 2 * rows
    early = None
    for lanes in halves(weight_ref.shape[-1]):
        first = dot(lhs_ref[: 2 * room], weight_ref, 0, lanes)
        middle = dot(lhs_ref[room : 3 * room], weight_ref, 1, lanes)
        last = dot(lhs_ref[2 * room :], weight_ref, 2, lanes)
        left = (spill_ref[0, :, lanes] + first[:room] + middle[:room]).reshape(count, rows, wide)
        right = (spill_ref[1, :, lanes] + middle[room:] + last[room:]).reshape(count, rows, wide)
        total = total_ref[:, :, :, lanes]
        if lanes.start == 0:
            near = total[:, :, 0, :] + first[room:].reshape(count, rows, wide)
            far = total[:, :, cols - 1, :] + last[:room].reshape(count, rows, wide)
            strips = jnp.concatenate([left, near, far, right], axis=1)
            strips_ref[...] = strips
            early = end_state([strips[frame] for frame in range(count)], pole_ref, lanes)
            end_ref[at : at + rows] = early[:rows].astype(end_ref.dtype)
            end_ref[at + rows :] = early[3 * rows :].astype(end_ref.dtype)
            continue
        col = lax.broadcasted_iota(jnp.int32, drive_ref.shape, 2)
        total += jnp.where(col == 0, first[room:].reshape(count, rows, 1, wide), 0.0)
        total += jnp.where(col == cols - 1, last[:room].reshape(count, rows, 1, wide), 0.0)
        drive_ref[...] = total
        state = end_state([total[frame] for frame in range(count)], pole_ref, lanes)
        col = lax.broadcasted_iota(jnp.int32, state.shape, 1)
        state = jnp.where(col == 1, early[rows : 2 * rows].reshape(rows, 1, wide), state)
        border = early[2 * rows : 3 * rows].reshape(rows, 1, wide)
        state = jnp.where(col == cols - 2, border, state)
        end_ref[:size] = state.reshape(size, wide).astype(end_ref.dtype)
        beside = jnp.concatenate([left, right], axis=1)
        beside_ref[...] = beside
        state = end_state([beside[frame] for frame in range(count)], pole_ref, lanes)
        end_ref[size:at] = state.astype(end_ref.dtype)


def spread(block, cols, count, of_lanes):
    _, lanes, inset = block
    value = of_lanes(lanes)
    if inset is None:
        return value
    other, columns = inset
    value, instead = jnp.broadcast_arrays(value, of_lanes(other))
    shape = (count, value.shape[1])
    col = lax.rem(lax.broadcasted_iota(jnp.int32, shape, 0), cols)
    return jnp.where((col == columns[0]) | (col == columns[1]), instead, value)


def entry_kernel(frames, cols, block, ends_ref, pole_ref, out_ref):
    rate = rate_of(pole_ref)
    count = ends_ref.shape[1]
    carried = spread(block, cols, count, lambda lanes: jnp.exp(frames * rate[:, lanes]))
    entry = jnp.zeros(ends_ref.shape[1:], jnp.float32)
    out_ref[0] = entry.astype(out_ref.dtype)
    for index in range(ends_ref.shape[0] - 1):
        entry = carried * entry + ends_ref[index].astype(jnp.float32)
        out_ref[index + 1] = entry.astype(out_ref.dtype)


def exchange(pieces, pole, frames, cols):
    groups = lax.axis_size("tm")
    arrivals = []
    for end, blocks in pieces:
        entries = []
        for block in blocks:
            shares = end[block[0]].reshape(groups, -1, end.shape[1])
            assert block[2] is None or shares.shape[1] % cols == 0
            shares = lax.all_to_all(shares, "tm", 0, 0)
            kernel = functools.partial(entry_kernel, frames, cols, block)
            entry = call(kernel, of(shares.shape, end.dtype), shares, pole)
            entries.append(lax.all_to_all(entry, "tm", 0, 0).reshape(-1, end.shape[1]))
        arrivals.append((jnp.concatenate(entries, axis=0),))
    return arrivals


def pick(values):
    group = lax.axis_index("tm")
    picked = values[-1]
    for index, value in enumerate(values[:-1]):
        picked = jnp.where(group == index, value, picked)
    return picked


def on_core(first, second):
    return jnp.where(lax.axis_index("sx") == 0, first, second)


def weigh(one, by_one, other, by_other):
    return by_one * one.astype(jnp.float32) + by_other * other.astype(jnp.float32)


def relay_kernel(frames, cols, blocks, end_ref, got_ref, pole_ref, out_ref):
    rate = rate_of(pole_ref)
    carried, twice = jnp.exp(frames * rate), jnp.exp(2 * frames * rate)
    none, same = jnp.zeros_like(rate), jnp.ones_like(rate)
    own = on_core(pick([carried, same, same, same]), pick([same, same, same, none]))
    got = on_core(pick([same, carried, carried, carried]), pick([none, none, twice, same]))
    for block in blocks:
        rows = block[0]
        count = rows.stop - rows.start
        by_own = spread(block, cols, count, lambda lanes: own[:, lanes])
        by_got = spread(block, cols, count, lambda lanes: got[:, lanes])
        out_ref[rows] = weigh(end_ref[rows], by_own, got_ref[rows], by_got).astype(out_ref.dtype)


def exchange_four(pieces, pole, frames, cols):
    def along(pairs, core):
        return [(2 * source + core, 2 * target + core) for source, target in pairs]

    axes = ("tm", "sx")
    down = [(0, 2), (1, 3)]
    first_round = along([(0, 1), (1, 0), (2, 3)], 0) + along(down, 1)
    second_round = along(down, 0) + along([(0, 1), (2, 3), (3, 2)], 1)
    arrivals = []
    for end, blocks in pieces:
        got = lax.ppermute(end, axes, first_round)
        kernel = functools.partial(relay_kernel, frames, cols, blocks)
        relayed = call(kernel, of(end.shape, end.dtype), end, got, pole)
        arrivals.append((got, lax.ppermute(relayed, axes, second_round)))
    return arrivals


class Mix:
    def __init__(self, lanes, count, pole_ref, scale_ref):
        self.rate = rate_of(pole_ref)[:, lanes]
        self.scale = scale_ref[:, lanes]
        self.count = count

    def entry(self, arrived_refs, rows):
        parts = [ref[rows].astype(jnp.float32) for ref in arrived_refs]
        if len(parts) == 1:
            return parts[0]
        carried = jnp.exp(self.count * self.rate)
        none, same = jnp.zeros_like(self.rate), jnp.ones_like(self.rate)
        early = on_core(pick([none, same, none, same]), pick([none, none, carried, carried]))
        late = on_core(pick([none, none, same, carried]), pick([none, same, same, same]))
        return weigh(parts[0], early, parts[1], late)

    def __call__(self, drives, entry, start):
        decay = jnp.exp(self.rate)
        reach = jnp.exp((self.count * lax.axis_index("tm")).astype(jnp.float32) * self.rate)
        state = reach * start + entry.reshape(start.shape)
        for drive in drives:
            state = decay * state + drive
            yield jax.nn.gelu(self.scale * state)


def no_border(cells, axis):
    col = lax.broadcasted_iota(jnp.int32, cells.shape, axis)
    return jnp.where((col == 0) | (col == cells.shape[axis] - 1), 0.0, cells)


def put_back(late, early, axis):
    cols = late.shape[axis]
    col = lax.broadcasted_iota(jnp.int32, late.shape, axis)
    late = jnp.where(col == 1, pltpu.roll(early, 1, axis), late)
    return jnp.where(col == cols - 2, pltpu.roll(early, cols - 1, axis), late)


def mixed_kernel(lanes, rounds, *refs):
    drive_ref, start_ref, pole_ref, scale_ref, *arrived_refs, lhs_ref = refs
    early_refs, late_refs = arrived_refs[:rounds], arrived_refs[rounds:]
    count, rows, cols, _ = drive_ref.shape
    wide = lanes.stop - lanes.start
    size = rows * cols
    stride = lhs_ref.shape[0] // count
    room = (stride - size) // 2
    mix = Mix(lanes, count, pole_ref, scale_ref)
    first = lanes.start == 0
    held = lanes if first else slice(None)
    block = 8
    if first:
        for frame in range(count):
            put_row(lhs_ref, frame * stride + room, size, jnp.zeros((cols, wide), lhs_ref.dtype))
    for row in range(0, rows, block):
        here = slice(row, row + block)
        drives = [drive_ref[frame, here, :, held] for frame in range(count)]
        cells = slice(row * cols, (row + block) * cols)
        entry = mix.entry(early_refs, cells).reshape(block, cols, wide)
        if not first:
            entry = put_back(mix.entry(late_refs, cells).reshape(entry.shape), entry, 1)
        for frame, tile in enumerate(mix(drives, entry, start_ref[here, :, lanes])):
            if first:
                tile = no_border(tile, 1)
            tile = tile.reshape(block * cols, wide).astype(lhs_ref.dtype)
            put_cells(lhs_ref, frame * stride + room, size, cols, row * cols, tile)


def strip_start_kernel(start_ref, sides_ref, out_ref):
    rows, cols, _ = start_ref.shape
    start = start_ref[...]
    out_ref[:rows] = sides_ref[:rows]
    out_ref[rows : 2 * rows] = start[:, 0, :]
    out_ref[2 * rows : 3 * rows] = start[:, cols - 1, :]
    out_ref[3 * rows :] = sides_ref[rows:]


def inside(slot):
    chip, chips = lax.axis_index("sy"), lax.axis_size("sy")
    return {0: (chip > 0).astype(jnp.float32), 3: (chip < chips - 1).astype(jnp.float32)}.get(slot, 1.0)


def give_kernel(parts, rounds, *refs):
    total_ref, drive_ref, beside_ref, strips_ref, *refs = refs
    start_ref, strip_start_ref, pole_ref, scale_ref, *arrived_refs, give_ref = refs
    early_refs, late_refs = arrived_refs[:rounds], arrived_refs[rounds:]
    count, rows, cols, wide = drive_ref.shape
    size = rows * cols
    inner = inner_row(rows)
    zero, one = is_core(0), is_core(1)
    early, late = (Mix(lanes, count, pole_ref, scale_ref) for lanes in parts)
    row = pl.ds(pl.multiple_of(inner * cols, cols), cols)
    which = lax.broadcasted_iota(jnp.int32, (cols, wide), 0)

    def near(at):
        return pl.ds(pl.multiple_of(at + jnp.where(inner == 0, 0, rows - cols), cols), cols)

    def end(cells):
        return zero * cells[cols - 1 :] + one * cells[:1]

    def rows_of(cells):
        table = jnp.zeros(which.shape, jnp.float32)
        for index, cell in cells:
            table = jnp.where(which == index, cell, table)
        return table

    entry = put_back(late.entry(late_refs, row), late.entry(early_refs, row), 0)
    drives = [drive_ref[frame, inner] for frame in range(count)]
    tile = late(drives, entry, start_ref[inner, :, parts[1]])
    drives = [total_ref[frame, inner, :, parts[0]] for frame in range(count)]
    first = early(drives, early.entry(early_refs, row), start_ref[inner, :, parts[0]])

    slots = [(0, 0), (1, 3)]
    entry = rows_of([(i, end(late.entry(late_refs, near(size + i * rows)))) for i, _ in slots])
    start = rows_of([(i, end(strip_start_ref[near(slot * rows), parts[1]])) for i, slot in slots])
    drives = [
        rows_of([(i, end(beside_ref[frame, near(i * rows)])) for i, _ in slots])
        for frame in range(count)
    ]
    beside = late(drives, entry, start)

    slots = [(2 + slot, slot) for slot in range(4)]
    grid = early.entry(late_refs, row)
    at = size + 2 * rows
    entry = rows_of(
        [
            (2, end(early.entry(late_refs, near(at)))),
            (3, grid[1:2]),
            (4, grid[cols - 2 : cols - 1]),
            (5, end(early.entry(late_refs, near(at + rows)))),
        ]
    )
    start = rows_of([(i, end(strip_start_ref[near(slot * rows), parts[0]])) for i, slot in slots])
    drives = [
        rows_of([(i, end(strips_ref[frame, near(slot * rows)])) for i, slot in slots])
        for frame in range(count)
    ]
    strips = early(drives, entry, start)
    for frame, cells in enumerate(zip(tile, first, beside, strips)):
        give_ref[frame, :cols] = cells[0].astype(give_ref.dtype)
        ends = jnp.where(which < 2, cells[2], cells[3])
        ends = jnp.where((which == 0) | (which == 2), inside(0) * ends, ends)
        ends = jnp.where((which == 1) | (which == 5), inside(3) * ends, ends)
        give_ref[frame, cols : 2 * cols] = ends.astype(give_ref.dtype)
        give_ref[frame, 2 * cols :] = no_border(cells[1], 0).astype(give_ref.dtype)


def late_kernel(parts, rounds, *refs):
    beside_ref, strips_ref, strip_start_ref, pole_ref, scale_ref, *refs = refs
    *late_refs, beside_out_ref, strips_out_ref = refs
    count, room, wide = beside_ref.shape
    rows = room // 2
    size = late_refs[0].shape[0] - 4 * rows
    cols = size // rows
    early, late = (Mix(lanes, count, pole_ref, scale_ref) for lanes in parts)

    def column(cells, index):
        return cells[index * rows : (index + 1) * rows]

    starts = [strip_start_ref[slot * rows : (slot + 1) * rows, parts[1]] for slot in (0, 3)]
    entry = late.entry(late_refs, slice(size, size + 2 * rows))
    drives = [beside_ref[frame] for frame in range(count)]
    beside = late(drives, entry, jnp.concatenate(starts, axis=0))
    grid = early.entry(late_refs, slice(0, size)).reshape(rows, cols, wide)
    sides = early.entry(late_refs, slice(size + 2 * rows, size + 4 * rows))
    entry = [sides[:rows], grid[:, 1, :], grid[:, cols - 2, :], sides[rows:]]
    drives = [strips_ref[frame] for frame in range(count)]
    strips = early(drives, jnp.concatenate(entry, axis=0), strip_start_ref[:, parts[0]])
    for frame, (sides, strip) in enumerate(zip(beside, strips)):
        sides = [column(sides, 0) * inside(0), column(sides, 1) * inside(3)]
        strip = [column(strip, slot) * inside(slot) for slot in range(4)]
        beside_out_ref[frame] = jnp.concatenate(sides, axis=0).astype(beside_out_ref.dtype)
        strips_out_ref[frame] = jnp.concatenate(strip, axis=0).astype(strips_out_ref.dtype)


def put_columns_taps(lhs_ref, slots, columns, ends):
    rows = columns.shape[0] // len(slots)
    columns, ends = columns.astype(jnp.float32), ends.astype(jnp.float32)
    for index, at in enumerate(slots):
        column, end = columns[index * rows : (index + 1) * rows], ends[index : index + 1]
        lhs_ref[at : at + rows] = row_taps(column, end, end).astype(lhs_ref.dtype)


def tile_sum(tile, inputs, lanes, room, lhs_ref, weight_ref):
    count, rows, cols, wide = tile
    size = rows * cols
    col = lax.broadcasted_iota(jnp.int32, tile[1:], 1)

    def beside(cells):
        return cells.reshape(rows, 1, wide) if room else 0.0

    for frame in range(count):
        at = frame * (size + 2 * room)
        end = at + room + size
        total = dot(lhs_ref[at + room : end], weight_ref, 1, lanes, inputs).reshape(tile[1:])
        first = dot(lhs_ref[at:end], weight_ref, 0, lanes, inputs)
        shifted = pltpu.roll(first[room:].reshape(tile[1:]), 1, 1)
        total += jnp.where(col == 0, beside(first[:room]), shifted)
        last = dot(lhs_ref[at + room : end + room], weight_ref, 2, lanes, inputs)
        shifted = pltpu.roll(last[:size].reshape(tile[1:]), cols - 1, 1)
        yield total + jnp.where(col == cols - 1, beside(last[size:]), shifted)


def strip_sum(tile, inputs, lanes, lhs_ref, weight_ref):
    count, rows, cols, wide = tile
    room = count * rows
    col = lax.broadcasted_iota(jnp.int32, tile, 2)
    first = dot(lhs_ref[: 2 * room], weight_ref, 0, lanes, inputs)
    middle = dot(lhs_ref[room : 3 * room], weight_ref, 1, lanes, inputs)
    last = dot(lhs_ref[2 * room :], weight_ref, 2, lanes, inputs)
    total = 0.0
    for at, cells in (
        (0, first[:room] + middle[:room]),
        (1, first[room:]),
        (cols - 2, last[:room]),
        (cols - 1, middle[room:] + last[room:]),
    ):
        total = jnp.where(col == at, cells.reshape(count, rows, 1, wide), total)
    return total


def row_sum(tile, inputs, lanes, given, weight_ref):
    count, rows, cols, wide = tile
    tap = jnp.where(lax.axis_index("sx") == 0, weight_ref.shape[0] - 1, 0)
    col = lax.broadcasted_iota(jnp.int32, (count, cols, wide), 1)

    def product(column):
        weight = weight_ref[pl.ds(tap, 1), column, inputs, lanes].reshape(given.shape[1], wide)
        total = jnp.dot(given, weight, preferred_element_type=jnp.float32)
        return total.reshape(count, cols, wide)

    total = product(1)
    total += jnp.where(col == 0, 0.0, pltpu.roll(product(0), 1, 1))
    return total + jnp.where(col == cols - 1, 0.0, pltpu.roll(product(2), cols - 1, 1))


def further_kernel(inputs, lanes, lhs_ref, weight_ref, out_ref):
    tiles = tile_sum(out_ref.shape, inputs, lanes, 0, lhs_ref, weight_ref)
    for frame, total in enumerate(tiles):
        out_ref[frame] = total


def result_kernel(
    parts, _, got_ref, beside_ref, strips_ref, weight_ref, *refs
):
    *before_refs, out_ref, lhs_ref, held_ref, strip_lhs_ref, sems = refs
    count, rows, cols, _ = held_ref.shape
    size, room = rows * cols, count * rows
    stride = size + 2 * rows
    for frame in range(count):
        at = frame * stride
        put_row(lhs_ref, at + rows, size, got_ref[frame, :cols])
        ends = got_ref[frame, cols : 2 * cols]
        put_columns_taps(lhs_ref, (at, at + rows + size), beside_ref[frame], ends)
        slots = [slot * room + frame * rows for slot in range(4)]
        put_columns_taps(strip_lhs_ref, slots, strips_ref[frame], ends.astype(jnp.float32)[2:])

    def store(frame, part):
        here = (frame, slice(None), slice(None), parts[part])
        return pltpu.make_async_copy(held_ref.at[here], out_ref.at[here], sems.at[frame, part])

    given = jnp.concatenate([got_ref[frame, 2 * cols :] for frame in range(count)], axis=0)
    for part, lanes in enumerate(parts):
        tile = (count, rows, cols, lanes.stop - lanes.start)
        row = lax.broadcasted_iota(jnp.int32, tile[1:], 0)
        reached = row_sum(tile, parts[0], lanes, given, weight_ref)
        strips = strip_sum(tile, parts[0], lanes, strip_lhs_ref, weight_ref)
        tiles = tile_sum(tile, parts[1], lanes, rows, lhs_ref, weight_ref)
        for frame, total in enumerate(tiles):
            total += before_refs[part][frame] + strips[frame]
            total += jnp.where(row == inner_row(rows), reached[frame][None], 0.0)
            held_ref[frame, :, :, lanes] = total.astype(held_ref.dtype)
            store(frame, part).start()
    for part in range(len(parts)):
        for frame in range(count):
            store(frame, part).wait()


def on_device(frames, input_weight, output_weight, pole_index, gelu_scale, start_state):
    count, rows, cols, channels = frames.shape
    size, room = rows * cols, count * rows
    wide = 3 * channels
    assert lax.axis_size("sx") == 2
    narrow = frames.dtype
    pole, scale = pole_index[None], gelu_scale[None]

    shapes = (
        of((count * cols + (2 * count + 1) * rows, channels), narrow),
        of((2 * count + 1, rows, channels), narrow),
    )
    edges = call(
        edges_kernel,
        shapes,
        frames,
        scratch=[pltpu.VMEM((count, channels // 128, size, 128), jnp.float32)],
        flops=EDGES_COST,
    )
    give, keep = call(
        start_edges_kernel,
        shapes,
        start_state,
        *edges,
        aliases={1: 0, 2: 1},
    )
    got, mine = trade_columns(give, keep, count * cols)
    taps = of((count * size, wide), narrow)
    parts = halves(channels)
    half = channels // 2
    inner = of((count, rows, cols, half), jnp.float32)
    *main, early, _ = call(
        main_kernel,
        (
            of(frames.shape, jnp.float32),
            of((2, room, channels), jnp.float32),
            of((size, half), narrow),
            taps,
        ),
        call(taps_kernel, taps, frames),
        got,
        input_weight,
        pole,
        aliases={0: 3},
        flops=18 * frames.size * channels,
    )
    mine, total, spill = lax.optimization_barrier((mine, *main))
    halo, sides = call(
        halo_kernel,
        (of((4 * room, wide), narrow), of((2 * rows, channels), jnp.float32)),
        mine,
        swap_cores(mine),
    )
    drive, beside, strips, late = call(
        drive_kernel,
        (
            inner,
            of((count, 2 * rows, half), jnp.float32),
            of((count, 4 * rows, half), jnp.float32),
            of((size + 4 * rows, half), narrow),
        ),
        halo,
        input_weight,
        total,
        spill,
        pole,
        flops=36 * room * channels * channels,
    )
    at = size + 2 * rows
    tile = slice(0, size)
    pieces = [
        (early, [(tile, parts[0], (parts[1], (0, cols - 1)))]),
        (
            late,
            [
                (tile, parts[1], (parts[0], (1, cols - 2))),
                (slice(size, at), parts[1], None),
                (slice(at, at + 2 * rows), parts[0], None),
            ],
        ),
    ]
    exchanged = exchange_four if lax.axis_size("tm") == 4 else exchange
    early, late = exchanged(pieces, pole, count, cols)
    rounds = len(early)

    mixing = (start_state, pole, scale)
    taps = of((count * size, 3 * half), narrow)
    lhs = call(functools.partial(mixed_kernel, parts[0], rounds), taps, total, *mixing, *early)
    strip_start = call(strip_start_kernel, of((4 * rows, channels), jnp.float32), start_state, sides)
    flops = 18 * inner.size * half
    first_sum, second_sum = (
        call(
            functools.partial(further_kernel, parts[0], lanes), inner, lhs, output_weight, flops=flops
        )
        for lanes in parts
    )
    *late, first_sum, second_sum = lax.optimization_barrier((*late, first_sum, second_sum))
    give = call(
        functools.partial(give_kernel, parts, rounds),
        of((count, 3 * cols, half), narrow),
        total,
        drive,
        beside,
        strips,
        start_state,
        strip_start,
        pole,
        scale,
        *early,
        *late,
    )
    beside, strips = call(
        functools.partial(late_kernel, parts, rounds),
        (of(beside.shape, narrow), of(strips.shape, narrow)),
        beside,
        strips,
        strip_start,
        pole,
        scale,
        *late,
    )
    taps = of((count * size + 2 * room, 3 * half), narrow)
    lhs = call(
        functools.partial(mixed_kernel, parts[1], rounds), taps, drive, *mixing, *early, *late
    )
    result, _ = call(
        functools.partial(result_kernel, parts),
        (of(frames.shape, narrow), taps),
        lhs,
        swap_cores(give),
        beside,
        strips,
        output_weight,
        first_sum,
        second_sum,
        out_specs=(HBM, WHOLE),
        aliases={0: 1},
        scratch=[
            pltpu.VMEM(frames.shape, narrow),
            pltpu.VMEM((4 * room, 3 * half), narrow),
            pltpu.SemaphoreType.DMA((count, len(parts))),
        ],
        flops=2 * flops,
    )
    return result


def solution(mesh):
    return jax.shard_map(
        on_device,
        mesh=mesh,
        in_specs=(P("tm", "sx", "sy", None), P(), P(), P(), P(), P("sx", "sy", None)),
        out_specs=P("tm", "sx", "sy", None),
        check_vma=False,
    )
```

```python
import functools
import math

import jax
import jax.numpy as jnp
from jax import lax
from jax.experimental import pallas as pl
from jax.experimental.pallas import tpu as pltpu
from jax.sharding import PartitionSpec as P

NPOLES = 16
VMEM_LIMIT = 24 * 1024 * 1024
WHOLE = pl.BlockSpec(memory_space=pltpu.VMEM)
HBM = pl.BlockSpec(memory_space=pltpu.HBM)
EDGES_COST = 2_000_000_000


def call(kernel, out_shape, *args, scratch=(), flops=0, out_specs=None, aliases=None):
    outs = jax.tree.leaves(out_shape)
    moved = sum(leaf.size * leaf.dtype.itemsize for leaf in (*args, *outs))
    return pl.pallas_call(
        kernel,
        in_specs=[WHOLE] * len(args),
        out_specs=out_specs or jax.tree.map(lambda _: WHOLE, out_shape),
        out_shape=out_shape,
        scratch_shapes=scratch,
        input_output_aliases=aliases or {},
        compiler_params=pltpu.CompilerParams(vmem_limit_bytes=VMEM_LIMIT),
        cost_estimate=pl.CostEstimate(flops=flops, bytes_accessed=moved, transcendentals=0),
    )(*args)


def of(shape, dtype):
    return jax.ShapeDtypeStruct(shape, dtype)


def is_core(which):
    return (lax.axis_index("sx") == which).astype(jnp.float32)


def rate_of(pole_ref):
    pole = pole_ref[...].astype(jnp.float32)
    return -0.001 * jnp.exp(pole * (math.log(300.0) / (NPOLES - 1)))


def inner_row(rows):
    return jnp.where(lax.axis_index("sx") == 0, rows - 1, 0)


def swap_cores(array):
    return lax.ppermute(array, "sx", [(0, 1), (1, 0)])


def put_columns(index, left, right, give_ref, keep_ref):
    zero, one = is_core(0), is_core(1)
    count, rows, _ = keep_ref.shape
    at = give_ref.shape[0] - (count - index) * rows
    give_ref[at : at + rows] = (zero * left + one * right).astype(give_ref.dtype)
    keep_ref[index] = (zero * right + one * left).astype(keep_ref.dtype)


def edges_kernel(cells_ref, give_ref, keep_ref, wide_ref):
    count, rows, cols, channels = cells_ref.shape
    for frame in range(count):
        give_ref[frame * cols : (frame + 1) * cols] = cells_ref[frame, inner_row(rows)]
        tile = cells_ref[frame].reshape(rows * cols, channels).astype(jnp.float32)
        lanes = wide_ref.shape[-1]
        for part in range(channels // lanes):
            wide_ref[frame, part] = tile[:, part * lanes : (part + 1) * lanes]

        def column(col):
            parts = [
                wide_ref[frame, part, pl.ds(col, rows, stride=cols), :]
                for part in range(channels // lanes)
            ]
            return jnp.concatenate(parts, axis=1)

        for depth in range(2):
            left, right = column(depth), column(cols - 1 - depth)
            put_columns(2 * frame + depth, left, right, give_ref, keep_ref)


def start_edges_kernel(start_ref, _, __, give_ref, keep_ref):
    tile, cols = start_ref[...], start_ref.shape[1]
    index = keep_ref.shape[0] - 1
    put_columns(index, tile[:, 0, :], tile[:, cols - 1, :], give_ref, keep_ref)


def trade_columns(give, keep, at):
    chips = lax.axis_size("sy")
    got = swap_cores(give)
    pairs = [(chip, chips + chip + 1) for chip in range(chips - 1)]
    pairs += [(after, before) for before, after in pairs]
    columns = jnp.concatenate([keep, got[at:].reshape(keep.shape)], axis=1)
    return got, lax.ppermute(columns, ("sx", "sy"), pairs)


def put_cells(lhs_ref, at, size, cols, first, cells):
    count, channels = cells.shape
    upper, lower = min(count, size - cols - first), max(0, cols - first)
    here = at + first
    lhs_ref[here : here + count, channels : 2 * channels] = cells
    lhs_ref[here + cols : here + cols + upper, :channels] = cells[:upper]
    lhs_ref[here + lower - cols : here + count - cols, 2 * channels :] = cells[lower:]


def put_row(lhs_ref, at, size, row):
    cols, channels = row.shape
    row = row.astype(jnp.float32)
    last = slice(at + size - cols, at + size)
    lhs_ref[at : at + cols, :channels] = (is_core(1) * row).astype(lhs_ref.dtype)
    lhs_ref[last, 2 * channels :] = (is_core(0) * row).astype(lhs_ref.dtype)


def taps_kernel(cells_ref, lhs_ref):
    count, rows, cols, channels = cells_ref.shape
    size = rows * cols
    for frame in range(count):
        put_cells(lhs_ref, frame * size, size, cols, 0, cells_ref[frame].reshape(size, channels))


def row_taps(column, above, below):
    rows = column.shape[0]
    row = lax.broadcasted_iota(jnp.int32, column.shape, 0)
    up = jnp.where(row == 0, is_core(1) * above, pltpu.roll(column, 1, 0))
    down = jnp.where(row == rows - 1, is_core(0) * below, pltpu.roll(column, rows - 1, 0))
    return jnp.concatenate([up, column, down], axis=1)


def halves(channels):
    return slice(0, channels // 2), slice(channels // 2, channels)


def end_state(frames, pole_ref, lanes):
    decay = jnp.exp(rate_of(pole_ref))[:, lanes]
    state = frames[0]
    for frame in frames[1:]:
        state = decay * state + frame
    return state


def dot(lhs, weight_ref, column, lanes, inputs=slice(None)):
    weight = weight_ref[:, column, inputs, lanes].reshape(lhs.shape[1], -1)
    return jnp.dot(lhs, weight, preferred_element_type=jnp.float32)


def main_kernel(_, got_ref, weight_ref, pole_ref, total_ref, spill_ref, end_ref, lhs_ref):
    count, rows, cols, _ = total_ref.shape
    size = rows * cols
    for frame in range(count):
        put_row(lhs_ref, frame * size, size, got_ref[frame * cols : (frame + 1) * cols])
    states = []
    for lanes in halves(weight_ref.shape[-1]):
        tile = (rows, cols, lanes.stop - lanes.start)
        col = lax.broadcasted_iota(jnp.int32, tile, 1)
        totals = []
        for frame in range(count):
            cells = lhs_ref[frame * size : (frame + 1) * size]
            here = slice(frame * rows, (frame + 1) * rows)
            total = dot(cells, weight_ref, 1, lanes).reshape(tile)
            first = dot(cells, weight_ref, 0, lanes).reshape(tile)
            spill_ref[1, here, lanes] = first[:, cols - 1, :]
            total += jnp.where(col == 0, 0.0, pltpu.roll(first, 1, 1))
            last = dot(cells, weight_ref, 2, lanes).reshape(tile)
            spill_ref[0, here, lanes] = last[:, 0, :]
            total += jnp.where(col == cols - 1, 0.0, pltpu.roll(last, cols - 1, 1))
            total_ref[frame, :, :, lanes] = total
            totals.append(total)
        states.append(end_state(totals, pole_ref, lanes))
    state = jnp.where(col == 0, pltpu.roll(states[1], cols - 1, 1), states[0])
    state = jnp.where(col == cols - 1, pltpu.roll(states[1], 1, 1), state)
    end_ref[...] = state.reshape(end_ref.shape).astype(end_ref.dtype)


def halo_kernel(mine_ref, theirs_ref, lhs_ref, start_ref):
    rows = mine_ref.shape[1] // 2
    count = mine_ref.shape[0] // 2
    room = count * rows
    zero, one = is_core(0), is_core(1)
    core = lax.axis_index("sx")
    slots = ((1, 0), (2, 3))
    for frame in range(count):
        for depth in range(2):
            own = mine_ref[2 * frame + depth].astype(jnp.float32)
            other = theirs_ref[2 * frame + depth].astype(jnp.float32)
            own = row_taps(own[rows:], own[rows - 1 : rows], own[:1])
            other = row_taps(other[:rows], other[2 * rows - 1 :], other[rows : rows + 1])
            for swapped, taps in enumerate((own, other)):
                slot = jnp.where(core == swapped, slots[1][depth], slots[0][depth])
                at = pl.multiple_of(slot * room + frame * rows, rows)
                lhs_ref[pl.ds(at, rows)] = taps.astype(lhs_ref.dtype)
    own = mine_ref[2 * count, rows:].astype(jnp.float32)
    other = theirs_ref[2 * count, :rows].astype(jnp.float32)
    start_ref[:rows] = zero * other + one * own
    start_ref[rows:] = zero * own + one * other


def drive_kernel(
    lhs_ref, weight_ref, total_ref, spill_ref, pole_ref, drive_ref, beside_ref, strips_ref, end_ref
):
    count, rows, cols, wide = drive_ref.shape
    room, size = count * rows, rows * cols
    at = size + 2 * rows
    early = None
    for lanes in halves(weight_ref.shape[-1]):
        first = dot(lhs_ref[: 2 * room], weight_ref, 0, lanes)
        middle = dot(lhs_ref[room : 3 * room], weight_ref, 1, lanes)
        last = dot(lhs_ref[2 * room :], weight_ref, 2, lanes)
        left = (spill_ref[0, :, lanes] + first[:room] + middle[:room]).reshape(count, rows, wide)
        right = (spill_ref[1, :, lanes] + middle[room:] + last[room:]).reshape(count, rows, wide)
        total = total_ref[:, :, :, lanes]
        if lanes.start == 0:
            near = total[:, :, 0, :] + first[room:].reshape(count, rows, wide)
            far = total[:, :, cols - 1, :] + last[:room].reshape(count, rows, wide)
            strips = jnp.concatenate([left, near, far, right], axis=1)
            strips_ref[...] = strips
            early = end_state([strips[frame] for frame in range(count)], pole_ref, lanes)
            end_ref[at : at + rows] = early[:rows].astype(end_ref.dtype)
            end_ref[at + rows :] = early[3 * rows :].astype(end_ref.dtype)
            continue
        col = lax.broadcasted_iota(jnp.int32, drive_ref.shape, 2)
        total += jnp.where(col == 0, first[room:].reshape(count, rows, 1, wide), 0.0)
        total += jnp.where(col == cols - 1, last[:room].reshape(count, rows, 1, wide), 0.0)
        drive_ref[...] = total
        state = end_state([total[frame] for frame in range(count)], pole_ref, lanes)
        col = lax.broadcasted_iota(jnp.int32, state.shape, 1)
        state = jnp.where(col == 1, early[rows : 2 * rows].reshape(rows, 1, wide), state)
        border = early[2 * rows : 3 * rows].reshape(rows, 1, wide)
        state = jnp.where(col == cols - 2, border, state)
        end_ref[:size] = state.reshape(size, wide).astype(end_ref.dtype)
        beside = jnp.concatenate([left, right], axis=1)
        beside_ref[...] = beside
        state = end_state([beside[frame] for frame in range(count)], pole_ref, lanes)
        end_ref[size:at] = state.astype(end_ref.dtype)


def spread(block, cols, count, of_lanes):
    _, lanes, inset = block
    value = of_lanes(lanes)
    if inset is None:
        return value
    other, columns = inset
    value, instead = jnp.broadcast_arrays(value, of_lanes(other))
    shape = (count, value.shape[1])
    col = lax.rem(lax.broadcasted_iota(jnp.int32, shape, 0), cols)
    return jnp.where((col == columns[0]) | (col == columns[1]), instead, value)


def entry_kernel(frames, cols, block, ends_ref, pole_ref, out_ref):
    rate = rate_of(pole_ref)
    count = ends_ref.shape[1]
    carried = spread(block, cols, count, lambda lanes: jnp.exp(frames * rate[:, lanes]))
    entry = jnp.zeros(ends_ref.shape[1:], jnp.float32)
    out_ref[0] = entry.astype(out_ref.dtype)
    for index in range(ends_ref.shape[0] - 1):
        entry = carried * entry + ends_ref[index].astype(jnp.float32)
        out_ref[index + 1] = entry.astype(out_ref.dtype)


def exchange(pieces, pole, frames, cols):
    groups = lax.axis_size("tm")
    arrivals = []
    for end, blocks in pieces:
        entries = []
        for block in blocks:
            shares = end[block[0]].reshape(groups, -1, end.shape[1])
            assert block[2] is None or shares.shape[1] % cols == 0
            shares = lax.all_to_all(shares, "tm", 0, 0)
            kernel = functools.partial(entry_kernel, frames, cols, block)
            entry = call(kernel, of(shares.shape, end.dtype), shares, pole)
            entries.append(lax.all_to_all(entry, "tm", 0, 0).reshape(-1, end.shape[1]))
        arrivals.append((jnp.concatenate(entries, axis=0),))
    return arrivals


def pick(values):
    group = lax.axis_index("tm")
    picked = values[-1]
    for index, value in enumerate(values[:-1]):
        picked = jnp.where(group == index, value, picked)
    return picked


def on_core(first, second):
    return jnp.where(lax.axis_index("sx") == 0, first, second)


def weigh(one, by_one, other, by_other):
    return by_one * one.astype(jnp.float32) + by_other * other.astype(jnp.float32)


def relay_kernel(frames, cols, blocks, end_ref, got_ref, pole_ref, out_ref):
    rate = rate_of(pole_ref)
    carried, twice = jnp.exp(frames * rate), jnp.exp(2 * frames * rate)
    none, same = jnp.zeros_like(rate), jnp.ones_like(rate)
    own = on_core(pick([carried, same, same, same]), pick([same, same, same, none]))
    got = on_core(pick([same, carried, carried, carried]), pick([none, none, twice, same]))
    for block in blocks:
        rows = block[0]
        count = rows.stop - rows.start
        by_own = spread(block, cols, count, lambda lanes: own[:, lanes])
        by_got = spread(block, cols, count, lambda lanes: got[:, lanes])
        out_ref[rows] = weigh(end_ref[rows], by_own, got_ref[rows], by_got).astype(out_ref.dtype)


def exchange_four(pieces, pole, frames, cols):
    def along(pairs, core):
        return [(2 * source + core, 2 * target + core) for source, target in pairs]

    axes = ("tm", "sx")
    down = [(0, 2), (1, 3)]
    first_round = along([(0, 1), (1, 0), (2, 3)], 0) + along(down, 1)
    second_round = along(down, 0) + along([(0, 1), (2, 3), (3, 2)], 1)
    arrivals = []
    for end, blocks in pieces:
        got = lax.ppermute(end, axes, first_round)
        kernel = functools.partial(relay_kernel, frames, cols, blocks)
        relayed = call(kernel, of(end.shape, end.dtype), end, got, pole)
        arrivals.append((got, lax.ppermute(relayed, axes, second_round)))
    return arrivals


class Mix:
    def __init__(self, lanes, count, pole_ref, scale_ref):
        self.rate = rate_of(pole_ref)[:, lanes]
        self.scale = scale_ref[:, lanes]
        self.count = count

    def entry(self, arrived_refs, rows):
        parts = [ref[rows].astype(jnp.float32) for ref in arrived_refs]
        if len(parts) == 1:
            return parts[0]
        carried = jnp.exp(self.count * self.rate)
        none, same = jnp.zeros_like(self.rate), jnp.ones_like(self.rate)
        early = on_core(pick([none, same, none, same]), pick([none, none, carried, carried]))
        late = on_core(pick([none, none, same, carried]), pick([none, same, same, same]))
        return weigh(parts[0], early, parts[1], late)

    def __call__(self, drives, entry, start):
        decay = jnp.exp(self.rate)
        reach = jnp.exp((self.count * lax.axis_index("tm")).astype(jnp.float32) * self.rate)
        state = reach * start + entry.reshape(start.shape)
        for drive in drives:
            state = decay * state + drive
            yield jax.nn.gelu(self.scale * state)


def no_border(cells, axis):
    col = lax.broadcasted_iota(jnp.int32, cells.shape, axis)
    return jnp.where((col == 0) | (col == cells.shape[axis] - 1), 0.0, cells)


def put_back(late, early, axis):
    cols = late.shape[axis]
    col = lax.broadcasted_iota(jnp.int32, late.shape, axis)
    late = jnp.where(col == 1, pltpu.roll(early, 1, axis), late)
    return jnp.where(col == cols - 2, pltpu.roll(early, cols - 1, axis), late)


def mixed_kernel(lanes, rounds, *refs):
    drive_ref, start_ref, pole_ref, scale_ref, *arrived_refs, lhs_ref = refs
    early_refs, late_refs = arrived_refs[:rounds], arrived_refs[rounds:]
    count, rows, cols, _ = drive_ref.shape
    wide = lanes.stop - lanes.start
    size = rows * cols
    stride = lhs_ref.shape[0] // count
    room = (stride - size) // 2
    mix = Mix(lanes, count, pole_ref, scale_ref)
    first = lanes.start == 0
    held = lanes if first else slice(None)
    block = 8
    if first:
        for frame in range(count):
            put_row(lhs_ref, frame * stride + room, size, jnp.zeros((cols, wide), lhs_ref.dtype))
    for row in range(0, rows, block):
        here = slice(row, row + block)
        drives = [drive_ref[frame, here, :, held] for frame in range(count)]
        cells = slice(row * cols, (row + block) * cols)
        entry = mix.entry(early_refs, cells).reshape(block, cols, wide)
        if not first:
            entry = put_back(mix.entry(late_refs, cells).reshape(entry.shape), entry, 1)
        for frame, tile in enumerate(mix(drives, entry, start_ref[here, :, lanes])):
            if first:
                tile = no_border(tile, 1)
            tile = tile.reshape(block * cols, wide).astype(lhs_ref.dtype)
            put_cells(lhs_ref, frame * stride + room, size, cols, row * cols, tile)


def strip_start_kernel(start_ref, sides_ref, out_ref):
    rows, cols, _ = start_ref.shape
    start = start_ref[...]
    out_ref[:rows] = sides_ref[:rows]
    out_ref[rows : 2 * rows] = start[:, 0, :]
    out_ref[2 * rows : 3 * rows] = start[:, cols - 1, :]
    out_ref[3 * rows :] = sides_ref[rows:]


def inside(slot):
    chip, chips = lax.axis_index("sy"), lax.axis_size("sy")
    return {0: (chip > 0).astype(jnp.float32), 3: (chip < chips - 1).astype(jnp.float32)}.get(slot, 1.0)


def give_kernel(parts, rounds, *refs):
    total_ref, drive_ref, beside_ref, strips_ref, *refs = refs
    start_ref, strip_start_ref, pole_ref, scale_ref, *arrived_refs, give_ref = refs
    early_refs, late_refs = arrived_refs[:rounds], arrived_refs[rounds:]
    count, rows, cols, wide = drive_ref.shape
    size = rows * cols
    inner = inner_row(rows)
    zero, one = is_core(0), is_core(1)
    early, late = (Mix(lanes, count, pole_ref, scale_ref) for lanes in parts)
    row = pl.ds(pl.multiple_of(inner * cols, cols), cols)
    which = lax.broadcasted_iota(jnp.int32, (cols, wide), 0)

    def near(at):
        return pl.ds(pl.multiple_of(at + jnp.where(inner == 0, 0, rows - cols), cols), cols)

    def end(cells):
        return zero * cells[cols - 1 :] + one * cells[:1]

    def rows_of(cells):
        table = jnp.zeros(which.shape, jnp.float32)
        for index, cell in cells:
            table = jnp.where(which == index, cell, table)
        return table

    entry = put_back(late.entry(late_refs, row), late.entry(early_refs, row), 0)
    drives = [drive_ref[frame, inner] for frame in range(count)]
    tile = late(drives, entry, start_ref[inner, :, parts[1]])
    drives = [total_ref[frame, inner, :, parts[0]] for frame in range(count)]
    first = early(drives, early.entry(early_refs, row), start_ref[inner, :, parts[0]])

    slots = [(0, 0), (1, 3)]
    entry = rows_of([(i, end(late.entry(late_refs, near(size + i * rows)))) for i, _ in slots])
    start = rows_of([(i, end(strip_start_ref[near(slot * rows), parts[1]])) for i, slot in slots])
    drives = [
        rows_of([(i, end(beside_ref[frame, near(i * rows)])) for i, _ in slots])
        for frame in range(count)
    ]
    beside = late(drives, entry, start)

    slots = [(2 + slot, slot) for slot in range(4)]
    grid = early.entry(late_refs, row)
    at = size + 2 * rows
    entry = rows_of(
        [
            (2, end(early.entry(late_refs, near(at)))),
            (3, grid[1:2]),
            (4, grid[cols - 2 : cols - 1]),
            (5, end(early.entry(late_refs, near(at + rows)))),
        ]
    )
    start = rows_of([(i, end(strip_start_ref[near(slot * rows), parts[0]])) for i, slot in slots])
    drives = [
        rows_of([(i, end(strips_ref[frame, near(slot * rows)])) for i, slot in slots])
        for frame in range(count)
    ]
    strips = early(drives, entry, start)
    for frame, cells in enumerate(zip(tile, first, beside, strips)):
        give_ref[frame, :cols] = cells[0].astype(give_ref.dtype)
        ends = jnp.where(which < 2, cells[2], cells[3])
        ends = jnp.where((which == 0) | (which == 2), inside(0) * ends, ends)
        ends = jnp.where((which == 1) | (which == 5), inside(3) * ends, ends)
        give_ref[frame, cols : 2 * cols] = ends.astype(give_ref.dtype)
        give_ref[frame, 2 * cols :] = no_border(cells[1], 0).astype(give_ref.dtype)


def late_kernel(parts, rounds, *refs):
    beside_ref, strips_ref, strip_start_ref, pole_ref, scale_ref, *refs = refs
    *late_refs, beside_out_ref, strips_out_ref = refs
    count, room, wide = beside_ref.shape
    rows = room // 2
    size = late_refs[0].shape[0] - 4 * rows
    cols = size // rows
    early, late = (Mix(lanes, count, pole_ref, scale_ref) for lanes in parts)

    def column(cells, index):
        return cells[index * rows : (index + 1) * rows]

    starts = [strip_start_ref[slot * rows : (slot + 1) * rows, parts[1]] for slot in (0, 3)]
    entry = late.entry(late_refs, slice(size, size + 2 * rows))
    drives = [beside_ref[frame] for frame in range(count)]
    beside = late(drives, entry, jnp.concatenate(starts, axis=0))
    grid = early.entry(late_refs, slice(0, size)).reshape(rows, cols, wide)
    sides = early.entry(late_refs, slice(size + 2 * rows, size + 4 * rows))
    entry = [sides[:rows], grid[:, 1, :], grid[:, cols - 2, :], sides[rows:]]
    drives = [strips_ref[frame] for frame in range(count)]
    strips = early(drives, jnp.concatenate(entry, axis=0), strip_start_ref[:, parts[0]])
    for frame, (sides, strip) in enumerate(zip(beside, strips)):
        sides = [column(sides, 0) * inside(0), column(sides, 1) * inside(3)]
        strip = [column(strip, slot) * inside(slot) for slot in range(4)]
        beside_out_ref[frame] = jnp.concatenate(sides, axis=0).astype(beside_out_ref.dtype)
        strips_out_ref[frame] = jnp.concatenate(strip, axis=0).astype(strips_out_ref.dtype)


def put_columns_taps(lhs_ref, slots, columns, ends):
    rows = columns.shape[0] // len(slots)
    columns, ends = columns.astype(jnp.float32), ends.astype(jnp.float32)
    for index, at in enumerate(slots):
        column, end = columns[index * rows : (index + 1) * rows], ends[index : index + 1]
        lhs_ref[at : at + rows] = row_taps(column, end, end).astype(lhs_ref.dtype)


def tile_sum(tile, inputs, lanes, room, lhs_ref, weight_ref):
    count, rows, cols, wide = tile
    size = rows * cols
    col = lax.broadcasted_iota(jnp.int32, tile[1:], 1)

    def beside(cells):
        return cells.reshape(rows, 1, wide) if room else 0.0

    for frame in range(count):
        at = frame * (size + 2 * room)
        end = at + room + size
        total = dot(lhs_ref[at + room : end], weight_ref, 1, lanes, inputs).reshape(tile[1:])
        first = dot(lhs_ref[at:end], weight_ref, 0, lanes, inputs)
        shifted = pltpu.roll(first[room:].reshape(tile[1:]), 1, 1)
        total += jnp.where(col == 0, beside(first[:room]), shifted)
        last = dot(lhs_ref[at + room : end + room], weight_ref, 2, lanes, inputs)
        shifted = pltpu.roll(last[:size].reshape(tile[1:]), cols - 1, 1)
        yield total + jnp.where(col == cols - 1, beside(last[size:]), shifted)


def strip_slots(count, rows, cols):
    room, given = count * rows, count * cols
    strips = [given, given + room, 2 * given + 2 * room, 2 * given + 3 * room]
    return strips, [0, given + 2 * room, 2 * given + 4 * room]


def strip_sum(tile, inputs, lanes, lhs_ref, weight_ref):
    count, rows, cols, wide = tile
    room, given = count * rows, count * cols
    strips, _ = strip_slots(count, rows, cols)
    first = dot(lhs_ref[: strips[1] + room], weight_ref, 0, lanes, inputs)
    middle = dot(lhs_ref[strips[1] : strips[2] + room], weight_ref, 1, lanes, inputs)
    last = dot(lhs_ref[strips[2] :], weight_ref, 2, lanes, inputs)
    col = lax.broadcasted_iota(jnp.int32, (count, cols, wide), 1)

    def row_of(cells):
        return cells.reshape(count, cols, wide)

    reached = row_of(middle[room : room + given])
    reached += jnp.where(col == 0, 0.0, pltpu.roll(row_of(first[:given]), 1, 1))
    reached += jnp.where(col == cols - 1, 0.0, pltpu.roll(row_of(last[2 * room :]), cols - 1, 1))
    row = lax.broadcasted_iota(jnp.int32, tile, 1)
    col = lax.broadcasted_iota(jnp.int32, tile, 2)
    total = jnp.where(row == inner_row(rows), reached.reshape(count, 1, cols, wide), 0.0)
    for at, cells in (
        (0, first[given : given + room] + middle[:room]),
        (1, first[given + room :]),
        (cols - 2, last[:room]),
        (cols - 1, middle[room + given :] + last[room : 2 * room]),
    ):
        total += jnp.where(col == at, cells.reshape(count, rows, 1, wide), 0.0)
    return total


def further_kernel(inputs, lanes, lhs_ref, weight_ref, out_ref):
    tiles = tile_sum(out_ref.shape, inputs, lanes, 0, lhs_ref, weight_ref)
    for frame, total in enumerate(tiles):
        out_ref[frame] = total


def result_kernel(
    parts, _, got_ref, beside_ref, strips_ref, weight_ref, *refs
):
    *before_refs, out_ref, lhs_ref, held_ref, strip_lhs_ref, sems = refs
    count, rows, cols, _ = held_ref.shape
    size = rows * cols
    stride = size + 2 * rows
    strips_at, given_at = strip_slots(count, rows, cols)
    for frame in range(count):
        at = frame * stride
        put_row(lhs_ref, at + rows, size, got_ref[frame, :cols])
        ends = got_ref[frame, cols : 2 * cols]
        put_columns_taps(lhs_ref, (at, at + rows + size), beside_ref[frame], ends)
        slots = [slot + frame * rows for slot in strips_at]
        put_columns_taps(strip_lhs_ref, slots, strips_ref[frame], ends.astype(jnp.float32)[2:])
        given = got_ref[frame, 2 * cols :].astype(jnp.float32)
        given = [is_core(1) * given, jnp.zeros_like(given), is_core(0) * given]
        given = jnp.concatenate(given, axis=1).astype(strip_lhs_ref.dtype)
        for at in given_at:
            strip_lhs_ref[at + frame * cols : at + (frame + 1) * cols] = given

    def store(frame, part):
        here = (frame, slice(None), slice(None), parts[part])
        return pltpu.make_async_copy(held_ref.at[here], out_ref.at[here], sems.at[frame, part])

    for part, lanes in enumerate(parts):
        tile = (count, rows, cols, lanes.stop - lanes.start)
        strips = strip_sum(tile, parts[0], lanes, strip_lhs_ref, weight_ref)
        tiles = tile_sum(tile, parts[1], lanes, rows, lhs_ref, weight_ref)
        for frame, total in enumerate(tiles):
            total += before_refs[part][frame] + strips[frame]
            held_ref[frame, :, :, lanes] = total.astype(held_ref.dtype)
            store(frame, part).start()
    for part in range(len(parts)):
        for frame in range(count):
            store(frame, part).wait()


def on_device(frames, input_weight, output_weight, pole_index, gelu_scale, start_state):
    count, rows, cols, channels = frames.shape
    size, room = rows * cols, count * rows
    wide = 3 * channels
    assert lax.axis_size("sx") == 2
    narrow = frames.dtype
    pole, scale = pole_index[None], gelu_scale[None]

    shapes = (
        of((count * cols + (2 * count + 1) * rows, channels), narrow),
        of((2 * count + 1, rows, channels), narrow),
    )
    edges = call(
        edges_kernel,
        shapes,
        frames,
        scratch=[pltpu.VMEM((count, channels // 128, size, 128), jnp.float32)],
        flops=EDGES_COST,
    )
    give, keep = call(
        start_edges_kernel,
        shapes,
        start_state,
        *edges,
        aliases={1: 0, 2: 1},
    )
    got, mine = trade_columns(give, keep, count * cols)
    taps = of((count * size, wide), narrow)
    parts = halves(channels)
    half = channels // 2
    inner = of((count, rows, cols, half), jnp.float32)
    *main, early, _ = call(
        main_kernel,
        (
            of(frames.shape, jnp.float32),
            of((2, room, channels), jnp.float32),
            of((size, half), narrow),
            taps,
        ),
        call(taps_kernel, taps, frames),
        got,
        input_weight,
        pole,
        aliases={0: 3},
        flops=18 * frames.size * channels,
    )
    mine, total, spill = lax.optimization_barrier((mine, *main))
    halo, sides = call(
        halo_kernel,
        (of((4 * room, wide), narrow), of((2 * rows, channels), jnp.float32)),
        mine,
        swap_cores(mine),
    )
    drive, beside, strips, late = call(
        drive_kernel,
        (
            inner,
            of((count, 2 * rows, half), jnp.float32),
            of((count, 4 * rows, half), jnp.float32),
            of((size + 4 * rows, half), narrow),
        ),
        halo,
        input_weight,
        total,
        spill,
        pole,
        flops=36 * room * channels * channels,
    )
    at = size + 2 * rows
    tile = slice(0, size)
    pieces = [
        (early, [(tile, parts[0], (parts[1], (0, cols - 1)))]),
        (
            late,
            [
                (tile, parts[1], (parts[0], (1, cols - 2))),
                (slice(size, at), parts[1], None),
                (slice(at, at + 2 * rows), parts[0], None),
            ],
        ),
    ]
    exchanged = exchange_four if lax.axis_size("tm") == 4 else exchange
    early, late = exchanged(pieces, pole, count, cols)
    rounds = len(early)

    mixing = (start_state, pole, scale)
    taps = of((count * size, 3 * half), narrow)
    lhs = call(functools.partial(mixed_kernel, parts[0], rounds), taps, total, *mixing, *early)
    strip_start = call(strip_start_kernel, of((4 * rows, channels), jnp.float32), start_state, sides)
    flops = 18 * inner.size * half
    first_sum, second_sum = (
        call(
            functools.partial(further_kernel, parts[0], lanes), inner, lhs, output_weight, flops=flops
        )
        for lanes in parts
    )
    *late, first_sum, second_sum = lax.optimization_barrier((*late, first_sum, second_sum))
    give = call(
        functools.partial(give_kernel, parts, rounds),
        of((count, 3 * cols, half), narrow),
        total,
        drive,
        beside,
        strips,
        start_state,
        strip_start,
        pole,
        scale,
        *early,
        *late,
    )
    beside, strips = call(
        functools.partial(late_kernel, parts, rounds),
        (of(beside.shape, narrow), of(strips.shape, narrow)),
        beside,
        strips,
        strip_start,
        pole,
        scale,
        *late,
    )
    taps = of((count * size + 2 * room, 3 * half), narrow)
    lhs = call(
        functools.partial(mixed_kernel, parts[1], rounds), taps, drive, *mixing, *early, *late
    )
    result, _ = call(
        functools.partial(result_kernel, parts),
        (of(frames.shape, narrow), taps),
        lhs,
        swap_cores(give),
        beside,
        strips,
        output_weight,
        first_sum,
        second_sum,
        out_specs=(HBM, WHOLE),
        aliases={0: 1},
        scratch=[
            pltpu.VMEM(frames.shape, narrow),
            pltpu.VMEM((4 * room + 3 * count * cols, 3 * half), narrow),
            pltpu.SemaphoreType.DMA((count, len(parts))),
        ],
        flops=2 * flops,
    )
    return result


def solution(mesh):
    return jax.shard_map(
        on_device,
        mesh=mesh,
        in_specs=(P("tm", "sx", "sy", None), P(), P(), P(), P(), P("sx", "sy", None)),
        out_specs=P("tm", "sx", "sy", None),
        check_vma=False,
    )
```

```python
import functools
import math

import jax
import jax.numpy as jnp
from jax import lax
from jax.experimental import pallas as pl
from jax.experimental.pallas import tpu as pltpu
from jax.sharding import PartitionSpec as P

NPOLES = 16
VMEM_LIMIT = 24 * 1024 * 1024
WHOLE = pl.BlockSpec(memory_space=pltpu.VMEM)
HBM = pl.BlockSpec(memory_space=pltpu.HBM)
EDGES_COST = 2_000_000_000


def call(kernel, out_shape, *args, scratch=(), flops=0, out_specs=None, aliases=None):
    outs = jax.tree.leaves(out_shape)
    moved = sum(leaf.size * leaf.dtype.itemsize for leaf in (*args, *outs))
    return pl.pallas_call(
        kernel,
        in_specs=[WHOLE] * len(args),
        out_specs=out_specs or jax.tree.map(lambda _: WHOLE, out_shape),
        out_shape=out_shape,
        scratch_shapes=scratch,
        input_output_aliases=aliases or {},
        compiler_params=pltpu.CompilerParams(vmem_limit_bytes=VMEM_LIMIT),
        cost_estimate=pl.CostEstimate(flops=flops, bytes_accessed=moved, transcendentals=0),
    )(*args)


def of(shape, dtype):
    return jax.ShapeDtypeStruct(shape, dtype)


def is_core(which):
    return (lax.axis_index("sx") == which).astype(jnp.float32)


def rate_of(pole_ref):
    pole = pole_ref[...].astype(jnp.float32)
    return -0.001 * jnp.exp(pole * (math.log(300.0) / (NPOLES - 1)))


def inner_row(rows):
    return jnp.where(lax.axis_index("sx") == 0, rows - 1, 0)


def swap_cores(array):
    return lax.ppermute(array, "sx", [(0, 1), (1, 0)])


def put_columns(index, left, right, give_ref, keep_ref):
    zero, one = is_core(0), is_core(1)
    count, rows, _ = keep_ref.shape
    at = give_ref.shape[0] - (count - index) * rows
    give_ref[at : at + rows] = (zero * left + one * right).astype(give_ref.dtype)
    keep_ref[index] = (zero * right + one * left).astype(keep_ref.dtype)


def edges_kernel(cells_ref, give_ref, keep_ref, wide_ref):
    count, rows, cols, channels = cells_ref.shape
    for frame in range(count):
        give_ref[frame * cols : (frame + 1) * cols] = cells_ref[frame, inner_row(rows)]
        tile = cells_ref[frame].reshape(rows * cols, channels).astype(jnp.float32)
        lanes = wide_ref.shape[-1]
        for part in range(channels // lanes):
            wide_ref[frame, part] = tile[:, part * lanes : (part + 1) * lanes]

        def column(col):
            parts = [
                wide_ref[frame, part, pl.ds(col, rows, stride=cols), :]
                for part in range(channels // lanes)
            ]
            return jnp.concatenate(parts, axis=1)

        for depth in range(2):
            left, right = column(depth), column(cols - 1 - depth)
            put_columns(2 * frame + depth, left, right, give_ref, keep_ref)


def start_edges_kernel(start_ref, _, __, give_ref, keep_ref):
    tile, cols = start_ref[...], start_ref.shape[1]
    index = keep_ref.shape[0] - 1
    put_columns(index, tile[:, 0, :], tile[:, cols - 1, :], give_ref, keep_ref)


def trade_columns(give, keep, at):
    chips = lax.axis_size("sy")
    got = swap_cores(give)
    pairs = [(chip, chips + chip + 1) for chip in range(chips - 1)]
    pairs += [(after, before) for before, after in pairs]
    columns = jnp.concatenate([keep, got[at:].reshape(keep.shape)], axis=1)
    return got, lax.ppermute(columns, ("sx", "sy"), pairs)


def put_cells(lhs_ref, at, size, cols, first, cells):
    count, channels = cells.shape
    upper, lower = min(count, size - cols - first), max(0, cols - first)
    here = at + first
    lhs_ref[here : here + count, channels : 2 * channels] = cells
    lhs_ref[here + cols : here + cols + upper, :channels] = cells[:upper]
    lhs_ref[here + lower - cols : here + count - cols, 2 * channels :] = cells[lower:]


def put_row(lhs_ref, at, size, row):
    cols, channels = row.shape
    row = row.astype(jnp.float32)
    last = slice(at + size - cols, at + size)
    lhs_ref[at : at + cols, :channels] = (is_core(1) * row).astype(lhs_ref.dtype)
    lhs_ref[last, 2 * channels :] = (is_core(0) * row).astype(lhs_ref.dtype)


def taps_kernel(cells_ref, lhs_ref):
    count, rows, cols, channels = cells_ref.shape
    size = rows * cols
    for frame in range(count):
        put_cells(lhs_ref, frame * size, size, cols, 0, cells_ref[frame].reshape(size, channels))


def row_taps(column, above, below):
    rows = column.shape[0]
    row = lax.broadcasted_iota(jnp.int32, column.shape, 0)
    up = jnp.where(row == 0, is_core(1) * above, pltpu.roll(column, 1, 0))
    down = jnp.where(row == rows - 1, is_core(0) * below, pltpu.roll(column, rows - 1, 0))
    return jnp.concatenate([up, column, down], axis=1)


SLAB = 8


def add_columns(cells, columns):
    rows, cols, wide = cells.shape
    col = lax.broadcasted_iota(jnp.int32, (rows, SLAB, wide), 1)

    def slab(start):
        total = 0.0
        for at, column in columns:
            if start <= at < start + SLAB:
                total = jnp.where(col == at - start, column, total)
        return cells[:, start : start + SLAB] + total

    middle = [cells[:, SLAB : cols - SLAB]] if cols > 2 * SLAB else []
    return jnp.concatenate([slab(0), *middle, slab(cols - SLAB)], axis=1)


def with_column(cells, at, column):
    rows, cols, wide = cells.shape
    start = 0 if at == 0 else cols - SLAB
    col = lax.broadcasted_iota(jnp.int32, (rows, SLAB, wide), 1)
    slab = jnp.where(col == at - start, column, cells[:, start : start + SLAB])
    if at == 0:
        return jnp.concatenate([slab, cells[:, SLAB:]], axis=1)
    return jnp.concatenate([cells[:, :start], slab], axis=1)


def halves(channels):
    return slice(0, channels // 2), slice(channels // 2, channels)


def end_state(frames, pole_ref, lanes):
    decay = jnp.exp(rate_of(pole_ref))[:, lanes]
    state = frames[0]
    for frame in frames[1:]:
        state = decay * state + frame
    return state


def dot(lhs, weight_ref, column, lanes, inputs=slice(None)):
    weight = weight_ref[:, column, inputs, lanes].reshape(lhs.shape[1], -1)
    return jnp.dot(lhs, weight, preferred_element_type=jnp.float32)


def main_kernel(_, got_ref, weight_ref, pole_ref, total_ref, spill_ref, end_ref, lhs_ref):
    count, rows, cols, _ = total_ref.shape
    size = rows * cols
    for frame in range(count):
        put_row(lhs_ref, frame * size, size, got_ref[frame * cols : (frame + 1) * cols])
    states = []
    for lanes in halves(weight_ref.shape[-1]):
        tile = (rows, cols, lanes.stop - lanes.start)
        col = lax.broadcasted_iota(jnp.int32, tile, 1)
        totals = []
        for frame in range(count):
            cells = lhs_ref[frame * size : (frame + 1) * size]
            here = slice(frame * rows, (frame + 1) * rows)
            total = dot(cells, weight_ref, 1, lanes).reshape(tile)
            first = dot(cells, weight_ref, 0, lanes).reshape(tile)
            spill_ref[1, here, lanes] = first[:, cols - 1, :]
            total += with_column(pltpu.roll(first, 1, 1), 0, 0.0)
            last = dot(cells, weight_ref, 2, lanes).reshape(tile)
            spill_ref[0, here, lanes] = last[:, 0, :]
            total += with_column(pltpu.roll(last, cols - 1, 1), cols - 1, 0.0)
            total_ref[frame, :, :, lanes] = total
            totals.append(total)
        states.append(end_state(totals, pole_ref, lanes))
    state = jnp.where(col == 0, pltpu.roll(states[1], cols - 1, 1), states[0])
    state = jnp.where(col == cols - 1, pltpu.roll(states[1], 1, 1), state)
    end_ref[...] = state.reshape(end_ref.shape).astype(end_ref.dtype)


def halo_kernel(mine_ref, theirs_ref, lhs_ref, start_ref):
    rows = mine_ref.shape[1] // 2
    count = mine_ref.shape[0] // 2
    room = count * rows
    zero, one = is_core(0), is_core(1)
    core = lax.axis_index("sx")
    slots = ((1, 0), (2, 3))
    for frame in range(count):
        for depth in range(2):
            own = mine_ref[2 * frame + depth].astype(jnp.float32)
            other = theirs_ref[2 * frame + depth].astype(jnp.float32)
            own = row_taps(own[rows:], own[rows - 1 : rows], own[:1])
            other = row_taps(other[:rows], other[2 * rows - 1 :], other[rows : rows + 1])
            for swapped, taps in enumerate((own, other)):
                slot = jnp.where(core == swapped, slots[1][depth], slots[0][depth])
                at = pl.multiple_of(slot * room + frame * rows, rows)
                lhs_ref[pl.ds(at, rows)] = taps.astype(lhs_ref.dtype)
    own = mine_ref[2 * count, rows:].astype(jnp.float32)
    other = theirs_ref[2 * count, :rows].astype(jnp.float32)
    start_ref[:rows] = zero * other + one * own
    start_ref[rows:] = zero * own + one * other


def drive_kernel(
    lhs_ref, weight_ref, total_ref, spill_ref, pole_ref, drive_ref, beside_ref, strips_ref, end_ref
):
    count, rows, cols, wide = drive_ref.shape
    room, size = count * rows, rows * cols
    at = size + 2 * rows
    early = None
    for lanes in halves(weight_ref.shape[-1]):
        first = dot(lhs_ref[: 2 * room], weight_ref, 0, lanes)
        middle = dot(lhs_ref[room : 3 * room], weight_ref, 1, lanes)
        last = dot(lhs_ref[2 * room :], weight_ref, 2, lanes)
        left = (spill_ref[0, :, lanes] + first[:room] + middle[:room]).reshape(count, rows, wide)
        right = (spill_ref[1, :, lanes] + middle[room:] + last[room:]).reshape(count, rows, wide)
        total = total_ref[:, :, :, lanes]
        if lanes.start == 0:
            near = total[:, :, 0, :] + first[room:].reshape(count, rows, wide)
            far = total[:, :, cols - 1, :] + last[:room].reshape(count, rows, wide)
            strips = jnp.concatenate([left, near, far, right], axis=1)
            strips_ref[...] = strips
            early = end_state([strips[frame] for frame in range(count)], pole_ref, lanes)
            end_ref[at : at + rows] = early[:rows].astype(end_ref.dtype)
            end_ref[at + rows :] = early[3 * rows :].astype(end_ref.dtype)
            continue
        col = lax.broadcasted_iota(jnp.int32, drive_ref.shape, 2)
        total += jnp.where(col == 0, first[room:].reshape(count, rows, 1, wide), 0.0)
        total += jnp.where(col == cols - 1, last[:room].reshape(count, rows, 1, wide), 0.0)
        drive_ref[...] = total
        state = end_state([total[frame] for frame in range(count)], pole_ref, lanes)
        col = lax.broadcasted_iota(jnp.int32, state.shape, 1)
        state = jnp.where(col == 1, early[rows : 2 * rows].reshape(rows, 1, wide), state)
        border = early[2 * rows : 3 * rows].reshape(rows, 1, wide)
        state = jnp.where(col == cols - 2, border, state)
        end_ref[:size] = state.reshape(size, wide).astype(end_ref.dtype)
        beside = jnp.concatenate([left, right], axis=1)
        beside_ref[...] = beside
        state = end_state([beside[frame] for frame in range(count)], pole_ref, lanes)
        end_ref[size:at] = state.astype(end_ref.dtype)


def spread(block, cols, count, of_lanes):
    _, lanes, inset = block
    value = of_lanes(lanes)
    if inset is None:
        return value
    other, columns = inset
    value, instead = jnp.broadcast_arrays(value, of_lanes(other))
    shape = (count, value.shape[1])
    col = lax.rem(lax.broadcasted_iota(jnp.int32, shape, 0), cols)
    return jnp.where((col == columns[0]) | (col == columns[1]), instead, value)


def entry_kernel(frames, cols, block, ends_ref, pole_ref, out_ref):
    rate = rate_of(pole_ref)
    count = ends_ref.shape[1]
    carried = spread(block, cols, count, lambda lanes: jnp.exp(frames * rate[:, lanes]))
    entry = jnp.zeros(ends_ref.shape[1:], jnp.float32)
    out_ref[0] = entry.astype(out_ref.dtype)
    for index in range(ends_ref.shape[0] - 1):
        entry = carried * entry + ends_ref[index].astype(jnp.float32)
        out_ref[index + 1] = entry.astype(out_ref.dtype)


def exchange(pieces, pole, frames, cols):
    groups = lax.axis_size("tm")
    arrivals = []
    for end, blocks in pieces:
        entries = []
        for block in blocks:
            shares = end[block[0]].reshape(groups, -1, end.shape[1])
            assert block[2] is None or shares.shape[1] % cols == 0
            shares = lax.all_to_all(shares, "tm", 0, 0)
            kernel = functools.partial(entry_kernel, frames, cols, block)
            entry = call(kernel, of(shares.shape, end.dtype), shares, pole)
            entries.append(lax.all_to_all(entry, "tm", 0, 0).reshape(-1, end.shape[1]))
        arrivals.append((jnp.concatenate(entries, axis=0),))
    return arrivals


def pick(values):
    group = lax.axis_index("tm")
    picked = values[-1]
    for index, value in enumerate(values[:-1]):
        picked = jnp.where(group == index, value, picked)
    return picked


def on_core(first, second):
    return jnp.where(lax.axis_index("sx") == 0, first, second)


def weigh(one, by_one, other, by_other):
    return by_one * one.astype(jnp.float32) + by_other * other.astype(jnp.float32)


def relay_kernel(frames, cols, blocks, end_ref, got_ref, pole_ref, out_ref):
    rate = rate_of(pole_ref)
    carried, twice = jnp.exp(frames * rate), jnp.exp(2 * frames * rate)
    none, same = jnp.zeros_like(rate), jnp.ones_like(rate)
    own = on_core(pick([carried, same, same, same]), pick([same, same, same, none]))
    got = on_core(pick([same, carried, carried, carried]), pick([none, none, twice, same]))
    for block in blocks:
        rows = block[0]
        count = rows.stop - rows.start
        by_own = spread(block, cols, count, lambda lanes: own[:, lanes])
        by_got = spread(block, cols, count, lambda lanes: got[:, lanes])
        out_ref[rows] = weigh(end_ref[rows], by_own, got_ref[rows], by_got).astype(out_ref.dtype)


def exchange_four(pieces, pole, frames, cols):
    def along(pairs, core):
        return [(2 * source + core, 2 * target + core) for source, target in pairs]

    axes = ("tm", "sx")
    down = [(0, 2), (1, 3)]
    first_round = along([(0, 1), (1, 0), (2, 3)], 0) + along(down, 1)
    second_round = along(down, 0) + along([(0, 1), (2, 3), (3, 2)], 1)
    arrivals = []
    for end, blocks in pieces:
        got = lax.ppermute(end, axes, first_round)
        kernel = functools.partial(relay_kernel, frames, cols, blocks)
        relayed = call(kernel, of(end.shape, end.dtype), end, got, pole)
        arrivals.append((got, lax.ppermute(relayed, axes, second_round)))
    return arrivals


class Mix:
    def __init__(self, lanes, count, pole_ref, scale_ref):
        self.rate = rate_of(pole_ref)[:, lanes]
        self.scale = scale_ref[:, lanes]
        self.count = count

    def entry(self, arrived_refs, rows):
        parts = [ref[rows].astype(jnp.float32) for ref in arrived_refs]
        if len(parts) == 1:
            return parts[0]
        carried = jnp.exp(self.count * self.rate)
        none, same = jnp.zeros_like(self.rate), jnp.ones_like(self.rate)
        early = on_core(pick([none, same, none, same]), pick([none, none, carried, carried]))
        late = on_core(pick([none, none, same, carried]), pick([none, same, same, same]))
        return weigh(parts[0], early, parts[1], late)

    def __call__(self, drives, entry, start):
        decay = jnp.exp(self.rate)
        reach = jnp.exp((self.count * lax.axis_index("tm")).astype(jnp.float32) * self.rate)
        state = reach * start + entry.reshape(start.shape)
        for drive in drives:
            state = decay * state + drive
            yield jax.nn.gelu(self.scale * state)


def no_border(cells, axis):
    col = lax.broadcasted_iota(jnp.int32, cells.shape, axis)
    return jnp.where((col == 0) | (col == cells.shape[axis] - 1), 0.0, cells)


def put_back(late, early, axis):
    cols = late.shape[axis]
    col = lax.broadcasted_iota(jnp.int32, late.shape, axis)
    late = jnp.where(col == 1, pltpu.roll(early, 1, axis), late)
    return jnp.where(col == cols - 2, pltpu.roll(early, cols - 1, axis), late)


def mixed_kernel(lanes, rounds, *refs):
    drive_ref, start_ref, pole_ref, scale_ref, *arrived_refs, lhs_ref = refs
    early_refs, late_refs = arrived_refs[:rounds], arrived_refs[rounds:]
    count, rows, cols, _ = drive_ref.shape
    wide = lanes.stop - lanes.start
    size = rows * cols
    stride = lhs_ref.shape[0] // count
    room = (stride - size) // 2
    mix = Mix(lanes, count, pole_ref, scale_ref)
    first = lanes.start == 0
    held = lanes if first else slice(None)
    block = 8
    if first:
        for frame in range(count):
            put_row(lhs_ref, frame * stride + room, size, jnp.zeros((cols, wide), lhs_ref.dtype))
    for row in range(0, rows, block):
        here = slice(row, row + block)
        drives = [drive_ref[frame, here, :, held] for frame in range(count)]
        cells = slice(row * cols, (row + block) * cols)
        entry = mix.entry(early_refs, cells).reshape(block, cols, wide)
        if not first:
            entry = put_back(mix.entry(late_refs, cells).reshape(entry.shape), entry, 1)
        for frame, tile in enumerate(mix(drives, entry, start_ref[here, :, lanes])):
            if first:
                tile = no_border(tile, 1)
            tile = tile.reshape(block * cols, wide).astype(lhs_ref.dtype)
            put_cells(lhs_ref, frame * stride + room, size, cols, row * cols, tile)


def strip_start_kernel(start_ref, sides_ref, out_ref):
    rows, cols, _ = start_ref.shape
    start = start_ref[...]
    out_ref[:rows] = sides_ref[:rows]
    out_ref[rows : 2 * rows] = start[:, 0, :]
    out_ref[2 * rows : 3 * rows] = start[:, cols - 1, :]
    out_ref[3 * rows :] = sides_ref[rows:]


def inside(slot):
    chip, chips = lax.axis_index("sy"), lax.axis_size("sy")
    return {0: (chip > 0).astype(jnp.float32), 3: (chip < chips - 1).astype(jnp.float32)}.get(slot, 1.0)


def give_kernel(parts, rounds, *refs):
    total_ref, drive_ref, beside_ref, strips_ref, *refs = refs
    start_ref, strip_start_ref, pole_ref, scale_ref, *arrived_refs, give_ref = refs
    early_refs, late_refs = arrived_refs[:rounds], arrived_refs[rounds:]
    count, rows, cols, wide = drive_ref.shape
    size = rows * cols
    inner = inner_row(rows)
    zero, one = is_core(0), is_core(1)
    early, late = (Mix(lanes, count, pole_ref, scale_ref) for lanes in parts)
    row = pl.ds(pl.multiple_of(inner * cols, cols), cols)
    which = lax.broadcasted_iota(jnp.int32, (cols, wide), 0)

    def near(at):
        return pl.ds(pl.multiple_of(at + jnp.where(inner == 0, 0, rows - cols), cols), cols)

    def end(cells):
        return zero * cells[cols - 1 :] + one * cells[:1]

    def rows_of(cells):
        table = jnp.zeros(which.shape, jnp.float32)
        for index, cell in cells:
            table = jnp.where(which == index, cell, table)
        return table

    entry = put_back(late.entry(late_refs, row), late.entry(early_refs, row), 0)
    drives = [drive_ref[frame, inner] for frame in range(count)]
    tile = late(drives, entry, start_ref[inner, :, parts[1]])
    drives = [total_ref[frame, inner, :, parts[0]] for frame in range(count)]
    first = early(drives, early.entry(early_refs, row), start_ref[inner, :, parts[0]])

    slots = [(0, 0), (1, 3)]
    entry = rows_of([(i, end(late.entry(late_refs, near(size + i * rows)))) for i, _ in slots])
    start = rows_of([(i, end(strip_start_ref[near(slot * rows), parts[1]])) for i, slot in slots])
    drives = [
        rows_of([(i, end(beside_ref[frame, near(i * rows)])) for i, _ in slots])
        for frame in range(count)
    ]
    beside = late(drives, entry, start)

    slots = [(2 + slot, slot) for slot in range(4)]
    grid = early.entry(late_refs, row)
    at = size + 2 * rows
    entry = rows_of(
        [
            (2, end(early.entry(late_refs, near(at)))),
            (3, grid[1:2]),
            (4, grid[cols - 2 : cols - 1]),
            (5, end(early.entry(late_refs, near(at + rows)))),
        ]
    )
    start = rows_of([(i, end(strip_start_ref[near(slot * rows), parts[0]])) for i, slot in slots])
    drives = [
        rows_of([(i, end(strips_ref[frame, near(slot * rows)])) for i, slot in slots])
        for frame in range(count)
    ]
    strips = early(drives, entry, start)
    for frame, cells in enumerate(zip(tile, first, beside, strips)):
        give_ref[frame, :cols] = cells[0].astype(give_ref.dtype)
        ends = jnp.where(which < 2, cells[2], cells[3])
        ends = jnp.where((which == 0) | (which == 2), inside(0) * ends, ends)
        ends = jnp.where((which == 1) | (which == 5), inside(3) * ends, ends)
        give_ref[frame, cols : 2 * cols] = ends.astype(give_ref.dtype)
        give_ref[frame, 2 * cols :] = no_border(cells[1], 0).astype(give_ref.dtype)


def late_kernel(parts, rounds, *refs):
    beside_ref, strips_ref, strip_start_ref, pole_ref, scale_ref, *refs = refs
    *late_refs, beside_out_ref, strips_out_ref = refs
    count, room, wide = beside_ref.shape
    rows = room // 2
    size = late_refs[0].shape[0] - 4 * rows
    cols = size // rows
    early, late = (Mix(lanes, count, pole_ref, scale_ref) for lanes in parts)

    def column(cells, index):
        return cells[index * rows : (index + 1) * rows]

    starts = [strip_start_ref[slot * rows : (slot + 1) * rows, parts[1]] for slot in (0, 3)]
    entry = late.entry(late_refs, slice(size, size + 2 * rows))
    drives = [beside_ref[frame] for frame in range(count)]
    beside = late(drives, entry, jnp.concatenate(starts, axis=0))
    grid = early.entry(late_refs, slice(0, size)).reshape(rows, cols, wide)
    sides = early.entry(late_refs, slice(size + 2 * rows, size + 4 * rows))
    entry = [sides[:rows], grid[:, 1, :], grid[:, cols - 2, :], sides[rows:]]
    drives = [strips_ref[frame] for frame in range(count)]
    strips = early(drives, jnp.concatenate(entry, axis=0), strip_start_ref[:, parts[0]])
    for frame, (sides, strip) in enumerate(zip(beside, strips)):
        sides = [column(sides, 0) * inside(0), column(sides, 1) * inside(3)]
        strip = [column(strip, slot) * inside(slot) for slot in range(4)]
        beside_out_ref[frame] = jnp.concatenate(sides, axis=0).astype(beside_out_ref.dtype)
        strips_out_ref[frame] = jnp.concatenate(strip, axis=0).astype(strips_out_ref.dtype)


def put_columns_taps(lhs_ref, slots, columns, ends):
    rows = columns.shape[0] // len(slots)
    columns, ends = columns.astype(jnp.float32), ends.astype(jnp.float32)
    for index, at in enumerate(slots):
        column, end = columns[index * rows : (index + 1) * rows], ends[index : index + 1]
        lhs_ref[at : at + rows] = row_taps(column, end, end).astype(lhs_ref.dtype)


def tile_sum(tile, inputs, lanes, room, lhs_ref, weight_ref):
    count, rows, cols, wide = tile
    size = rows * cols

    def beside(cells):
        return cells.reshape(rows, 1, wide) if room else 0.0

    for frame in range(count):
        at = frame * (size + 2 * room)
        end = at + room + size
        total = dot(lhs_ref[at + room : end], weight_ref, 1, lanes, inputs).reshape(tile[1:])
        first = dot(lhs_ref[at:end], weight_ref, 0, lanes, inputs)
        shifted = pltpu.roll(first[room:].reshape(tile[1:]), 1, 1)
        total += with_column(shifted, 0, beside(first[:room]))
        last = dot(lhs_ref[at + room : end + room], weight_ref, 2, lanes, inputs)
        shifted = pltpu.roll(last[:size].reshape(tile[1:]), cols - 1, 1)
        yield total + with_column(shifted, cols - 1, beside(last[size:]))


def strip_slots(count, rows, cols):
    room, given = count * rows, count * cols
    strips = [given, given + room, 2 * given + 2 * room, 2 * given + 3 * room]
    return strips, [0, given + 2 * room, 2 * given + 4 * room]


def strip_sum(tile, inputs, lanes, lhs_ref, weight_ref):
    count, rows, cols, wide = tile
    room, given = count * rows, count * cols
    strips, _ = strip_slots(count, rows, cols)
    first = dot(lhs_ref[: strips[1] + room], weight_ref, 0, lanes, inputs)
    middle = dot(lhs_ref[strips[1] : strips[2] + room], weight_ref, 1, lanes, inputs)
    last = dot(lhs_ref[strips[2] :], weight_ref, 2, lanes, inputs)
    col = lax.broadcasted_iota(jnp.int32, (count, cols, wide), 1)

    def row_of(cells):
        return cells.reshape(count, cols, wide)

    reached = row_of(middle[room : room + given])
    reached += jnp.where(col == 0, 0.0, pltpu.roll(row_of(first[:given]), 1, 1))
    reached += jnp.where(col == cols - 1, 0.0, pltpu.roll(row_of(last[2 * room :]), cols - 1, 1))
    columns = [
        (0, first[given : given + room] + middle[:room]),
        (1, first[given + room :]),
        (cols - 2, last[:room]),
        (cols - 1, middle[room + given :] + last[room : 2 * room]),
    ]
    return [(at, cells.reshape(count, rows, 1, wide)) for at, cells in columns], reached


def further_kernel(inputs, lanes, lhs_ref, weight_ref, out_ref):
    tiles = tile_sum(out_ref.shape, inputs, lanes, 0, lhs_ref, weight_ref)
    for frame, total in enumerate(tiles):
        out_ref[frame] = total


def result_kernel(
    parts, _, got_ref, beside_ref, strips_ref, weight_ref, *refs
):
    *before_refs, out_ref, lhs_ref, held_ref, strip_lhs_ref, sems = refs
    count, rows, cols, _ = held_ref.shape
    size = rows * cols
    stride = size + 2 * rows
    strips_at, given_at = strip_slots(count, rows, cols)
    for frame in range(count):
        at = frame * stride
        put_row(lhs_ref, at + rows, size, got_ref[frame, :cols])
        ends = got_ref[frame, cols : 2 * cols]
        put_columns_taps(lhs_ref, (at, at + rows + size), beside_ref[frame], ends)
        slots = [slot + frame * rows for slot in strips_at]
        put_columns_taps(strip_lhs_ref, slots, strips_ref[frame], ends.astype(jnp.float32)[2:])
        given = got_ref[frame, 2 * cols :].astype(jnp.float32)
        given = [is_core(1) * given, jnp.zeros_like(given), is_core(0) * given]
        given = jnp.concatenate(given, axis=1).astype(strip_lhs_ref.dtype)
        for at in given_at:
            strip_lhs_ref[at + frame * cols : at + (frame + 1) * cols] = given

    def store(frame, part):
        here = (frame, slice(None), slice(None), parts[part])
        return pltpu.make_async_copy(held_ref.at[here], out_ref.at[here], sems.at[frame, part])

    for part, lanes in enumerate(parts):
        tile = (count, rows, cols, lanes.stop - lanes.start)
        columns, reached = strip_sum(tile, parts[0], lanes, strip_lhs_ref, weight_ref)
        tiles = tile_sum(tile, parts[1], lanes, rows, lhs_ref, weight_ref)
        for frame, total in enumerate(tiles):
            total += before_refs[part][frame]
            total = add_columns(total, [(at, cells[frame]) for at, cells in columns])
            row = reached[frame][None]
            ends = total[:1] + is_core(1) * row, total[rows - 1 :] + is_core(0) * row
            total = jnp.concatenate([ends[0], total[1 : rows - 1], ends[1]], axis=0)
            held_ref[frame, :, :, lanes] = total.astype(held_ref.dtype)
            store(frame, part).start()
    for part in range(len(parts)):
        for frame in range(count):
            store(frame, part).wait()


def on_device(frames, input_weight, output_weight, pole_index, gelu_scale, start_state):
    count, rows, cols, channels = frames.shape
    size, room = rows * cols, count * rows
    wide = 3 * channels
    assert lax.axis_size("sx") == 2
    narrow = frames.dtype
    pole, scale = pole_index[None], gelu_scale[None]

    shapes = (
        of((count * cols + (2 * count + 1) * rows, channels), narrow),
        of((2 * count + 1, rows, channels), narrow),
    )
    edges = call(
        edges_kernel,
        shapes,
        frames,
        scratch=[pltpu.VMEM((count, channels // 128, size, 128), jnp.float32)],
        flops=EDGES_COST,
    )
    give, keep = call(
        start_edges_kernel,
        shapes,
        start_state,
        *edges,
        aliases={1: 0, 2: 1},
    )
    got, mine = trade_columns(give, keep, count * cols)
    taps = of((count * size, wide), narrow)
    parts = halves(channels)
    half = channels // 2
    inner = of((count, rows, cols, half), jnp.float32)
    *main, early, _ = call(
        main_kernel,
        (
            of(frames.shape, jnp.float32),
            of((2, room, channels), jnp.float32),
            of((size, half), narrow),
            taps,
        ),
        call(taps_kernel, taps, frames),
        got,
        input_weight,
        pole,
        aliases={0: 3},
        flops=18 * frames.size * channels,
    )
    mine, total, spill = lax.optimization_barrier((mine, *main))
    halo, sides = call(
        halo_kernel,
        (of((4 * room, wide), narrow), of((2 * rows, channels), jnp.float32)),
        mine,
        swap_cores(mine),
    )
    drive, beside, strips, late = call(
        drive_kernel,
        (
            inner,
            of((count, 2 * rows, half), jnp.float32),
            of((count, 4 * rows, half), jnp.float32),
            of((size + 4 * rows, half), narrow),
        ),
        halo,
        input_weight,
        total,
        spill,
        pole,
        flops=36 * room * channels * channels,
    )
    at = size + 2 * rows
    tile = slice(0, size)
    pieces = [
        (early, [(tile, parts[0], (parts[1], (0, cols - 1)))]),
        (
            late,
            [
                (tile, parts[1], (parts[0], (1, cols - 2))),
                (slice(size, at), parts[1], None),
                (slice(at, at + 2 * rows), parts[0], None),
            ],
        ),
    ]
    exchanged = exchange_four if lax.axis_size("tm") == 4 else exchange
    early, late = exchanged(pieces, pole, count, cols)
    rounds = len(early)

    mixing = (start_state, pole, scale)
    taps = of((count * size, 3 * half), narrow)
    lhs = call(functools.partial(mixed_kernel, parts[0], rounds), taps, total, *mixing, *early)
    strip_start = call(strip_start_kernel, of((4 * rows, channels), jnp.float32), start_state, sides)
    flops = 18 * inner.size * half
    first_sum, second_sum = (
        call(
            functools.partial(further_kernel, parts[0], lanes), inner, lhs, output_weight, flops=flops
        )
        for lanes in parts
    )
    *late, first_sum, second_sum = lax.optimization_barrier((*late, first_sum, second_sum))
    give = call(
        functools.partial(give_kernel, parts, rounds),
        of((count, 3 * cols, half), narrow),
        total,
        drive,
        beside,
        strips,
        start_state,
        strip_start,
        pole,
        scale,
        *early,
        *late,
    )
    beside, strips = call(
        functools.partial(late_kernel, parts, rounds),
        (of(beside.shape, narrow), of(strips.shape, narrow)),
        beside,
        strips,
        strip_start,
        pole,
        scale,
        *late,
    )
    taps = of((count * size + 2 * room, 3 * half), narrow)
    lhs = call(
        functools.partial(mixed_kernel, parts[1], rounds), taps, drive, *mixing, *early, *late
    )
    result, _ = call(
        functools.partial(result_kernel, parts),
        (of(frames.shape, narrow), taps),
        lhs,
        swap_cores(give),
        beside,
        strips,
        output_weight,
        first_sum,
        second_sum,
        out_specs=(HBM, WHOLE),
        aliases={0: 1},
        scratch=[
            pltpu.VMEM(frames.shape, narrow),
            pltpu.VMEM((4 * room + 3 * count * cols, 3 * half), narrow),
            pltpu.SemaphoreType.DMA((count, len(parts))),
        ],
        flops=2 * flops,
    )
    return result


def solution(mesh):
    return jax.shard_map(
        on_device,
        mesh=mesh,
        in_specs=(P("tm", "sx", "sy", None), P(), P(), P(), P(), P("sx", "sy", None)),
        out_specs=P("tm", "sx", "sy", None),
        check_vma=False,
    )
```

```python
import functools
import math

import jax
import jax.numpy as jnp
from jax import lax
from jax.experimental import pallas as pl
from jax.experimental.pallas import tpu as pltpu
from jax.sharding import PartitionSpec as P

NPOLES = 16
VMEM_LIMIT = 24 * 1024 * 1024
WHOLE = pl.BlockSpec(memory_space=pltpu.VMEM)
HBM = pl.BlockSpec(memory_space=pltpu.HBM)
EDGES_COST = 2_000_000_000


def call(kernel, out_shape, *args, scratch=(), flops=0, out_specs=None, aliases=None):
    outs = jax.tree.leaves(out_shape)
    moved = sum(leaf.size * leaf.dtype.itemsize for leaf in (*args, *outs))
    return pl.pallas_call(
        kernel,
        in_specs=[WHOLE] * len(args),
        out_specs=out_specs or jax.tree.map(lambda _: WHOLE, out_shape),
        out_shape=out_shape,
        scratch_shapes=scratch,
        input_output_aliases=aliases or {},
        compiler_params=pltpu.CompilerParams(vmem_limit_bytes=VMEM_LIMIT),
        cost_estimate=pl.CostEstimate(flops=flops, bytes_accessed=moved, transcendentals=0),
    )(*args)


def of(shape, dtype):
    return jax.ShapeDtypeStruct(shape, dtype)


def is_core(which):
    return (lax.axis_index("sx") == which).astype(jnp.float32)


def rate_of(pole_ref):
    pole = pole_ref[...].astype(jnp.float32)
    return -0.001 * jnp.exp(pole * (math.log(300.0) / (NPOLES - 1)))


def inner_row(rows):
    return jnp.where(lax.axis_index("sx") == 0, rows - 1, 0)


def swap_cores(array):
    return lax.ppermute(array, "sx", [(0, 1), (1, 0)])


def put_columns(index, left, right, give_ref, keep_ref):
    zero, one = is_core(0), is_core(1)
    count, rows, _ = keep_ref.shape
    at = give_ref.shape[0] - (count - index) * rows
    give_ref[at : at + rows] = (zero * left + one * right).astype(give_ref.dtype)
    keep_ref[index] = (zero * right + one * left).astype(keep_ref.dtype)


def edges_kernel(cells_ref, give_ref, keep_ref, wide_ref):
    count, rows, cols, channels = cells_ref.shape
    for frame in range(count):
        give_ref[frame * cols : (frame + 1) * cols] = cells_ref[frame, inner_row(rows)]
        tile = cells_ref[frame].reshape(rows * cols, channels).astype(jnp.float32)
        lanes = wide_ref.shape[-1]
        for part in range(channels // lanes):
            wide_ref[frame, part] = tile[:, part * lanes : (part + 1) * lanes]

        def column(col):
            parts = [
                wide_ref[frame, part, pl.ds(col, rows, stride=cols), :]
                for part in range(channels // lanes)
            ]
            return jnp.concatenate(parts, axis=1)

        for depth in range(2):
            left, right = column(depth), column(cols - 1 - depth)
            put_columns(2 * frame + depth, left, right, give_ref, keep_ref)


def start_edges_kernel(start_ref, _, __, give_ref, keep_ref):
    tile, cols = start_ref[...], start_ref.shape[1]
    index = keep_ref.shape[0] - 1
    put_columns(index, tile[:, 0, :], tile[:, cols - 1, :], give_ref, keep_ref)


def trade_columns(give, keep, at):
    chips = lax.axis_size("sy")
    got = swap_cores(give)
    pairs = [(chip, chips + chip + 1) for chip in range(chips - 1)]
    pairs += [(after, before) for before, after in pairs]
    columns = jnp.concatenate([keep, got[at:].reshape(keep.shape)], axis=1)
    return got, lax.ppermute(columns, ("sx", "sy"), pairs)


def put_cells(lhs_ref, at, size, cols, first, cells):
    count, channels = cells.shape
    upper, lower = min(count, size - cols - first), max(0, cols - first)
    here = at + first
    lhs_ref[here : here + count, channels : 2 * channels] = cells
    lhs_ref[here + cols : here + cols + upper, :channels] = cells[:upper]
    lhs_ref[here + lower - cols : here + count - cols, 2 * channels :] = cells[lower:]


def put_row(lhs_ref, at, size, row):
    cols, channels = row.shape
    row = row.astype(jnp.float32)
    last = slice(at + size - cols, at + size)
    lhs_ref[at : at + cols, :channels] = (is_core(1) * row).astype(lhs_ref.dtype)
    lhs_ref[last, 2 * channels :] = (is_core(0) * row).astype(lhs_ref.dtype)


def taps_kernel(cells_ref, lhs_ref):
    count, rows, cols, channels = cells_ref.shape
    size = rows * cols
    for frame in range(count):
        put_cells(lhs_ref, frame * size, size, cols, 0, cells_ref[frame].reshape(size, channels))


def row_taps(column, above, below):
    rows = column.shape[0]
    row = lax.broadcasted_iota(jnp.int32, column.shape, 0)
    up = jnp.where(row == 0, is_core(1) * above, pltpu.roll(column, 1, 0))
    down = jnp.where(row == rows - 1, is_core(0) * below, pltpu.roll(column, rows - 1, 0))
    return jnp.concatenate([up, column, down], axis=1)


SLAB = 8


def add_columns(cells, columns):
    rows, cols, wide = cells.shape
    col = lax.broadcasted_iota(jnp.int32, (rows, SLAB, wide), 1)

    def slab(start):
        total = 0.0
        for at, column in columns:
            if start <= at < start + SLAB:
                total = jnp.where(col == at - start, column, total)
        return cells[:, start : start + SLAB] + total

    middle = [cells[:, SLAB : cols - SLAB]] if cols > 2 * SLAB else []
    return jnp.concatenate([slab(0), *middle, slab(cols - SLAB)], axis=1)


def with_column(cells, at, column):
    rows, cols, wide = cells.shape
    start = 0 if at == 0 else cols - SLAB
    col = lax.broadcasted_iota(jnp.int32, (rows, SLAB, wide), 1)
    slab = jnp.where(col == at - start, column, cells[:, start : start + SLAB])
    if at == 0:
        return jnp.concatenate([slab, cells[:, SLAB:]], axis=1)
    return jnp.concatenate([cells[:, :start], slab], axis=1)


def halves(channels):
    return slice(0, channels // 2), slice(channels // 2, channels)


def end_state(frames, pole_ref, lanes):
    decay = jnp.exp(rate_of(pole_ref))[:, lanes]
    state = frames[0]
    for frame in frames[1:]:
        state = decay * state + frame
    return state


def dot(lhs, weight_ref, column, lanes, inputs=slice(None)):
    weight = weight_ref[:, column, inputs, lanes].reshape(lhs.shape[1], -1)
    return jnp.dot(lhs, weight, preferred_element_type=jnp.float32)


def main_kernel(_, got_ref, weight_ref, pole_ref, total_ref, spill_ref, end_ref, lhs_ref):
    count, rows, cols, _ = total_ref.shape
    size = rows * cols
    for frame in range(count):
        put_row(lhs_ref, frame * size, size, got_ref[frame * cols : (frame + 1) * cols])
    states = []
    for lanes in halves(weight_ref.shape[-1]):
        tile = (rows, cols, lanes.stop - lanes.start)
        col = lax.broadcasted_iota(jnp.int32, tile, 1)
        totals = []
        for frame in range(count):
            cells = lhs_ref[frame * size : (frame + 1) * size]
            here = slice(frame * rows, (frame + 1) * rows)
            total = dot(cells, weight_ref, 1, lanes).reshape(tile)
            first = dot(cells, weight_ref, 0, lanes).reshape(tile)
            spill_ref[1, here, lanes] = first[:, cols - 1, :]
            total += with_column(pltpu.roll(first, 1, 1), 0, 0.0)
            last = dot(cells, weight_ref, 2, lanes).reshape(tile)
            spill_ref[0, here, lanes] = last[:, 0, :]
            total += with_column(pltpu.roll(last, cols - 1, 1), cols - 1, 0.0)
            total_ref[frame, :, :, lanes] = total
            totals.append(total)
        states.append(end_state(totals, pole_ref, lanes))
    state = jnp.where(col == 0, pltpu.roll(states[1], cols - 1, 1), states[0])
    state = jnp.where(col == cols - 1, pltpu.roll(states[1], 1, 1), state)
    end_ref[...] = state.reshape(end_ref.shape).astype(end_ref.dtype)


def halo_kernel(mine_ref, theirs_ref, lhs_ref, start_ref):
    rows = mine_ref.shape[1] // 2
    count = mine_ref.shape[0] // 2
    room = count * rows
    zero, one = is_core(0), is_core(1)
    core = lax.axis_index("sx")
    slots = ((1, 0), (2, 3))
    for frame in range(count):
        for depth in range(2):
            own = mine_ref[2 * frame + depth].astype(jnp.float32)
            other = theirs_ref[2 * frame + depth].astype(jnp.float32)
            own = row_taps(own[rows:], own[rows - 1 : rows], own[:1])
            other = row_taps(other[:rows], other[2 * rows - 1 :], other[rows : rows + 1])
            for swapped, taps in enumerate((own, other)):
                slot = jnp.where(core == swapped, slots[1][depth], slots[0][depth])
                at = pl.multiple_of(slot * room + frame * rows, rows)
                lhs_ref[pl.ds(at, rows)] = taps.astype(lhs_ref.dtype)
    own = mine_ref[2 * count, rows:].astype(jnp.float32)
    other = theirs_ref[2 * count, :rows].astype(jnp.float32)
    start_ref[:rows] = zero * other + one * own
    start_ref[rows:] = zero * own + one * other


def drive_kernel(
    lhs_ref, weight_ref, total_ref, spill_ref, pole_ref, drive_ref, beside_ref, strips_ref, end_ref
):
    count, rows, cols, wide = drive_ref.shape
    room, size = count * rows, rows * cols
    at = size + 2 * rows
    early = None
    for lanes in halves(weight_ref.shape[-1]):
        first = dot(lhs_ref[: 2 * room], weight_ref, 0, lanes)
        middle = dot(lhs_ref[room : 3 * room], weight_ref, 1, lanes)
        last = dot(lhs_ref[2 * room :], weight_ref, 2, lanes)
        left = (spill_ref[0, :, lanes] + first[:room] + middle[:room]).reshape(count, rows, wide)
        right = (spill_ref[1, :, lanes] + middle[room:] + last[room:]).reshape(count, rows, wide)
        total = total_ref[:, :, :, lanes]
        if lanes.start == 0:
            near = total[:, :, 0, :] + first[room:].reshape(count, rows, wide)
            far = total[:, :, cols - 1, :] + last[:room].reshape(count, rows, wide)
            strips = jnp.concatenate([left, near, far, right], axis=1)
            strips_ref[...] = strips
            early = end_state([strips[frame] for frame in range(count)], pole_ref, lanes)
            end_ref[at : at + rows] = early[:rows].astype(end_ref.dtype)
            end_ref[at + rows :] = early[3 * rows :].astype(end_ref.dtype)
            continue
        col = lax.broadcasted_iota(jnp.int32, drive_ref.shape, 2)
        total += jnp.where(col == 0, first[room:].reshape(count, rows, 1, wide), 0.0)
        total += jnp.where(col == cols - 1, last[:room].reshape(count, rows, 1, wide), 0.0)
        drive_ref[...] = total
        state = end_state([total[frame] for frame in range(count)], pole_ref, lanes)
        col = lax.broadcasted_iota(jnp.int32, state.shape, 1)
        state = jnp.where(col == 1, early[rows : 2 * rows].reshape(rows, 1, wide), state)
        border = early[2 * rows : 3 * rows].reshape(rows, 1, wide)
        state = jnp.where(col == cols - 2, border, state)
        end_ref[:size] = state.reshape(size, wide).astype(end_ref.dtype)
        beside = jnp.concatenate([left, right], axis=1)
        beside_ref[...] = beside
        state = end_state([beside[frame] for frame in range(count)], pole_ref, lanes)
        end_ref[size:at] = state.astype(end_ref.dtype)


def spread(block, cols, count, of_lanes):
    _, lanes, inset = block
    value = of_lanes(lanes)
    if inset is None:
        return value
    other, columns = inset
    value, instead = jnp.broadcast_arrays(value, of_lanes(other))
    shape = (count, value.shape[1])
    col = lax.rem(lax.broadcasted_iota(jnp.int32, shape, 0), cols)
    return jnp.where((col == columns[0]) | (col == columns[1]), instead, value)


def entry_kernel(frames, cols, block, ends_ref, pole_ref, out_ref):
    rate = rate_of(pole_ref)
    count = ends_ref.shape[1]
    carried = spread(block, cols, count, lambda lanes: jnp.exp(frames * rate[:, lanes]))
    entry = jnp.zeros(ends_ref.shape[1:], jnp.float32)
    out_ref[0] = entry.astype(out_ref.dtype)
    for index in range(ends_ref.shape[0] - 1):
        entry = carried * entry + ends_ref[index].astype(jnp.float32)
        out_ref[index + 1] = entry.astype(out_ref.dtype)


def exchange(pieces, pole, frames, cols):
    groups = lax.axis_size("tm")
    arrivals = []
    for end, blocks in pieces:
        entries = []
        for block in blocks:
            shares = end[block[0]].reshape(groups, -1, end.shape[1])
            assert block[2] is None or shares.shape[1] % cols == 0
            shares = lax.all_to_all(shares, "tm", 0, 0)
            kernel = functools.partial(entry_kernel, frames, cols, block)
            entry = call(kernel, of(shares.shape, end.dtype), shares, pole)
            entries.append(lax.all_to_all(entry, "tm", 0, 0).reshape(-1, end.shape[1]))
        arrivals.append((jnp.concatenate(entries, axis=0),))
    return arrivals


def pick(values):
    group = lax.axis_index("tm")
    picked = values[-1]
    for index, value in enumerate(values[:-1]):
        picked = jnp.where(group == index, value, picked)
    return picked


def on_core(first, second):
    return jnp.where(lax.axis_index("sx") == 0, first, second)


def weigh(one, by_one, other, by_other):
    return by_one * one.astype(jnp.float32) + by_other * other.astype(jnp.float32)


def relay_kernel(frames, cols, blocks, end_ref, got_ref, pole_ref, out_ref):
    rate = rate_of(pole_ref)
    carried, twice = jnp.exp(frames * rate), jnp.exp(2 * frames * rate)
    none, same = jnp.zeros_like(rate), jnp.ones_like(rate)
    own = on_core(pick([carried, same, same, same]), pick([same, same, same, none]))
    got = on_core(pick([same, carried, carried, carried]), pick([none, none, twice, same]))
    for block in blocks:
        rows = block[0]
        count = rows.stop - rows.start
        by_own = spread(block, cols, count, lambda lanes: own[:, lanes])
        by_got = spread(block, cols, count, lambda lanes: got[:, lanes])
        out_ref[rows] = weigh(end_ref[rows], by_own, got_ref[rows], by_got).astype(out_ref.dtype)


def exchange_four(pieces, pole, frames, cols):
    def along(pairs, core):
        return [(2 * source + core, 2 * target + core) for source, target in pairs]

    axes = ("tm", "sx")
    down = [(0, 2), (1, 3)]
    first_round = along([(0, 1), (1, 0), (2, 3)], 0) + along(down, 1)
    second_round = along(down, 0) + along([(0, 1), (2, 3), (3, 2)], 1)
    arrivals = []
    for end, blocks in pieces:
        got = lax.ppermute(end, axes, first_round)
        kernel = functools.partial(relay_kernel, frames, cols, blocks)
        relayed = call(kernel, of(end.shape, end.dtype), end, got, pole)
        arrivals.append((got, lax.ppermute(relayed, axes, second_round)))
    return arrivals


class Mix:
    def __init__(self, lanes, count, pole_ref, scale_ref):
        self.rate = rate_of(pole_ref)[:, lanes]
        self.scale = scale_ref[:, lanes]
        self.count = count

    def entry(self, arrived_refs, rows):
        parts = [ref[rows].astype(jnp.float32) for ref in arrived_refs]
        if len(parts) == 1:
            return parts[0]
        carried = jnp.exp(self.count * self.rate)
        none, same = jnp.zeros_like(self.rate), jnp.ones_like(self.rate)
        early = on_core(pick([none, same, none, same]), pick([none, none, carried, carried]))
        late = on_core(pick([none, none, same, carried]), pick([none, same, same, same]))
        return weigh(parts[0], early, parts[1], late)

    def __call__(self, drives, entry, start):
        decay = jnp.exp(self.rate)
        reach = jnp.exp((self.count * lax.axis_index("tm")).astype(jnp.float32) * self.rate)
        state = reach * start + entry.reshape(start.shape)
        for drive in drives:
            state = decay * state + drive
            yield jax.nn.gelu(self.scale * state)


def no_border(cells, axis):
    col = lax.broadcasted_iota(jnp.int32, cells.shape, axis)
    return jnp.where((col == 0) | (col == cells.shape[axis] - 1), 0.0, cells)


def put_back(late, early, axis):
    cols = late.shape[axis]
    col = lax.broadcasted_iota(jnp.int32, late.shape, axis)
    late = jnp.where(col == 1, pltpu.roll(early, 1, axis), late)
    return jnp.where(col == cols - 2, pltpu.roll(early, cols - 1, axis), late)


def mixed_kernel(lanes, rounds, *refs):
    drive_ref, start_ref, pole_ref, scale_ref, *arrived_refs, lhs_ref = refs
    early_refs, late_refs = arrived_refs[:rounds], arrived_refs[rounds:]
    count, rows, cols, _ = drive_ref.shape
    wide = lanes.stop - lanes.start
    size = rows * cols
    stride = lhs_ref.shape[0] // count
    room = (stride - size) // 2
    mix = Mix(lanes, count, pole_ref, scale_ref)
    first = lanes.start == 0
    held = lanes if first else slice(None)
    block = 8
    for row in range(0, rows, block):
        here = slice(row, row + block)
        drives = [drive_ref[frame, here, :, held] for frame in range(count)]
        cells = slice(row * cols, (row + block) * cols)
        entry = mix.entry(early_refs, cells).reshape(block, cols, wide)
        if not first:
            entry = put_back(mix.entry(late_refs, cells).reshape(entry.shape), entry, 1)
        for frame, tile in enumerate(mix(drives, entry, start_ref[here, :, lanes])):
            if first:
                tile = no_border(tile, 1)
            tile = tile.reshape(block * cols, wide).astype(lhs_ref.dtype)
            put_cells(lhs_ref, frame * stride + room, size, cols, row * cols, tile)


def middle_kernel(lanes, *refs):
    total_ref, start_ref, pole_ref, scale_ref, *arrived_refs, give_ref = refs
    count, rows, cols, _ = total_ref.shape
    mix = Mix(lanes, count, pole_ref, scale_ref)
    inner = inner_row(rows)
    drives = [total_ref[frame, inner, :, lanes] for frame in range(count)]
    entry = mix.entry(arrived_refs, pl.ds(pl.multiple_of(inner * cols, cols), cols))
    for frame, cells in enumerate(mix(drives, entry, start_ref[inner, :, lanes])):
        give_ref[frame] = no_border(cells, 0).astype(give_ref.dtype)


def strip_start_kernel(start_ref, sides_ref, out_ref):
    rows, cols, _ = start_ref.shape
    start = start_ref[...]
    out_ref[:rows] = sides_ref[:rows]
    out_ref[rows : 2 * rows] = start[:, 0, :]
    out_ref[2 * rows : 3 * rows] = start[:, cols - 1, :]
    out_ref[3 * rows :] = sides_ref[rows:]


def inside(slot):
    chip, chips = lax.axis_index("sy"), lax.axis_size("sy")
    return {0: (chip > 0).astype(jnp.float32), 3: (chip < chips - 1).astype(jnp.float32)}.get(slot, 1.0)


def give_kernel(parts, rounds, *refs):
    drive_ref, beside_ref, strips_ref, *refs = refs
    start_ref, strip_start_ref, pole_ref, scale_ref, *arrived_refs, give_ref = refs
    early_refs, late_refs = arrived_refs[:rounds], arrived_refs[rounds:]
    count, rows, cols, wide = drive_ref.shape
    size = rows * cols
    inner = inner_row(rows)
    zero, one = is_core(0), is_core(1)
    early, late = (Mix(lanes, count, pole_ref, scale_ref) for lanes in parts)
    row = pl.ds(pl.multiple_of(inner * cols, cols), cols)
    which = lax.broadcasted_iota(jnp.int32, (cols, wide), 0)

    def near(at):
        return pl.ds(pl.multiple_of(at + jnp.where(inner == 0, 0, rows - cols), cols), cols)

    def end(cells):
        return zero * cells[cols - 1 :] + one * cells[:1]

    def rows_of(cells):
        table = jnp.zeros(which.shape, jnp.float32)
        for index, cell in cells:
            table = jnp.where(which == index, cell, table)
        return table

    entry = put_back(late.entry(late_refs, row), late.entry(early_refs, row), 0)
    drives = [drive_ref[frame, inner] for frame in range(count)]
    tile = late(drives, entry, start_ref[inner, :, parts[1]])

    slots = [(0, 0), (1, 3)]
    entry = rows_of([(i, end(late.entry(late_refs, near(size + i * rows)))) for i, _ in slots])
    start = rows_of([(i, end(strip_start_ref[near(slot * rows), parts[1]])) for i, slot in slots])
    drives = [
        rows_of([(i, end(beside_ref[frame, near(i * rows)])) for i, _ in slots])
        for frame in range(count)
    ]
    beside = late(drives, entry, start)

    slots = [(2 + slot, slot) for slot in range(4)]
    grid = early.entry(late_refs, row)
    at = size + 2 * rows
    entry = rows_of(
        [
            (2, end(early.entry(late_refs, near(at)))),
            (3, grid[1:2]),
            (4, grid[cols - 2 : cols - 1]),
            (5, end(early.entry(late_refs, near(at + rows)))),
        ]
    )
    start = rows_of([(i, end(strip_start_ref[near(slot * rows), parts[0]])) for i, slot in slots])
    drives = [
        rows_of([(i, end(strips_ref[frame, near(slot * rows)])) for i, slot in slots])
        for frame in range(count)
    ]
    strips = early(drives, entry, start)
    for frame, cells in enumerate(zip(tile, beside, strips)):
        give_ref[frame, :cols] = cells[0].astype(give_ref.dtype)
        ends = jnp.where(which < 2, cells[1], cells[2])
        ends = jnp.where((which == 0) | (which == 2), inside(0) * ends, ends)
        ends = jnp.where((which == 1) | (which == 5), inside(3) * ends, ends)
        give_ref[frame, cols:] = ends.astype(give_ref.dtype)


def late_kernel(parts, rounds, *refs):
    beside_ref, strips_ref, strip_start_ref, pole_ref, scale_ref, *refs = refs
    *late_refs, beside_out_ref, strips_out_ref = refs
    count, room, wide = beside_ref.shape
    rows = room // 2
    size = late_refs[0].shape[0] - 4 * rows
    cols = size // rows
    early, late = (Mix(lanes, count, pole_ref, scale_ref) for lanes in parts)

    def column(cells, index):
        return cells[index * rows : (index + 1) * rows]

    starts = [strip_start_ref[slot * rows : (slot + 1) * rows, parts[1]] for slot in (0, 3)]
    entry = late.entry(late_refs, slice(size, size + 2 * rows))
    drives = [beside_ref[frame] for frame in range(count)]
    beside = late(drives, entry, jnp.concatenate(starts, axis=0))
    grid = early.entry(late_refs, slice(0, size)).reshape(rows, cols, wide)
    sides = early.entry(late_refs, slice(size + 2 * rows, size + 4 * rows))
    entry = [sides[:rows], grid[:, 1, :], grid[:, cols - 2, :], sides[rows:]]
    drives = [strips_ref[frame] for frame in range(count)]
    strips = early(drives, jnp.concatenate(entry, axis=0), strip_start_ref[:, parts[0]])
    for frame, (sides, strip) in enumerate(zip(beside, strips)):
        sides = [column(sides, 0) * inside(0), column(sides, 1) * inside(3)]
        strip = [column(strip, slot) * inside(slot) for slot in range(4)]
        beside_out_ref[frame] = jnp.concatenate(sides, axis=0).astype(beside_out_ref.dtype)
        strips_out_ref[frame] = jnp.concatenate(strip, axis=0).astype(strips_out_ref.dtype)


def put_columns_taps(lhs_ref, slots, columns, ends):
    rows = columns.shape[0] // len(slots)
    columns, ends = columns.astype(jnp.float32), ends.astype(jnp.float32)
    for index, at in enumerate(slots):
        column, end = columns[index * rows : (index + 1) * rows], ends[index : index + 1]
        lhs_ref[at : at + rows] = row_taps(column, end, end).astype(lhs_ref.dtype)


def tile_sum(tile, inputs, lanes, room, lhs_ref, weight_ref):
    count, rows, cols, wide = tile
    size = rows * cols

    def beside(cells):
        return cells.reshape(rows, 1, wide) if room else 0.0

    for frame in range(count):
        at = frame * (size + 2 * room)
        end = at + room + size
        total = dot(lhs_ref[at + room : end], weight_ref, 1, lanes, inputs).reshape(tile[1:])
        first = dot(lhs_ref[at:end], weight_ref, 0, lanes, inputs)
        shifted = pltpu.roll(first[room:].reshape(tile[1:]), 1, 1)
        total += with_column(shifted, 0, beside(first[:room]))
        last = dot(lhs_ref[at + room : end + room], weight_ref, 2, lanes, inputs)
        shifted = pltpu.roll(last[:size].reshape(tile[1:]), cols - 1, 1)
        yield total + with_column(shifted, cols - 1, beside(last[size:]))


def strip_sum(tile, inputs, lanes, lhs_ref, weight_ref):
    count, rows, cols, wide = tile
    room = count * rows
    first = dot(lhs_ref[: 2 * room], weight_ref, 0, lanes, inputs)
    middle = dot(lhs_ref[room : 3 * room], weight_ref, 1, lanes, inputs)
    last = dot(lhs_ref[2 * room :], weight_ref, 2, lanes, inputs)
    columns = [
        (0, first[:room] + middle[:room]),
        (1, first[room:]),
        (cols - 2, last[:room]),
        (cols - 1, middle[room:] + last[room:]),
    ]
    return [(at, cells.reshape(count, rows, 1, wide)) for at, cells in columns]


def opening_kernel(inputs, lanes, _, got_ref, weight_ref, out_ref, lhs_ref):
    count, rows, cols, _ = out_ref.shape
    size = rows * cols
    for frame in range(count):
        put_row(lhs_ref, frame * size, size, got_ref[frame])
    further_kernel(inputs, lanes, lhs_ref, weight_ref, out_ref)


def further_kernel(inputs, lanes, lhs_ref, weight_ref, out_ref):
    tiles = tile_sum(out_ref.shape, inputs, lanes, 0, lhs_ref, weight_ref)
    for frame, total in enumerate(tiles):
        out_ref[frame] = total


def result_kernel(
    parts, _, got_ref, beside_ref, strips_ref, weight_ref, *refs
):
    *before_refs, out_ref, lhs_ref, held_ref, strip_lhs_ref, sems = refs
    count, rows, cols, _ = held_ref.shape
    size, room = rows * cols, count * rows
    stride = size + 2 * rows
    for frame in range(count):
        at = frame * stride
        put_row(lhs_ref, at + rows, size, got_ref[frame, :cols])
        ends = got_ref[frame, cols:]
        put_columns_taps(lhs_ref, (at, at + rows + size), beside_ref[frame], ends)
        slots = [slot * room + frame * rows for slot in range(4)]
        put_columns_taps(strip_lhs_ref, slots, strips_ref[frame], ends.astype(jnp.float32)[2:])

    def store(frame, part):
        here = (frame, slice(None), slice(None), parts[part])
        return pltpu.make_async_copy(held_ref.at[here], out_ref.at[here], sems.at[frame, part])

    for part, lanes in enumerate(parts):
        tile = (count, rows, cols, lanes.stop - lanes.start)
        columns = strip_sum(tile, parts[0], lanes, strip_lhs_ref, weight_ref)
        tiles = tile_sum(tile, parts[1], lanes, rows, lhs_ref, weight_ref)
        for frame, total in enumerate(tiles):
            total += before_refs[part][frame]
            total = add_columns(total, [(at, cells[frame]) for at, cells in columns])
            held_ref[frame, :, :, lanes] = total.astype(held_ref.dtype)
            store(frame, part).start()
    for part in range(len(parts)):
        for frame in range(count):
            store(frame, part).wait()


def on_device(frames, input_weight, output_weight, pole_index, gelu_scale, start_state):
    count, rows, cols, channels = frames.shape
    size, room = rows * cols, count * rows
    wide = 3 * channels
    assert lax.axis_size("sx") == 2
    narrow = frames.dtype
    pole, scale = pole_index[None], gelu_scale[None]

    shapes = (
        of((count * cols + (2 * count + 1) * rows, channels), narrow),
        of((2 * count + 1, rows, channels), narrow),
    )
    edges = call(
        edges_kernel,
        shapes,
        frames,
        scratch=[pltpu.VMEM((count, channels // 128, size, 128), jnp.float32)],
        flops=EDGES_COST,
    )
    give, keep = call(
        start_edges_kernel,
        shapes,
        start_state,
        *edges,
        aliases={1: 0, 2: 1},
    )
    got, mine = trade_columns(give, keep, count * cols)
    taps = of((count * size, wide), narrow)
    parts = halves(channels)
    half = channels // 2
    inner = of((count, rows, cols, half), jnp.float32)
    *main, early, _ = call(
        main_kernel,
        (
            of(frames.shape, jnp.float32),
            of((2, room, channels), jnp.float32),
            of((size, half), narrow),
            taps,
        ),
        call(taps_kernel, taps, frames),
        got,
        input_weight,
        pole,
        aliases={0: 3},
        flops=18 * frames.size * channels,
    )
    mine, total, spill = lax.optimization_barrier((mine, *main))
    halo, sides = call(
        halo_kernel,
        (of((4 * room, wide), narrow), of((2 * rows, channels), jnp.float32)),
        mine,
        swap_cores(mine),
    )
    drive, beside, strips, late = call(
        drive_kernel,
        (
            inner,
            of((count, 2 * rows, half), jnp.float32),
            of((count, 4 * rows, half), jnp.float32),
            of((size + 4 * rows, half), narrow),
        ),
        halo,
        input_weight,
        total,
        spill,
        pole,
        flops=36 * room * channels * channels,
    )
    at = size + 2 * rows
    tile = slice(0, size)
    pieces = [
        (early, [(tile, parts[0], (parts[1], (0, cols - 1)))]),
        (
            late,
            [
                (tile, parts[1], (parts[0], (1, cols - 2))),
                (slice(size, at), parts[1], None),
                (slice(at, at + 2 * rows), parts[0], None),
            ],
        ),
    ]
    exchanged = exchange_four if lax.axis_size("tm") == 4 else exchange
    early, late = exchanged(pieces, pole, count, cols)
    rounds = len(early)

    mixing = (start_state, pole, scale)
    taps = of((count * size, 3 * half), narrow)
    give = call(
        functools.partial(middle_kernel, parts[0]),
        of((count, cols, half), narrow),
        total,
        *mixing,
        *early,
    )
    lhs = call(functools.partial(mixed_kernel, parts[0], rounds), taps, total, *mixing, *early)
    strip_start = call(strip_start_kernel, of((4 * rows, channels), jnp.float32), start_state, sides)
    flops = 18 * inner.size * half
    first_sum, lhs = call(
        functools.partial(opening_kernel, parts[0], parts[0]),
        (inner, taps),
        lhs,
        swap_cores(give),
        output_weight,
        aliases={0: 1},
        flops=flops,
    )
    second_sum = call(
        functools.partial(further_kernel, parts[0], parts[1]),
        inner,
        lhs,
        output_weight,
        flops=flops,
    )
    *late, first_sum, second_sum = lax.optimization_barrier((*late, first_sum, second_sum))
    give = call(
        functools.partial(give_kernel, parts, rounds),
        of((count, 2 * cols, half), narrow),
        drive,
        beside,
        strips,
        start_state,
        strip_start,
        pole,
        scale,
        *early,
        *late,
    )
    beside, strips = call(
        functools.partial(late_kernel, parts, rounds),
        (of(beside.shape, narrow), of(strips.shape, narrow)),
        beside,
        strips,
        strip_start,
        pole,
        scale,
        *late,
    )
    taps = of((count * size + 2 * room, 3 * half), narrow)
    lhs = call(
        functools.partial(mixed_kernel, parts[1], rounds), taps, drive, *mixing, *early, *late
    )
    result, _ = call(
        functools.partial(result_kernel, parts),
        (of(frames.shape, narrow), taps),
        lhs,
        swap_cores(give),
        beside,
        strips,
        output_weight,
        first_sum,
        second_sum,
        out_specs=(HBM, WHOLE),
        aliases={0: 1},
        scratch=[
            pltpu.VMEM(frames.shape, narrow),
            pltpu.VMEM((4 * room, 3 * half), narrow),
            pltpu.SemaphoreType.DMA((count, len(parts))),
        ],
        flops=2 * flops,
    )
    return result


def solution(mesh):
    return jax.shard_map(
        on_device,
        mesh=mesh,
        in_specs=(P("tm", "sx", "sy", None), P(), P(), P(), P(), P("sx", "sy", None)),
        out_specs=P("tm", "sx", "sy", None),
        check_vma=False,
    )
```

```python
import functools
import math

import jax
import jax.numpy as jnp
from jax import lax
from jax.experimental import pallas as pl
from jax.experimental.pallas import tpu as pltpu
from jax.sharding import PartitionSpec as P

NPOLES = 16
VMEM_LIMIT = 24 * 1024 * 1024
WHOLE = pl.BlockSpec(memory_space=pltpu.VMEM)
HBM = pl.BlockSpec(memory_space=pltpu.HBM)
EDGES_COST = 2_000_000_000


def call(kernel, out_shape, *args, scratch=(), flops=0, out_specs=None, aliases=None):
    outs = jax.tree.leaves(out_shape)
    moved = sum(leaf.size * leaf.dtype.itemsize for leaf in (*args, *outs))
    return pl.pallas_call(
        kernel,
        in_specs=[WHOLE] * len(args),
        out_specs=out_specs or jax.tree.map(lambda _: WHOLE, out_shape),
        out_shape=out_shape,
        scratch_shapes=scratch,
        input_output_aliases=aliases or {},
        compiler_params=pltpu.CompilerParams(vmem_limit_bytes=VMEM_LIMIT),
        cost_estimate=pl.CostEstimate(flops=flops, bytes_accessed=moved, transcendentals=0),
    )(*args)


def of(shape, dtype):
    return jax.ShapeDtypeStruct(shape, dtype)


def is_core(which):
    return (lax.axis_index("sx") == which).astype(jnp.float32)


def rate_of(pole_ref):
    pole = pole_ref[...].astype(jnp.float32)
    return -0.001 * jnp.exp(pole * (math.log(300.0) / (NPOLES - 1)))


def inner_row(rows):
    return jnp.where(lax.axis_index("sx") == 0, rows - 1, 0)


def swap_cores(array):
    return lax.ppermute(array, "sx", [(0, 1), (1, 0)])


def put_columns(index, left, right, give_ref, keep_ref):
    zero, one = is_core(0), is_core(1)
    count, rows, _ = keep_ref.shape
    at = give_ref.shape[0] - (count - index) * rows
    give_ref[at : at + rows] = (zero * left + one * right).astype(give_ref.dtype)
    keep_ref[index] = (zero * right + one * left).astype(keep_ref.dtype)


def edges_kernel(cells_ref, give_ref, keep_ref, wide_ref):
    count, rows, cols, channels = cells_ref.shape
    for frame in range(count):
        give_ref[frame * cols : (frame + 1) * cols] = cells_ref[frame, inner_row(rows)]
        tile = cells_ref[frame].reshape(rows * cols, channels).astype(jnp.float32)
        lanes = wide_ref.shape[-1]
        for part in range(channels // lanes):
            wide_ref[frame, part] = tile[:, part * lanes : (part + 1) * lanes]

        def column(col):
            parts = [
                wide_ref[frame, part, pl.ds(col, rows, stride=cols), :]
                for part in range(channels // lanes)
            ]
            return jnp.concatenate(parts, axis=1)

        for depth in range(2):
            left, right = column(depth), column(cols - 1 - depth)
            put_columns(2 * frame + depth, left, right, give_ref, keep_ref)


def start_edges_kernel(start_ref, _, __, give_ref, keep_ref):
    tile, cols = start_ref[...], start_ref.shape[1]
    index = keep_ref.shape[0] - 1
    put_columns(index, tile[:, 0, :], tile[:, cols - 1, :], give_ref, keep_ref)


def trade_columns(give, keep, at):
    chips = lax.axis_size("sy")
    got = swap_cores(give)
    pairs = [(chip, chips + chip + 1) for chip in range(chips - 1)]
    pairs += [(after, before) for before, after in pairs]
    columns = jnp.concatenate([keep, got[at:].reshape(keep.shape)], axis=1)
    return got, lax.ppermute(columns, ("sx", "sy"), pairs)


def put_cells(lhs_ref, at, size, cols, first, cells):
    count, channels = cells.shape
    upper, lower = min(count, size - cols - first), max(0, cols - first)
    here = at + first
    lhs_ref[here : here + count, channels : 2 * channels] = cells
    lhs_ref[here + cols : here + cols + upper, :channels] = cells[:upper]
    lhs_ref[here + lower - cols : here + count - cols, 2 * channels :] = cells[lower:]


def put_row(lhs_ref, at, size, row):
    cols, channels = row.shape
    row = row.astype(jnp.float32)
    last = slice(at + size - cols, at + size)
    lhs_ref[at : at + cols, :channels] = (is_core(1) * row).astype(lhs_ref.dtype)
    lhs_ref[last, 2 * channels :] = (is_core(0) * row).astype(lhs_ref.dtype)


def taps_kernel(cells_ref, lhs_ref):
    count, rows, cols, channels = cells_ref.shape
    size = rows * cols
    for frame in range(count):
        put_cells(lhs_ref, frame * size, size, cols, 0, cells_ref[frame].reshape(size, channels))


def row_taps(column, above, below):
    rows = column.shape[0]
    row = lax.broadcasted_iota(jnp.int32, column.shape, 0)
    up = jnp.where(row == 0, is_core(1) * above, pltpu.roll(column, 1, 0))
    down = jnp.where(row == rows - 1, is_core(0) * below, pltpu.roll(column, rows - 1, 0))
    return jnp.concatenate([up, column, down], axis=1)


SLAB = 8


def halves(channels):
    return slice(0, channels // 2), slice(channels // 2, channels)


def end_state(frames, pole_ref, lanes):
    decay = jnp.exp(rate_of(pole_ref))[:, lanes]
    state = frames[0]
    for frame in frames[1:]:
        state = decay * state + frame
    return state


def dot(lhs, weight_ref, column, lanes, inputs=slice(None)):
    weight = weight_ref[:, column, inputs, lanes].reshape(lhs.shape[1], -1)
    return jnp.dot(lhs, weight, preferred_element_type=jnp.float32)


def main_kernel(_, got_ref, weight_ref, pole_ref, total_ref, spill_ref, end_ref, lhs_ref):
    count, rows, cols, _ = total_ref.shape
    size = rows * cols
    for frame in range(count):
        put_row(lhs_ref, frame * size, size, got_ref[frame * cols : (frame + 1) * cols])
    states = []
    for lanes in halves(weight_ref.shape[-1]):
        tile = (rows, cols, lanes.stop - lanes.start)
        col = lax.broadcasted_iota(jnp.int32, tile, 1)
        totals = []
        for frame in range(count):
            cells = lhs_ref[frame * size : (frame + 1) * size]
            here = slice(frame * rows, (frame + 1) * rows)
            total = dot(cells, weight_ref, 1, lanes).reshape(tile)
            first = dot(cells, weight_ref, 0, lanes).reshape(tile)
            spill_ref[1, here, lanes] = first[:, cols - 1, :]
            total += jnp.where(col == 0, 0.0, pltpu.roll(first, 1, 1))
            last = dot(cells, weight_ref, 2, lanes).reshape(tile)
            spill_ref[0, here, lanes] = last[:, 0, :]
            total += jnp.where(col == cols - 1, 0.0, pltpu.roll(last, cols - 1, 1))
            total_ref[frame, :, :, lanes] = total
            totals.append(total)
        states.append(end_state(totals, pole_ref, lanes))
    state, other = states
    col = lax.broadcasted_iota(jnp.int32, (rows, SLAB, state.shape[2]), 1)
    last = slice(cols - SLAB, cols)
    left = jnp.where(col == 0, pltpu.roll(other[:, :SLAB], SLAB - 1, 1), state[:, :SLAB])
    right = jnp.where(col == SLAB - 1, pltpu.roll(other[:, last], 1, 1), state[:, last])
    middle = [state[:, SLAB : cols - SLAB]] if cols > 2 * SLAB else []
    state = jnp.concatenate([left, *middle, right], axis=1)
    end_ref[...] = state.reshape(end_ref.shape).astype(end_ref.dtype)


def halo_kernel(mine_ref, theirs_ref, lhs_ref, start_ref):
    rows = mine_ref.shape[1] // 2
    count = mine_ref.shape[0] // 2
    room = count * rows
    zero, one = is_core(0), is_core(1)
    core = lax.axis_index("sx")
    slots = ((1, 0), (2, 3))
    for frame in range(count):
        for depth in range(2):
            own = mine_ref[2 * frame + depth].astype(jnp.float32)
            other = theirs_ref[2 * frame + depth].astype(jnp.float32)
            own = row_taps(own[rows:], own[rows - 1 : rows], own[:1])
            other = row_taps(other[:rows], other[2 * rows - 1 :], other[rows : rows + 1])
            for swapped, taps in enumerate((own, other)):
                slot = jnp.where(core == swapped, slots[1][depth], slots[0][depth])
                at = pl.multiple_of(slot * room + frame * rows, rows)
                lhs_ref[pl.ds(at, rows)] = taps.astype(lhs_ref.dtype)
    own = mine_ref[2 * count, rows:].astype(jnp.float32)
    other = theirs_ref[2 * count, :rows].astype(jnp.float32)
    start_ref[:rows] = zero * other + one * own
    start_ref[rows:] = zero * own + one * other


def drive_kernel(
    lhs_ref, weight_ref, total_ref, spill_ref, pole_ref, drive_ref, beside_ref, strips_ref, end_ref
):
    count, rows, cols, wide = drive_ref.shape
    room, size = count * rows, rows * cols
    at = size + 2 * rows
    early = None
    for lanes in halves(weight_ref.shape[-1]):
        first = dot(lhs_ref[: 2 * room], weight_ref, 0, lanes)
        middle = dot(lhs_ref[room : 3 * room], weight_ref, 1, lanes)
        last = dot(lhs_ref[2 * room :], weight_ref, 2, lanes)
        left = (spill_ref[0, :, lanes] + first[:room] + middle[:room]).reshape(count, rows, wide)
        right = (spill_ref[1, :, lanes] + middle[room:] + last[room:]).reshape(count, rows, wide)
        total = total_ref[:, :, :, lanes]
        if lanes.start == 0:
            near = total[:, :, 0, :] + first[room:].reshape(count, rows, wide)
            far = total[:, :, cols - 1, :] + last[:room].reshape(count, rows, wide)
            strips = jnp.concatenate([left, near, far, right], axis=1)
            strips_ref[...] = strips
            early = end_state([strips[frame] for frame in range(count)], pole_ref, lanes)
            end_ref[at : at + rows] = early[:rows].astype(end_ref.dtype)
            end_ref[at + rows :] = early[3 * rows :].astype(end_ref.dtype)
            continue
        col = lax.broadcasted_iota(jnp.int32, drive_ref.shape, 2)
        total += jnp.where(col == 0, first[room:].reshape(count, rows, 1, wide), 0.0)
        total += jnp.where(col == cols - 1, last[:room].reshape(count, rows, 1, wide), 0.0)
        drive_ref[...] = total
        state = end_state([total[frame] for frame in range(count)], pole_ref, lanes)
        col = lax.broadcasted_iota(jnp.int32, state.shape, 1)
        state = jnp.where(col == 1, early[rows : 2 * rows].reshape(rows, 1, wide), state)
        border = early[2 * rows : 3 * rows].reshape(rows, 1, wide)
        state = jnp.where(col == cols - 2, border, state)
        end_ref[:size] = state.reshape(size, wide).astype(end_ref.dtype)
        beside = jnp.concatenate([left, right], axis=1)
        beside_ref[...] = beside
        state = end_state([beside[frame] for frame in range(count)], pole_ref, lanes)
        end_ref[size:at] = state.astype(end_ref.dtype)


def spread(block, cols, count, of_lanes):
    _, lanes, inset = block
    value = of_lanes(lanes)
    if inset is None:
        return value
    other, columns = inset
    value, instead = jnp.broadcast_arrays(value, of_lanes(other))
    shape = (count, value.shape[1])
    col = lax.rem(lax.broadcasted_iota(jnp.int32, shape, 0), cols)
    return jnp.where((col == columns[0]) | (col == columns[1]), instead, value)


def entry_kernel(frames, cols, block, ends_ref, pole_ref, out_ref):
    rate = rate_of(pole_ref)
    count = ends_ref.shape[1]
    carried = spread(block, cols, count, lambda lanes: jnp.exp(frames * rate[:, lanes]))
    entry = jnp.zeros(ends_ref.shape[1:], jnp.float32)
    out_ref[0] = entry.astype(out_ref.dtype)
    for index in range(ends_ref.shape[0] - 1):
        entry = carried * entry + ends_ref[index].astype(jnp.float32)
        out_ref[index + 1] = entry.astype(out_ref.dtype)


def exchange(pieces, pole, frames, cols):
    groups = lax.axis_size("tm")
    arrivals = []
    for end, blocks in pieces:
        entries = []
        for block in blocks:
            shares = end[block[0]].reshape(groups, -1, end.shape[1])
            assert block[2] is None or shares.shape[1] % cols == 0
            shares = lax.all_to_all(shares, "tm", 0, 0)
            kernel = functools.partial(entry_kernel, frames, cols, block)
            entry = call(kernel, of(shares.shape, end.dtype), shares, pole)
            entries.append(lax.all_to_all(entry, "tm", 0, 0).reshape(-1, end.shape[1]))
        arrivals.append((jnp.concatenate(entries, axis=0),))
    return arrivals


def pick(values):
    group = lax.axis_index("tm")
    picked = values[-1]
    for index, value in enumerate(values[:-1]):
        picked = jnp.where(group == index, value, picked)
    return picked


def on_core(first, second):
    return jnp.where(lax.axis_index("sx") == 0, first, second)


def weigh(one, by_one, other, by_other):
    return by_one * one.astype(jnp.float32) + by_other * other.astype(jnp.float32)


def relay_kernel(frames, cols, blocks, end_ref, got_ref, pole_ref, out_ref):
    rate = rate_of(pole_ref)
    carried, twice = jnp.exp(frames * rate), jnp.exp(2 * frames * rate)
    none, same = jnp.zeros_like(rate), jnp.ones_like(rate)
    own = on_core(pick([carried, same, same, same]), pick([same, same, same, none]))
    got = on_core(pick([same, carried, carried, carried]), pick([none, none, twice, same]))
    for block in blocks:
        rows = block[0]
        count = rows.stop - rows.start
        by_own = spread(block, cols, count, lambda lanes: own[:, lanes])
        by_got = spread(block, cols, count, lambda lanes: got[:, lanes])
        out_ref[rows] = weigh(end_ref[rows], by_own, got_ref[rows], by_got).astype(out_ref.dtype)


def exchange_four(pieces, pole, frames, cols):
    def along(pairs, core):
        return [(2 * source + core, 2 * target + core) for source, target in pairs]

    axes = ("tm", "sx")
    down = [(0, 2), (1, 3)]
    first_round = along([(0, 1), (1, 0), (2, 3)], 0) + along(down, 1)
    second_round = along(down, 0) + along([(0, 1), (2, 3), (3, 2)], 1)
    arrivals = []
    for end, blocks in pieces:
        got = lax.ppermute(end, axes, first_round)
        kernel = functools.partial(relay_kernel, frames, cols, blocks)
        relayed = call(kernel, of(end.shape, end.dtype), end, got, pole)
        arrivals.append((got, lax.ppermute(relayed, axes, second_round)))
    return arrivals


class Mix:
    def __init__(self, lanes, count, pole_ref, scale_ref):
        self.rate = rate_of(pole_ref)[:, lanes]
        self.scale = scale_ref[:, lanes]
        self.count = count

    def entry(self, arrived_refs, rows):
        parts = [ref[rows].astype(jnp.float32) for ref in arrived_refs]
        if len(parts) == 1:
            return parts[0]
        carried = jnp.exp(self.count * self.rate)
        none, same = jnp.zeros_like(self.rate), jnp.ones_like(self.rate)
        early = on_core(pick([none, same, none, same]), pick([none, none, carried, carried]))
        late = on_core(pick([none, none, same, carried]), pick([none, same, same, same]))
        return weigh(parts[0], early, parts[1], late)

    def __call__(self, drives, entry, start):
        decay = jnp.exp(self.rate)
        reach = jnp.exp((self.count * lax.axis_index("tm")).astype(jnp.float32) * self.rate)
        state = reach * start + entry.reshape(start.shape)
        for drive in drives:
            state = decay * state + drive
            yield jax.nn.gelu(self.scale * state)


def no_border(cells, axis):
    col = lax.broadcasted_iota(jnp.int32, cells.shape, axis)
    return jnp.where((col == 0) | (col == cells.shape[axis] - 1), 0.0, cells)


def put_back(late, early, axis):
    cols = late.shape[axis]
    col = lax.broadcasted_iota(jnp.int32, late.shape, axis)
    late = jnp.where(col == 1, pltpu.roll(early, 1, axis), late)
    return jnp.where(col == cols - 2, pltpu.roll(early, cols - 1, axis), late)


def mixed_kernel(lanes, rounds, *refs):
    drive_ref, start_ref, pole_ref, scale_ref, *arrived_refs, lhs_ref = refs
    early_refs, late_refs = arrived_refs[:rounds], arrived_refs[rounds:]
    count, rows, cols, _ = drive_ref.shape
    wide = lanes.stop - lanes.start
    size = rows * cols
    stride = lhs_ref.shape[0] // count
    room = (stride - size) // 2
    mix = Mix(lanes, count, pole_ref, scale_ref)
    first = lanes.start == 0
    held = lanes if first else slice(None)
    block = 8
    for row in range(0, rows, block):
        here = slice(row, row + block)
        drives = [drive_ref[frame, here, :, held] for frame in range(count)]
        cells = slice(row * cols, (row + block) * cols)
        entry = mix.entry(early_refs, cells).reshape(block, cols, wide)
        if not first:
            entry = put_back(mix.entry(late_refs, cells).reshape(entry.shape), entry, 1)
        for frame, tile in enumerate(mix(drives, entry, start_ref[here, :, lanes])):
            if first:
                tile = no_border(tile, 1)
            tile = tile.reshape(block * cols, wide).astype(lhs_ref.dtype)
            put_cells(lhs_ref, frame * stride + room, size, cols, row * cols, tile)


def middle_kernel(lanes, *refs):
    total_ref, start_ref, pole_ref, scale_ref, *arrived_refs, give_ref = refs
    count, rows, cols, _ = total_ref.shape
    mix = Mix(lanes, count, pole_ref, scale_ref)
    inner = inner_row(rows)
    drives = [total_ref[frame, inner, :, lanes] for frame in range(count)]
    entry = mix.entry(arrived_refs, pl.ds(pl.multiple_of(inner * cols, cols), cols))
    for frame, cells in enumerate(mix(drives, entry, start_ref[inner, :, lanes])):
        give_ref[frame] = no_border(cells, 0).astype(give_ref.dtype)


def strip_start_kernel(start_ref, sides_ref, out_ref):
    rows, cols, _ = start_ref.shape
    start = start_ref[...]
    out_ref[:rows] = sides_ref[:rows]
    out_ref[rows : 2 * rows] = start[:, 0, :]
    out_ref[2 * rows : 3 * rows] = start[:, cols - 1, :]
    out_ref[3 * rows :] = sides_ref[rows:]


def inside(slot):
    chip, chips = lax.axis_index("sy"), lax.axis_size("sy")
    return {0: (chip > 0).astype(jnp.float32), 3: (chip < chips - 1).astype(jnp.float32)}.get(slot, 1.0)


def give_kernel(parts, rounds, *refs):
    drive_ref, beside_ref, strips_ref, *refs = refs
    start_ref, strip_start_ref, pole_ref, scale_ref, *arrived_refs, give_ref = refs
    early_refs, late_refs = arrived_refs[:rounds], arrived_refs[rounds:]
    count, rows, cols, wide = drive_ref.shape
    size = rows * cols
    inner = inner_row(rows)
    zero, one = is_core(0), is_core(1)
    early, late = (Mix(lanes, count, pole_ref, scale_ref) for lanes in parts)
    row = pl.ds(pl.multiple_of(inner * cols, cols), cols)
    which = lax.broadcasted_iota(jnp.int32, (cols, wide), 0)

    def near(at):
        return pl.ds(pl.multiple_of(at + jnp.where(inner == 0, 0, rows - cols), cols), cols)

    def end(cells):
        return zero * cells[cols - 1 :] + one * cells[:1]

    def rows_of(cells):
        table = jnp.zeros(which.shape, jnp.float32)
        for index, cell in cells:
            table = jnp.where(which == index, cell, table)
        return table

    entry = put_back(late.entry(late_refs, row), late.entry(early_refs, row), 0)
    drives = [drive_ref[frame, inner] for frame in range(count)]
    tile = late(drives, entry, start_ref[inner, :, parts[1]])

    slots = [(0, 0), (1, 3)]
    entry = rows_of([(i, end(late.entry(late_refs, near(size + i * rows)))) for i, _ in slots])
    start = rows_of([(i, end(strip_start_ref[near(slot * rows), parts[1]])) for i, slot in slots])
    drives = [
        rows_of([(i, end(beside_ref[frame, near(i * rows)])) for i, _ in slots])
        for frame in range(count)
    ]
    beside = late(drives, entry, start)

    slots = [(2 + slot, slot) for slot in range(4)]
    grid = early.entry(late_refs, row)
    at = size + 2 * rows
    entry = rows_of(
        [
            (2, end(early.entry(late_refs, near(at)))),
            (3, grid[1:2]),
            (4, grid[cols - 2 : cols - 1]),
            (5, end(early.entry(late_refs, near(at + rows)))),
        ]
    )
    start = rows_of([(i, end(strip_start_ref[near(slot * rows), parts[0]])) for i, slot in slots])
    drives = [
        rows_of([(i, end(strips_ref[frame, near(slot * rows)])) for i, slot in slots])
        for frame in range(count)
    ]
    strips = early(drives, entry, start)
    for frame, cells in enumerate(zip(tile, beside, strips)):
        give_ref[frame, :cols] = cells[0].astype(give_ref.dtype)
        ends = jnp.where(which < 2, cells[1], cells[2])
        ends = jnp.where((which == 0) | (which == 2), inside(0) * ends, ends)
        ends = jnp.where((which == 1) | (which == 5), inside(3) * ends, ends)
        give_ref[frame, cols:] = ends.astype(give_ref.dtype)


def late_kernel(parts, rounds, *refs):
    beside_ref, strips_ref, strip_start_ref, pole_ref, scale_ref, *refs = refs
    *late_refs, beside_out_ref, strips_out_ref = refs
    count, room, wide = beside_ref.shape
    rows = room // 2
    size = late_refs[0].shape[0] - 4 * rows
    cols = size // rows
    early, late = (Mix(lanes, count, pole_ref, scale_ref) for lanes in parts)

    def column(cells, index):
        return cells[index * rows : (index + 1) * rows]

    starts = [strip_start_ref[slot * rows : (slot + 1) * rows, parts[1]] for slot in (0, 3)]
    entry = late.entry(late_refs, slice(size, size + 2 * rows))
    drives = [beside_ref[frame] for frame in range(count)]
    beside = late(drives, entry, jnp.concatenate(starts, axis=0))
    grid = early.entry(late_refs, slice(0, size)).reshape(rows, cols, wide)
    sides = early.entry(late_refs, slice(size + 2 * rows, size + 4 * rows))
    entry = [sides[:rows], grid[:, 1, :], grid[:, cols - 2, :], sides[rows:]]
    drives = [strips_ref[frame] for frame in range(count)]
    strips = early(drives, jnp.concatenate(entry, axis=0), strip_start_ref[:, parts[0]])
    for frame, (sides, strip) in enumerate(zip(beside, strips)):
        sides = [column(sides, 0) * inside(0), column(sides, 1) * inside(3)]
        strip = [column(strip, slot) * inside(slot) for slot in range(4)]
        beside_out_ref[frame] = jnp.concatenate(sides, axis=0).astype(beside_out_ref.dtype)
        strips_out_ref[frame] = jnp.concatenate(strip, axis=0).astype(strips_out_ref.dtype)


def put_columns_taps(lhs_ref, slots, columns, ends):
    rows = columns.shape[0] // len(slots)
    columns, ends = columns.astype(jnp.float32), ends.astype(jnp.float32)
    for index, at in enumerate(slots):
        column, end = columns[index * rows : (index + 1) * rows], ends[index : index + 1]
        lhs_ref[at : at + rows] = row_taps(column, end, end).astype(lhs_ref.dtype)


def tile_sum(tile, inputs, lanes, room, lhs_ref, weight_ref):
    count, rows, cols, wide = tile
    size = rows * cols
    col = lax.broadcasted_iota(jnp.int32, tile[1:], 1)

    def beside(cells):
        return cells.reshape(rows, 1, wide) if room else 0.0

    for frame in range(count):
        at = frame * (size + 2 * room)
        end = at + room + size
        total = dot(lhs_ref[at + room : end], weight_ref, 1, lanes, inputs).reshape(tile[1:])
        first = dot(lhs_ref[at:end], weight_ref, 0, lanes, inputs)
        shifted = pltpu.roll(first[room:].reshape(tile[1:]), 1, 1)
        total += jnp.where(col == 0, beside(first[:room]), shifted)
        last = dot(lhs_ref[at + room : end + room], weight_ref, 2, lanes, inputs)
        shifted = pltpu.roll(last[:size].reshape(tile[1:]), cols - 1, 1)
        yield total + jnp.where(col == cols - 1, beside(last[size:]), shifted)


def strip_sum(tile, inputs, lanes, lhs_ref, weight_ref):
    count, rows, cols, wide = tile
    room = count * rows
    first = dot(lhs_ref[: 2 * room], weight_ref, 0, lanes, inputs)
    middle = dot(lhs_ref[room : 3 * room], weight_ref, 1, lanes, inputs)
    last = dot(lhs_ref[2 * room :], weight_ref, 2, lanes, inputs)
    col = lax.broadcasted_iota(jnp.int32, tile, 2)
    total = 0.0
    for at, cells in (
        (0, first[:room] + middle[:room]),
        (1, first[room:]),
        (cols - 2, last[:room]),
        (cols - 1, middle[room:] + last[room:]),
    ):
        total = jnp.where(col == at, cells.reshape(count, rows, 1, wide), total)
    return total


def opening_kernel(inputs, lanes, _, got_ref, weight_ref, out_ref, lhs_ref):
    count, rows, cols, _ = out_ref.shape
    size = rows * cols
    for frame in range(count):
        put_row(lhs_ref, frame * size, size, got_ref[frame])
    further_kernel(inputs, lanes, lhs_ref, weight_ref, out_ref)


def further_kernel(inputs, lanes, lhs_ref, weight_ref, out_ref):
    tiles = tile_sum(out_ref.shape, inputs, lanes, 0, lhs_ref, weight_ref)
    for frame, total in enumerate(tiles):
        out_ref[frame] = total


def result_kernel(
    parts, _, got_ref, beside_ref, strips_ref, weight_ref, *refs
):
    *before_refs, out_ref, lhs_ref, held_ref, strip_lhs_ref, sems = refs
    count, rows, cols, _ = held_ref.shape
    size, room = rows * cols, count * rows
    stride = size + 2 * rows
    for frame in range(count):
        at = frame * stride
        put_row(lhs_ref, at + rows, size, got_ref[frame, :cols])
        ends = got_ref[frame, cols:]
        put_columns_taps(lhs_ref, (at, at + rows + size), beside_ref[frame], ends)
        slots = [slot * room + frame * rows for slot in range(4)]
        put_columns_taps(strip_lhs_ref, slots, strips_ref[frame], ends.astype(jnp.float32)[2:])

    def store(frame, part):
        here = (frame, slice(None), slice(None), parts[part])
        return pltpu.make_async_copy(held_ref.at[here], out_ref.at[here], sems.at[frame, part])

    for part, lanes in enumerate(parts):
        tile = (count, rows, cols, lanes.stop - lanes.start)
        strips = strip_sum(tile, parts[0], lanes, strip_lhs_ref, weight_ref)
        tiles = tile_sum(tile, parts[1], lanes, rows, lhs_ref, weight_ref)
        for frame, total in enumerate(tiles):
            total += before_refs[part][frame] + strips[frame]
            held_ref[frame, :, :, lanes] = total.astype(held_ref.dtype)
            store(frame, part).start()
    for part in range(len(parts)):
        for frame in range(count):
            store(frame, part).wait()


def on_device(frames, input_weight, output_weight, pole_index, gelu_scale, start_state):
    count, rows, cols, channels = frames.shape
    size, room = rows * cols, count * rows
    wide = 3 * channels
    assert lax.axis_size("sx") == 2
    narrow = frames.dtype
    pole, scale = pole_index[None], gelu_scale[None]

    shapes = (
        of((count * cols + (2 * count + 1) * rows, channels), narrow),
        of((2 * count + 1, rows, channels), narrow),
    )
    edges = call(
        edges_kernel,
        shapes,
        frames,
        scratch=[pltpu.VMEM((count, channels // 128, size, 128), jnp.float32)],
        flops=EDGES_COST,
    )
    give, keep = call(
        start_edges_kernel,
        shapes,
        start_state,
        *edges,
        aliases={1: 0, 2: 1},
    )
    got, mine = trade_columns(give, keep, count * cols)
    taps = of((count * size, wide), narrow)
    parts = halves(channels)
    half = channels // 2
    inner = of((count, rows, cols, half), jnp.float32)
    *main, early, _ = call(
        main_kernel,
        (
            of(frames.shape, jnp.float32),
            of((2, room, channels), jnp.float32),
            of((size, half), narrow),
            taps,
        ),
        call(taps_kernel, taps, frames),
        got,
        input_weight,
        pole,
        aliases={0: 3},
        flops=18 * frames.size * channels,
    )
    mine, total, spill = lax.optimization_barrier((mine, *main))
    halo, sides = call(
        halo_kernel,
        (of((4 * room, wide), narrow), of((2 * rows, channels), jnp.float32)),
        mine,
        swap_cores(mine),
    )
    drive, beside, strips, late = call(
        drive_kernel,
        (
            inner,
            of((count, 2 * rows, half), jnp.float32),
            of((count, 4 * rows, half), jnp.float32),
            of((size + 4 * rows, half), narrow),
        ),
        halo,
        input_weight,
        total,
        spill,
        pole,
        flops=36 * room * channels * channels,
    )
    at = size + 2 * rows
    tile = slice(0, size)
    pieces = [
        (early, [(tile, parts[0], (parts[1], (0, cols - 1)))]),
        (
            late,
            [
                (tile, parts[1], (parts[0], (1, cols - 2))),
                (slice(size, at), parts[1], None),
                (slice(at, at + 2 * rows), parts[0], None),
            ],
        ),
    ]
    exchanged = exchange_four if lax.axis_size("tm") == 4 else exchange
    early, late = exchanged(pieces, pole, count, cols)
    rounds = len(early)

    mixing = (start_state, pole, scale)
    taps = of((count * size, 3 * half), narrow)
    give = call(
        functools.partial(middle_kernel, parts[0]),
        of((count, cols, half), narrow),
        total,
        *mixing,
        *early,
    )
    lhs = call(functools.partial(mixed_kernel, parts[0], rounds), taps, total, *mixing, *early)
    strip_start = call(strip_start_kernel, of((4 * rows, channels), jnp.float32), start_state, sides)
    flops = 18 * inner.size * half
    first_sum, lhs = call(
        functools.partial(opening_kernel, parts[0], parts[0]),
        (inner, taps),
        lhs,
        swap_cores(give),
        output_weight,
        aliases={0: 1},
        flops=flops,
    )
    second_sum = call(
        functools.partial(further_kernel, parts[0], parts[1]),
        inner,
        lhs,
        output_weight,
        flops=flops,
    )
    *late, first_sum, second_sum = lax.optimization_barrier((*late, first_sum, second_sum))
    give = call(
        functools.partial(give_kernel, parts, rounds),
        of((count, 2 * cols, half), narrow),
        drive,
        beside,
        strips,
        start_state,
        strip_start,
        pole,
        scale,
        *early,
        *late,
    )
    beside, strips = call(
        functools.partial(late_kernel, parts, rounds),
        (of(beside.shape, narrow), of(strips.shape, narrow)),
        beside,
        strips,
        strip_start,
        pole,
        scale,
        *late,
    )
    taps = of((count * size + 2 * room, 3 * half), narrow)
    lhs = call(
        functools.partial(mixed_kernel, parts[1], rounds), taps, drive, *mixing, *early, *late
    )
    result, _ = call(
        functools.partial(result_kernel, parts),
        (of(frames.shape, narrow), taps),
        lhs,
        swap_cores(give),
        beside,
        strips,
        output_weight,
        first_sum,
        second_sum,
        out_specs=(HBM, WHOLE),
        aliases={0: 1},
        scratch=[
            pltpu.VMEM(frames.shape, narrow),
            pltpu.VMEM((4 * room, 3 * half), narrow),
            pltpu.SemaphoreType.DMA((count, len(parts))),
        ],
        flops=2 * flops,
    )
    return result


def solution(mesh):
    return jax.shard_map(
        on_device,
        mesh=mesh,
        in_specs=(P("tm", "sx", "sy", None), P(), P(), P(), P(), P("sx", "sy", None)),
        out_specs=P("tm", "sx", "sy", None),
        check_vma=False,
    )
```

```python
import functools
import math

import jax
import jax.numpy as jnp
from jax import lax
from jax.experimental import pallas as pl
from jax.experimental.pallas import tpu as pltpu
from jax.sharding import PartitionSpec as P

NPOLES = 16
VMEM_LIMIT = 24 * 1024 * 1024
WHOLE = pl.BlockSpec(memory_space=pltpu.VMEM)
HBM = pl.BlockSpec(memory_space=pltpu.HBM)
EDGES_COST = 2_000_000_000


def call(kernel, out_shape, *args, scratch=(), flops=0, out_specs=None, aliases=None):
    outs = jax.tree.leaves(out_shape)
    moved = sum(leaf.size * leaf.dtype.itemsize for leaf in (*args, *outs))
    return pl.pallas_call(
        kernel,
        in_specs=[WHOLE] * len(args),
        out_specs=out_specs or jax.tree.map(lambda _: WHOLE, out_shape),
        out_shape=out_shape,
        scratch_shapes=scratch,
        input_output_aliases=aliases or {},
        compiler_params=pltpu.CompilerParams(vmem_limit_bytes=VMEM_LIMIT),
        cost_estimate=pl.CostEstimate(flops=flops, bytes_accessed=moved, transcendentals=0),
    )(*args)


def of(shape, dtype):
    return jax.ShapeDtypeStruct(shape, dtype)


def is_core(which):
    return (lax.axis_index("sx") == which).astype(jnp.float32)


def rate_of(pole_ref):
    pole = pole_ref[...].astype(jnp.float32)
    return -0.001 * jnp.exp(pole * (math.log(300.0) / (NPOLES - 1)))


def inner_row(rows):
    return jnp.where(lax.axis_index("sx") == 0, rows - 1, 0)


def swap_cores(array):
    return lax.ppermute(array, "sx", [(0, 1), (1, 0)])


def put_columns(index, left, right, give_ref, keep_ref):
    zero, one = is_core(0), is_core(1)
    count, rows, _ = keep_ref.shape
    at = give_ref.shape[0] - (count - index) * rows
    give_ref[at : at + rows] = (zero * left + one * right).astype(give_ref.dtype)
    keep_ref[index] = (zero * right + one * left).astype(keep_ref.dtype)


def columns_of(tile, wide_ref, picked):
    rows, cols, channels = tile.shape
    parts, _, lanes = wide_ref.shape
    tile = tile.reshape(rows * cols, channels)
    for part in range(parts):
        wide_ref[part] = tile[:, part * lanes : (part + 1) * lanes]
    return [
        jnp.concatenate(
            [wide_ref[part, pl.ds(col, rows, stride=cols), :] for part in range(parts)], axis=1
        )
        for col in picked
    ]


def edges_kernel(cells_ref, give_ref, keep_ref, wide_ref):
    count, rows, cols, channels = cells_ref.shape
    for frame in range(count):
        give_ref[frame * cols : (frame + 1) * cols] = cells_ref[frame, inner_row(rows)]
        tile = cells_ref[frame].astype(jnp.float32)
        picked = (0, 1, cols - 1, cols - 2)
        columns = columns_of(tile, wide_ref.at[frame], picked)
        for depth in range(2):
            left, right = columns[depth], columns[2 + depth]
            put_columns(2 * frame + depth, left, right, give_ref, keep_ref)


def start_edges_kernel(start_ref, _, __, give_ref, keep_ref, wide_ref):
    cols = start_ref.shape[1]
    left, right = columns_of(start_ref[...], wide_ref, (0, cols - 1))
    put_columns(keep_ref.shape[0] - 1, left, right, give_ref, keep_ref)


def trade_columns(give, keep, at):
    chips = lax.axis_size("sy")
    got = swap_cores(give)
    pairs = [(chip, chips + chip + 1) for chip in range(chips - 1)]
    pairs += [(after, before) for before, after in pairs]
    columns = jnp.concatenate([keep, got[at:].reshape(keep.shape)], axis=1)
    return got, lax.ppermute(columns, ("sx", "sy"), pairs)


def put_cells(lhs_ref, at, size, cols, first, cells):
    count, channels = cells.shape
    upper, lower = min(count, size - cols - first), max(0, cols - first)
    here = at + first
    lhs_ref[here : here + count, channels : 2 * channels] = cells
    lhs_ref[here + cols : here + cols + upper, :channels] = cells[:upper]
    lhs_ref[here + lower - cols : here + count - cols, 2 * channels :] = cells[lower:]


def put_row(lhs_ref, at, size, row):
    cols, channels = row.shape
    row = row.astype(jnp.float32)
    last = slice(at + size - cols, at + size)
    lhs_ref[at : at + cols, :channels] = (is_core(1) * row).astype(lhs_ref.dtype)
    lhs_ref[last, 2 * channels :] = (is_core(0) * row).astype(lhs_ref.dtype)


def taps_kernel(cells_ref, lhs_ref):
    count, rows, cols, channels = cells_ref.shape
    size = rows * cols
    for frame in range(count):
        put_cells(lhs_ref, frame * size, size, cols, 0, cells_ref[frame].reshape(size, channels))


def row_taps(column, above, below):
    rows = column.shape[0]
    row = lax.broadcasted_iota(jnp.int32, column.shape, 0)
    up = jnp.where(row == 0, is_core(1) * above, pltpu.roll(column, 1, 0))
    down = jnp.where(row == rows - 1, is_core(0) * below, pltpu.roll(column, rows - 1, 0))
    return jnp.concatenate([up, column, down], axis=1)


SLAB = 8


def halves(channels):
    return slice(0, channels // 2), slice(channels // 2, channels)


def end_state(frames, pole_ref, lanes):
    decay = jnp.exp(rate_of(pole_ref))[:, lanes]
    state = frames[0]
    for frame in frames[1:]:
        state = decay * state + frame
    return state


def dot(lhs, weight_ref, column, lanes, inputs=slice(None)):
    weight = weight_ref[:, column, inputs, lanes].reshape(lhs.shape[1], -1)
    return jnp.dot(lhs, weight, preferred_element_type=jnp.float32)


def main_kernel(_, got_ref, weight_ref, pole_ref, total_ref, spill_ref, end_ref, lhs_ref):
    count, rows, cols, _ = total_ref.shape
    size = rows * cols
    for frame in range(count):
        put_row(lhs_ref, frame * size, size, got_ref[frame * cols : (frame + 1) * cols])
    states = []
    for lanes in halves(weight_ref.shape[-1]):
        tile = (rows, cols, lanes.stop - lanes.start)
        col = lax.broadcasted_iota(jnp.int32, tile, 1)
        totals = []
        for frame in range(count):
            cells = lhs_ref[frame * size : (frame + 1) * size]
            here = slice(frame * rows, (frame + 1) * rows)
            total = dot(cells, weight_ref, 1, lanes).reshape(tile)
            first = dot(cells, weight_ref, 0, lanes).reshape(tile)
            spill_ref[1, here, lanes] = first[:, cols - 1, :]
            total += jnp.where(col == 0, 0.0, pltpu.roll(first, 1, 1))
            last = dot(cells, weight_ref, 2, lanes).reshape(tile)
            spill_ref[0, here, lanes] = last[:, 0, :]
            total += jnp.where(col == cols - 1, 0.0, pltpu.roll(last, cols - 1, 1))
            total_ref[frame, :, :, lanes] = total
            totals.append(total)
        states.append(end_state(totals, pole_ref, lanes))
    state, other = states
    col = lax.broadcasted_iota(jnp.int32, (rows, SLAB, state.shape[2]), 1)
    last = slice(cols - SLAB, cols)
    left = jnp.where(col == 0, pltpu.roll(other[:, :SLAB], SLAB - 1, 1), state[:, :SLAB])
    right = jnp.where(col == SLAB - 1, pltpu.roll(other[:, last], 1, 1), state[:, last])
    middle = [state[:, SLAB : cols - SLAB]] if cols > 2 * SLAB else []
    state = jnp.concatenate([left, *middle, right], axis=1)
    end_ref[...] = state.reshape(end_ref.shape).astype(end_ref.dtype)


def halo_kernel(mine_ref, theirs_ref, lhs_ref, start_ref):
    rows = mine_ref.shape[1] // 2
    count = mine_ref.shape[0] // 2
    room = count * rows
    zero, one = is_core(0), is_core(1)
    core = lax.axis_index("sx")
    slots = ((1, 0), (2, 3))
    for frame in range(count):
        for depth in range(2):
            own = mine_ref[2 * frame + depth].astype(jnp.float32)
            other = theirs_ref[2 * frame + depth].astype(jnp.float32)
            own = row_taps(own[rows:], own[rows - 1 : rows], own[:1])
            other = row_taps(other[:rows], other[2 * rows - 1 :], other[rows : rows + 1])
            for swapped, taps in enumerate((own, other)):
                slot = jnp.where(core == swapped, slots[1][depth], slots[0][depth])
                at = pl.multiple_of(slot * room + frame * rows, rows)
                lhs_ref[pl.ds(at, rows)] = taps.astype(lhs_ref.dtype)
    own = mine_ref[2 * count, rows:].astype(jnp.float32)
    other = theirs_ref[2 * count, :rows].astype(jnp.float32)
    start_ref[:rows] = zero * other + one * own
    start_ref[rows:] = zero * own + one * other


def drive_kernel(
    lhs_ref, weight_ref, total_ref, spill_ref, pole_ref, drive_ref, beside_ref, strips_ref, end_ref
):
    count, rows, cols, wide = drive_ref.shape
    room, size = count * rows, rows * cols
    at = size + 2 * rows
    early = None
    for lanes in halves(weight_ref.shape[-1]):
        first = dot(lhs_ref[: 2 * room], weight_ref, 0, lanes)
        middle = dot(lhs_ref[room : 3 * room], weight_ref, 1, lanes)
        last = dot(lhs_ref[2 * room :], weight_ref, 2, lanes)
        left = (spill_ref[0, :, lanes] + first[:room] + middle[:room]).reshape(count, rows, wide)
        right = (spill_ref[1, :, lanes] + middle[room:] + last[room:]).reshape(count, rows, wide)
        total = total_ref[:, :, :, lanes]
        if lanes.start == 0:
            near = total[:, :, 0, :] + first[room:].reshape(count, rows, wide)
            far = total[:, :, cols - 1, :] + last[:room].reshape(count, rows, wide)
            strips = jnp.concatenate([left, near, far, right], axis=1)
            strips_ref[...] = strips
            early = end_state([strips[frame] for frame in range(count)], pole_ref, lanes)
            end_ref[at : at + rows] = early[:rows].astype(end_ref.dtype)
            end_ref[at + rows :] = early[3 * rows :].astype(end_ref.dtype)
            continue
        col = lax.broadcasted_iota(jnp.int32, drive_ref.shape, 2)
        total += jnp.where(col == 0, first[room:].reshape(count, rows, 1, wide), 0.0)
        total += jnp.where(col == cols - 1, last[:room].reshape(count, rows, 1, wide), 0.0)
        drive_ref[...] = total
        state = end_state([total[frame] for frame in range(count)], pole_ref, lanes)
        col = lax.broadcasted_iota(jnp.int32, state.shape, 1)
        state = jnp.where(col == 1, early[rows : 2 * rows].reshape(rows, 1, wide), state)
        border = early[2 * rows : 3 * rows].reshape(rows, 1, wide)
        state = jnp.where(col == cols - 2, border, state)
        end_ref[:size] = state.reshape(size, wide).astype(end_ref.dtype)
        beside = jnp.concatenate([left, right], axis=1)
        beside_ref[...] = beside
        state = end_state([beside[frame] for frame in range(count)], pole_ref, lanes)
        end_ref[size:at] = state.astype(end_ref.dtype)


def spread(block, cols, count, of_lanes):
    _, lanes, inset = block
    value = of_lanes(lanes)
    if inset is None:
        return value
    other, columns = inset
    value, instead = jnp.broadcast_arrays(value, of_lanes(other))
    shape = (count, value.shape[1])
    col = lax.rem(lax.broadcasted_iota(jnp.int32, shape, 0), cols)
    return jnp.where((col == columns[0]) | (col == columns[1]), instead, value)


def entry_kernel(frames, cols, block, ends_ref, pole_ref, out_ref):
    rate = rate_of(pole_ref)
    count = ends_ref.shape[1]
    carried = spread(block, cols, count, lambda lanes: jnp.exp(frames * rate[:, lanes]))
    entry = jnp.zeros(ends_ref.shape[1:], jnp.float32)
    out_ref[0] = entry.astype(out_ref.dtype)
    for index in range(ends_ref.shape[0] - 1):
        entry = carried * entry + ends_ref[index].astype(jnp.float32)
        out_ref[index + 1] = entry.astype(out_ref.dtype)


def exchange(pieces, pole, frames, cols):
    groups = lax.axis_size("tm")
    arrivals = []
    for end, blocks in pieces:
        entries = []
        for block in blocks:
            shares = end[block[0]].reshape(groups, -1, end.shape[1])
            assert block[2] is None or shares.shape[1] % cols == 0
            shares = lax.all_to_all(shares, "tm", 0, 0)
            kernel = functools.partial(entry_kernel, frames, cols, block)
            entry = call(kernel, of(shares.shape, end.dtype), shares, pole)
            entries.append(lax.all_to_all(entry, "tm", 0, 0).reshape(-1, end.shape[1]))
        arrivals.append((jnp.concatenate(entries, axis=0),))
    return arrivals


def pick(values):
    group = lax.axis_index("tm")
    picked = values[-1]
    for index, value in enumerate(values[:-1]):
        picked = jnp.where(group == index, value, picked)
    return picked


def on_core(first, second):
    return jnp.where(lax.axis_index("sx") == 0, first, second)


def weigh(one, by_one, other, by_other):
    return by_one * one.astype(jnp.float32) + by_other * other.astype(jnp.float32)


def relay_kernel(frames, cols, blocks, end_ref, got_ref, pole_ref, out_ref):
    rate = rate_of(pole_ref)
    carried, twice = jnp.exp(frames * rate), jnp.exp(2 * frames * rate)
    none, same = jnp.zeros_like(rate), jnp.ones_like(rate)
    own = on_core(pick([carried, same, same, same]), pick([same, same, same, none]))
    got = on_core(pick([same, carried, carried, carried]), pick([none, none, twice, same]))
    for block in blocks:
        rows = block[0]
        count = rows.stop - rows.start
        by_own = spread(block, cols, count, lambda lanes: own[:, lanes])
        by_got = spread(block, cols, count, lambda lanes: got[:, lanes])
        out_ref[rows] = weigh(end_ref[rows], by_own, got_ref[rows], by_got).astype(out_ref.dtype)


def exchange_four(pieces, pole, frames, cols):
    def along(pairs, core):
        return [(2 * source + core, 2 * target + core) for source, target in pairs]

    axes = ("tm", "sx")
    down = [(0, 2), (1, 3)]
    first_round = along([(0, 1), (1, 0), (2, 3)], 0) + along(down, 1)
    second_round = along(down, 0) + along([(0, 1), (2, 3), (3, 2)], 1)
    arrivals = []
    for end, blocks in pieces:
        got = lax.ppermute(end, axes, first_round)
        kernel = functools.partial(relay_kernel, frames, cols, blocks)
        relayed = call(kernel, of(end.shape, end.dtype), end, got, pole)
        arrivals.append((got, lax.ppermute(relayed, axes, second_round)))
    return arrivals


class Mix:
    def __init__(self, lanes, count, pole_ref, scale_ref):
        self.rate = rate_of(pole_ref)[:, lanes]
        self.scale = scale_ref[:, lanes]
        self.count = count

    def entry(self, arrived_refs, rows):
        parts = [ref[rows].astype(jnp.float32) for ref in arrived_refs]
        if len(parts) == 1:
            return parts[0]
        carried = jnp.exp(self.count * self.rate)
        none, same = jnp.zeros_like(self.rate), jnp.ones_like(self.rate)
        early = on_core(pick([none, same, none, same]), pick([none, none, carried, carried]))
        late = on_core(pick([none, none, same, carried]), pick([none, same, same, same]))
        return weigh(parts[0], early, parts[1], late)

    def __call__(self, drives, entry, start):
        decay = jnp.exp(self.rate)
        reach = jnp.exp((self.count * lax.axis_index("tm")).astype(jnp.float32) * self.rate)
        state = reach * start + entry.reshape(start.shape)
        for drive in drives:
            state = decay * state + drive
            yield jax.nn.gelu(self.scale * state)


def no_border(cells, axis):
    col = lax.broadcasted_iota(jnp.int32, cells.shape, axis)
    return jnp.where((col == 0) | (col == cells.shape[axis] - 1), 0.0, cells)


def put_back(late, early, axis):
    cols = late.shape[axis]
    col = lax.broadcasted_iota(jnp.int32, late.shape, axis)
    late = jnp.where(col == 1, pltpu.roll(early, 1, axis), late)
    return jnp.where(col == cols - 2, pltpu.roll(early, cols - 1, axis), late)


def mixed_kernel(lanes, rounds, *refs):
    drive_ref, start_ref, pole_ref, scale_ref, *arrived_refs, lhs_ref = refs
    early_refs, late_refs = arrived_refs[:rounds], arrived_refs[rounds:]
    count, rows, cols, _ = drive_ref.shape
    wide = lanes.stop - lanes.start
    size = rows * cols
    stride = lhs_ref.shape[0] // count
    room = (stride - size) // 2
    mix = Mix(lanes, count, pole_ref, scale_ref)
    first = lanes.start == 0
    held = lanes if first else slice(None)
    block = 8
    for row in range(0, rows, block):
        here = slice(row, row + block)
        drives = [drive_ref[frame, here, :, held] for frame in range(count)]
        cells = slice(row * cols, (row + block) * cols)
        entry = mix.entry(early_refs, cells).reshape(block, cols, wide)
        if not first:
            entry = put_back(mix.entry(late_refs, cells).reshape(entry.shape), entry, 1)
        for frame, tile in enumerate(mix(drives, entry, start_ref[here, :, lanes])):
            if first:
                tile = no_border(tile, 1)
            tile = tile.reshape(block * cols, wide).astype(lhs_ref.dtype)
            put_cells(lhs_ref, frame * stride + room, size, cols, row * cols, tile)


def middle_kernel(lanes, *refs):
    total_ref, start_ref, pole_ref, scale_ref, *arrived_refs, give_ref = refs
    count, rows, cols, _ = total_ref.shape
    mix = Mix(lanes, count, pole_ref, scale_ref)
    inner = inner_row(rows)
    drives = [total_ref[frame, inner, :, lanes] for frame in range(count)]
    entry = mix.entry(arrived_refs, pl.ds(pl.multiple_of(inner * cols, cols), cols))
    for frame, cells in enumerate(mix(drives, entry, start_ref[inner, :, lanes])):
        give_ref[frame] = no_border(cells, 0).astype(give_ref.dtype)


def strip_start_kernel(start_ref, sides_ref, out_ref):
    rows, cols, _ = start_ref.shape
    start = start_ref[...]
    out_ref[:rows] = sides_ref[:rows]
    out_ref[rows : 2 * rows] = start[:, 0, :]
    out_ref[2 * rows : 3 * rows] = start[:, cols - 1, :]
    out_ref[3 * rows :] = sides_ref[rows:]


def inside(slot):
    chip, chips = lax.axis_index("sy"), lax.axis_size("sy")
    return {0: (chip > 0).astype(jnp.float32), 3: (chip < chips - 1).astype(jnp.float32)}.get(slot, 1.0)


def give_kernel(parts, rounds, *refs):
    drive_ref, beside_ref, strips_ref, *refs = refs
    start_ref, strip_start_ref, pole_ref, scale_ref, *arrived_refs, give_ref = refs
    early_refs, late_refs = arrived_refs[:rounds], arrived_refs[rounds:]
    count, rows, cols, wide = drive_ref.shape
    size = rows * cols
    inner = inner_row(rows)
    zero, one = is_core(0), is_core(1)
    early, late = (Mix(lanes, count, pole_ref, scale_ref) for lanes in parts)
    row = pl.ds(pl.multiple_of(inner * cols, cols), cols)
    which = lax.broadcasted_iota(jnp.int32, (cols, wide), 0)

    def near(at):
        return pl.ds(pl.multiple_of(at + jnp.where(inner == 0, 0, rows - cols), cols), cols)

    def end(cells):
        return zero * cells[cols - 1 :] + one * cells[:1]

    def rows_of(cells):
        table = jnp.zeros(which.shape, jnp.float32)
        for index, cell in cells:
            table = jnp.where(which == index, cell, table)
        return table

    entry = put_back(late.entry(late_refs, row), late.entry(early_refs, row), 0)
    drives = [drive_ref[frame, inner] for frame in range(count)]
    tile = late(drives, entry, start_ref[inner, :, parts[1]])

    slots = [(0, 0), (1, 3)]
    entry = rows_of([(i, end(late.entry(late_refs, near(size + i * rows)))) for i, _ in slots])
    start = rows_of([(i, end(strip_start_ref[near(slot * rows), parts[1]])) for i, slot in slots])
    drives = [
        rows_of([(i, end(beside_ref[frame, near(i * rows)])) for i, _ in slots])
        for frame in range(count)
    ]
    beside = late(drives, entry, start)

    slots = [(2 + slot, slot) for slot in range(4)]
    grid = early.entry(late_refs, row)
    at = size + 2 * rows
    entry = rows_of(
        [
            (2, end(early.entry(late_refs, near(at)))),
            (3, grid[1:2]),
            (4, grid[cols - 2 : cols - 1]),
            (5, end(early.entry(late_refs, near(at + rows)))),
        ]
    )
    start = rows_of([(i, end(strip_start_ref[near(slot * rows), parts[0]])) for i, slot in slots])
    drives = [
        rows_of([(i, end(strips_ref[frame, near(slot * rows)])) for i, slot in slots])
        for frame in range(count)
    ]
    strips = early(drives, entry, start)
    for frame, cells in enumerate(zip(tile, beside, strips)):
        give_ref[frame, :cols] = cells[0].astype(give_ref.dtype)
        ends = jnp.where(which < 2, cells[1], cells[2])
        ends = jnp.where((which == 0) | (which == 2), inside(0) * ends, ends)
        ends = jnp.where((which == 1) | (which == 5), inside(3) * ends, ends)
        give_ref[frame, cols:] = ends.astype(give_ref.dtype)


def late_kernel(parts, rounds, *refs):
    beside_ref, strips_ref, strip_start_ref, pole_ref, scale_ref, *refs = refs
    *late_refs, beside_out_ref, strips_out_ref = refs
    count, room, wide = beside_ref.shape
    rows = room // 2
    size = late_refs[0].shape[0] - 4 * rows
    cols = size // rows
    early, late = (Mix(lanes, count, pole_ref, scale_ref) for lanes in parts)

    def column(cells, index):
        return cells[index * rows : (index + 1) * rows]

    starts = [strip_start_ref[slot * rows : (slot + 1) * rows, parts[1]] for slot in (0, 3)]
    entry = late.entry(late_refs, slice(size, size + 2 * rows))
    drives = [beside_ref[frame] for frame in range(count)]
    beside = late(drives, entry, jnp.concatenate(starts, axis=0))
    grid = early.entry(late_refs, slice(0, size)).reshape(rows, cols, wide)
    sides = early.entry(late_refs, slice(size + 2 * rows, size + 4 * rows))
    entry = [sides[:rows], grid[:, 1, :], grid[:, cols - 2, :], sides[rows:]]
    drives = [strips_ref[frame] for frame in range(count)]
    strips = early(drives, jnp.concatenate(entry, axis=0), strip_start_ref[:, parts[0]])
    for frame, (sides, strip) in enumerate(zip(beside, strips)):
        sides = [column(sides, 0) * inside(0), column(sides, 1) * inside(3)]
        strip = [column(strip, slot) * inside(slot) for slot in range(4)]
        beside_out_ref[frame] = jnp.concatenate(sides, axis=0).astype(beside_out_ref.dtype)
        strips_out_ref[frame] = jnp.concatenate(strip, axis=0).astype(strips_out_ref.dtype)


def put_columns_taps(lhs_ref, slots, columns, ends):
    rows = columns.shape[0] // len(slots)
    columns, ends = columns.astype(jnp.float32), ends.astype(jnp.float32)
    for index, at in enumerate(slots):
        column, end = columns[index * rows : (index + 1) * rows], ends[index : index + 1]
        lhs_ref[at : at + rows] = row_taps(column, end, end).astype(lhs_ref.dtype)


def tile_sum(tile, inputs, lanes, room, lhs_ref, weight_ref):
    count, rows, cols, wide = tile
    size = rows * cols
    col = lax.broadcasted_iota(jnp.int32, tile[1:], 1)

    def beside(cells):
        return cells.reshape(rows, 1, wide) if room else 0.0

    for frame in range(count):
        at = frame * (size + 2 * room)
        end = at + room + size
        total = dot(lhs_ref[at + room : end], weight_ref, 1, lanes, inputs).reshape(tile[1:])
        first = dot(lhs_ref[at:end], weight_ref, 0, lanes, inputs)
        shifted = pltpu.roll(first[room:].reshape(tile[1:]), 1, 1)
        total += jnp.where(col == 0, beside(first[:room]), shifted)
        last = dot(lhs_ref[at + room : end + room], weight_ref, 2, lanes, inputs)
        shifted = pltpu.roll(last[:size].reshape(tile[1:]), cols - 1, 1)
        yield total + jnp.where(col == cols - 1, beside(last[size:]), shifted)


def strip_sum(tile, inputs, lanes, lhs_ref, weight_ref):
    count, rows, cols, wide = tile
    room = count * rows
    first = dot(lhs_ref[: 2 * room], weight_ref, 0, lanes, inputs)
    middle = dot(lhs_ref[room : 3 * room], weight_ref, 1, lanes, inputs)
    last = dot(lhs_ref[2 * room :], weight_ref, 2, lanes, inputs)
    col = lax.broadcasted_iota(jnp.int32, tile, 2)
    total = 0.0
    for at, cells in (
        (0, first[:room] + middle[:room]),
        (1, first[room:]),
        (cols - 2, last[:room]),
        (cols - 1, middle[room:] + last[room:]),
    ):
        total = jnp.where(col == at, cells.reshape(count, rows, 1, wide), total)
    return total


def opening_kernel(inputs, lanes, _, got_ref, weight_ref, out_ref, lhs_ref):
    count, rows, cols, _ = out_ref.shape
    size = rows * cols
    for frame in range(count):
        put_row(lhs_ref, frame * size, size, got_ref[frame])
    further_kernel(inputs, lanes, lhs_ref, weight_ref, out_ref)


def further_kernel(inputs, lanes, lhs_ref, weight_ref, out_ref):
    tiles = tile_sum(out_ref.shape, inputs, lanes, 0, lhs_ref, weight_ref)
    for frame, total in enumerate(tiles):
        out_ref[frame] = total


def result_kernel(
    parts, _, got_ref, beside_ref, strips_ref, weight_ref, *refs
):
    *before_refs, out_ref, lhs_ref, held_ref, strip_lhs_ref, sems = refs
    count, rows, cols, _ = held_ref.shape
    size, room = rows * cols, count * rows
    stride = size + 2 * rows
    for frame in range(count):
        at = frame * stride
        put_row(lhs_ref, at + rows, size, got_ref[frame, :cols])
        ends = got_ref[frame, cols:]
        put_columns_taps(lhs_ref, (at, at + rows + size), beside_ref[frame], ends)
        slots = [slot * room + frame * rows for slot in range(4)]
        put_columns_taps(strip_lhs_ref, slots, strips_ref[frame], ends.astype(jnp.float32)[2:])

    def store(frame, part):
        here = (frame, slice(None), slice(None), parts[part])
        return pltpu.make_async_copy(held_ref.at[here], out_ref.at[here], sems.at[frame, part])

    for part, lanes in enumerate(parts):
        tile = (count, rows, cols, lanes.stop - lanes.start)
        strips = strip_sum(tile, parts[0], lanes, strip_lhs_ref, weight_ref)
        tiles = tile_sum(tile, parts[1], lanes, rows, lhs_ref, weight_ref)
        for frame, total in enumerate(tiles):
            total += before_refs[part][frame] + strips[frame]
            held_ref[frame, :, :, lanes] = total.astype(held_ref.dtype)
            store(frame, part).start()
    for part in range(len(parts)):
        for frame in range(count):
            store(frame, part).wait()


def on_device(frames, input_weight, output_weight, pole_index, gelu_scale, start_state):
    count, rows, cols, channels = frames.shape
    size, room = rows * cols, count * rows
    wide = 3 * channels
    assert lax.axis_size("sx") == 2
    narrow = frames.dtype
    pole, scale = pole_index[None], gelu_scale[None]

    shapes = (
        of((count * cols + (2 * count + 1) * rows, channels), narrow),
        of((2 * count + 1, rows, channels), narrow),
    )
    edges = call(
        edges_kernel,
        shapes,
        frames,
        scratch=[pltpu.VMEM((count, channels // 128, size, 128), jnp.float32)],
        flops=EDGES_COST,
    )
    give, keep = call(
        start_edges_kernel,
        shapes,
        start_state,
        *edges,
        aliases={1: 0, 2: 1},
        scratch=[pltpu.VMEM((channels // 128, size, 128), jnp.float32)],
    )
    got, mine = trade_columns(give, keep, count * cols)
    taps = of((count * size, wide), narrow)
    parts = halves(channels)
    half = channels // 2
    inner = of((count, rows, cols, half), jnp.float32)
    *main, early, _ = call(
        main_kernel,
        (
            of(frames.shape, jnp.float32),
            of((2, room, channels), jnp.float32),
            of((size, half), narrow),
            taps,
        ),
        call(taps_kernel, taps, frames),
        got,
        input_weight,
        pole,
        aliases={0: 3},
        flops=18 * frames.size * channels,
    )
    mine, total, spill = lax.optimization_barrier((mine, *main))
    halo, sides = call(
        halo_kernel,
        (of((4 * room, wide), narrow), of((2 * rows, channels), jnp.float32)),
        mine,
        swap_cores(mine),
    )
    drive, beside, strips, late = call(
        drive_kernel,
        (
            inner,
            of((count, 2 * rows, half), jnp.float32),
            of((count, 4 * rows, half), jnp.float32),
            of((size + 4 * rows, half), narrow),
        ),
        halo,
        input_weight,
        total,
        spill,
        pole,
        flops=36 * room * channels * channels,
    )
    at = size + 2 * rows
    tile = slice(0, size)
    pieces = [
        (early, [(tile, parts[0], (parts[1], (0, cols - 1)))]),
        (
            late,
            [
                (tile, parts[1], (parts[0], (1, cols - 2))),
                (slice(size, at), parts[1], None),
                (slice(at, at + 2 * rows), parts[0], None),
            ],
        ),
    ]
    exchanged = exchange_four if lax.axis_size("tm") == 4 else exchange
    early, late = exchanged(pieces, pole, count, cols)
    rounds = len(early)

    mixing = (start_state, pole, scale)
    taps = of((count * size, 3 * half), narrow)
    give = call(
        functools.partial(middle_kernel, parts[0]),
        of((count, cols, half), narrow),
        total,
        *mixing,
        *early,
    )
    lhs = call(functools.partial(mixed_kernel, parts[0], rounds), taps, total, *mixing, *early)
    strip_start = call(strip_start_kernel, of((4 * rows, channels), jnp.float32), start_state, sides)
    flops = 18 * inner.size * half
    lhs, strip_start = lax.optimization_barrier((lhs, strip_start))
    first_sum, lhs = call(
        functools.partial(opening_kernel, parts[0], parts[0]),
        (inner, taps),
        lhs,
        swap_cores(give),
        output_weight,
        aliases={0: 1},
        flops=flops,
    )
    second_sum = call(
        functools.partial(further_kernel, parts[0], parts[1]),
        inner,
        lhs,
        output_weight,
        flops=flops,
    )
    *late, first_sum, second_sum = lax.optimization_barrier((*late, first_sum, second_sum))
    give = call(
        functools.partial(give_kernel, parts, rounds),
        of((count, 2 * cols, half), narrow),
        drive,
        beside,
        strips,
        start_state,
        strip_start,
        pole,
        scale,
        *early,
        *late,
    )
    beside, strips = call(
        functools.partial(late_kernel, parts, rounds),
        (of(beside.shape, narrow), of(strips.shape, narrow)),
        beside,
        strips,
        strip_start,
        pole,
        scale,
        *late,
    )
    taps = of((count * size + 2 * room, 3 * half), narrow)
    lhs = call(
        functools.partial(mixed_kernel, parts[1], rounds), taps, drive, *mixing, *early, *late
    )
    result, _ = call(
        functools.partial(result_kernel, parts),
        (of(frames.shape, narrow), taps),
        lhs,
        swap_cores(give),
        beside,
        strips,
        output_weight,
        first_sum,
        second_sum,
        out_specs=(HBM, WHOLE),
        aliases={0: 1},
        scratch=[
            pltpu.VMEM(frames.shape, narrow),
            pltpu.VMEM((4 * room, 3 * half), narrow),
            pltpu.SemaphoreType.DMA((count, len(parts))),
        ],
        flops=2 * flops,
    )
    return result


def solution(mesh):
    return jax.shard_map(
        on_device,
        mesh=mesh,
        in_specs=(P("tm", "sx", "sy", None), P(), P(), P(), P(), P("sx", "sy", None)),
        out_specs=P("tm", "sx", "sy", None),
        check_vma=False,
    )
```

```python
import functools
import math

import jax
import jax.numpy as jnp
from jax import lax
from jax.experimental import pallas as pl
from jax.experimental.pallas import tpu as pltpu
from jax.sharding import PartitionSpec as P

NPOLES = 16
VMEM_LIMIT = 24 * 1024 * 1024
WHOLE = pl.BlockSpec(memory_space=pltpu.VMEM)
HBM = pl.BlockSpec(memory_space=pltpu.HBM)
EDGES_COST = 2_000_000_000


def call(kernel, out_shape, *args, scratch=(), flops=0, out_specs=None, aliases=None):
    outs = jax.tree.leaves(out_shape)
    moved = sum(leaf.size * leaf.dtype.itemsize for leaf in (*args, *outs))
    return pl.pallas_call(
        kernel,
        in_specs=[WHOLE] * len(args),
        out_specs=out_specs or jax.tree.map(lambda _: WHOLE, out_shape),
        out_shape=out_shape,
        scratch_shapes=scratch,
        input_output_aliases=aliases or {},
        compiler_params=pltpu.CompilerParams(vmem_limit_bytes=VMEM_LIMIT),
        cost_estimate=pl.CostEstimate(flops=flops, bytes_accessed=moved, transcendentals=0),
    )(*args)


def of(shape, dtype):
    return jax.ShapeDtypeStruct(shape, dtype)


def is_core(which):
    return (lax.axis_index("sx") == which).astype(jnp.float32)


def rate_of(pole_ref):
    pole = pole_ref[...].astype(jnp.float32)
    return -0.001 * jnp.exp(pole * (math.log(300.0) / (NPOLES - 1)))


def inner_row(rows):
    return jnp.where(lax.axis_index("sx") == 0, rows - 1, 0)


def swap_cores(array):
    return lax.ppermute(array, "sx", [(0, 1), (1, 0)])


def put_columns(index, left, right, give_ref, keep_ref):
    zero, one = is_core(0), is_core(1)
    count, rows, _ = keep_ref.shape
    at = give_ref.shape[0] - (count - index) * rows
    give_ref[at : at + rows] = (zero * left + one * right).astype(give_ref.dtype)
    keep_ref[index] = (zero * right + one * left).astype(keep_ref.dtype)


def columns_of(tile, wide_ref, picked):
    rows, cols, channels = tile.shape
    parts, _, lanes = wide_ref.shape
    tile = tile.reshape(rows * cols, channels)
    for part in range(parts):
        wide_ref[part] = tile[:, part * lanes : (part + 1) * lanes]
    return [
        jnp.concatenate(
            [wide_ref[part, pl.ds(col, rows, stride=cols), :] for part in range(parts)], axis=1
        )
        for col in picked
    ]


def edges_kernel(cells_ref, give_ref, keep_ref, wide_ref):
    count, rows, cols, channels = cells_ref.shape
    for frame in range(count):
        give_ref[frame * cols : (frame + 1) * cols] = cells_ref[frame, inner_row(rows)]
        tile = cells_ref[frame].astype(jnp.float32)
        picked = (0, 1, cols - 1, cols - 2)
        columns = columns_of(tile, wide_ref.at[frame], picked)
        for depth in range(2):
            left, right = columns[depth], columns[2 + depth]
            put_columns(2 * frame + depth, left, right, give_ref, keep_ref)


def start_edges_kernel(start_ref, _, __, give_ref, keep_ref, wide_ref):
    cols = start_ref.shape[1]
    left, right = columns_of(start_ref[...], wide_ref, (0, cols - 1))
    put_columns(keep_ref.shape[0] - 1, left, right, give_ref, keep_ref)


def trade_columns(give, keep, at):
    chips = lax.axis_size("sy")
    got = swap_cores(give)
    pairs = [(chip, chips + chip + 1) for chip in range(chips - 1)]
    pairs += [(after, before) for before, after in pairs]
    columns = jnp.concatenate([keep, got[at:].reshape(keep.shape)], axis=1)
    return got, lax.ppermute(columns, ("sx", "sy"), pairs)


def put_cells(lhs_ref, at, size, cols, first, cells):
    count, channels = cells.shape
    upper, lower = min(count, size - cols - first), max(0, cols - first)
    here = at + first
    lhs_ref[here : here + count, channels : 2 * channels] = cells
    lhs_ref[here + cols : here + cols + upper, :channels] = cells[:upper]
    lhs_ref[here + lower - cols : here + count - cols, 2 * channels :] = cells[lower:]


def put_row(lhs_ref, at, size, row):
    cols, channels = row.shape
    row = row.astype(jnp.float32)
    last = slice(at + size - cols, at + size)
    lhs_ref[at : at + cols, :channels] = (is_core(1) * row).astype(lhs_ref.dtype)
    lhs_ref[last, 2 * channels :] = (is_core(0) * row).astype(lhs_ref.dtype)


def taps_kernel(cells_ref, lhs_ref):
    count, rows, cols, channels = cells_ref.shape
    size = rows * cols
    for frame in range(count):
        put_cells(lhs_ref, frame * size, size, cols, 0, cells_ref[frame].reshape(size, channels))


def row_taps(column, above, below):
    rows = column.shape[0]
    row = lax.broadcasted_iota(jnp.int32, column.shape, 0)
    up = jnp.where(row == 0, is_core(1) * above, pltpu.roll(column, 1, 0))
    down = jnp.where(row == rows - 1, is_core(0) * below, pltpu.roll(column, rows - 1, 0))
    return jnp.concatenate([up, column, down], axis=1)


SLAB = 8


def halves(channels):
    return slice(0, channels // 2), slice(channels // 2, channels)


def end_state(frames, pole_ref, lanes):
    decay = jnp.exp(rate_of(pole_ref))[:, lanes]
    state = frames[0]
    for frame in frames[1:]:
        state = decay * state + frame
    return state


def dot(lhs, weight_ref, column, lanes, inputs=slice(None)):
    weight = weight_ref[:, column, inputs, lanes].reshape(lhs.shape[1], -1)
    return jnp.dot(lhs, weight, preferred_element_type=jnp.float32)


def main_kernel(_, got_ref, weight_ref, pole_ref, total_ref, spill_ref, end_ref, lhs_ref):
    count, rows, cols, _ = total_ref.shape
    size = rows * cols
    for frame in range(count):
        put_row(lhs_ref, frame * size, size, got_ref[frame * cols : (frame + 1) * cols])
    states = []
    for lanes in halves(weight_ref.shape[-1]):
        tile = (rows, cols, lanes.stop - lanes.start)
        col = lax.broadcasted_iota(jnp.int32, tile, 1)
        totals = []
        for frame in range(count):
            cells = lhs_ref[frame * size : (frame + 1) * size]
            here = slice(frame * rows, (frame + 1) * rows)
            total = dot(cells, weight_ref, 1, lanes).reshape(tile)
            first = dot(cells, weight_ref, 0, lanes).reshape(tile)
            spill_ref[1, here, lanes] = first[:, cols - 1, :]
            total += jnp.where(col == 0, 0.0, pltpu.roll(first, 1, 1))
            last = dot(cells, weight_ref, 2, lanes).reshape(tile)
            spill_ref[0, here, lanes] = last[:, 0, :]
            total += jnp.where(col == cols - 1, 0.0, pltpu.roll(last, cols - 1, 1))
            total_ref[frame, :, :, lanes] = total
            totals.append(total)
        states.append(end_state(totals, pole_ref, lanes))
    state, other = states
    col = lax.broadcasted_iota(jnp.int32, (rows, SLAB, state.shape[2]), 1)
    last = slice(cols - SLAB, cols)
    left = jnp.where(col == 0, pltpu.roll(other[:, :SLAB], SLAB - 1, 1), state[:, :SLAB])
    right = jnp.where(col == SLAB - 1, pltpu.roll(other[:, last], 1, 1), state[:, last])
    middle = [state[:, SLAB : cols - SLAB]] if cols > 2 * SLAB else []
    state = jnp.concatenate([left, *middle, right], axis=1)
    end_ref[...] = state.reshape(end_ref.shape).astype(end_ref.dtype)


def halo_kernel(mine_ref, theirs_ref, lhs_ref, start_ref):
    rows = mine_ref.shape[1] // 2
    count = mine_ref.shape[0] // 2
    room = count * rows
    zero, one = is_core(0), is_core(1)
    core = lax.axis_index("sx")
    slots = ((1, 0), (2, 3))
    for frame in range(count):
        for depth in range(2):
            own = mine_ref[2 * frame + depth].astype(jnp.float32)
            other = theirs_ref[2 * frame + depth].astype(jnp.float32)
            own = row_taps(own[rows:], own[rows - 1 : rows], own[:1])
            other = row_taps(other[:rows], other[2 * rows - 1 :], other[rows : rows + 1])
            for swapped, taps in enumerate((own, other)):
                slot = jnp.where(core == swapped, slots[1][depth], slots[0][depth])
                at = pl.multiple_of(slot * room + frame * rows, rows)
                lhs_ref[pl.ds(at, rows)] = taps.astype(lhs_ref.dtype)
    own = mine_ref[2 * count, rows:].astype(jnp.float32)
    other = theirs_ref[2 * count, :rows].astype(jnp.float32)
    start_ref[:rows] = zero * other + one * own
    start_ref[rows:] = zero * own + one * other


def drive_kernel(
    lhs_ref, weight_ref, total_ref, spill_ref, pole_ref, drive_ref, beside_ref, strips_ref, end_ref
):
    count, rows, cols, wide = drive_ref.shape
    room, size = count * rows, rows * cols
    at = size + 2 * rows
    early = None
    for lanes in halves(weight_ref.shape[-1]):
        first = dot(lhs_ref[: 2 * room], weight_ref, 0, lanes)
        middle = dot(lhs_ref[room : 3 * room], weight_ref, 1, lanes)
        last = dot(lhs_ref[2 * room :], weight_ref, 2, lanes)
        left = (spill_ref[0, :, lanes] + first[:room] + middle[:room]).reshape(count, rows, wide)
        right = (spill_ref[1, :, lanes] + middle[room:] + last[room:]).reshape(count, rows, wide)
        total = total_ref[:, :, :, lanes]
        if lanes.start == 0:
            near = total[:, :, 0, :] + first[room:].reshape(count, rows, wide)
            far = total[:, :, cols - 1, :] + last[:room].reshape(count, rows, wide)
            strips = jnp.concatenate([left, near, far, right], axis=1)
            strips_ref[...] = strips
            early = end_state([strips[frame] for frame in range(count)], pole_ref, lanes)
            end_ref[at : at + rows] = early[:rows].astype(end_ref.dtype)
            end_ref[at + rows :] = early[3 * rows :].astype(end_ref.dtype)
            continue
        col = lax.broadcasted_iota(jnp.int32, drive_ref.shape, 2)
        total += jnp.where(col == 0, first[room:].reshape(count, rows, 1, wide), 0.0)
        total += jnp.where(col == cols - 1, last[:room].reshape(count, rows, 1, wide), 0.0)
        drive_ref[...] = total
        state = end_state([total[frame] for frame in range(count)], pole_ref, lanes)
        col = lax.broadcasted_iota(jnp.int32, state.shape, 1)
        state = jnp.where(col == 1, early[rows : 2 * rows].reshape(rows, 1, wide), state)
        border = early[2 * rows : 3 * rows].reshape(rows, 1, wide)
        state = jnp.where(col == cols - 2, border, state)
        end_ref[:size] = state.reshape(size, wide).astype(end_ref.dtype)
        beside = jnp.concatenate([left, right], axis=1)
        beside_ref[...] = beside
        state = end_state([beside[frame] for frame in range(count)], pole_ref, lanes)
        end_ref[size:at] = state.astype(end_ref.dtype)


def spread(block, cols, count, of_lanes):
    _, lanes, inset = block
    value = of_lanes(lanes)
    if inset is None:
        return value
    other, columns = inset
    value, instead = jnp.broadcast_arrays(value, of_lanes(other))
    shape = (count, value.shape[1])
    col = lax.rem(lax.broadcasted_iota(jnp.int32, shape, 0), cols)
    return jnp.where((col == columns[0]) | (col == columns[1]), instead, value)


def entry_kernel(frames, cols, block, ends_ref, pole_ref, out_ref):
    rate = rate_of(pole_ref)
    count = ends_ref.shape[1]
    carried = spread(block, cols, count, lambda lanes: jnp.exp(frames * rate[:, lanes]))
    entry = jnp.zeros(ends_ref.shape[1:], jnp.float32)
    out_ref[0] = entry.astype(out_ref.dtype)
    for index in range(ends_ref.shape[0] - 1):
        entry = carried * entry + ends_ref[index].astype(jnp.float32)
        out_ref[index + 1] = entry.astype(out_ref.dtype)


def exchange(pieces, pole, frames, cols):
    groups = lax.axis_size("tm")
    arrivals = []
    for end, blocks in pieces:
        entries = []
        for block in blocks:
            shares = end[block[0]].reshape(groups, -1, end.shape[1])
            assert block[2] is None or shares.shape[1] % cols == 0
            shares = lax.all_to_all(shares, "tm", 0, 0)
            kernel = functools.partial(entry_kernel, frames, cols, block)
            entry = call(kernel, of(shares.shape, end.dtype), shares, pole)
            entries.append(lax.all_to_all(entry, "tm", 0, 0).reshape(-1, end.shape[1]))
        arrivals.append((jnp.concatenate(entries, axis=0),))
    return arrivals


def pick(values):
    group = lax.axis_index("tm")
    picked = values[-1]
    for index, value in enumerate(values[:-1]):
        picked = jnp.where(group == index, value, picked)
    return picked


def on_core(first, second):
    return jnp.where(lax.axis_index("sx") == 0, first, second)


def weigh(one, by_one, other, by_other):
    return by_one * one.astype(jnp.float32) + by_other * other.astype(jnp.float32)


def relay_kernel(frames, cols, blocks, end_ref, got_ref, pole_ref, out_ref):
    rate = rate_of(pole_ref)
    carried, twice = jnp.exp(frames * rate), jnp.exp(2 * frames * rate)
    none, same = jnp.zeros_like(rate), jnp.ones_like(rate)
    own = on_core(pick([carried, same, same, same]), pick([same, same, same, none]))
    got = on_core(pick([same, carried, carried, carried]), pick([none, none, twice, same]))
    for block in blocks:
        rows = block[0]
        count = rows.stop - rows.start
        by_own = spread(block, cols, count, lambda lanes: own[:, lanes])
        by_got = spread(block, cols, count, lambda lanes: got[:, lanes])
        out_ref[rows] = weigh(end_ref[rows], by_own, got_ref[rows], by_got).astype(out_ref.dtype)


def exchange_four(pieces, pole, frames, cols):
    def along(pairs, core):
        return [(2 * source + core, 2 * target + core) for source, target in pairs]

    axes = ("tm", "sx")
    down = [(0, 2), (1, 3)]
    first_round = along([(0, 1), (1, 0), (2, 3)], 0) + along(down, 1)
    second_round = along(down, 0) + along([(0, 1), (2, 3), (3, 2)], 1)
    arrivals = []
    for end, blocks in pieces:
        got = lax.ppermute(end, axes, first_round)
        kernel = functools.partial(relay_kernel, frames, cols, blocks)
        relayed = call(kernel, of(end.shape, end.dtype), end, got, pole)
        arrivals.append((got, lax.ppermute(relayed, axes, second_round)))
    return arrivals


def gelu(x):
    slope = math.sqrt(2.0 / math.pi)
    half = 0.5 * x
    return half + half * jnp.tanh(x * (slope + (slope * 0.044715) * (x * x)))


class Mix:
    def __init__(self, lanes, count, pole_ref, scale_ref):
        self.rate = rate_of(pole_ref)[:, lanes]
        self.scale = scale_ref[:, lanes]
        self.count = count

    def entry(self, arrived_refs, rows):
        parts = [ref[rows].astype(jnp.float32) for ref in arrived_refs]
        if len(parts) == 1:
            return parts[0]
        carried = jnp.exp(self.count * self.rate)
        none, same = jnp.zeros_like(self.rate), jnp.ones_like(self.rate)
        early = on_core(pick([none, same, none, same]), pick([none, none, carried, carried]))
        late = on_core(pick([none, none, same, carried]), pick([none, same, same, same]))
        return weigh(parts[0], early, parts[1], late)

    def __call__(self, drives, entry, start):
        decay = jnp.exp(self.rate)
        reach = jnp.exp((self.count * lax.axis_index("tm")).astype(jnp.float32) * self.rate)
        state = reach * start + entry.reshape(start.shape)
        for drive in drives:
            state = decay * state + drive
            yield gelu(self.scale * state)


def no_border(cells, axis):
    col = lax.broadcasted_iota(jnp.int32, cells.shape, axis)
    return jnp.where((col == 0) | (col == cells.shape[axis] - 1), 0.0, cells)


def put_back(late, early, axis):
    cols = late.shape[axis]
    col = lax.broadcasted_iota(jnp.int32, late.shape, axis)
    late = jnp.where(col == 1, pltpu.roll(early, 1, axis), late)
    return jnp.where(col == cols - 2, pltpu.roll(early, cols - 1, axis), late)


def mixed_kernel(lanes, rounds, *refs):
    drive_ref, start_ref, pole_ref, scale_ref, *arrived_refs, lhs_ref = refs
    early_refs, late_refs = arrived_refs[:rounds], arrived_refs[rounds:]
    count, rows, cols, _ = drive_ref.shape
    wide = lanes.stop - lanes.start
    size = rows * cols
    stride = lhs_ref.shape[0] // count
    room = (stride - size) // 2
    mix = Mix(lanes, count, pole_ref, scale_ref)
    first = lanes.start == 0
    held = lanes if first else slice(None)
    block = 8
    for row in range(0, rows, block):
        here = slice(row, row + block)
        drives = [drive_ref[frame, here, :, held] for frame in range(count)]
        cells = slice(row * cols, (row + block) * cols)
        entry = mix.entry(early_refs, cells).reshape(block, cols, wide)
        if not first:
            entry = put_back(mix.entry(late_refs, cells).reshape(entry.shape), entry, 1)
        for frame, tile in enumerate(mix(drives, entry, start_ref[here, :, lanes])):
            if first:
                tile = no_border(tile, 1)
            tile = tile.reshape(block * cols, wide).astype(lhs_ref.dtype)
            put_cells(lhs_ref, frame * stride + room, size, cols, row * cols, tile)


def middle_kernel(lanes, *refs):
    total_ref, start_ref, pole_ref, scale_ref, *arrived_refs, give_ref = refs
    count, rows, cols, _ = total_ref.shape
    mix = Mix(lanes, count, pole_ref, scale_ref)
    inner = inner_row(rows)
    drives = [total_ref[frame, inner, :, lanes] for frame in range(count)]
    entry = mix.entry(arrived_refs, pl.ds(pl.multiple_of(inner * cols, cols), cols))
    for frame, cells in enumerate(mix(drives, entry, start_ref[inner, :, lanes])):
        give_ref[frame] = no_border(cells, 0).astype(give_ref.dtype)


def strip_start_kernel(start_ref, sides_ref, out_ref):
    rows, cols, _ = start_ref.shape
    start = start_ref[...]
    out_ref[:rows] = sides_ref[:rows]
    out_ref[rows : 2 * rows] = start[:, 0, :]
    out_ref[2 * rows : 3 * rows] = start[:, cols - 1, :]
    out_ref[3 * rows :] = sides_ref[rows:]


def inside(slot):
    chip, chips = lax.axis_index("sy"), lax.axis_size("sy")
    return {0: (chip > 0).astype(jnp.float32), 3: (chip < chips - 1).astype(jnp.float32)}.get(slot, 1.0)


def give_kernel(parts, rounds, *refs):
    drive_ref, beside_ref, strips_ref, *refs = refs
    start_ref, strip_start_ref, pole_ref, scale_ref, *arrived_refs, give_ref = refs
    early_refs, late_refs = arrived_refs[:rounds], arrived_refs[rounds:]
    count, rows, cols, wide = drive_ref.shape
    size = rows * cols
    inner = inner_row(rows)
    zero, one = is_core(0), is_core(1)
    early, late = (Mix(lanes, count, pole_ref, scale_ref) for lanes in parts)
    row = pl.ds(pl.multiple_of(inner * cols, cols), cols)
    which = lax.broadcasted_iota(jnp.int32, (cols, wide), 0)

    def near(at):
        return pl.ds(pl.multiple_of(at + jnp.where(inner == 0, 0, rows - cols), cols), cols)

    def end(cells):
        return zero * cells[cols - 1 :] + one * cells[:1]

    def rows_of(cells):
        table = jnp.zeros(which.shape, jnp.float32)
        for index, cell in cells:
            table = jnp.where(which == index, cell, table)
        return table

    entry = put_back(late.entry(late_refs, row), late.entry(early_refs, row), 0)
    drives = [drive_ref[frame, inner] for frame in range(count)]
    tile = late(drives, entry, start_ref[inner, :, parts[1]])

    slots = [(0, 0), (1, 3)]
    entry = rows_of([(i, end(late.entry(late_refs, near(size + i * rows)))) for i, _ in slots])
    start = rows_of([(i, end(strip_start_ref[near(slot * rows), parts[1]])) for i, slot in slots])
    drives = [
        rows_of([(i, end(beside_ref[frame, near(i * rows)])) for i, _ in slots])
        for frame in range(count)
    ]
    beside = late(drives, entry, start)

    slots = [(2 + slot, slot) for slot in range(4)]
    grid = early.entry(late_refs, row)
    at = size + 2 * rows
    entry = rows_of(
        [
            (2, end(early.entry(late_refs, near(at)))),
            (3, grid[1:2]),
            (4, grid[cols - 2 : cols - 1]),
            (5, end(early.entry(late_refs, near(at + rows)))),
        ]
    )
    start = rows_of([(i, end(strip_start_ref[near(slot * rows), parts[0]])) for i, slot in slots])
    drives = [
        rows_of([(i, end(strips_ref[frame, near(slot * rows)])) for i, slot in slots])
        for frame in range(count)
    ]
    strips = early(drives, entry, start)
    for frame, cells in enumerate(zip(tile, beside, strips)):
        give_ref[frame, :cols] = cells[0].astype(give_ref.dtype)
        ends = jnp.where(which < 2, cells[1], cells[2])
        ends = jnp.where((which == 0) | (which == 2), inside(0) * ends, ends)
        ends = jnp.where((which == 1) | (which == 5), inside(3) * ends, ends)
        give_ref[frame, cols:] = ends.astype(give_ref.dtype)


def late_kernel(parts, rounds, *refs):
    beside_ref, strips_ref, strip_start_ref, pole_ref, scale_ref, *refs = refs
    *late_refs, beside_out_ref, strips_out_ref = refs
    count, room, wide = beside_ref.shape
    rows = room // 2
    size = late_refs[0].shape[0] - 4 * rows
    cols = size // rows
    early, late = (Mix(lanes, count, pole_ref, scale_ref) for lanes in parts)

    def column(cells, index):
        return cells[index * rows : (index + 1) * rows]

    starts = [strip_start_ref[slot * rows : (slot + 1) * rows, parts[1]] for slot in (0, 3)]
    entry = late.entry(late_refs, slice(size, size + 2 * rows))
    drives = [beside_ref[frame] for frame in range(count)]
    beside = late(drives, entry, jnp.concatenate(starts, axis=0))
    grid = early.entry(late_refs, slice(0, size)).reshape(rows, cols, wide)
    sides = early.entry(late_refs, slice(size + 2 * rows, size + 4 * rows))
    entry = [sides[:rows], grid[:, 1, :], grid[:, cols - 2, :], sides[rows:]]
    drives = [strips_ref[frame] for frame in range(count)]
    strips = early(drives, jnp.concatenate(entry, axis=0), strip_start_ref[:, parts[0]])
    for frame, (sides, strip) in enumerate(zip(beside, strips)):
        sides = [column(sides, 0) * inside(0), column(sides, 1) * inside(3)]
        strip = [column(strip, slot) * inside(slot) for slot in range(4)]
        beside_out_ref[frame] = jnp.concatenate(sides, axis=0).astype(beside_out_ref.dtype)
        strips_out_ref[frame] = jnp.concatenate(strip, axis=0).astype(strips_out_ref.dtype)


def put_columns_taps(lhs_ref, slots, columns, ends):
    rows = columns.shape[0] // len(slots)
    columns, ends = columns.astype(jnp.float32), ends.astype(jnp.float32)
    for index, at in enumerate(slots):
        column, end = columns[index * rows : (index + 1) * rows], ends[index : index + 1]
        lhs_ref[at : at + rows] = row_taps(column, end, end).astype(lhs_ref.dtype)


def tile_sum(tile, inputs, lanes, room, lhs_ref, weight_ref):
    count, rows, cols, wide = tile
    size = rows * cols
    col = lax.broadcasted_iota(jnp.int32, tile[1:], 1)

    def beside(cells):
        return cells.reshape(rows, 1, wide) if room else 0.0

    for frame in range(count):
        at = frame * (size + 2 * room)
        end = at + room + size
        total = dot(lhs_ref[at + room : end], weight_ref, 1, lanes, inputs).reshape(tile[1:])
        first = dot(lhs_ref[at:end], weight_ref, 0, lanes, inputs)
        shifted = pltpu.roll(first[room:].reshape(tile[1:]), 1, 1)
        total += jnp.where(col == 0, beside(first[:room]), shifted)
        last = dot(lhs_ref[at + room : end + room], weight_ref, 2, lanes, inputs)
        shifted = pltpu.roll(last[:size].reshape(tile[1:]), cols - 1, 1)
        yield total + jnp.where(col == cols - 1, beside(last[size:]), shifted)


def strip_sum(tile, inputs, lanes, lhs_ref, weight_ref):
    count, rows, cols, wide = tile
    room = count * rows
    first = dot(lhs_ref[: 2 * room], weight_ref, 0, lanes, inputs)
    middle = dot(lhs_ref[room : 3 * room], weight_ref, 1, lanes, inputs)
    last = dot(lhs_ref[2 * room :], weight_ref, 2, lanes, inputs)
    col = lax.broadcasted_iota(jnp.int32, tile, 2)
    total = 0.0
    for at, cells in (
        (0, first[:room] + middle[:room]),
        (1, first[room:]),
        (cols - 2, last[:room]),
        (cols - 1, middle[room:] + last[room:]),
    ):
        total = jnp.where(col == at, cells.reshape(count, rows, 1, wide), total)
    return total


def opening_kernel(inputs, lanes, _, got_ref, weight_ref, out_ref, lhs_ref):
    count, rows, cols, _ = out_ref.shape
    size = rows * cols
    for frame in range(count):
        put_row(lhs_ref, frame * size, size, got_ref[frame])
    further_kernel(inputs, lanes, lhs_ref, weight_ref, out_ref)


def further_kernel(inputs, lanes, lhs_ref, weight_ref, out_ref):
    tiles = tile_sum(out_ref.shape, inputs, lanes, 0, lhs_ref, weight_ref)
    for frame, total in enumerate(tiles):
        out_ref[frame] = total


def result_kernel(
    parts, _, got_ref, beside_ref, strips_ref, weight_ref, *refs
):
    *before_refs, out_ref, lhs_ref, held_ref, strip_lhs_ref, sems = refs
    count, rows, cols, _ = held_ref.shape
    size, room = rows * cols, count * rows
    stride = size + 2 * rows
    for frame in range(count):
        at = frame * stride
        put_row(lhs_ref, at + rows, size, got_ref[frame, :cols])
        ends = got_ref[frame, cols:]
        put_columns_taps(lhs_ref, (at, at + rows + size), beside_ref[frame], ends)
        slots = [slot * room + frame * rows for slot in range(4)]
        put_columns_taps(strip_lhs_ref, slots, strips_ref[frame], ends.astype(jnp.float32)[2:])

    def store(frame, part):
        here = (frame, slice(None), slice(None), parts[part])
        return pltpu.make_async_copy(held_ref.at[here], out_ref.at[here], sems.at[frame, part])

    for part, lanes in enumerate(parts):
        tile = (count, rows, cols, lanes.stop - lanes.start)
        strips = strip_sum(tile, parts[0], lanes, strip_lhs_ref, weight_ref)
        tiles = tile_sum(tile, parts[1], lanes, rows, lhs_ref, weight_ref)
        for frame, total in enumerate(tiles):
            total += before_refs[part][frame] + strips[frame]
            held_ref[frame, :, :, lanes] = total.astype(held_ref.dtype)
            store(frame, part).start()
    for part in range(len(parts)):
        for frame in range(count):
            store(frame, part).wait()


def on_device(frames, input_weight, output_weight, pole_index, gelu_scale, start_state):
    count, rows, cols, channels = frames.shape
    size, room = rows * cols, count * rows
    wide = 3 * channels
    assert lax.axis_size("sx") == 2
    narrow = frames.dtype
    pole, scale = pole_index[None], gelu_scale[None]

    shapes = (
        of((count * cols + (2 * count + 1) * rows, channels), narrow),
        of((2 * count + 1, rows, channels), narrow),
    )
    edges = call(
        edges_kernel,
        shapes,
        frames,
        scratch=[pltpu.VMEM((count, channels // 128, size, 128), jnp.float32)],
        flops=EDGES_COST,
    )
    give, keep = call(
        start_edges_kernel,
        shapes,
        start_state,
        *edges,
        aliases={1: 0, 2: 1},
        scratch=[pltpu.VMEM((channels // 128, size, 128), jnp.float32)],
    )
    got, mine = trade_columns(give, keep, count * cols)
    taps = of((count * size, wide), narrow)
    parts = halves(channels)
    half = channels // 2
    inner = of((count, rows, cols, half), jnp.float32)
    *main, early, _ = call(
        main_kernel,
        (
            of(frames.shape, jnp.float32),
            of((2, room, channels), jnp.float32),
            of((size, half), narrow),
            taps,
        ),
        call(taps_kernel, taps, frames),
        got,
        input_weight,
        pole,
        aliases={0: 3},
        flops=18 * frames.size * channels,
    )
    mine, total, spill = lax.optimization_barrier((mine, *main))
    halo, sides = call(
        halo_kernel,
        (of((4 * room, wide), narrow), of((2 * rows, channels), jnp.float32)),
        mine,
        swap_cores(mine),
    )
    drive, beside, strips, late = call(
        drive_kernel,
        (
            inner,
            of((count, 2 * rows, half), jnp.float32),
            of((count, 4 * rows, half), jnp.float32),
            of((size + 4 * rows, half), narrow),
        ),
        halo,
        input_weight,
        total,
        spill,
        pole,
        flops=36 * room * channels * channels,
    )
    at = size + 2 * rows
    tile = slice(0, size)
    pieces = [
        (early, [(tile, parts[0], (parts[1], (0, cols - 1)))]),
        (
            late,
            [
                (tile, parts[1], (parts[0], (1, cols - 2))),
                (slice(size, at), parts[1], None),
                (slice(at, at + 2 * rows), parts[0], None),
            ],
        ),
    ]
    exchanged = exchange_four if lax.axis_size("tm") == 4 else exchange
    early, late = exchanged(pieces, pole, count, cols)
    rounds = len(early)

    mixing = (start_state, pole, scale)
    taps = of((count * size, 3 * half), narrow)
    give = call(
        functools.partial(middle_kernel, parts[0]),
        of((count, cols, half), narrow),
        total,
        *mixing,
        *early,
    )
    lhs = call(functools.partial(mixed_kernel, parts[0], rounds), taps, total, *mixing, *early)
    strip_start = call(strip_start_kernel, of((4 * rows, channels), jnp.float32), start_state, sides)
    flops = 18 * inner.size * half
    lhs, strip_start = lax.optimization_barrier((lhs, strip_start))
    first_sum, lhs = call(
        functools.partial(opening_kernel, parts[0], parts[0]),
        (inner, taps),
        lhs,
        swap_cores(give),
        output_weight,
        aliases={0: 1},
        flops=flops,
    )
    second_sum = call(
        functools.partial(further_kernel, parts[0], parts[1]),
        inner,
        lhs,
        output_weight,
        flops=flops,
    )
    *late, first_sum, second_sum = lax.optimization_barrier((*late, first_sum, second_sum))
    give = call(
        functools.partial(give_kernel, parts, rounds),
        of((count, 2 * cols, half), narrow),
        drive,
        beside,
        strips,
        start_state,
        strip_start,
        pole,
        scale,
        *early,
        *late,
    )
    beside, strips = call(
        functools.partial(late_kernel, parts, rounds),
        (of(beside.shape, narrow), of(strips.shape, narrow)),
        beside,
        strips,
        strip_start,
        pole,
        scale,
        *late,
    )
    taps = of((count * size + 2 * room, 3 * half), narrow)
    lhs = call(
        functools.partial(mixed_kernel, parts[1], rounds), taps, drive, *mixing, *early, *late
    )
    result, _ = call(
        functools.partial(result_kernel, parts),
        (of(frames.shape, narrow), taps),
        lhs,
        swap_cores(give),
        beside,
        strips,
        output_weight,
        first_sum,
        second_sum,
        out_specs=(HBM, WHOLE),
        aliases={0: 1},
        scratch=[
            pltpu.VMEM(frames.shape, narrow),
            pltpu.VMEM((4 * room, 3 * half), narrow),
            pltpu.SemaphoreType.DMA((count, len(parts))),
        ],
        flops=2 * flops,
    )
    return result


def solution(mesh):
    return jax.shard_map(
        on_device,
        mesh=mesh,
        in_specs=(P("tm", "sx", "sy", None), P(), P(), P(), P(), P("sx", "sy", None)),
        out_specs=P("tm", "sx", "sy", None),
        check_vma=False,
    )
```

```python
import functools
import math

import jax
import jax.numpy as jnp
from jax import lax
from jax.experimental import pallas as pl
from jax.experimental.pallas import tpu as pltpu
from jax.sharding import PartitionSpec as P

NPOLES = 16
VMEM_LIMIT = 24 * 1024 * 1024
WHOLE = pl.BlockSpec(memory_space=pltpu.VMEM)
HBM = pl.BlockSpec(memory_space=pltpu.HBM)
EDGES_COST = 2_000_000_000


def call(kernel, out_shape, *args, scratch=(), flops=0, out_specs=None, aliases=None):
    outs = jax.tree.leaves(out_shape)
    moved = sum(leaf.size * leaf.dtype.itemsize for leaf in (*args, *outs))
    return pl.pallas_call(
        kernel,
        in_specs=[WHOLE] * len(args),
        out_specs=out_specs or jax.tree.map(lambda _: WHOLE, out_shape),
        out_shape=out_shape,
        scratch_shapes=scratch,
        input_output_aliases=aliases or {},
        compiler_params=pltpu.CompilerParams(vmem_limit_bytes=VMEM_LIMIT),
        cost_estimate=pl.CostEstimate(flops=flops, bytes_accessed=moved, transcendentals=0),
    )(*args)


def of(shape, dtype):
    return jax.ShapeDtypeStruct(shape, dtype)


def is_core(which):
    return (lax.axis_index("sx") == which).astype(jnp.float32)


def rate_of(pole_ref):
    pole = pole_ref[...].astype(jnp.float32)
    return -0.001 * jnp.exp(pole * (math.log(300.0) / (NPOLES - 1)))


def inner_row(rows):
    return jnp.where(lax.axis_index("sx") == 0, rows - 1, 0)


def swap_cores(array):
    return lax.ppermute(array, "sx", [(0, 1), (1, 0)])


def put_columns(index, left, right, give_ref, keep_ref):
    zero, one = is_core(0), is_core(1)
    count, rows, _ = keep_ref.shape
    at = give_ref.shape[0] - (count - index) * rows
    give_ref[at : at + rows] = (zero * left + one * right).astype(give_ref.dtype)
    keep_ref[index] = (zero * right + one * left).astype(keep_ref.dtype)


def columns_of(tile, wide_ref, picked):
    rows, cols, channels = tile.shape
    parts, _, lanes = wide_ref.shape
    tile = tile.reshape(rows * cols, channels)
    for part in range(parts):
        wide_ref[part] = tile[:, part * lanes : (part + 1) * lanes]
    return [
        jnp.concatenate(
            [wide_ref[part, pl.ds(col, rows, stride=cols), :] for part in range(parts)], axis=1
        )
        for col in picked
    ]


def edges_kernel(cells_ref, give_ref, keep_ref, wide_ref):
    count, rows, cols, channels = cells_ref.shape
    for frame in range(count):
        give_ref[frame * cols : (frame + 1) * cols] = cells_ref[frame, inner_row(rows)]
        tile = cells_ref[frame].astype(jnp.float32)
        picked = (0, 1, cols - 1, cols - 2)
        columns = columns_of(tile, wide_ref.at[frame], picked)
        for depth in range(2):
            left, right = columns[depth], columns[2 + depth]
            put_columns(2 * frame + depth, left, right, give_ref, keep_ref)


def start_edges_kernel(start_ref, _, __, give_ref, keep_ref, wide_ref):
    cols = start_ref.shape[1]
    left, right = columns_of(start_ref[...], wide_ref, (0, cols - 1))
    put_columns(keep_ref.shape[0] - 1, left, right, give_ref, keep_ref)


def trade_columns(give, keep, at):
    chips = lax.axis_size("sy")
    got = swap_cores(give)
    pairs = [(chip, chips + chip + 1) for chip in range(chips - 1)]
    pairs += [(after, before) for before, after in pairs]
    columns = jnp.concatenate([keep, got[at:].reshape(keep.shape)], axis=1)
    return got, lax.ppermute(columns, ("sx", "sy"), pairs)


def put_cells(lhs_ref, at, size, cols, first, cells):
    count, channels = cells.shape
    upper, lower = min(count, size - cols - first), max(0, cols - first)
    here = at + first
    lhs_ref[here : here + count, channels : 2 * channels] = cells
    lhs_ref[here + cols : here + cols + upper, :channels] = cells[:upper]
    lhs_ref[here + lower - cols : here + count - cols, 2 * channels :] = cells[lower:]


def put_row(lhs_ref, at, size, row):
    cols, channels = row.shape
    row = row.astype(jnp.float32)
    last = slice(at + size - cols, at + size)
    lhs_ref[at : at + cols, :channels] = (is_core(1) * row).astype(lhs_ref.dtype)
    lhs_ref[last, 2 * channels :] = (is_core(0) * row).astype(lhs_ref.dtype)


def taps_kernel(cells_ref, lhs_ref):
    count, rows, cols, channels = cells_ref.shape
    size = rows * cols
    for frame in range(count):
        put_cells(lhs_ref, frame * size, size, cols, 0, cells_ref[frame].reshape(size, channels))


def row_taps(column, above, below):
    rows = column.shape[0]
    row = lax.broadcasted_iota(jnp.int32, column.shape, 0)
    up = jnp.where(row == 0, is_core(1) * above, pltpu.roll(column, 1, 0))
    down = jnp.where(row == rows - 1, is_core(0) * below, pltpu.roll(column, rows - 1, 0))
    return jnp.concatenate([up, column, down], axis=1)


SLAB = 8


def halves(channels):
    return slice(0, channels // 2), slice(channels // 2, channels)


def end_state(frames, pole_ref, lanes):
    decay = jnp.exp(rate_of(pole_ref))[:, lanes]
    state = frames[0]
    for frame in frames[1:]:
        state = decay * state + frame
    return state


def dot(lhs, weight_ref, column, lanes, inputs=slice(None)):
    weight = weight_ref[:, column, inputs, lanes].reshape(lhs.shape[1], -1)
    return jnp.dot(lhs, weight, preferred_element_type=jnp.float32)


def main_kernel(_, got_ref, weight_ref, pole_ref, total_ref, spill_ref, end_ref, lhs_ref):
    count, rows, cols, _ = total_ref.shape
    size = rows * cols
    for frame in range(count):
        put_row(lhs_ref, frame * size, size, got_ref[frame * cols : (frame + 1) * cols])
    states = []
    for lanes in halves(weight_ref.shape[-1]):
        tile = (rows, cols, lanes.stop - lanes.start)
        col = lax.broadcasted_iota(jnp.int32, tile, 1)
        totals = []
        for frame in range(count):
            cells = lhs_ref[frame * size : (frame + 1) * size]
            here = slice(frame * rows, (frame + 1) * rows)
            total = dot(cells, weight_ref, 1, lanes).reshape(tile)
            first = dot(cells, weight_ref, 0, lanes).reshape(tile)
            spill_ref[1, here, lanes] = first[:, cols - 1, :]
            total += jnp.where(col == 0, 0.0, pltpu.roll(first, 1, 1))
            last = dot(cells, weight_ref, 2, lanes).reshape(tile)
            spill_ref[0, here, lanes] = last[:, 0, :]
            total += jnp.where(col == cols - 1, 0.0, pltpu.roll(last, cols - 1, 1))
            total_ref[frame, :, :, lanes] = total
            totals.append(total)
        states.append(end_state(totals, pole_ref, lanes))
    state, other = states
    col = lax.broadcasted_iota(jnp.int32, (rows, SLAB, state.shape[2]), 1)
    last = slice(cols - SLAB, cols)
    left = jnp.where(col == 0, pltpu.roll(other[:, :SLAB], SLAB - 1, 1), state[:, :SLAB])
    right = jnp.where(col == SLAB - 1, pltpu.roll(other[:, last], 1, 1), state[:, last])
    middle = [state[:, SLAB : cols - SLAB]] if cols > 2 * SLAB else []
    state = jnp.concatenate([left, *middle, right], axis=1)
    end_ref[...] = state.reshape(end_ref.shape).astype(end_ref.dtype)


def halo_kernel(mine_ref, theirs_ref, lhs_ref, start_ref):
    rows = mine_ref.shape[1] // 2
    count = mine_ref.shape[0] // 2
    room = count * rows
    zero, one = is_core(0), is_core(1)
    core = lax.axis_index("sx")
    slots = ((1, 0), (2, 3))
    for frame in range(count):
        for depth in range(2):
            own = mine_ref[2 * frame + depth].astype(jnp.float32)
            other = theirs_ref[2 * frame + depth].astype(jnp.float32)
            own = row_taps(own[rows:], own[rows - 1 : rows], own[:1])
            other = row_taps(other[:rows], other[2 * rows - 1 :], other[rows : rows + 1])
            for swapped, taps in enumerate((own, other)):
                slot = jnp.where(core == swapped, slots[1][depth], slots[0][depth])
                at = pl.multiple_of(slot * room + frame * rows, rows)
                lhs_ref[pl.ds(at, rows)] = taps.astype(lhs_ref.dtype)
    own = mine_ref[2 * count, rows:].astype(jnp.float32)
    other = theirs_ref[2 * count, :rows].astype(jnp.float32)
    start_ref[:rows] = zero * other + one * own
    start_ref[rows:] = zero * own + one * other


def drive_kernel(
    lhs_ref, weight_ref, total_ref, spill_ref, pole_ref, drive_ref, beside_ref, strips_ref, end_ref
):
    count, rows, cols, wide = drive_ref.shape
    room, size = count * rows, rows * cols
    at = size + 2 * rows
    early = None
    for lanes in halves(weight_ref.shape[-1]):
        first = dot(lhs_ref[: 2 * room], weight_ref, 0, lanes)
        middle = dot(lhs_ref[room : 3 * room], weight_ref, 1, lanes)
        last = dot(lhs_ref[2 * room :], weight_ref, 2, lanes)
        left = (spill_ref[0, :, lanes] + first[:room] + middle[:room]).reshape(count, rows, wide)
        right = (spill_ref[1, :, lanes] + middle[room:] + last[room:]).reshape(count, rows, wide)
        total = total_ref[:, :, :, lanes]
        if lanes.start == 0:
            near = total[:, :, 0, :] + first[room:].reshape(count, rows, wide)
            far = total[:, :, cols - 1, :] + last[:room].reshape(count, rows, wide)
            strips = jnp.concatenate([left, near, far, right], axis=1)
            strips_ref[...] = strips
            early = end_state([strips[frame] for frame in range(count)], pole_ref, lanes)
            end_ref[at : at + rows] = early[:rows].astype(end_ref.dtype)
            end_ref[at + rows :] = early[3 * rows :].astype(end_ref.dtype)
            continue
        col = lax.broadcasted_iota(jnp.int32, drive_ref.shape, 2)
        total += jnp.where(col == 0, first[room:].reshape(count, rows, 1, wide), 0.0)
        total += jnp.where(col == cols - 1, last[:room].reshape(count, rows, 1, wide), 0.0)
        drive_ref[...] = total
        state = end_state([total[frame] for frame in range(count)], pole_ref, lanes)
        col = lax.broadcasted_iota(jnp.int32, state.shape, 1)
        state = jnp.where(col == 1, early[rows : 2 * rows].reshape(rows, 1, wide), state)
        border = early[2 * rows : 3 * rows].reshape(rows, 1, wide)
        state = jnp.where(col == cols - 2, border, state)
        end_ref[:size] = state.reshape(size, wide).astype(end_ref.dtype)
        beside = jnp.concatenate([left, right], axis=1)
        beside_ref[...] = beside
        state = end_state([beside[frame] for frame in range(count)], pole_ref, lanes)
        end_ref[size:at] = state.astype(end_ref.dtype)


def spread(block, cols, count, of_lanes):
    _, lanes, inset = block
    value = of_lanes(lanes)
    if inset is None:
        return value
    other, columns = inset
    value, instead = jnp.broadcast_arrays(value, of_lanes(other))
    shape = (count, value.shape[1])
    col = lax.rem(lax.broadcasted_iota(jnp.int32, shape, 0), cols)
    return jnp.where((col == columns[0]) | (col == columns[1]), instead, value)


def entry_kernel(frames, cols, block, ends_ref, pole_ref, out_ref):
    rate = rate_of(pole_ref)
    count = ends_ref.shape[1]
    carried = spread(block, cols, count, lambda lanes: jnp.exp(frames * rate[:, lanes]))
    entry = jnp.zeros(ends_ref.shape[1:], jnp.float32)
    out_ref[0] = entry.astype(out_ref.dtype)
    for index in range(ends_ref.shape[0] - 1):
        entry = carried * entry + ends_ref[index].astype(jnp.float32)
        out_ref[index + 1] = entry.astype(out_ref.dtype)


def exchange(pieces, pole, frames, cols):
    groups = lax.axis_size("tm")
    arrivals = []
    for end, blocks in pieces:
        entries = []
        for block in blocks:
            shares = end[block[0]].reshape(groups, -1, end.shape[1])
            assert block[2] is None or shares.shape[1] % cols == 0
            shares = lax.all_to_all(shares, "tm", 0, 0)
            kernel = functools.partial(entry_kernel, frames, cols, block)
            entry = call(kernel, of(shares.shape, end.dtype), shares, pole)
            entries.append(lax.all_to_all(entry, "tm", 0, 0).reshape(-1, end.shape[1]))
        arrivals.append((jnp.concatenate(entries, axis=0),))
    return arrivals


def pick(values):
    group = lax.axis_index("tm")
    picked = values[-1]
    for index, value in enumerate(values[:-1]):
        picked = jnp.where(group == index, value, picked)
    return picked


def on_core(first, second):
    return jnp.where(lax.axis_index("sx") == 0, first, second)


def weigh(one, by_one, other, by_other):
    return by_one * one.astype(jnp.float32) + by_other * other.astype(jnp.float32)


def relay_kernel(frames, cols, blocks, end_ref, got_ref, pole_ref, out_ref):
    rate = rate_of(pole_ref)
    carried, twice = jnp.exp(frames * rate), jnp.exp(2 * frames * rate)
    none, same = jnp.zeros_like(rate), jnp.ones_like(rate)
    own = on_core(pick([carried, same, same, same]), pick([same, same, same, none]))
    got = on_core(pick([same, carried, carried, carried]), pick([none, none, twice, same]))
    for block in blocks:
        rows = block[0]
        count = rows.stop - rows.start
        by_own = spread(block, cols, count, lambda lanes: own[:, lanes])
        by_got = spread(block, cols, count, lambda lanes: got[:, lanes])
        out_ref[rows] = weigh(end_ref[rows], by_own, got_ref[rows], by_got).astype(out_ref.dtype)


def exchange_four(pieces, pole, frames, cols):
    def along(pairs, core):
        return [(2 * source + core, 2 * target + core) for source, target in pairs]

    axes = ("tm", "sx")
    down = [(0, 2), (1, 3)]
    first_round = along([(0, 1), (1, 0), (2, 3)], 0) + along(down, 1)
    second_round = along(down, 0) + along([(0, 1), (2, 3), (3, 2)], 1)
    arrivals = []
    for end, blocks in pieces:
        got = lax.ppermute(end, axes, first_round)
        kernel = functools.partial(relay_kernel, frames, cols, blocks)
        relayed = call(kernel, of(end.shape, end.dtype), end, got, pole)
        arrivals.append((got, lax.ppermute(relayed, axes, second_round)))
    return arrivals


def gelu(x):
    slope = math.sqrt(2.0 / math.pi)
    half = 0.5 * x
    return half + half * jnp.tanh(x * (slope + (slope * 0.044715) * (x * x)))


class Mix:
    def __init__(self, lanes, count, pole_ref, scale_ref):
        self.rate = rate_of(pole_ref)[:, lanes]
        self.scale = scale_ref[:, lanes]
        self.count = count

    def entry(self, arrived_refs, rows):
        parts = [ref[rows].astype(jnp.float32) for ref in arrived_refs]
        if len(parts) == 1:
            return parts[0]
        carried = jnp.exp(self.count * self.rate)
        none, same = jnp.zeros_like(self.rate), jnp.ones_like(self.rate)
        early = on_core(pick([none, same, none, same]), pick([none, none, carried, carried]))
        late = on_core(pick([none, none, same, carried]), pick([none, same, same, same]))
        return weigh(parts[0], early, parts[1], late)

    def __call__(self, drives, entry, start):
        decay = jnp.exp(self.rate)
        reach = jnp.exp((self.count * lax.axis_index("tm")).astype(jnp.float32) * self.rate)
        state = reach * start + entry.reshape(start.shape)
        for drive in drives:
            state = decay * state + drive
            yield gelu(self.scale * state)


def no_border(cells, axis):
    col = lax.broadcasted_iota(jnp.int32, cells.shape, axis)
    return jnp.where((col == 0) | (col == cells.shape[axis] - 1), 0.0, cells)


def put_back(late, early, axis):
    cols = late.shape[axis]

    def slab(cells, start):
        return lax.slice_in_dim(cells, start, start + SLAB, axis=axis)

    first, last = slab(late, 0), slab(late, cols - SLAB)
    col = lax.broadcasted_iota(jnp.int32, first.shape, axis)
    first = jnp.where(col == 1, pltpu.roll(slab(early, 0), 1, axis), first)
    moved = pltpu.roll(slab(early, cols - SLAB), SLAB - 1, axis)
    last = jnp.where(col == SLAB - 2, moved, last)
    middle = [lax.slice_in_dim(late, SLAB, cols - SLAB, axis=axis)] if cols > 2 * SLAB else []
    return jnp.concatenate([first, *middle, last], axis=axis)


def mixed_kernel(lanes, rounds, *refs):
    drive_ref, start_ref, pole_ref, scale_ref, *arrived_refs, lhs_ref = refs
    early_refs, late_refs = arrived_refs[:rounds], arrived_refs[rounds:]
    count, rows, cols, _ = drive_ref.shape
    wide = lanes.stop - lanes.start
    size = rows * cols
    stride = lhs_ref.shape[0] // count
    room = (stride - size) // 2
    mix = Mix(lanes, count, pole_ref, scale_ref)
    first = lanes.start == 0
    held = lanes if first else slice(None)
    block = 8
    for row in range(0, rows, block):
        here = slice(row, row + block)
        drives = [drive_ref[frame, here, :, held] for frame in range(count)]
        cells = slice(row * cols, (row + block) * cols)
        entry = mix.entry(early_refs, cells).reshape(block, cols, wide)
        if not first:
            entry = put_back(mix.entry(late_refs, cells).reshape(entry.shape), entry, 1)
        for frame, tile in enumerate(mix(drives, entry, start_ref[here, :, lanes])):
            if first:
                tile = no_border(tile, 1)
            tile = tile.reshape(block * cols, wide).astype(lhs_ref.dtype)
            put_cells(lhs_ref, frame * stride + room, size, cols, row * cols, tile)


def middle_kernel(lanes, *refs):
    total_ref, start_ref, pole_ref, scale_ref, *arrived_refs, give_ref = refs
    count, rows, cols, _ = total_ref.shape
    mix = Mix(lanes, count, pole_ref, scale_ref)
    inner = inner_row(rows)
    drives = [total_ref[frame, inner, :, lanes] for frame in range(count)]
    entry = mix.entry(arrived_refs, pl.ds(pl.multiple_of(inner * cols, cols), cols))
    for frame, cells in enumerate(mix(drives, entry, start_ref[inner, :, lanes])):
        give_ref[frame] = no_border(cells, 0).astype(give_ref.dtype)


def strip_start_kernel(start_ref, sides_ref, out_ref):
    rows, cols, _ = start_ref.shape
    start = start_ref[...]
    out_ref[:rows] = sides_ref[:rows]
    out_ref[rows : 2 * rows] = start[:, 0, :]
    out_ref[2 * rows : 3 * rows] = start[:, cols - 1, :]
    out_ref[3 * rows :] = sides_ref[rows:]


def inside(slot):
    chip, chips = lax.axis_index("sy"), lax.axis_size("sy")
    return {0: (chip > 0).astype(jnp.float32), 3: (chip < chips - 1).astype(jnp.float32)}.get(slot, 1.0)


def give_kernel(parts, rounds, *refs):
    drive_ref, beside_ref, strips_ref, *refs = refs
    start_ref, strip_start_ref, pole_ref, scale_ref, *arrived_refs, give_ref = refs
    early_refs, late_refs = arrived_refs[:rounds], arrived_refs[rounds:]
    count, rows, cols, wide = drive_ref.shape
    size = rows * cols
    inner = inner_row(rows)
    zero, one = is_core(0), is_core(1)
    early, late = (Mix(lanes, count, pole_ref, scale_ref) for lanes in parts)
    row = pl.ds(pl.multiple_of(inner * cols, cols), cols)
    which = lax.broadcasted_iota(jnp.int32, (cols, wide), 0)

    def near(at):
        return pl.ds(pl.multiple_of(at + jnp.where(inner == 0, 0, rows - cols), cols), cols)

    def end(cells):
        return zero * cells[cols - 1 :] + one * cells[:1]

    def rows_of(cells):
        table = jnp.zeros(which.shape, jnp.float32)
        for index, cell in cells:
            table = jnp.where(which == index, cell, table)
        return table

    entry = put_back(late.entry(late_refs, row), late.entry(early_refs, row), 0)
    drives = [drive_ref[frame, inner] for frame in range(count)]
    tile = late(drives, entry, start_ref[inner, :, parts[1]])

    slots = [(0, 0), (1, 3)]
    entry = rows_of([(i, end(late.entry(late_refs, near(size + i * rows)))) for i, _ in slots])
    start = rows_of([(i, end(strip_start_ref[near(slot * rows), parts[1]])) for i, slot in slots])
    drives = [
        rows_of([(i, end(beside_ref[frame, near(i * rows)])) for i, _ in slots])
        for frame in range(count)
    ]
    beside = late(drives, entry, start)

    slots = [(2 + slot, slot) for slot in range(4)]
    grid = early.entry(late_refs, row)
    at = size + 2 * rows
    entry = rows_of(
        [
            (2, end(early.entry(late_refs, near(at)))),
            (3, grid[1:2]),
            (4, grid[cols - 2 : cols - 1]),
            (5, end(early.entry(late_refs, near(at + rows)))),
        ]
    )
    start = rows_of([(i, end(strip_start_ref[near(slot * rows), parts[0]])) for i, slot in slots])
    drives = [
        rows_of([(i, end(strips_ref[frame, near(slot * rows)])) for i, slot in slots])
        for frame in range(count)
    ]
    strips = early(drives, entry, start)
    for frame, cells in enumerate(zip(tile, beside, strips)):
        give_ref[frame, :cols] = cells[0].astype(give_ref.dtype)
        ends = jnp.where(which < 2, cells[1], cells[2])
        ends = jnp.where((which == 0) | (which == 2), inside(0) * ends, ends)
        ends = jnp.where((which == 1) | (which == 5), inside(3) * ends, ends)
        give_ref[frame, cols:] = ends.astype(give_ref.dtype)


def late_kernel(parts, rounds, *refs):
    beside_ref, strips_ref, strip_start_ref, pole_ref, scale_ref, *refs = refs
    *late_refs, beside_out_ref, strips_out_ref = refs
    count, room, wide = beside_ref.shape
    rows = room // 2
    size = late_refs[0].shape[0] - 4 * rows
    cols = size // rows
    early, late = (Mix(lanes, count, pole_ref, scale_ref) for lanes in parts)

    def column(cells, index):
        return cells[index * rows : (index + 1) * rows]

    starts = [strip_start_ref[slot * rows : (slot + 1) * rows, parts[1]] for slot in (0, 3)]
    entry = late.entry(late_refs, slice(size, size + 2 * rows))
    drives = [beside_ref[frame] for frame in range(count)]
    beside = late(drives, entry, jnp.concatenate(starts, axis=0))
    grid = early.entry(late_refs, slice(0, size)).reshape(rows, cols, wide)
    sides = early.entry(late_refs, slice(size + 2 * rows, size + 4 * rows))
    entry = [sides[:rows], grid[:, 1, :], grid[:, cols - 2, :], sides[rows:]]
    drives = [strips_ref[frame] for frame in range(count)]
    strips = early(drives, jnp.concatenate(entry, axis=0), strip_start_ref[:, parts[0]])
    for frame, (sides, strip) in enumerate(zip(beside, strips)):
        sides = [column(sides, 0) * inside(0), column(sides, 1) * inside(3)]
        strip = [column(strip, slot) * inside(slot) for slot in range(4)]
        beside_out_ref[frame] = jnp.concatenate(sides, axis=0).astype(beside_out_ref.dtype)
        strips_out_ref[frame] = jnp.concatenate(strip, axis=0).astype(strips_out_ref.dtype)


def put_columns_taps(lhs_ref, slots, columns, ends):
    rows = columns.shape[0] // len(slots)
    columns, ends = columns.astype(jnp.float32), ends.astype(jnp.float32)
    for index, at in enumerate(slots):
        column, end = columns[index * rows : (index + 1) * rows], ends[index : index + 1]
        lhs_ref[at : at + rows] = row_taps(column, end, end).astype(lhs_ref.dtype)


def tile_sum(tile, inputs, lanes, room, lhs_ref, weight_ref):
    count, rows, cols, wide = tile
    size = rows * cols
    col = lax.broadcasted_iota(jnp.int32, tile[1:], 1)

    def beside(cells):
        return cells.reshape(rows, 1, wide) if room else 0.0

    for frame in range(count):
        at = frame * (size + 2 * room)
        end = at + room + size
        total = dot(lhs_ref[at + room : end], weight_ref, 1, lanes, inputs).reshape(tile[1:])
        first = dot(lhs_ref[at:end], weight_ref, 0, lanes, inputs)
        shifted = pltpu.roll(first[room:].reshape(tile[1:]), 1, 1)
        total += jnp.where(col == 0, beside(first[:room]), shifted)
        last = dot(lhs_ref[at + room : end + room], weight_ref, 2, lanes, inputs)
        shifted = pltpu.roll(last[:size].reshape(tile[1:]), cols - 1, 1)
        yield total + jnp.where(col == cols - 1, beside(last[size:]), shifted)


def strip_sum(tile, inputs, lanes, lhs_ref, weight_ref):
    count, rows, cols, wide = tile
    room = count * rows
    first = dot(lhs_ref[: 2 * room], weight_ref, 0, lanes, inputs)
    middle = dot(lhs_ref[room : 3 * room], weight_ref, 1, lanes, inputs)
    last = dot(lhs_ref[2 * room :], weight_ref, 2, lanes, inputs)
    col = lax.broadcasted_iota(jnp.int32, tile, 2)
    total = 0.0
    for at, cells in (
        (0, first[:room] + middle[:room]),
        (1, first[room:]),
        (cols - 2, last[:room]),
        (cols - 1, middle[room:] + last[room:]),
    ):
        total = jnp.where(col == at, cells.reshape(count, rows, 1, wide), total)
    return total


def opening_kernel(inputs, lanes, _, got_ref, weight_ref, out_ref, lhs_ref):
    count, rows, cols, _ = out_ref.shape
    size = rows * cols
    for frame in range(count):
        put_row(lhs_ref, frame * size, size, got_ref[frame])
    further_kernel(inputs, lanes, lhs_ref, weight_ref, out_ref)


def further_kernel(inputs, lanes, lhs_ref, weight_ref, out_ref):
    tiles = tile_sum(out_ref.shape, inputs, lanes, 0, lhs_ref, weight_ref)
    for frame, total in enumerate(tiles):
        out_ref[frame] = total


def result_kernel(
    parts, _, got_ref, beside_ref, strips_ref, weight_ref, *refs
):
    *before_refs, out_ref, lhs_ref, held_ref, strip_lhs_ref, sems = refs
    count, rows, cols, _ = held_ref.shape
    size, room = rows * cols, count * rows
    stride = size + 2 * rows
    for frame in range(count):
        at = frame * stride
        put_row(lhs_ref, at + rows, size, got_ref[frame, :cols])
        ends = got_ref[frame, cols:]
        put_columns_taps(lhs_ref, (at, at + rows + size), beside_ref[frame], ends)
        slots = [slot * room + frame * rows for slot in range(4)]
        put_columns_taps(strip_lhs_ref, slots, strips_ref[frame], ends.astype(jnp.float32)[2:])

    def store(frame, part):
        here = (frame, slice(None), slice(None), parts[part])
        return pltpu.make_async_copy(held_ref.at[here], out_ref.at[here], sems.at[frame, part])

    for part, lanes in enumerate(parts):
        tile = (count, rows, cols, lanes.stop - lanes.start)
        strips = strip_sum(tile, parts[0], lanes, strip_lhs_ref, weight_ref)
        tiles = tile_sum(tile, parts[1], lanes, rows, lhs_ref, weight_ref)
        for frame, total in enumerate(tiles):
            total += before_refs[part][frame] + strips[frame]
            held_ref[frame, :, :, lanes] = total.astype(held_ref.dtype)
            store(frame, part).start()
    for part in range(len(parts)):
        for frame in range(count):
            store(frame, part).wait()


def on_device(frames, input_weight, output_weight, pole_index, gelu_scale, start_state):
    count, rows, cols, channels = frames.shape
    size, room = rows * cols, count * rows
    wide = 3 * channels
    assert lax.axis_size("sx") == 2
    narrow = frames.dtype
    pole, scale = pole_index[None], gelu_scale[None]

    shapes = (
        of((count * cols + (2 * count + 1) * rows, channels), narrow),
        of((2 * count + 1, rows, channels), narrow),
    )
    edges = call(
        edges_kernel,
        shapes,
        frames,
        scratch=[pltpu.VMEM((count, channels // 128, size, 128), jnp.float32)],
        flops=EDGES_COST,
    )
    give, keep = call(
        start_edges_kernel,
        shapes,
        start_state,
        *edges,
        aliases={1: 0, 2: 1},
        scratch=[pltpu.VMEM((channels // 128, size, 128), jnp.float32)],
    )
    got, mine = trade_columns(give, keep, count * cols)
    taps = of((count * size, wide), narrow)
    parts = halves(channels)
    half = channels // 2
    inner = of((count, rows, cols, half), jnp.float32)
    *main, early, _ = call(
        main_kernel,
        (
            of(frames.shape, jnp.float32),
            of((2, room, channels), jnp.float32),
            of((size, half), narrow),
            taps,
        ),
        call(taps_kernel, taps, frames),
        got,
        input_weight,
        pole,
        aliases={0: 3},
        flops=18 * frames.size * channels,
    )
    mine, total, spill = lax.optimization_barrier((mine, *main))
    halo, sides = call(
        halo_kernel,
        (of((4 * room, wide), narrow), of((2 * rows, channels), jnp.float32)),
        mine,
        swap_cores(mine),
    )
    drive, beside, strips, late = call(
        drive_kernel,
        (
            inner,
            of((count, 2 * rows, half), jnp.float32),
            of((count, 4 * rows, half), jnp.float32),
            of((size + 4 * rows, half), narrow),
        ),
        halo,
        input_weight,
        total,
        spill,
        pole,
        flops=36 * room * channels * channels,
    )
    at = size + 2 * rows
    tile = slice(0, size)
    pieces = [
        (early, [(tile, parts[0], (parts[1], (0, cols - 1)))]),
        (
            late,
            [
                (tile, parts[1], (parts[0], (1, cols - 2))),
                (slice(size, at), parts[1], None),
                (slice(at, at + 2 * rows), parts[0], None),
            ],
        ),
    ]
    exchanged = exchange_four if lax.axis_size("tm") == 4 else exchange
    early, late = exchanged(pieces, pole, count, cols)
    rounds = len(early)

    mixing = (start_state, pole, scale)
    taps = of((count * size, 3 * half), narrow)
    give = call(
        functools.partial(middle_kernel, parts[0]),
        of((count, cols, half), narrow),
        total,
        *mixing,
        *early,
    )
    lhs = call(functools.partial(mixed_kernel, parts[0], rounds), taps, total, *mixing, *early)
    strip_start = call(strip_start_kernel, of((4 * rows, channels), jnp.float32), start_state, sides)
    flops = 18 * inner.size * half
    lhs, strip_start = lax.optimization_barrier((lhs, strip_start))
    first_sum, lhs = call(
        functools.partial(opening_kernel, parts[0], parts[0]),
        (inner, taps),
        lhs,
        swap_cores(give),
        output_weight,
        aliases={0: 1},
        flops=flops,
    )
    second_sum = call(
        functools.partial(further_kernel, parts[0], parts[1]),
        inner,
        lhs,
        output_weight,
        flops=flops,
    )
    *late, first_sum, second_sum = lax.optimization_barrier((*late, first_sum, second_sum))
    give = call(
        functools.partial(give_kernel, parts, rounds),
        of((count, 2 * cols, half), narrow),
        drive,
        beside,
        strips,
        start_state,
        strip_start,
        pole,
        scale,
        *early,
        *late,
    )
    beside, strips = call(
        functools.partial(late_kernel, parts, rounds),
        (of(beside.shape, narrow), of(strips.shape, narrow)),
        beside,
        strips,
        strip_start,
        pole,
        scale,
        *late,
    )
    taps = of((count * size + 2 * room, 3 * half), narrow)
    lhs = call(
        functools.partial(mixed_kernel, parts[1], rounds), taps, drive, *mixing, *early, *late
    )
    result, _ = call(
        functools.partial(result_kernel, parts),
        (of(frames.shape, narrow), taps),
        lhs,
        swap_cores(give),
        beside,
        strips,
        output_weight,
        first_sum,
        second_sum,
        out_specs=(HBM, WHOLE),
        aliases={0: 1},
        scratch=[
            pltpu.VMEM(frames.shape, narrow),
            pltpu.VMEM((4 * room, 3 * half), narrow),
            pltpu.SemaphoreType.DMA((count, len(parts))),
        ],
        flops=2 * flops,
    )
    return result


def solution(mesh):
    return jax.shard_map(
        on_device,
        mesh=mesh,
        in_specs=(P("tm", "sx", "sy", None), P(), P(), P(), P(), P("sx", "sy", None)),
        out_specs=P("tm", "sx", "sy", None),
        check_vma=False,
    )
```

```python
import functools
import math

import jax
import jax.numpy as jnp
from jax import lax
from jax.experimental import pallas as pl
from jax.experimental.pallas import tpu as pltpu
from jax.sharding import PartitionSpec as P

NPOLES = 16
VMEM_LIMIT = 24 * 1024 * 1024
WHOLE = pl.BlockSpec(memory_space=pltpu.VMEM)
HBM = pl.BlockSpec(memory_space=pltpu.HBM)
EDGES_COST = 2_000_000_000


def call(kernel, out_shape, *args, scratch=(), flops=0, out_specs=None, aliases=None):
    outs = jax.tree.leaves(out_shape)
    moved = sum(leaf.size * leaf.dtype.itemsize for leaf in (*args, *outs))
    return pl.pallas_call(
        kernel,
        in_specs=[WHOLE] * len(args),
        out_specs=out_specs or jax.tree.map(lambda _: WHOLE, out_shape),
        out_shape=out_shape,
        scratch_shapes=scratch,
        input_output_aliases=aliases or {},
        compiler_params=pltpu.CompilerParams(vmem_limit_bytes=VMEM_LIMIT),
        cost_estimate=pl.CostEstimate(flops=flops, bytes_accessed=moved, transcendentals=0),
    )(*args)


def of(shape, dtype):
    return jax.ShapeDtypeStruct(shape, dtype)


def is_core(which):
    return (lax.axis_index("sx") == which).astype(jnp.float32)


def rate_of(pole_ref):
    pole = pole_ref[...].astype(jnp.float32)
    return -0.001 * jnp.exp(pole * (math.log(300.0) / (NPOLES - 1)))


def inner_row(rows):
    return jnp.where(lax.axis_index("sx") == 0, rows - 1, 0)


def swap_cores(array):
    return lax.ppermute(array, "sx", [(0, 1), (1, 0)])


def put_columns(index, left, right, give_ref, keep_ref):
    zero, one = is_core(0), is_core(1)
    count, rows, _ = keep_ref.shape
    at = give_ref.shape[0] - (count - index) * rows
    give_ref[at : at + rows] = (zero * left + one * right).astype(give_ref.dtype)
    keep_ref[index] = (zero * right + one * left).astype(keep_ref.dtype)


def columns_of(tile, wide_ref, picked):
    rows, cols, channels = tile.shape
    parts, _, lanes = wide_ref.shape
    tile = tile.reshape(rows * cols, channels)
    for part in range(parts):
        wide_ref[part] = tile[:, part * lanes : (part + 1) * lanes]
    return [
        jnp.concatenate(
            [wide_ref[part, pl.ds(col, rows, stride=cols), :] for part in range(parts)], axis=1
        )
        for col in picked
    ]


def edges_kernel(cells_ref, give_ref, keep_ref, wide_ref):
    count, rows, cols, channels = cells_ref.shape
    for frame in range(count):
        give_ref[frame * cols : (frame + 1) * cols] = cells_ref[frame, inner_row(rows)]
        tile = cells_ref[frame].astype(jnp.float32)
        picked = (0, 1, cols - 1, cols - 2)
        columns = columns_of(tile, wide_ref.at[frame], picked)
        for depth in range(2):
            left, right = columns[depth], columns[2 + depth]
            put_columns(2 * frame + depth, left, right, give_ref, keep_ref)


def start_edges_kernel(start_ref, _, __, give_ref, keep_ref, wide_ref):
    cols = start_ref.shape[1]
    left, right = columns_of(start_ref[...], wide_ref, (0, cols - 1))
    put_columns(keep_ref.shape[0] - 1, left, right, give_ref, keep_ref)


def trade_columns(give, keep, at):
    chips = lax.axis_size("sy")
    got = swap_cores(give)
    pairs = [(chip, chips + chip + 1) for chip in range(chips - 1)]
    pairs += [(after, before) for before, after in pairs]
    columns = jnp.concatenate([keep, got[at:].reshape(keep.shape)], axis=1)
    return got, lax.ppermute(columns, ("sx", "sy"), pairs)


def put_cells(lhs_ref, at, size, cols, first, cells):
    count, channels = cells.shape
    upper, lower = min(count, size - cols - first), max(0, cols - first)
    here = at + first
    lhs_ref[here : here + count, channels : 2 * channels] = cells
    lhs_ref[here + cols : here + cols + upper, :channels] = cells[:upper]
    lhs_ref[here + lower - cols : here + count - cols, 2 * channels :] = cells[lower:]


def put_row(lhs_ref, at, size, row):
    cols, channels = row.shape
    row = row.astype(jnp.float32)
    last = slice(at + size - cols, at + size)
    lhs_ref[at : at + cols, :channels] = (is_core(1) * row).astype(lhs_ref.dtype)
    lhs_ref[last, 2 * channels :] = (is_core(0) * row).astype(lhs_ref.dtype)


def taps_kernel(cells_ref, lhs_ref):
    count, rows, cols, channels = cells_ref.shape
    size = rows * cols
    for frame in range(count):
        put_cells(lhs_ref, frame * size, size, cols, 0, cells_ref[frame].reshape(size, channels))


def row_taps(column, above, below):
    rows = column.shape[0]
    row = lax.broadcasted_iota(jnp.int32, column.shape, 0)
    up = jnp.where(row == 0, is_core(1) * above, pltpu.roll(column, 1, 0))
    down = jnp.where(row == rows - 1, is_core(0) * below, pltpu.roll(column, rows - 1, 0))
    return jnp.concatenate([up, column, down], axis=1)


SLAB = 8


def halves(channels):
    return slice(0, channels // 2), slice(channels // 2, channels)


def end_state(frames, pole_ref, lanes):
    decay = jnp.exp(rate_of(pole_ref))[:, lanes]
    state = frames[0]
    for frame in frames[1:]:
        state = decay * state + frame
    return state


def dot(lhs, weight_ref, column, lanes, inputs=slice(None)):
    weight = weight_ref[:, column, inputs, lanes].reshape(lhs.shape[1], -1)
    return jnp.dot(lhs, weight, preferred_element_type=jnp.float32)


def main_kernel(_, got_ref, weight_ref, pole_ref, total_ref, spill_ref, end_ref, lhs_ref):
    count, rows, cols, _ = total_ref.shape
    size = rows * cols
    for frame in range(count):
        put_row(lhs_ref, frame * size, size, got_ref[frame * cols : (frame + 1) * cols])
    states = []
    for lanes in halves(weight_ref.shape[-1]):
        tile = (rows, cols, lanes.stop - lanes.start)
        col = lax.broadcasted_iota(jnp.int32, tile, 1)
        totals = []
        for frame in range(count):
            cells = lhs_ref[frame * size : (frame + 1) * size]
            here = slice(frame * rows, (frame + 1) * rows)
            total = dot(cells, weight_ref, 1, lanes).reshape(tile)
            first = dot(cells, weight_ref, 0, lanes).reshape(tile)
            spill_ref[1, here, lanes] = first[:, cols - 1, :]
            total += jnp.where(col == 0, 0.0, pltpu.roll(first, 1, 1))
            last = dot(cells, weight_ref, 2, lanes).reshape(tile)
            spill_ref[0, here, lanes] = last[:, 0, :]
            total += jnp.where(col == cols - 1, 0.0, pltpu.roll(last, cols - 1, 1))
            total_ref[frame, :, :, lanes] = total
            totals.append(total)
        states.append(end_state(totals, pole_ref, lanes))
    state, other = states
    col = lax.broadcasted_iota(jnp.int32, (rows, SLAB, state.shape[2]), 1)
    last = slice(cols - SLAB, cols)
    left = jnp.where(col == 0, pltpu.roll(other[:, :SLAB], SLAB - 1, 1), state[:, :SLAB])
    right = jnp.where(col == SLAB - 1, pltpu.roll(other[:, last], 1, 1), state[:, last])
    middle = [state[:, SLAB : cols - SLAB]] if cols > 2 * SLAB else []
    state = jnp.concatenate([left, *middle, right], axis=1)
    end_ref[...] = state.reshape(end_ref.shape).astype(end_ref.dtype)


def halo_kernel(mine_ref, theirs_ref, lhs_ref, start_ref):
    rows = mine_ref.shape[1] // 2
    count = mine_ref.shape[0] // 2
    room = count * rows
    zero, one = is_core(0), is_core(1)
    core = lax.axis_index("sx")
    slots = ((1, 0), (2, 3))
    for frame in range(count):
        for depth in range(2):
            own = mine_ref[2 * frame + depth].astype(jnp.float32)
            other = theirs_ref[2 * frame + depth].astype(jnp.float32)
            own = row_taps(own[rows:], own[rows - 1 : rows], own[:1])
            other = row_taps(other[:rows], other[2 * rows - 1 :], other[rows : rows + 1])
            for swapped, taps in enumerate((own, other)):
                slot = jnp.where(core == swapped, slots[1][depth], slots[0][depth])
                at = pl.multiple_of(slot * room + frame * rows, rows)
                lhs_ref[pl.ds(at, rows)] = taps.astype(lhs_ref.dtype)
    own = mine_ref[2 * count, rows:].astype(jnp.float32)
    other = theirs_ref[2 * count, :rows].astype(jnp.float32)
    start_ref[:rows] = zero * other + one * own
    start_ref[rows:] = zero * own + one * other


def drive_kernel(
    lhs_ref, weight_ref, total_ref, spill_ref, pole_ref, drive_ref, beside_ref, strips_ref, end_ref
):
    count, rows, cols, wide = drive_ref.shape
    room, size = count * rows, rows * cols
    at = size + 2 * rows
    early = None
    for lanes in halves(weight_ref.shape[-1]):
        first = dot(lhs_ref[: 2 * room], weight_ref, 0, lanes)
        middle = dot(lhs_ref[room : 3 * room], weight_ref, 1, lanes)
        last = dot(lhs_ref[2 * room :], weight_ref, 2, lanes)
        left = (spill_ref[0, :, lanes] + first[:room] + middle[:room]).reshape(count, rows, wide)
        right = (spill_ref[1, :, lanes] + middle[room:] + last[room:]).reshape(count, rows, wide)
        total = total_ref[:, :, :, lanes]
        if lanes.start == 0:
            near = total[:, :, 0, :] + first[room:].reshape(count, rows, wide)
            far = total[:, :, cols - 1, :] + last[:room].reshape(count, rows, wide)
            strips = jnp.concatenate([left, near, far, right], axis=1)
            strips_ref[...] = strips
            early = end_state([strips[frame] for frame in range(count)], pole_ref, lanes)
            end_ref[at : at + rows] = early[:rows].astype(end_ref.dtype)
            end_ref[at + rows :] = early[3 * rows :].astype(end_ref.dtype)
            continue
        col = lax.broadcasted_iota(jnp.int32, drive_ref.shape, 2)
        total += jnp.where(col == 0, first[room:].reshape(count, rows, 1, wide), 0.0)
        total += jnp.where(col == cols - 1, last[:room].reshape(count, rows, 1, wide), 0.0)
        drive_ref[...] = total
        state = end_state([total[frame] for frame in range(count)], pole_ref, lanes)
        col = lax.broadcasted_iota(jnp.int32, state.shape, 1)
        state = jnp.where(col == 1, early[rows : 2 * rows].reshape(rows, 1, wide), state)
        border = early[2 * rows : 3 * rows].reshape(rows, 1, wide)
        state = jnp.where(col == cols - 2, border, state)
        end_ref[:size] = state.reshape(size, wide).astype(end_ref.dtype)
        beside = jnp.concatenate([left, right], axis=1)
        beside_ref[...] = beside
        state = end_state([beside[frame] for frame in range(count)], pole_ref, lanes)
        end_ref[size:at] = state.astype(end_ref.dtype)


def spread(block, cols, count, of_lanes):
    _, lanes, inset = block
    value = of_lanes(lanes)
    if inset is None:
        return value
    other, columns = inset
    value, instead = jnp.broadcast_arrays(value, of_lanes(other))
    shape = (count, value.shape[1])
    col = lax.rem(lax.broadcasted_iota(jnp.int32, shape, 0), cols)
    return jnp.where((col == columns[0]) | (col == columns[1]), instead, value)


def entry_kernel(frames, cols, block, ends_ref, pole_ref, out_ref):
    rate = rate_of(pole_ref)
    count = ends_ref.shape[1]
    carried = spread(block, cols, count, lambda lanes: jnp.exp(frames * rate[:, lanes]))
    entry = jnp.zeros(ends_ref.shape[1:], jnp.float32)
    out_ref[0] = entry.astype(out_ref.dtype)
    for index in range(ends_ref.shape[0] - 1):
        entry = carried * entry + ends_ref[index].astype(jnp.float32)
        out_ref[index + 1] = entry.astype(out_ref.dtype)


def exchange(pieces, pole, frames, cols):
    groups = lax.axis_size("tm")
    arrivals = []
    for end, blocks in pieces:
        entries = []
        for block in blocks:
            shares = end[block[0]].reshape(groups, -1, end.shape[1])
            assert block[2] is None or shares.shape[1] % cols == 0
            shares = lax.all_to_all(shares, "tm", 0, 0)
            kernel = functools.partial(entry_kernel, frames, cols, block)
            entry = call(kernel, of(shares.shape, end.dtype), shares, pole)
            entries.append(lax.all_to_all(entry, "tm", 0, 0).reshape(-1, end.shape[1]))
        arrivals.append((jnp.concatenate(entries, axis=0),))
    return arrivals


def pick(values):
    group = lax.axis_index("tm")
    picked = values[-1]
    for index, value in enumerate(values[:-1]):
        picked = jnp.where(group == index, value, picked)
    return picked


def on_core(first, second):
    return jnp.where(lax.axis_index("sx") == 0, first, second)


def weigh(one, by_one, other, by_other):
    return by_one * one.astype(jnp.float32) + by_other * other.astype(jnp.float32)


def relay_kernel(frames, cols, blocks, end_ref, got_ref, pole_ref, out_ref):
    rate = rate_of(pole_ref)
    carried, twice = jnp.exp(frames * rate), jnp.exp(2 * frames * rate)
    none, same = jnp.zeros_like(rate), jnp.ones_like(rate)
    own = on_core(pick([carried, same, same, same]), pick([same, same, same, none]))
    got = on_core(pick([same, carried, carried, carried]), pick([none, none, twice, same]))
    for block in blocks:
        rows = block[0]
        count = rows.stop - rows.start
        by_own = spread(block, cols, count, lambda lanes: own[:, lanes])
        by_got = spread(block, cols, count, lambda lanes: got[:, lanes])
        out_ref[rows] = weigh(end_ref[rows], by_own, got_ref[rows], by_got).astype(out_ref.dtype)


def exchange_four(pieces, pole, frames, cols):
    def along(pairs, core):
        return [(2 * source + core, 2 * target + core) for source, target in pairs]

    axes = ("tm", "sx")
    down = [(0, 2), (1, 3)]
    first_round = along([(0, 1), (1, 0), (2, 3)], 0) + along(down, 1)
    second_round = along(down, 0) + along([(0, 1), (2, 3), (3, 2)], 1)
    arrivals = []
    for end, blocks in pieces:
        got = lax.ppermute(end, axes, first_round)
        kernel = functools.partial(relay_kernel, frames, cols, blocks)
        relayed = call(kernel, of(end.shape, end.dtype), end, got, pole)
        arrivals.append((got, lax.ppermute(relayed, axes, second_round)))
    return arrivals


def gelu(x):
    slope = math.sqrt(2.0 / math.pi)
    half = 0.5 * x
    return half + half * jnp.tanh(x * (slope + (slope * 0.044715) * (x * x)))


class Mix:
    def __init__(self, lanes, count, pole_ref, scale_ref):
        self.rate = rate_of(pole_ref)[:, lanes]
        self.scale = scale_ref[:, lanes]
        self.count = count

    def entry(self, arrived_refs, rows):
        parts = [ref[rows].astype(jnp.float32) for ref in arrived_refs]
        if len(parts) == 1:
            return parts[0]
        carried = jnp.exp(self.count * self.rate)
        none, same = jnp.zeros_like(self.rate), jnp.ones_like(self.rate)
        early = on_core(pick([none, same, none, same]), pick([none, none, carried, carried]))
        late = on_core(pick([none, none, same, carried]), pick([none, same, same, same]))
        return weigh(parts[0], early, parts[1], late)

    def __call__(self, drives, entry, start):
        decay = jnp.exp(self.rate)
        reach = jnp.exp((self.count * lax.axis_index("tm")).astype(jnp.float32) * self.rate)
        state = reach * start + entry.reshape(start.shape)
        for drive in drives:
            state = decay * state + drive
            yield gelu(self.scale * state)


def no_border(cells, axis):
    col = lax.broadcasted_iota(jnp.int32, cells.shape, axis)
    return jnp.where((col == 0) | (col == cells.shape[axis] - 1), 0.0, cells)


def put_back(late, early, axis):
    cols = late.shape[axis]

    def slab(cells, start):
        return lax.slice_in_dim(cells, start, start + SLAB, axis=axis)

    first, last = slab(late, 0), slab(late, cols - SLAB)
    col = lax.broadcasted_iota(jnp.int32, first.shape, axis)
    first = jnp.where(col == 1, pltpu.roll(slab(early, 0), 1, axis), first)
    moved = pltpu.roll(slab(early, cols - SLAB), SLAB - 1, axis)
    last = jnp.where(col == SLAB - 2, moved, last)
    middle = [lax.slice_in_dim(late, SLAB, cols - SLAB, axis=axis)] if cols > 2 * SLAB else []
    return jnp.concatenate([first, *middle, last], axis=axis)


def mixed_kernel(lanes, rounds, *refs):
    drive_ref, start_ref, pole_ref, scale_ref, *arrived_refs, lhs_ref = refs
    early_refs, late_refs = arrived_refs[:rounds], arrived_refs[rounds:]
    count, rows, cols, _ = drive_ref.shape
    wide = lanes.stop - lanes.start
    size = rows * cols
    stride = lhs_ref.shape[0] // count
    room = (stride - size) // 2
    mix = Mix(lanes, count, pole_ref, scale_ref)
    first = lanes.start == 0
    held = lanes if first else slice(None)
    block = 8
    for row in range(0, rows, block):
        here = slice(row, row + block)
        drives = [drive_ref[frame, here, :, held] for frame in range(count)]
        cells = slice(row * cols, (row + block) * cols)
        entry = mix.entry(early_refs, cells).reshape(block, cols, wide)
        if not first:
            entry = put_back(mix.entry(late_refs, cells).reshape(entry.shape), entry, 1)
        for frame, tile in enumerate(mix(drives, entry, start_ref[here, :, lanes])):
            if first:
                tile = no_border(tile, 1)
            tile = tile.reshape(block * cols, wide).astype(lhs_ref.dtype)
            put_cells(lhs_ref, frame * stride + room, size, cols, row * cols, tile)


def middle_kernel(lanes, *refs):
    total_ref, start_ref, pole_ref, scale_ref, *arrived_refs, give_ref = refs
    count, rows, cols, _ = total_ref.shape
    mix = Mix(lanes, count, pole_ref, scale_ref)
    inner = inner_row(rows)
    drives = [total_ref[frame, inner, :, lanes] for frame in range(count)]
    entry = mix.entry(arrived_refs, pl.ds(pl.multiple_of(inner * cols, cols), cols))
    for frame, cells in enumerate(mix(drives, entry, start_ref[inner, :, lanes])):
        give_ref[frame] = no_border(cells, 0).astype(give_ref.dtype)


def strip_start_kernel(start_ref, sides_ref, out_ref):
    rows, cols, _ = start_ref.shape
    start = start_ref[...]
    out_ref[:rows] = sides_ref[:rows]
    out_ref[rows : 2 * rows] = start[:, 0, :]
    out_ref[2 * rows : 3 * rows] = start[:, cols - 1, :]
    out_ref[3 * rows :] = sides_ref[rows:]


def inside(slot):
    chip, chips = lax.axis_index("sy"), lax.axis_size("sy")
    return {0: (chip > 0).astype(jnp.float32), 3: (chip < chips - 1).astype(jnp.float32)}.get(slot, 1.0)


def give_kernel(parts, rounds, *refs):
    drive_ref, beside_ref, strips_ref, *refs = refs
    start_ref, strip_start_ref, pole_ref, scale_ref, *arrived_refs, give_ref = refs
    early_refs, late_refs = arrived_refs[:rounds], arrived_refs[rounds:]
    count, rows, cols, wide = drive_ref.shape
    size = rows * cols
    inner = inner_row(rows)
    zero, one = is_core(0), is_core(1)
    early, late = (Mix(lanes, count, pole_ref, scale_ref) for lanes in parts)
    row = pl.ds(pl.multiple_of(inner * cols, cols), cols)
    which = lax.broadcasted_iota(jnp.int32, (cols, wide), 0)

    def near(at):
        return pl.ds(pl.multiple_of(at + jnp.where(inner == 0, 0, rows - cols), cols), cols)

    def end(cells):
        return zero * cells[cols - 1 :] + one * cells[:1]

    def rows_of(cells):
        table = jnp.zeros(which.shape, jnp.float32)
        for index, cell in cells:
            table = jnp.where(which == index, cell, table)
        return table

    entry = put_back(late.entry(late_refs, row), late.entry(early_refs, row), 0)
    drives = [drive_ref[frame, inner] for frame in range(count)]
    tile = late(drives, entry, start_ref[inner, :, parts[1]])

    slots = [(0, 0), (1, 3)]
    entry = rows_of([(i, end(late.entry(late_refs, near(size + i * rows)))) for i, _ in slots])
    start = rows_of([(i, end(strip_start_ref[near(slot * rows), parts[1]])) for i, slot in slots])
    drives = [
        rows_of([(i, end(beside_ref[frame, near(i * rows)])) for i, _ in slots])
        for frame in range(count)
    ]
    beside = late(drives, entry, start)

    slots = [(2 + slot, slot) for slot in range(4)]
    grid = early.entry(late_refs, row)
    at = size + 2 * rows
    entry = rows_of(
        [
            (2, end(early.entry(late_refs, near(at)))),
            (3, grid[1:2]),
            (4, grid[cols - 2 : cols - 1]),
            (5, end(early.entry(late_refs, near(at + rows)))),
        ]
    )
    start = rows_of([(i, end(strip_start_ref[near(slot * rows), parts[0]])) for i, slot in slots])
    drives = [
        rows_of([(i, end(strips_ref[frame, near(slot * rows)])) for i, slot in slots])
        for frame in range(count)
    ]
    strips = early(drives, entry, start)
    for frame, cells in enumerate(zip(tile, beside, strips)):
        give_ref[frame, :cols] = cells[0].astype(give_ref.dtype)
        ends = jnp.where(which < 2, cells[1], cells[2])
        ends = jnp.where((which == 0) | (which == 2), inside(0) * ends, ends)
        ends = jnp.where((which == 1) | (which == 5), inside(3) * ends, ends)
        give_ref[frame, cols:] = ends.astype(give_ref.dtype)


def late_kernel(parts, rounds, *refs):
    beside_ref, strips_ref, strip_start_ref, pole_ref, scale_ref, *refs = refs
    *late_refs, beside_out_ref, strips_out_ref = refs
    count, room, wide = beside_ref.shape
    rows = room // 2
    size = late_refs[0].shape[0] - 4 * rows
    cols = size // rows
    early, late = (Mix(lanes, count, pole_ref, scale_ref) for lanes in parts)

    def column(cells, index):
        return cells[index * rows : (index + 1) * rows]

    starts = [strip_start_ref[slot * rows : (slot + 1) * rows, parts[1]] for slot in (0, 3)]
    entry = late.entry(late_refs, slice(size, size + 2 * rows))
    drives = [beside_ref[frame] for frame in range(count)]
    beside = late(drives, entry, jnp.concatenate(starts, axis=0))
    grid = early.entry(late_refs, slice(0, size)).reshape(rows, cols, wide)
    sides = early.entry(late_refs, slice(size + 2 * rows, size + 4 * rows))
    entry = [sides[:rows], grid[:, 1, :], grid[:, cols - 2, :], sides[rows:]]
    drives = [strips_ref[frame] for frame in range(count)]
    strips = early(drives, jnp.concatenate(entry, axis=0), strip_start_ref[:, parts[0]])
    for frame, (sides, strip) in enumerate(zip(beside, strips)):
        sides = [column(sides, 0) * inside(0), column(sides, 1) * inside(3)]
        strip = [column(strip, slot) * inside(slot) for slot in range(4)]
        beside_out_ref[frame] = jnp.concatenate(sides, axis=0).astype(beside_out_ref.dtype)
        strips_out_ref[frame] = jnp.concatenate(strip, axis=0).astype(strips_out_ref.dtype)


def put_columns_taps(lhs_ref, slots, columns, ends):
    rows = columns.shape[0] // len(slots)
    columns, ends = columns.astype(jnp.float32), ends.astype(jnp.float32)
    for index, at in enumerate(slots):
        column, end = columns[index * rows : (index + 1) * rows], ends[index : index + 1]
        lhs_ref[at : at + rows] = row_taps(column, end, end).astype(lhs_ref.dtype)


def tile_sum(tile, inputs, lanes, room, lhs_ref, weight_ref):
    count, rows, cols, wide = tile
    size = rows * cols
    col = lax.broadcasted_iota(jnp.int32, tile[1:], 1)

    def beside(cells):
        return cells.reshape(rows, 1, wide) if room else 0.0

    for frame in range(count):
        at = frame * (size + 2 * room)
        end = at + room + size
        total = dot(lhs_ref[at + room : end], weight_ref, 1, lanes, inputs).reshape(tile[1:])
        first = dot(lhs_ref[at:end], weight_ref, 0, lanes, inputs)
        shifted = pltpu.roll(first[room:].reshape(tile[1:]), 1, 1)
        total += jnp.where(col == 0, beside(first[:room]), shifted)
        last = dot(lhs_ref[at + room : end + room], weight_ref, 2, lanes, inputs)
        shifted = pltpu.roll(last[:size].reshape(tile[1:]), cols - 1, 1)
        yield total + jnp.where(col == cols - 1, beside(last[size:]), shifted)


def strip_sum(tile, inputs, lanes, lhs_ref, weight_ref):
    count, rows, cols, wide = tile
    room = count * rows
    first = dot(lhs_ref[: 2 * room], weight_ref, 0, lanes, inputs)
    middle = dot(lhs_ref[room : 3 * room], weight_ref, 1, lanes, inputs)
    last = dot(lhs_ref[2 * room :], weight_ref, 2, lanes, inputs)
    columns = [
        (0, first[:room] + middle[:room]),
        (1, first[room:]),
        (cols - 2, last[:room]),
        (cols - 1, middle[room:] + last[room:]),
    ]
    return [(at, cells.reshape(count, rows, 1, wide)) for at, cells in columns]


def opening_kernel(inputs, lanes, _, got_ref, weight_ref, out_ref, lhs_ref):
    count, rows, cols, _ = out_ref.shape
    size = rows * cols
    for frame in range(count):
        put_row(lhs_ref, frame * size, size, got_ref[frame])
    further_kernel(inputs, lanes, lhs_ref, weight_ref, out_ref)


def further_kernel(inputs, lanes, lhs_ref, weight_ref, out_ref):
    tiles = tile_sum(out_ref.shape, inputs, lanes, 0, lhs_ref, weight_ref)
    for frame, total in enumerate(tiles):
        out_ref[frame] = total


def result_kernel(
    parts, _, got_ref, beside_ref, strips_ref, weight_ref, *refs
):
    *before_refs, out_ref, lhs_ref, held_ref, strip_lhs_ref, sems = refs
    count, rows, cols, _ = held_ref.shape
    size, room = rows * cols, count * rows
    stride = size + 2 * rows
    for frame in range(count):
        at = frame * stride
        put_row(lhs_ref, at + rows, size, got_ref[frame, :cols])
        ends = got_ref[frame, cols:]
        put_columns_taps(lhs_ref, (at, at + rows + size), beside_ref[frame], ends)
        slots = [slot * room + frame * rows for slot in range(4)]
        put_columns_taps(strip_lhs_ref, slots, strips_ref[frame], ends.astype(jnp.float32)[2:])

    def store(frame, part):
        here = (frame, slice(None), slice(None), parts[part])
        return pltpu.make_async_copy(held_ref.at[here], out_ref.at[here], sems.at[frame, part])

    for part, lanes in enumerate(parts):
        tile = (count, rows, cols, lanes.stop - lanes.start)
        col = lax.broadcasted_iota(jnp.int32, tile[1:], 1)
        columns = strip_sum(tile, parts[0], lanes, strip_lhs_ref, weight_ref)
        tiles = tile_sum(tile, parts[1], lanes, rows, lhs_ref, weight_ref)
        for frame, total in enumerate(tiles):
            strips = 0.0
            for at, cells in columns:
                strips = jnp.where(col == at, cells[frame], strips)
            total += before_refs[part][frame] + strips
            held_ref[frame, :, :, lanes] = total.astype(held_ref.dtype)
            store(frame, part).start()
    for part in range(len(parts)):
        for frame in range(count):
            store(frame, part).wait()


def on_device(frames, input_weight, output_weight, pole_index, gelu_scale, start_state):
    count, rows, cols, channels = frames.shape
    size, room = rows * cols, count * rows
    wide = 3 * channels
    assert lax.axis_size("sx") == 2
    narrow = frames.dtype
    pole, scale = pole_index[None], gelu_scale[None]

    shapes = (
        of((count * cols + (2 * count + 1) * rows, channels), narrow),
        of((2 * count + 1, rows, channels), narrow),
    )
    edges = call(
        edges_kernel,
        shapes,
        frames,
        scratch=[pltpu.VMEM((count, channels // 128, size, 128), jnp.float32)],
        flops=EDGES_COST,
    )
    give, keep = call(
        start_edges_kernel,
        shapes,
        start_state,
        *edges,
        aliases={1: 0, 2: 1},
        scratch=[pltpu.VMEM((channels // 128, size, 128), jnp.float32)],
    )
    got, mine = trade_columns(give, keep, count * cols)
    taps = of((count * size, wide), narrow)
    parts = halves(channels)
    half = channels // 2
    inner = of((count, rows, cols, half), jnp.float32)
    *main, early, _ = call(
        main_kernel,
        (
            of(frames.shape, jnp.float32),
            of((2, room, channels), jnp.float32),
            of((size, half), narrow),
            taps,
        ),
        call(taps_kernel, taps, frames),
        got,
        input_weight,
        pole,
        aliases={0: 3},
        flops=18 * frames.size * channels,
    )
    mine, total, spill = lax.optimization_barrier((mine, *main))
    halo, sides = call(
        halo_kernel,
        (of((4 * room, wide), narrow), of((2 * rows, channels), jnp.float32)),
        mine,
        swap_cores(mine),
    )
    drive, beside, strips, late = call(
        drive_kernel,
        (
            inner,
            of((count, 2 * rows, half), jnp.float32),
            of((count, 4 * rows, half), jnp.float32),
            of((size + 4 * rows, half), narrow),
        ),
        halo,
        input_weight,
        total,
        spill,
        pole,
        flops=36 * room * channels * channels,
    )
    at = size + 2 * rows
    tile = slice(0, size)
    pieces = [
        (early, [(tile, parts[0], (parts[1], (0, cols - 1)))]),
        (
            late,
            [
                (tile, parts[1], (parts[0], (1, cols - 2))),
                (slice(size, at), parts[1], None),
                (slice(at, at + 2 * rows), parts[0], None),
            ],
        ),
    ]
    exchanged = exchange_four if lax.axis_size("tm") == 4 else exchange
    early, late = exchanged(pieces, pole, count, cols)
    rounds = len(early)

    mixing = (start_state, pole, scale)
    taps = of((count * size, 3 * half), narrow)
    give = call(
        functools.partial(middle_kernel, parts[0]),
        of((count, cols, half), narrow),
        total,
        *mixing,
        *early,
    )
    lhs = call(functools.partial(mixed_kernel, parts[0], rounds), taps, total, *mixing, *early)
    strip_start = call(strip_start_kernel, of((4 * rows, channels), jnp.float32), start_state, sides)
    flops = 18 * inner.size * half
    lhs, strip_start = lax.optimization_barrier((lhs, strip_start))
    first_sum, lhs = call(
        functools.partial(opening_kernel, parts[0], parts[0]),
        (inner, taps),
        lhs,
        swap_cores(give),
        output_weight,
        aliases={0: 1},
        flops=flops,
    )
    second_sum = call(
        functools.partial(further_kernel, parts[0], parts[1]),
        inner,
        lhs,
        output_weight,
        flops=flops,
    )
    *late, first_sum, second_sum = lax.optimization_barrier((*late, first_sum, second_sum))
    give = call(
        functools.partial(give_kernel, parts, rounds),
        of((count, 2 * cols, half), narrow),
        drive,
        beside,
        strips,
        start_state,
        strip_start,
        pole,
        scale,
        *early,
        *late,
    )
    beside, strips = call(
        functools.partial(late_kernel, parts, rounds),
        (of(beside.shape, narrow), of(strips.shape, narrow)),
        beside,
        strips,
        strip_start,
        pole,
        scale,
        *late,
    )
    taps = of((count * size + 2 * room, 3 * half), narrow)
    lhs = call(
        functools.partial(mixed_kernel, parts[1], rounds), taps, drive, *mixing, *early, *late
    )
    result, _ = call(
        functools.partial(result_kernel, parts),
        (of(frames.shape, narrow), taps),
        lhs,
        swap_cores(give),
        beside,
        strips,
        output_weight,
        first_sum,
        second_sum,
        out_specs=(HBM, WHOLE),
        aliases={0: 1},
        scratch=[
            pltpu.VMEM(frames.shape, narrow),
            pltpu.VMEM((4 * room, 3 * half), narrow),
            pltpu.SemaphoreType.DMA((count, len(parts))),
        ],
        flops=2 * flops,
    )
    return result


def solution(mesh):
    return jax.shard_map(
        on_device,
        mesh=mesh,
        in_specs=(P("tm", "sx", "sy", None), P(), P(), P(), P(), P("sx", "sy", None)),
        out_specs=P("tm", "sx", "sy", None),
        check_vma=False,
    )
```

```python
import functools
import math

import jax
import jax.numpy as jnp
from jax import lax
from jax.experimental import pallas as pl
from jax.experimental.pallas import tpu as pltpu
from jax.sharding import PartitionSpec as P

NPOLES = 16
VMEM_LIMIT = 24 * 1024 * 1024
WHOLE = pl.BlockSpec(memory_space=pltpu.VMEM)
HBM = pl.BlockSpec(memory_space=pltpu.HBM)
EDGES_COST = 2_000_000_000


def call(kernel, out_shape, *args, scratch=(), flops=0, out_specs=None, aliases=None):
    outs = jax.tree.leaves(out_shape)
    moved = sum(leaf.size * leaf.dtype.itemsize for leaf in (*args, *outs))
    return pl.pallas_call(
        kernel,
        in_specs=[WHOLE] * len(args),
        out_specs=out_specs or jax.tree.map(lambda _: WHOLE, out_shape),
        out_shape=out_shape,
        scratch_shapes=scratch,
        input_output_aliases=aliases or {},
        compiler_params=pltpu.CompilerParams(vmem_limit_bytes=VMEM_LIMIT),
        cost_estimate=pl.CostEstimate(flops=flops, bytes_accessed=moved, transcendentals=0),
    )(*args)


def of(shape, dtype):
    return jax.ShapeDtypeStruct(shape, dtype)


def is_core(which):
    return (lax.axis_index("sx") == which).astype(jnp.float32)


def rate_of(pole_ref):
    pole = pole_ref[...].astype(jnp.float32)
    return -0.001 * jnp.exp(pole * (math.log(300.0) / (NPOLES - 1)))


def inner_row(rows):
    return jnp.where(lax.axis_index("sx") == 0, rows - 1, 0)


def swap_cores(array):
    return lax.ppermute(array, "sx", [(0, 1), (1, 0)])


def put_columns(index, left, right, give_ref, keep_ref):
    zero, one = is_core(0), is_core(1)
    count, rows, _ = keep_ref.shape
    at = give_ref.shape[0] - (count - index) * rows
    give_ref[at : at + rows] = (zero * left + one * right).astype(give_ref.dtype)
    keep_ref[index] = (zero * right + one * left).astype(keep_ref.dtype)


def columns_of(tile, wide_ref, picked):
    rows, cols, channels = tile.shape
    parts, _, lanes = wide_ref.shape
    tile = tile.reshape(rows * cols, channels)
    for part in range(parts):
        wide_ref[part] = tile[:, part * lanes : (part + 1) * lanes]
    return [
        jnp.concatenate(
            [wide_ref[part, pl.ds(col, rows, stride=cols), :] for part in range(parts)], axis=1
        )
        for col in picked
    ]


def edges_kernel(cells_ref, give_ref, keep_ref, wide_ref):
    count, rows, cols, channels = cells_ref.shape
    for frame in range(count):
        give_ref[frame * cols : (frame + 1) * cols] = cells_ref[frame, inner_row(rows)]
        tile = cells_ref[frame].astype(jnp.float32)
        picked = (0, 1, cols - 1, cols - 2)
        columns = columns_of(tile, wide_ref.at[frame], picked)
        for depth in range(2):
            left, right = columns[depth], columns[2 + depth]
            put_columns(2 * frame + depth, left, right, give_ref, keep_ref)


def start_edges_kernel(start_ref, _, __, give_ref, keep_ref, wide_ref):
    cols = start_ref.shape[1]
    left, right = columns_of(start_ref[...], wide_ref, (0, cols - 1))
    put_columns(keep_ref.shape[0] - 1, left, right, give_ref, keep_ref)


def trade_columns(give, keep, at):
    chips = lax.axis_size("sy")
    got = swap_cores(give)
    pairs = [(chip, chips + chip + 1) for chip in range(chips - 1)]
    pairs += [(after, before) for before, after in pairs]
    columns = jnp.concatenate([keep, got[at:].reshape(keep.shape)], axis=1)
    return got, lax.ppermute(columns, ("sx", "sy"), pairs)


def put_cells(lhs_ref, at, size, cols, first, cells):
    count, channels = cells.shape
    upper, lower = min(count, size - cols - first), max(0, cols - first)
    here = at + first
    lhs_ref[here : here + count, channels : 2 * channels] = cells
    lhs_ref[here + cols : here + cols + upper, :channels] = cells[:upper]
    lhs_ref[here + lower - cols : here + count - cols, 2 * channels :] = cells[lower:]


def put_row(lhs_ref, at, size, row):
    cols, channels = row.shape
    row = row.astype(jnp.float32)
    last = slice(at + size - cols, at + size)
    lhs_ref[at : at + cols, :channels] = (is_core(1) * row).astype(lhs_ref.dtype)
    lhs_ref[last, 2 * channels :] = (is_core(0) * row).astype(lhs_ref.dtype)


def taps_kernel(cells_ref, lhs_ref):
    count, rows, cols, channels = cells_ref.shape
    size = rows * cols
    for frame in range(count):
        put_cells(lhs_ref, frame * size, size, cols, 0, cells_ref[frame].reshape(size, channels))


def row_taps(column, above, below):
    rows = column.shape[0]
    row = lax.broadcasted_iota(jnp.int32, column.shape, 0)
    up = jnp.where(row == 0, is_core(1) * above, pltpu.roll(column, 1, 0))
    down = jnp.where(row == rows - 1, is_core(0) * below, pltpu.roll(column, rows - 1, 0))
    return jnp.concatenate([up, column, down], axis=1)


SLAB = 8


def halves(channels):
    return slice(0, channels // 2), slice(channels // 2, channels)


def end_state(frames, pole_ref, lanes):
    decay = jnp.exp(rate_of(pole_ref))[:, lanes]
    state = frames[0]
    for frame in frames[1:]:
        state = decay * state + frame
    return state


def dot(lhs, weight_ref, column, lanes, inputs=slice(None)):
    weight = weight_ref[:, column, inputs, lanes].reshape(lhs.shape[1], -1)
    return jnp.dot(lhs, weight, preferred_element_type=jnp.float32)


def main_kernel(_, got_ref, weight_ref, pole_ref, total_ref, spill_ref, end_ref, lhs_ref):
    count, rows, cols, _ = total_ref.shape
    size = rows * cols
    for frame in range(count):
        put_row(lhs_ref, frame * size, size, got_ref[frame * cols : (frame + 1) * cols])
    states = []
    for lanes in halves(weight_ref.shape[-1]):
        tile = (count, rows, cols, lanes.stop - lanes.start)
        col = lax.broadcasted_iota(jnp.int32, tile, 2)
        total = dot(lhs_ref[...], weight_ref, 1, lanes).reshape(tile)
        first = dot(lhs_ref[...], weight_ref, 0, lanes).reshape(tile)
        spill_ref[1, :, lanes] = first[:, :, cols - 1, :].reshape(count * rows, -1)
        total += jnp.where(col == 0, 0.0, pltpu.roll(first, 1, 2))
        last = dot(lhs_ref[...], weight_ref, 2, lanes).reshape(tile)
        spill_ref[0, :, lanes] = last[:, :, 0, :].reshape(count * rows, -1)
        total += jnp.where(col == cols - 1, 0.0, pltpu.roll(last, cols - 1, 2))
        total_ref[:, :, :, lanes] = total
        totals = [total[frame] for frame in range(count)]
        states.append(end_state(totals, pole_ref, lanes))
    state, other = states
    col = lax.broadcasted_iota(jnp.int32, (rows, SLAB, state.shape[2]), 1)
    last = slice(cols - SLAB, cols)
    left = jnp.where(col == 0, pltpu.roll(other[:, :SLAB], SLAB - 1, 1), state[:, :SLAB])
    right = jnp.where(col == SLAB - 1, pltpu.roll(other[:, last], 1, 1), state[:, last])
    middle = [state[:, SLAB : cols - SLAB]] if cols > 2 * SLAB else []
    state = jnp.concatenate([left, *middle, right], axis=1)
    end_ref[...] = state.reshape(end_ref.shape).astype(end_ref.dtype)


def halo_kernel(mine_ref, theirs_ref, lhs_ref, start_ref):
    rows = mine_ref.shape[1] // 2
    count = mine_ref.shape[0] // 2
    room = count * rows
    zero, one = is_core(0), is_core(1)
    core = lax.axis_index("sx")
    slots = ((1, 0), (2, 3))
    for frame in range(count):
        for depth in range(2):
            own = mine_ref[2 * frame + depth].astype(jnp.float32)
            other = theirs_ref[2 * frame + depth].astype(jnp.float32)
            own = row_taps(own[rows:], own[rows - 1 : rows], own[:1])
            other = row_taps(other[:rows], other[2 * rows - 1 :], other[rows : rows + 1])
            for swapped, taps in enumerate((own, other)):
                slot = jnp.where(core == swapped, slots[1][depth], slots[0][depth])
                at = pl.multiple_of(slot * room + frame * rows, rows)
                lhs_ref[pl.ds(at, rows)] = taps.astype(lhs_ref.dtype)
    own = mine_ref[2 * count, rows:].astype(jnp.float32)
    other = theirs_ref[2 * count, :rows].astype(jnp.float32)
    start_ref[:rows] = zero * other + one * own
    start_ref[rows:] = zero * own + one * other


def drive_kernel(
    lhs_ref, weight_ref, total_ref, spill_ref, pole_ref, drive_ref, beside_ref, strips_ref, end_ref
):
    count, rows, cols, wide = drive_ref.shape
    room, size = count * rows, rows * cols
    at = size + 2 * rows
    early = None
    for lanes in halves(weight_ref.shape[-1]):
        first = dot(lhs_ref[: 2 * room], weight_ref, 0, lanes)
        middle = dot(lhs_ref[room : 3 * room], weight_ref, 1, lanes)
        last = dot(lhs_ref[2 * room :], weight_ref, 2, lanes)
        left = (spill_ref[0, :, lanes] + first[:room] + middle[:room]).reshape(count, rows, wide)
        right = (spill_ref[1, :, lanes] + middle[room:] + last[room:]).reshape(count, rows, wide)
        total = total_ref[:, :, :, lanes]
        if lanes.start == 0:
            near = total[:, :, 0, :] + first[room:].reshape(count, rows, wide)
            far = total[:, :, cols - 1, :] + last[:room].reshape(count, rows, wide)
            strips = jnp.concatenate([left, near, far, right], axis=1)
            strips_ref[...] = strips
            early = end_state([strips[frame] for frame in range(count)], pole_ref, lanes)
            end_ref[at : at + rows] = early[:rows].astype(end_ref.dtype)
            end_ref[at + rows :] = early[3 * rows :].astype(end_ref.dtype)
            continue
        col = lax.broadcasted_iota(jnp.int32, drive_ref.shape, 2)
        total += jnp.where(col == 0, first[room:].reshape(count, rows, 1, wide), 0.0)
        total += jnp.where(col == cols - 1, last[:room].reshape(count, rows, 1, wide), 0.0)
        drive_ref[...] = total
        state = end_state([total[frame] for frame in range(count)], pole_ref, lanes)
        col = lax.broadcasted_iota(jnp.int32, state.shape, 1)
        state = jnp.where(col == 1, early[rows : 2 * rows].reshape(rows, 1, wide), state)
        border = early[2 * rows : 3 * rows].reshape(rows, 1, wide)
        state = jnp.where(col == cols - 2, border, state)
        end_ref[:size] = state.reshape(size, wide).astype(end_ref.dtype)
        beside = jnp.concatenate([left, right], axis=1)
        beside_ref[...] = beside
        state = end_state([beside[frame] for frame in range(count)], pole_ref, lanes)
        end_ref[size:at] = state.astype(end_ref.dtype)


def spread(block, cols, count, of_lanes):
    _, lanes, inset = block
    value = of_lanes(lanes)
    if inset is None:
        return value
    other, columns = inset
    value, instead = jnp.broadcast_arrays(value, of_lanes(other))
    shape = (count, value.shape[1])
    col = lax.rem(lax.broadcasted_iota(jnp.int32, shape, 0), cols)
    return jnp.where((col == columns[0]) | (col == columns[1]), instead, value)


def entry_kernel(frames, cols, block, ends_ref, pole_ref, out_ref):
    rate = rate_of(pole_ref)
    count = ends_ref.shape[1]
    carried = spread(block, cols, count, lambda lanes: jnp.exp(frames * rate[:, lanes]))
    entry = jnp.zeros(ends_ref.shape[1:], jnp.float32)
    out_ref[0] = entry.astype(out_ref.dtype)
    for index in range(ends_ref.shape[0] - 1):
        entry = carried * entry + ends_ref[index].astype(jnp.float32)
        out_ref[index + 1] = entry.astype(out_ref.dtype)


def exchange(pieces, pole, frames, cols):
    groups = lax.axis_size("tm")
    arrivals = []
    for end, blocks in pieces:
        entries = []
        for block in blocks:
            shares = end[block[0]].reshape(groups, -1, end.shape[1])
            assert block[2] is None or shares.shape[1] % cols == 0
            shares = lax.all_to_all(shares, "tm", 0, 0)
            kernel = functools.partial(entry_kernel, frames, cols, block)
            entry = call(kernel, of(shares.shape, end.dtype), shares, pole)
            entries.append(lax.all_to_all(entry, "tm", 0, 0).reshape(-1, end.shape[1]))
        arrivals.append((jnp.concatenate(entries, axis=0),))
    return arrivals


def pick(values):
    group = lax.axis_index("tm")
    picked = values[-1]
    for index, value in enumerate(values[:-1]):
        picked = jnp.where(group == index, value, picked)
    return picked


def on_core(first, second):
    return jnp.where(lax.axis_index("sx") == 0, first, second)


def weigh(one, by_one, other, by_other):
    return by_one * one.astype(jnp.float32) + by_other * other.astype(jnp.float32)


def relay_kernel(frames, cols, blocks, end_ref, got_ref, pole_ref, out_ref):
    rate = rate_of(pole_ref)
    carried, twice = jnp.exp(frames * rate), jnp.exp(2 * frames * rate)
    none, same = jnp.zeros_like(rate), jnp.ones_like(rate)
    own = on_core(pick([carried, same, same, same]), pick([same, same, same, none]))
    got = on_core(pick([same, carried, carried, carried]), pick([none, none, twice, same]))
    for block in blocks:
        rows = block[0]
        count = rows.stop - rows.start
        by_own = spread(block, cols, count, lambda lanes: own[:, lanes])
        by_got = spread(block, cols, count, lambda lanes: got[:, lanes])
        out_ref[rows] = weigh(end_ref[rows], by_own, got_ref[rows], by_got).astype(out_ref.dtype)


def exchange_four(pieces, pole, frames, cols):
    def along(pairs, core):
        return [(2 * source + core, 2 * target + core) for source, target in pairs]

    axes = ("tm", "sx")
    down = [(0, 2), (1, 3)]
    first_round = along([(0, 1), (1, 0), (2, 3)], 0) + along(down, 1)
    second_round = along(down, 0) + along([(0, 1), (2, 3), (3, 2)], 1)
    arrivals = []
    for end, blocks in pieces:
        got = lax.ppermute(end, axes, first_round)
        kernel = functools.partial(relay_kernel, frames, cols, blocks)
        relayed = call(kernel, of(end.shape, end.dtype), end, got, pole)
        arrivals.append((got, lax.ppermute(relayed, axes, second_round)))
    return arrivals


def gelu(x):
    slope = math.sqrt(2.0 / math.pi)
    half = 0.5 * x
    return half + half * jnp.tanh(x * (slope + (slope * 0.044715) * (x * x)))


class Mix:
    def __init__(self, lanes, count, pole_ref, scale_ref):
        self.rate = rate_of(pole_ref)[:, lanes]
        self.scale = scale_ref[:, lanes]
        self.count = count

    def entry(self, arrived_refs, rows):
        parts = [ref[rows].astype(jnp.float32) for ref in arrived_refs]
        if len(parts) == 1:
            return parts[0]
        carried = jnp.exp(self.count * self.rate)
        none, same = jnp.zeros_like(self.rate), jnp.ones_like(self.rate)
        early = on_core(pick([none, same, none, same]), pick([none, none, carried, carried]))
        late = on_core(pick([none, none, same, carried]), pick([none, same, same, same]))
        return weigh(parts[0], early, parts[1], late)

    def __call__(self, drives, entry, start):
        decay = jnp.exp(self.rate)
        reach = jnp.exp((self.count * lax.axis_index("tm")).astype(jnp.float32) * self.rate)
        state = reach * start + entry.reshape(start.shape)
        for drive in drives:
            state = decay * state + drive
            yield gelu(self.scale * state)


def no_border(cells, axis):
    col = lax.broadcasted_iota(jnp.int32, cells.shape, axis)
    return jnp.where((col == 0) | (col == cells.shape[axis] - 1), 0.0, cells)


def put_back(late, early, axis):
    cols = late.shape[axis]

    def slab(cells, start):
        return lax.slice_in_dim(cells, start, start + SLAB, axis=axis)

    first, last = slab(late, 0), slab(late, cols - SLAB)
    col = lax.broadcasted_iota(jnp.int32, first.shape, axis)
    first = jnp.where(col == 1, pltpu.roll(slab(early, 0), 1, axis), first)
    moved = pltpu.roll(slab(early, cols - SLAB), SLAB - 1, axis)
    last = jnp.where(col == SLAB - 2, moved, last)
    middle = [lax.slice_in_dim(late, SLAB, cols - SLAB, axis=axis)] if cols > 2 * SLAB else []
    return jnp.concatenate([first, *middle, last], axis=axis)


def mixed_kernel(lanes, rounds, *refs):
    drive_ref, start_ref, pole_ref, scale_ref, *arrived_refs, lhs_ref = refs
    early_refs, late_refs = arrived_refs[:rounds], arrived_refs[rounds:]
    count, rows, cols, _ = drive_ref.shape
    wide = lanes.stop - lanes.start
    size = rows * cols
    stride = lhs_ref.shape[0] // count
    room = (stride - size) // 2
    mix = Mix(lanes, count, pole_ref, scale_ref)
    first = lanes.start == 0
    held = lanes if first else slice(None)
    block = 8
    for row in range(0, rows, block):
        here = slice(row, row + block)
        drives = [drive_ref[frame, here, :, held] for frame in range(count)]
        cells = slice(row * cols, (row + block) * cols)
        entry = mix.entry(early_refs, cells).reshape(block, cols, wide)
        if not first:
            entry = put_back(mix.entry(late_refs, cells).reshape(entry.shape), entry, 1)
        for frame, tile in enumerate(mix(drives, entry, start_ref[here, :, lanes])):
            if first:
                tile = no_border(tile, 1)
            tile = tile.reshape(block * cols, wide).astype(lhs_ref.dtype)
            put_cells(lhs_ref, frame * stride + room, size, cols, row * cols, tile)


def middle_kernel(lanes, *refs):
    total_ref, start_ref, pole_ref, scale_ref, *arrived_refs, give_ref = refs
    count, rows, cols, _ = total_ref.shape
    mix = Mix(lanes, count, pole_ref, scale_ref)
    inner = inner_row(rows)
    drives = [total_ref[frame, inner, :, lanes] for frame in range(count)]
    entry = mix.entry(arrived_refs, pl.ds(pl.multiple_of(inner * cols, cols), cols))
    for frame, cells in enumerate(mix(drives, entry, start_ref[inner, :, lanes])):
        give_ref[frame] = no_border(cells, 0).astype(give_ref.dtype)


def strip_start_kernel(start_ref, sides_ref, out_ref):
    rows, cols, _ = start_ref.shape
    start = start_ref[...]
    out_ref[:rows] = sides_ref[:rows]
    out_ref[rows : 2 * rows] = start[:, 0, :]
    out_ref[2 * rows : 3 * rows] = start[:, cols - 1, :]
    out_ref[3 * rows :] = sides_ref[rows:]


def inside(slot):
    chip, chips = lax.axis_index("sy"), lax.axis_size("sy")
    return {0: (chip > 0).astype(jnp.float32), 3: (chip < chips - 1).astype(jnp.float32)}.get(slot, 1.0)


def give_kernel(parts, rounds, *refs):
    drive_ref, beside_ref, strips_ref, *refs = refs
    start_ref, strip_start_ref, pole_ref, scale_ref, *arrived_refs, give_ref = refs
    early_refs, late_refs = arrived_refs[:rounds], arrived_refs[rounds:]
    count, rows, cols, wide = drive_ref.shape
    size = rows * cols
    inner = inner_row(rows)
    zero, one = is_core(0), is_core(1)
    early, late = (Mix(lanes, count, pole_ref, scale_ref) for lanes in parts)
    row = pl.ds(pl.multiple_of(inner * cols, cols), cols)
    which = lax.broadcasted_iota(jnp.int32, (cols, wide), 0)

    def near(at):
        return pl.ds(pl.multiple_of(at + jnp.where(inner == 0, 0, rows - cols), cols), cols)

    def end(cells):
        return zero * cells[cols - 1 :] + one * cells[:1]

    def rows_of(cells):
        table = jnp.zeros(which.shape, jnp.float32)
        for index, cell in cells:
            table = jnp.where(which == index, cell, table)
        return table

    entry = put_back(late.entry(late_refs, row), late.entry(early_refs, row), 0)
    drives = [drive_ref[frame, inner] for frame in range(count)]
    tile = late(drives, entry, start_ref[inner, :, parts[1]])

    slots = [(0, 0), (1, 3)]
    entry = rows_of([(i, end(late.entry(late_refs, near(size + i * rows)))) for i, _ in slots])
    start = rows_of([(i, end(strip_start_ref[near(slot * rows), parts[1]])) for i, slot in slots])
    drives = [
        rows_of([(i, end(beside_ref[frame, near(i * rows)])) for i, _ in slots])
        for frame in range(count)
    ]
    beside = late(drives, entry, start)

    slots = [(2 + slot, slot) for slot in range(4)]
    grid = early.entry(late_refs, row)
    at = size + 2 * rows
    entry = rows_of(
        [
            (2, end(early.entry(late_refs, near(at)))),
            (3, grid[1:2]),
            (4, grid[cols - 2 : cols - 1]),
            (5, end(early.entry(late_refs, near(at + rows)))),
        ]
    )
    start = rows_of([(i, end(strip_start_ref[near(slot * rows), parts[0]])) for i, slot in slots])
    drives = [
        rows_of([(i, end(strips_ref[frame, near(slot * rows)])) for i, slot in slots])
        for frame in range(count)
    ]
    strips = early(drives, entry, start)
    for frame, cells in enumerate(zip(tile, beside, strips)):
        give_ref[frame, :cols] = cells[0].astype(give_ref.dtype)
        ends = jnp.where(which < 2, cells[1], cells[2])
        ends = jnp.where((which == 0) | (which == 2), inside(0) * ends, ends)
        ends = jnp.where((which == 1) | (which == 5), inside(3) * ends, ends)
        give_ref[frame, cols:] = ends.astype(give_ref.dtype)


def late_kernel(parts, rounds, *refs):
    beside_ref, strips_ref, strip_start_ref, pole_ref, scale_ref, *refs = refs
    *late_refs, beside_out_ref, strips_out_ref = refs
    count, room, wide = beside_ref.shape
    rows = room // 2
    size = late_refs[0].shape[0] - 4 * rows
    cols = size // rows
    early, late = (Mix(lanes, count, pole_ref, scale_ref) for lanes in parts)

    def column(cells, index):
        return cells[index * rows : (index + 1) * rows]

    starts = [strip_start_ref[slot * rows : (slot + 1) * rows, parts[1]] for slot in (0, 3)]
    entry = late.entry(late_refs, slice(size, size + 2 * rows))
    drives = [beside_ref[frame] for frame in range(count)]
    beside = late(drives, entry, jnp.concatenate(starts, axis=0))
    grid = early.entry(late_refs, slice(0, size)).reshape(rows, cols, wide)
    sides = early.entry(late_refs, slice(size + 2 * rows, size + 4 * rows))
    entry = [sides[:rows], grid[:, 1, :], grid[:, cols - 2, :], sides[rows:]]
    drives = [strips_ref[frame] for frame in range(count)]
    strips = early(drives, jnp.concatenate(entry, axis=0), strip_start_ref[:, parts[0]])
    for frame, (sides, strip) in enumerate(zip(beside, strips)):
        sides = [column(sides, 0) * inside(0), column(sides, 1) * inside(3)]
        strip = [column(strip, slot) * inside(slot) for slot in range(4)]
        beside_out_ref[frame] = jnp.concatenate(sides, axis=0).astype(beside_out_ref.dtype)
        strips_out_ref[frame] = jnp.concatenate(strip, axis=0).astype(strips_out_ref.dtype)


def put_columns_taps(lhs_ref, slots, columns, ends):
    rows = columns.shape[0] // len(slots)
    columns, ends = columns.astype(jnp.float32), ends.astype(jnp.float32)
    for index, at in enumerate(slots):
        column, end = columns[index * rows : (index + 1) * rows], ends[index : index + 1]
        lhs_ref[at : at + rows] = row_taps(column, end, end).astype(lhs_ref.dtype)


def tile_sum(tile, inputs, lanes, room, lhs_ref, weight_ref):
    count, rows, cols, wide = tile
    size = rows * cols
    col = lax.broadcasted_iota(jnp.int32, tile[1:], 1)

    def beside(cells):
        return cells.reshape(rows, 1, wide) if room else 0.0

    for frame in range(count):
        at = frame * (size + 2 * room)
        end = at + room + size
        total = dot(lhs_ref[at + room : end], weight_ref, 1, lanes, inputs).reshape(tile[1:])
        first = dot(lhs_ref[at:end], weight_ref, 0, lanes, inputs)
        shifted = pltpu.roll(first[room:].reshape(tile[1:]), 1, 1)
        total += jnp.where(col == 0, beside(first[:room]), shifted)
        last = dot(lhs_ref[at + room : end + room], weight_ref, 2, lanes, inputs)
        shifted = pltpu.roll(last[:size].reshape(tile[1:]), cols - 1, 1)
        yield total + jnp.where(col == cols - 1, beside(last[size:]), shifted)


def strip_sum(tile, inputs, lanes, lhs_ref, weight_ref):
    count, rows, cols, wide = tile
    room = count * rows
    first = dot(lhs_ref[: 2 * room], weight_ref, 0, lanes, inputs)
    middle = dot(lhs_ref[room : 3 * room], weight_ref, 1, lanes, inputs)
    last = dot(lhs_ref[2 * room :], weight_ref, 2, lanes, inputs)
    columns = [
        (0, first[:room] + middle[:room]),
        (1, first[room:]),
        (cols - 2, last[:room]),
        (cols - 1, middle[room:] + last[room:]),
    ]
    return [(at, cells.reshape(count, rows, 1, wide)) for at, cells in columns]


def opening_kernel(inputs, lanes, _, got_ref, weight_ref, out_ref, lhs_ref):
    count, rows, cols, _ = out_ref.shape
    size = rows * cols
    for frame in range(count):
        put_row(lhs_ref, frame * size, size, got_ref[frame])
    further_kernel(inputs, lanes, lhs_ref, weight_ref, out_ref)


def further_kernel(inputs, lanes, lhs_ref, weight_ref, out_ref):
    tiles = tile_sum(out_ref.shape, inputs, lanes, 0, lhs_ref, weight_ref)
    for frame, total in enumerate(tiles):
        out_ref[frame] = total


def result_kernel(
    parts, _, got_ref, beside_ref, strips_ref, weight_ref, *refs
):
    *before_refs, out_ref, lhs_ref, held_ref, strip_lhs_ref, sems = refs
    count, rows, cols, _ = held_ref.shape
    size, room = rows * cols, count * rows
    stride = size + 2 * rows
    for frame in range(count):
        at = frame * stride
        put_row(lhs_ref, at + rows, size, got_ref[frame, :cols])
        ends = got_ref[frame, cols:]
        put_columns_taps(lhs_ref, (at, at + rows + size), beside_ref[frame], ends)
        slots = [slot * room + frame * rows for slot in range(4)]
        put_columns_taps(strip_lhs_ref, slots, strips_ref[frame], ends.astype(jnp.float32)[2:])

    def store(frame, part):
        here = (frame, slice(None), slice(None), parts[part])
        return pltpu.make_async_copy(held_ref.at[here], out_ref.at[here], sems.at[frame, part])

    for part, lanes in enumerate(parts):
        tile = (count, rows, cols, lanes.stop - lanes.start)
        col = lax.broadcasted_iota(jnp.int32, tile[1:], 1)
        columns = strip_sum(tile, parts[0], lanes, strip_lhs_ref, weight_ref)
        tiles = tile_sum(tile, parts[1], lanes, rows, lhs_ref, weight_ref)
        for frame, total in enumerate(tiles):
            strips = 0.0
            for at, cells in columns:
                strips = jnp.where(col == at, cells[frame], strips)
            total += before_refs[part][frame] + strips
            held_ref[frame, :, :, lanes] = total.astype(held_ref.dtype)
            store(frame, part).start()
    for part in range(len(parts)):
        for frame in range(count):
            store(frame, part).wait()


def on_device(frames, input_weight, output_weight, pole_index, gelu_scale, start_state):
    count, rows, cols, channels = frames.shape
    size, room = rows * cols, count * rows
    wide = 3 * channels
    assert lax.axis_size("sx") == 2
    narrow = frames.dtype
    pole, scale = pole_index[None], gelu_scale[None]

    shapes = (
        of((count * cols + (2 * count + 1) * rows, channels), narrow),
        of((2 * count + 1, rows, channels), narrow),
    )
    edges = call(
        edges_kernel,
        shapes,
        frames,
        scratch=[pltpu.VMEM((count, channels // 128, size, 128), jnp.float32)],
        flops=EDGES_COST,
    )
    give, keep = call(
        start_edges_kernel,
        shapes,
        start_state,
        *edges,
        aliases={1: 0, 2: 1},
        scratch=[pltpu.VMEM((channels // 128, size, 128), jnp.float32)],
    )
    got, mine = trade_columns(give, keep, count * cols)
    taps = of((count * size, wide), narrow)
    parts = halves(channels)
    half = channels // 2
    inner = of((count, rows, cols, half), jnp.float32)
    *main, early, _ = call(
        main_kernel,
        (
            of(frames.shape, jnp.float32),
            of((2, room, channels), jnp.float32),
            of((size, half), narrow),
            taps,
        ),
        call(taps_kernel, taps, frames),
        got,
        input_weight,
        pole,
        aliases={0: 3},
        flops=18 * frames.size * channels,
    )
    mine, total, spill = lax.optimization_barrier((mine, *main))
    halo, sides = call(
        halo_kernel,
        (of((4 * room, wide), narrow), of((2 * rows, channels), jnp.float32)),
        mine,
        swap_cores(mine),
    )
    drive, beside, strips, late = call(
        drive_kernel,
        (
            inner,
            of((count, 2 * rows, half), jnp.float32),
            of((count, 4 * rows, half), jnp.float32),
            of((size + 4 * rows, half), narrow),
        ),
        halo,
        input_weight,
        total,
        spill,
        pole,
        flops=36 * room * channels * channels,
    )
    at = size + 2 * rows
    tile = slice(0, size)
    pieces = [
        (early, [(tile, parts[0], (parts[1], (0, cols - 1)))]),
        (
            late,
            [
                (tile, parts[1], (parts[0], (1, cols - 2))),
                (slice(size, at), parts[1], None),
                (slice(at, at + 2 * rows), parts[0], None),
            ],
        ),
    ]
    exchanged = exchange_four if lax.axis_size("tm") == 4 else exchange
    early, late = exchanged(pieces, pole, count, cols)
    rounds = len(early)

    mixing = (start_state, pole, scale)
    taps = of((count * size, 3 * half), narrow)
    give = call(
        functools.partial(middle_kernel, parts[0]),
        of((count, cols, half), narrow),
        total,
        *mixing,
        *early,
    )
    lhs = call(functools.partial(mixed_kernel, parts[0], rounds), taps, total, *mixing, *early)
    strip_start = call(strip_start_kernel, of((4 * rows, channels), jnp.float32), start_state, sides)
    flops = 18 * inner.size * half
    lhs, strip_start = lax.optimization_barrier((lhs, strip_start))
    first_sum, lhs = call(
        functools.partial(opening_kernel, parts[0], parts[0]),
        (inner, taps),
        lhs,
        swap_cores(give),
        output_weight,
        aliases={0: 1},
        flops=flops,
    )
    second_sum = call(
        functools.partial(further_kernel, parts[0], parts[1]),
        inner,
        lhs,
        output_weight,
        flops=flops,
    )
    *late, first_sum, second_sum = lax.optimization_barrier((*late, first_sum, second_sum))
    give = call(
        functools.partial(give_kernel, parts, rounds),
        of((count, 2 * cols, half), narrow),
        drive,
        beside,
        strips,
        start_state,
        strip_start,
        pole,
        scale,
        *early,
        *late,
    )
    beside, strips = call(
        functools.partial(late_kernel, parts, rounds),
        (of(beside.shape, narrow), of(strips.shape, narrow)),
        beside,
        strips,
        strip_start,
        pole,
        scale,
        *late,
    )
    taps = of((count * size + 2 * room, 3 * half), narrow)
    lhs = call(
        functools.partial(mixed_kernel, parts[1], rounds), taps, drive, *mixing, *early, *late
    )
    result, _ = call(
        functools.partial(result_kernel, parts),
        (of(frames.shape, narrow), taps),
        lhs,
        swap_cores(give),
        beside,
        strips,
        output_weight,
        first_sum,
        second_sum,
        out_specs=(HBM, WHOLE),
        aliases={0: 1},
        scratch=[
            pltpu.VMEM(frames.shape, narrow),
            pltpu.VMEM((4 * room, 3 * half), narrow),
            pltpu.SemaphoreType.DMA((count, len(parts))),
        ],
        flops=2 * flops,
    )
    return result


def solution(mesh):
    return jax.shard_map(
        on_device,
        mesh=mesh,
        in_specs=(P("tm", "sx", "sy", None), P(), P(), P(), P(), P("sx", "sy", None)),
        out_specs=P("tm", "sx", "sy", None),
        check_vma=False,
    )
```

```python
import functools
import math

import jax
import jax.numpy as jnp
from jax import lax
from jax.experimental import pallas as pl
from jax.experimental.pallas import tpu as pltpu
from jax.sharding import PartitionSpec as P

NPOLES = 16
VMEM_LIMIT = 24 * 1024 * 1024
WHOLE = pl.BlockSpec(memory_space=pltpu.VMEM)
HBM = pl.BlockSpec(memory_space=pltpu.HBM)
EDGES_COST = 2_000_000_000


def call(kernel, out_shape, *args, scratch=(), flops=0, out_specs=None, aliases=None):
    outs = jax.tree.leaves(out_shape)
    moved = sum(leaf.size * leaf.dtype.itemsize for leaf in (*args, *outs))
    return pl.pallas_call(
        kernel,
        in_specs=[WHOLE] * len(args),
        out_specs=out_specs or jax.tree.map(lambda _: WHOLE, out_shape),
        out_shape=out_shape,
        scratch_shapes=scratch,
        input_output_aliases=aliases or {},
        compiler_params=pltpu.CompilerParams(vmem_limit_bytes=VMEM_LIMIT),
        cost_estimate=pl.CostEstimate(flops=flops, bytes_accessed=moved, transcendentals=0),
    )(*args)


def of(shape, dtype):
    return jax.ShapeDtypeStruct(shape, dtype)


def is_core(which):
    return (lax.axis_index("sx") == which).astype(jnp.float32)


def rate_of(pole_ref):
    pole = pole_ref[...].astype(jnp.float32)
    return -0.001 * jnp.exp(pole * (math.log(300.0) / (NPOLES - 1)))


def inner_row(rows):
    return jnp.where(lax.axis_index("sx") == 0, rows - 1, 0)


def swap_cores(array):
    return lax.ppermute(array, "sx", [(0, 1), (1, 0)])


def put_columns(index, left, right, give_ref, keep_ref):
    zero, one = is_core(0), is_core(1)
    count, rows, _ = keep_ref.shape
    at = give_ref.shape[0] - (count - index) * rows
    give_ref[at : at + rows] = (zero * left + one * right).astype(give_ref.dtype)
    keep_ref[index] = (zero * right + one * left).astype(keep_ref.dtype)


def columns_of(tile, wide_ref, picked):
    rows, cols, channels = tile.shape
    parts, _, lanes = wide_ref.shape
    tile = tile.reshape(rows * cols, channels)
    for part in range(parts):
        wide_ref[part] = tile[:, part * lanes : (part + 1) * lanes]
    return [
        jnp.concatenate(
            [wide_ref[part, pl.ds(col, rows, stride=cols), :] for part in range(parts)], axis=1
        )
        for col in picked
    ]


def edges_kernel(cells_ref, give_ref, keep_ref, wide_ref):
    count, rows, cols, channels = cells_ref.shape
    for frame in range(count):
        give_ref[frame * cols : (frame + 1) * cols] = cells_ref[frame, inner_row(rows)]
        tile = cells_ref[frame].astype(jnp.float32)
        picked = (0, 1, cols - 1, cols - 2)
        columns = columns_of(tile, wide_ref.at[frame], picked)
        for depth in range(2):
            left, right = columns[depth], columns[2 + depth]
            put_columns(2 * frame + depth, left, right, give_ref, keep_ref)


def start_edges_kernel(start_ref, _, __, give_ref, keep_ref, wide_ref):
    cols = start_ref.shape[1]
    left, right = columns_of(start_ref[...], wide_ref, (0, cols - 1))
    put_columns(keep_ref.shape[0] - 1, left, right, give_ref, keep_ref)


def trade_columns(give, keep, at):
    chips = lax.axis_size("sy")
    got = swap_cores(give)
    pairs = [(chip, chips + chip + 1) for chip in range(chips - 1)]
    pairs += [(after, before) for before, after in pairs]
    columns = jnp.concatenate([keep, got[at:].reshape(keep.shape)], axis=1)
    return got, lax.ppermute(columns, ("sx", "sy"), pairs)


def put_cells(lhs_ref, at, size, cols, first, cells):
    count, channels = cells.shape
    upper, lower = min(count, size - cols - first), max(0, cols - first)
    here = at + first
    lhs_ref[here : here + count, channels : 2 * channels] = cells
    lhs_ref[here + cols : here + cols + upper, :channels] = cells[:upper]
    lhs_ref[here + lower - cols : here + count - cols, 2 * channels :] = cells[lower:]


def put_row(lhs_ref, at, size, row):
    cols, channels = row.shape
    row = row.astype(jnp.float32)
    last = slice(at + size - cols, at + size)
    lhs_ref[at : at + cols, :channels] = (is_core(1) * row).astype(lhs_ref.dtype)
    lhs_ref[last, 2 * channels :] = (is_core(0) * row).astype(lhs_ref.dtype)


def taps_kernel(cells_ref, lhs_ref):
    count, rows, cols, channels = cells_ref.shape
    size = rows * cols
    for frame in range(count):
        put_cells(lhs_ref, frame * size, size, cols, 0, cells_ref[frame].reshape(size, channels))


def row_taps(column, above, below):
    rows = column.shape[0]
    row = lax.broadcasted_iota(jnp.int32, column.shape, 0)
    up = jnp.where(row == 0, is_core(1) * above, pltpu.roll(column, 1, 0))
    down = jnp.where(row == rows - 1, is_core(0) * below, pltpu.roll(column, rows - 1, 0))
    return jnp.concatenate([up, column, down], axis=1)


SLAB = 8


def halves(channels):
    return slice(0, channels // 2), slice(channels // 2, channels)


def end_state(frames, pole_ref, lanes):
    decay = jnp.exp(rate_of(pole_ref))[:, lanes]
    state = frames[0]
    for frame in frames[1:]:
        state = decay * state + frame
    return state


def dot(lhs, weight_ref, column, lanes, inputs=slice(None)):
    weight = weight_ref[:, column, inputs, lanes].reshape(lhs.shape[1], -1)
    return jnp.dot(lhs, weight, preferred_element_type=jnp.float32)


def main_kernel(_, got_ref, weight_ref, pole_ref, total_ref, spill_ref, end_ref, lhs_ref):
    count, rows, cols, _ = total_ref.shape
    size = rows * cols
    for frame in range(count):
        put_row(lhs_ref, frame * size, size, got_ref[frame * cols : (frame + 1) * cols])
    states = []
    for lanes in halves(weight_ref.shape[-1]):
        tile = (rows, cols, lanes.stop - lanes.start)
        col = lax.broadcasted_iota(jnp.int32, tile, 1)
        totals = []
        for frame in range(count):
            cells = lhs_ref[frame * size : (frame + 1) * size]
            here = slice(frame * rows, (frame + 1) * rows)
            total = dot(cells, weight_ref, 1, lanes).reshape(tile)
            first = dot(cells, weight_ref, 0, lanes).reshape(tile)
            spill_ref[1, here, lanes] = first[:, cols - 1, :]
            total += jnp.where(col == 0, 0.0, pltpu.roll(first, 1, 1))
            last = dot(cells, weight_ref, 2, lanes).reshape(tile)
            spill_ref[0, here, lanes] = last[:, 0, :]
            total += jnp.where(col == cols - 1, 0.0, pltpu.roll(last, cols - 1, 1))
            total_ref[frame, :, :, lanes] = total
            totals.append(total)
        states.append(end_state(totals, pole_ref, lanes))
    state, other = states
    col = lax.broadcasted_iota(jnp.int32, (rows, SLAB, state.shape[2]), 1)
    last = slice(cols - SLAB, cols)
    left = jnp.where(col == 0, pltpu.roll(other[:, :SLAB], SLAB - 1, 1), state[:, :SLAB])
    right = jnp.where(col == SLAB - 1, pltpu.roll(other[:, last], 1, 1), state[:, last])
    middle = [state[:, SLAB : cols - SLAB]] if cols > 2 * SLAB else []
    state = jnp.concatenate([left, *middle, right], axis=1)
    end_ref[...] = state.reshape(end_ref.shape).astype(end_ref.dtype)


def halo_kernel(mine_ref, theirs_ref, lhs_ref, start_ref):
    rows = mine_ref.shape[1] // 2
    count = mine_ref.shape[0] // 2
    room = count * rows
    zero, one = is_core(0), is_core(1)
    core = lax.axis_index("sx")
    slots = ((1, 0), (2, 3))
    for frame in range(count):
        for depth in range(2):
            own = mine_ref[2 * frame + depth].astype(jnp.float32)
            other = theirs_ref[2 * frame + depth].astype(jnp.float32)
            own = row_taps(own[rows:], own[rows - 1 : rows], own[:1])
            other = row_taps(other[:rows], other[2 * rows - 1 :], other[rows : rows + 1])
            for swapped, taps in enumerate((own, other)):
                slot = jnp.where(core == swapped, slots[1][depth], slots[0][depth])
                at = pl.multiple_of(slot * room + frame * rows, rows)
                lhs_ref[pl.ds(at, rows)] = taps.astype(lhs_ref.dtype)
    own = mine_ref[2 * count, rows:].astype(jnp.float32)
    other = theirs_ref[2 * count, :rows].astype(jnp.float32)
    start_ref[:rows] = zero * other + one * own
    start_ref[rows:] = zero * own + one * other


def drive_kernel(
    lhs_ref, weight_ref, total_ref, spill_ref, pole_ref, drive_ref, beside_ref, strips_ref, end_ref
):
    count, rows, cols, wide = drive_ref.shape
    room, size = count * rows, rows * cols
    at = size + 2 * rows
    early = None
    for lanes in halves(weight_ref.shape[-1]):
        first = dot(lhs_ref[: 2 * room], weight_ref, 0, lanes)
        middle = dot(lhs_ref[room : 3 * room], weight_ref, 1, lanes)
        last = dot(lhs_ref[2 * room :], weight_ref, 2, lanes)
        left = (spill_ref[0, :, lanes] + first[:room] + middle[:room]).reshape(count, rows, wide)
        right = (spill_ref[1, :, lanes] + middle[room:] + last[room:]).reshape(count, rows, wide)
        total = total_ref[:, :, :, lanes]
        if lanes.start == 0:
            near = total[:, :, 0, :] + first[room:].reshape(count, rows, wide)
            far = total[:, :, cols - 1, :] + last[:room].reshape(count, rows, wide)
            strips = jnp.concatenate([left, near, far, right], axis=1)
            strips_ref[...] = strips
            early = end_state([strips[frame] for frame in range(count)], pole_ref, lanes)
            end_ref[at : at + rows] = early[:rows].astype(end_ref.dtype)
            end_ref[at + rows :] = early[3 * rows :].astype(end_ref.dtype)
            continue
        col = lax.broadcasted_iota(jnp.int32, drive_ref.shape, 2)
        total += jnp.where(col == 0, first[room:].reshape(count, rows, 1, wide), 0.0)
        total += jnp.where(col == cols - 1, last[:room].reshape(count, rows, 1, wide), 0.0)
        drive_ref[...] = total
        state = end_state([total[frame] for frame in range(count)], pole_ref, lanes)
        col = lax.broadcasted_iota(jnp.int32, state.shape, 1)
        state = jnp.where(col == 1, early[rows : 2 * rows].reshape(rows, 1, wide), state)
        border = early[2 * rows : 3 * rows].reshape(rows, 1, wide)
        state = jnp.where(col == cols - 2, border, state)
        end_ref[:size] = state.reshape(size, wide).astype(end_ref.dtype)
        beside = jnp.concatenate([left, right], axis=1)
        beside_ref[...] = beside
        state = end_state([beside[frame] for frame in range(count)], pole_ref, lanes)
        end_ref[size:at] = state.astype(end_ref.dtype)


def spread(block, cols, count, of_lanes):
    _, lanes, inset = block
    value = of_lanes(lanes)
    if inset is None:
        return value
    other, columns = inset
    value, instead = jnp.broadcast_arrays(value, of_lanes(other))
    shape = (count, value.shape[1])
    col = lax.rem(lax.broadcasted_iota(jnp.int32, shape, 0), cols)
    return jnp.where((col == columns[0]) | (col == columns[1]), instead, value)


def entry_kernel(frames, cols, block, ends_ref, pole_ref, out_ref):
    rate = rate_of(pole_ref)
    count = ends_ref.shape[1]
    carried = spread(block, cols, count, lambda lanes: jnp.exp(frames * rate[:, lanes]))
    entry = jnp.zeros(ends_ref.shape[1:], jnp.float32)
    out_ref[0] = entry.astype(out_ref.dtype)
    for index in range(ends_ref.shape[0] - 1):
        entry = carried * entry + ends_ref[index].astype(jnp.float32)
        out_ref[index + 1] = entry.astype(out_ref.dtype)


def exchange(pieces, pole, frames, cols):
    groups = lax.axis_size("tm")
    arrivals = []
    for end, blocks in pieces:
        entries = []
        for block in blocks:
            shares = end[block[0]].reshape(groups, -1, end.shape[1])
            assert block[2] is None or shares.shape[1] % cols == 0
            shares = lax.all_to_all(shares, "tm", 0, 0)
            kernel = functools.partial(entry_kernel, frames, cols, block)
            entry = call(kernel, of(shares.shape, end.dtype), shares, pole)
            entries.append(lax.all_to_all(entry, "tm", 0, 0).reshape(-1, end.shape[1]))
        arrivals.append((jnp.concatenate(entries, axis=0),))
    return arrivals


def pick(values):
    group = lax.axis_index("tm")
    picked = values[-1]
    for index, value in enumerate(values[:-1]):
        picked = jnp.where(group == index, value, picked)
    return picked


def on_core(first, second):
    return jnp.where(lax.axis_index("sx") == 0, first, second)


def weigh(one, by_one, other, by_other):
    return by_one * one.astype(jnp.float32) + by_other * other.astype(jnp.float32)


def relay_kernel(frames, cols, blocks, end_ref, got_ref, pole_ref, out_ref):
    rate = rate_of(pole_ref)
    carried, twice = jnp.exp(frames * rate), jnp.exp(2 * frames * rate)
    none, same = jnp.zeros_like(rate), jnp.ones_like(rate)
    own = on_core(pick([carried, same, same, same]), pick([same, same, same, none]))
    got = on_core(pick([same, carried, carried, carried]), pick([none, none, twice, same]))
    for block in blocks:
        rows = block[0]
        count = rows.stop - rows.start
        by_own = spread(block, cols, count, lambda lanes: own[:, lanes])
        by_got = spread(block, cols, count, lambda lanes: got[:, lanes])
        out_ref[rows] = weigh(end_ref[rows], by_own, got_ref[rows], by_got).astype(out_ref.dtype)


def exchange_four(pieces, pole, frames, cols):
    def along(pairs, core):
        return [(2 * source + core, 2 * target + core) for source, target in pairs]

    axes = ("tm", "sx")
    down = [(0, 2), (1, 3)]
    first_round = along([(0, 1), (1, 0), (2, 3)], 0) + along(down, 1)
    second_round = along(down, 0) + along([(0, 1), (2, 3), (3, 2)], 1)
    arrivals = []
    for end, blocks in pieces:
        got = lax.ppermute(end, axes, first_round)
        kernel = functools.partial(relay_kernel, frames, cols, blocks)
        relayed = call(kernel, of(end.shape, end.dtype), end, got, pole)
        arrivals.append((got, lax.ppermute(relayed, axes, second_round)))
    return arrivals


def gelu(x):
    slope = math.sqrt(2.0 / math.pi)
    half = 0.5 * x
    return half + half * jnp.tanh(x * (slope + (slope * 0.044715) * (x * x)))


class Mix:
    def __init__(self, lanes, count, pole_ref, scale_ref):
        self.rate = rate_of(pole_ref)[:, lanes]
        self.scale = scale_ref[:, lanes]
        self.count = count

    def entry(self, arrived_refs, rows):
        parts = [ref[rows].astype(jnp.float32) for ref in arrived_refs]
        if len(parts) == 1:
            return parts[0]
        carried = jnp.exp(self.count * self.rate)
        none, same = jnp.zeros_like(self.rate), jnp.ones_like(self.rate)
        early = on_core(pick([none, same, none, same]), pick([none, none, carried, carried]))
        late = on_core(pick([none, none, same, carried]), pick([none, same, same, same]))
        return weigh(parts[0], early, parts[1], late)

    def __call__(self, drives, entry, start):
        decay = jnp.exp(self.rate)
        reach = jnp.exp((self.count * lax.axis_index("tm")).astype(jnp.float32) * self.rate)
        state = reach * start + entry.reshape(start.shape)
        for drive in drives:
            state = decay * state + drive
            yield gelu(self.scale * state)


def no_border(cells, axis):
    col = lax.broadcasted_iota(jnp.int32, cells.shape, axis)
    return jnp.where((col == 0) | (col == cells.shape[axis] - 1), 0.0, cells)


def put_back(late, early, axis):
    cols = late.shape[axis]

    def slab(cells, start):
        return lax.slice_in_dim(cells, start, start + SLAB, axis=axis)

    first, last = slab(late, 0), slab(late, cols - SLAB)
    col = lax.broadcasted_iota(jnp.int32, first.shape, axis)
    first = jnp.where(col == 1, pltpu.roll(slab(early, 0), 1, axis), first)
    moved = pltpu.roll(slab(early, cols - SLAB), SLAB - 1, axis)
    last = jnp.where(col == SLAB - 2, moved, last)
    middle = [lax.slice_in_dim(late, SLAB, cols - SLAB, axis=axis)] if cols > 2 * SLAB else []
    return jnp.concatenate([first, *middle, last], axis=axis)


def mixed_kernel(lanes, rounds, *refs):
    drive_ref, start_ref, pole_ref, scale_ref, *arrived_refs, lhs_ref = refs
    early_refs, late_refs = arrived_refs[:rounds], arrived_refs[rounds:]
    count, rows, cols, _ = drive_ref.shape
    wide = lanes.stop - lanes.start
    size = rows * cols
    stride = lhs_ref.shape[0] // count
    room = (stride - size) // 2
    mix = Mix(lanes, count, pole_ref, scale_ref)
    first = lanes.start == 0
    held = lanes if first else slice(None)
    block = 4
    for row in range(0, rows, block):
        here = slice(row, row + block)
        drives = [drive_ref[frame, here, :, held] for frame in range(count)]
        cells = slice(row * cols, (row + block) * cols)
        entry = mix.entry(early_refs, cells).reshape(block, cols, wide)
        if not first:
            entry = put_back(mix.entry(late_refs, cells).reshape(entry.shape), entry, 1)
        for frame, tile in enumerate(mix(drives, entry, start_ref[here, :, lanes])):
            if first:
                tile = no_border(tile, 1)
            tile = tile.reshape(block * cols, wide).astype(lhs_ref.dtype)
            put_cells(lhs_ref, frame * stride + room, size, cols, row * cols, tile)


def middle_kernel(lanes, *refs):
    total_ref, start_ref, pole_ref, scale_ref, *arrived_refs, give_ref = refs
    count, rows, cols, _ = total_ref.shape
    mix = Mix(lanes, count, pole_ref, scale_ref)
    inner = inner_row(rows)
    drives = [total_ref[frame, inner, :, lanes] for frame in range(count)]
    entry = mix.entry(arrived_refs, pl.ds(pl.multiple_of(inner * cols, cols), cols))
    for frame, cells in enumerate(mix(drives, entry, start_ref[inner, :, lanes])):
        give_ref[frame] = no_border(cells, 0).astype(give_ref.dtype)


def strip_start_kernel(start_ref, sides_ref, out_ref):
    rows, cols, _ = start_ref.shape
    start = start_ref[...]
    out_ref[:rows] = sides_ref[:rows]
    out_ref[rows : 2 * rows] = start[:, 0, :]
    out_ref[2 * rows : 3 * rows] = start[:, cols - 1, :]
    out_ref[3 * rows :] = sides_ref[rows:]


def inside(slot):
    chip, chips = lax.axis_index("sy"), lax.axis_size("sy")
    return {0: (chip > 0).astype(jnp.float32), 3: (chip < chips - 1).astype(jnp.float32)}.get(slot, 1.0)


def give_kernel(parts, rounds, *refs):
    drive_ref, beside_ref, strips_ref, *refs = refs
    start_ref, strip_start_ref, pole_ref, scale_ref, *arrived_refs, give_ref = refs
    early_refs, late_refs = arrived_refs[:rounds], arrived_refs[rounds:]
    count, rows, cols, wide = drive_ref.shape
    size = rows * cols
    inner = inner_row(rows)
    zero, one = is_core(0), is_core(1)
    early, late = (Mix(lanes, count, pole_ref, scale_ref) for lanes in parts)
    row = pl.ds(pl.multiple_of(inner * cols, cols), cols)
    which = lax.broadcasted_iota(jnp.int32, (cols, wide), 0)

    def near(at):
        return pl.ds(pl.multiple_of(at + jnp.where(inner == 0, 0, rows - cols), cols), cols)

    def end(cells):
        return zero * cells[cols - 1 :] + one * cells[:1]

    def rows_of(cells):
        table = jnp.zeros(which.shape, jnp.float32)
        for index, cell in cells:
            table = jnp.where(which == index, cell, table)
        return table

    entry = put_back(late.entry(late_refs, row), late.entry(early_refs, row), 0)
    drives = [drive_ref[frame, inner] for frame in range(count)]
    tile = late(drives, entry, start_ref[inner, :, parts[1]])

    slots = [(0, 0), (1, 3)]
    entry = rows_of([(i, end(late.entry(late_refs, near(size + i * rows)))) for i, _ in slots])
    start = rows_of([(i, end(strip_start_ref[near(slot * rows), parts[1]])) for i, slot in slots])
    drives = [
        rows_of([(i, end(beside_ref[frame, near(i * rows)])) for i, _ in slots])
        for frame in range(count)
    ]
    beside = late(drives, entry, start)

    slots = [(2 + slot, slot) for slot in range(4)]
    grid = early.entry(late_refs, row)
    at = size + 2 * rows
    entry = rows_of(
        [
            (2, end(early.entry(late_refs, near(at)))),
            (3, grid[1:2]),
            (4, grid[cols - 2 : cols - 1]),
            (5, end(early.entry(late_refs, near(at + rows)))),
        ]
    )
    start = rows_of([(i, end(strip_start_ref[near(slot * rows), parts[0]])) for i, slot in slots])
    drives = [
        rows_of([(i, end(strips_ref[frame, near(slot * rows)])) for i, slot in slots])
        for frame in range(count)
    ]
    strips = early(drives, entry, start)
    for frame, cells in enumerate(zip(tile, beside, strips)):
        give_ref[frame, :cols] = cells[0].astype(give_ref.dtype)
        ends = jnp.where(which < 2, cells[1], cells[2])
        ends = jnp.where((which == 0) | (which == 2), inside(0) * ends, ends)
        ends = jnp.where((which == 1) | (which == 5), inside(3) * ends, ends)
        give_ref[frame, cols:] = ends.astype(give_ref.dtype)


def late_kernel(parts, rounds, *refs):
    beside_ref, strips_ref, strip_start_ref, pole_ref, scale_ref, *refs = refs
    *late_refs, beside_out_ref, strips_out_ref = refs
    count, room, wide = beside_ref.shape
    rows = room // 2
    size = late_refs[0].shape[0] - 4 * rows
    cols = size // rows
    early, late = (Mix(lanes, count, pole_ref, scale_ref) for lanes in parts)

    def column(cells, index):
        return cells[index * rows : (index + 1) * rows]

    starts = [strip_start_ref[slot * rows : (slot + 1) * rows, parts[1]] for slot in (0, 3)]
    entry = late.entry(late_refs, slice(size, size + 2 * rows))
    drives = [beside_ref[frame] for frame in range(count)]
    beside = late(drives, entry, jnp.concatenate(starts, axis=0))
    grid = early.entry(late_refs, slice(0, size)).reshape(rows, cols, wide)
    sides = early.entry(late_refs, slice(size + 2 * rows, size + 4 * rows))
    entry = [sides[:rows], grid[:, 1, :], grid[:, cols - 2, :], sides[rows:]]
    drives = [strips_ref[frame] for frame in range(count)]
    strips = early(drives, jnp.concatenate(entry, axis=0), strip_start_ref[:, parts[0]])
    for frame, (sides, strip) in enumerate(zip(beside, strips)):
        sides = [column(sides, 0) * inside(0), column(sides, 1) * inside(3)]
        strip = [column(strip, slot) * inside(slot) for slot in range(4)]
        beside_out_ref[frame] = jnp.concatenate(sides, axis=0).astype(beside_out_ref.dtype)
        strips_out_ref[frame] = jnp.concatenate(strip, axis=0).astype(strips_out_ref.dtype)


def put_columns_taps(lhs_ref, slots, columns, ends):
    rows = columns.shape[0] // len(slots)
    columns, ends = columns.astype(jnp.float32), ends.astype(jnp.float32)
    for index, at in enumerate(slots):
        column, end = columns[index * rows : (index + 1) * rows], ends[index : index + 1]
        lhs_ref[at : at + rows] = row_taps(column, end, end).astype(lhs_ref.dtype)


def tile_sum(tile, inputs, lanes, room, lhs_ref, weight_ref):
    count, rows, cols, wide = tile
    size = rows * cols
    col = lax.broadcasted_iota(jnp.int32, tile[1:], 1)

    def beside(cells):
        return cells.reshape(rows, 1, wide) if room else 0.0

    for frame in range(count):
        at = frame * (size + 2 * room)
        end = at + room + size
        total = dot(lhs_ref[at + room : end], weight_ref, 1, lanes, inputs).reshape(tile[1:])
        first = dot(lhs_ref[at:end], weight_ref, 0, lanes, inputs)
        shifted = pltpu.roll(first[room:].reshape(tile[1:]), 1, 1)
        total += jnp.where(col == 0, beside(first[:room]), shifted)
        last = dot(lhs_ref[at + room : end + room], weight_ref, 2, lanes, inputs)
        shifted = pltpu.roll(last[:size].reshape(tile[1:]), cols - 1, 1)
        yield total + jnp.where(col == cols - 1, beside(last[size:]), shifted)


def strip_sum(tile, inputs, lanes, lhs_ref, weight_ref):
    count, rows, cols, wide = tile
    room = count * rows
    first = dot(lhs_ref[: 2 * room], weight_ref, 0, lanes, inputs)
    middle = dot(lhs_ref[room : 3 * room], weight_ref, 1, lanes, inputs)
    last = dot(lhs_ref[2 * room :], weight_ref, 2, lanes, inputs)
    columns = [
        (0, first[:room] + middle[:room]),
        (1, first[room:]),
        (cols - 2, last[:room]),
        (cols - 1, middle[room:] + last[room:]),
    ]
    return [(at, cells.reshape(count, rows, 1, wide)) for at, cells in columns]


def opening_kernel(inputs, lanes, _, got_ref, weight_ref, out_ref, lhs_ref):
    count, rows, cols, _ = out_ref.shape
    size = rows * cols
    for frame in range(count):
        put_row(lhs_ref, frame * size, size, got_ref[frame])
    further_kernel(inputs, lanes, lhs_ref, weight_ref, out_ref)


def further_kernel(inputs, lanes, lhs_ref, weight_ref, out_ref):
    tiles = tile_sum(out_ref.shape, inputs, lanes, 0, lhs_ref, weight_ref)
    for frame, total in enumerate(tiles):
        out_ref[frame] = total


def result_kernel(
    parts, _, got_ref, beside_ref, strips_ref, weight_ref, *refs
):
    *before_refs, out_ref, lhs_ref, held_ref, strip_lhs_ref, sems = refs
    count, rows, cols, _ = held_ref.shape
    size, room = rows * cols, count * rows
    stride = size + 2 * rows
    for frame in range(count):
        at = frame * stride
        put_row(lhs_ref, at + rows, size, got_ref[frame, :cols])
        ends = got_ref[frame, cols:]
        put_columns_taps(lhs_ref, (at, at + rows + size), beside_ref[frame], ends)
        slots = [slot * room + frame * rows for slot in range(4)]
        put_columns_taps(strip_lhs_ref, slots, strips_ref[frame], ends.astype(jnp.float32)[2:])

    def store(frame, part):
        here = (frame, slice(None), slice(None), parts[part])
        return pltpu.make_async_copy(held_ref.at[here], out_ref.at[here], sems.at[frame, part])

    for part, lanes in enumerate(parts):
        tile = (count, rows, cols, lanes.stop - lanes.start)
        col = lax.broadcasted_iota(jnp.int32, tile[1:], 1)
        columns = strip_sum(tile, parts[0], lanes, strip_lhs_ref, weight_ref)
        tiles = tile_sum(tile, parts[1], lanes, rows, lhs_ref, weight_ref)
        for frame, total in enumerate(tiles):
            strips = 0.0
            for at, cells in columns:
                strips = jnp.where(col == at, cells[frame], strips)
            total += before_refs[part][frame] + strips
            held_ref[frame, :, :, lanes] = total.astype(held_ref.dtype)
            store(frame, part).start()
    for part in range(len(parts)):
        for frame in range(count):
            store(frame, part).wait()


def on_device(frames, input_weight, output_weight, pole_index, gelu_scale, start_state):
    count, rows, cols, channels = frames.shape
    size, room = rows * cols, count * rows
    wide = 3 * channels
    assert lax.axis_size("sx") == 2
    narrow = frames.dtype
    pole, scale = pole_index[None], gelu_scale[None]

    shapes = (
        of((count * cols + (2 * count + 1) * rows, channels), narrow),
        of((2 * count + 1, rows, channels), narrow),
    )
    edges = call(
        edges_kernel,
        shapes,
        frames,
        scratch=[pltpu.VMEM((count, channels // 128, size, 128), jnp.float32)],
        flops=EDGES_COST,
    )
    give, keep = call(
        start_edges_kernel,
        shapes,
        start_state,
        *edges,
        aliases={1: 0, 2: 1},
        scratch=[pltpu.VMEM((channels // 128, size, 128), jnp.float32)],
    )
    got, mine = trade_columns(give, keep, count * cols)
    taps = of((count * size, wide), narrow)
    parts = halves(channels)
    half = channels // 2
    inner = of((count, rows, cols, half), jnp.float32)
    *main, early, _ = call(
        main_kernel,
        (
            of(frames.shape, jnp.float32),
            of((2, room, channels), jnp.float32),
            of((size, half), narrow),
            taps,
        ),
        call(taps_kernel, taps, frames),
        got,
        input_weight,
        pole,
        aliases={0: 3},
        flops=18 * frames.size * channels,
    )
    mine, total, spill = lax.optimization_barrier((mine, *main))
    halo, sides = call(
        halo_kernel,
        (of((4 * room, wide), narrow), of((2 * rows, channels), jnp.float32)),
        mine,
        swap_cores(mine),
    )
    drive, beside, strips, late = call(
        drive_kernel,
        (
            inner,
            of((count, 2 * rows, half), jnp.float32),
            of((count, 4 * rows, half), jnp.float32),
            of((size + 4 * rows, half), narrow),
        ),
        halo,
        input_weight,
        total,
        spill,
        pole,
        flops=36 * room * channels * channels,
    )
    at = size + 2 * rows
    tile = slice(0, size)
    pieces = [
        (early, [(tile, parts[0], (parts[1], (0, cols - 1)))]),
        (
            late,
            [
                (tile, parts[1], (parts[0], (1, cols - 2))),
                (slice(size, at), parts[1], None),
                (slice(at, at + 2 * rows), parts[0], None),
            ],
        ),
    ]
    exchanged = exchange_four if lax.axis_size("tm") == 4 else exchange
    early, late = exchanged(pieces, pole, count, cols)
    rounds = len(early)

    mixing = (start_state, pole, scale)
    taps = of((count * size, 3 * half), narrow)
    give = call(
        functools.partial(middle_kernel, parts[0]),
        of((count, cols, half), narrow),
        total,
        *mixing,
        *early,
    )
    lhs = call(functools.partial(mixed_kernel, parts[0], rounds), taps, total, *mixing, *early)
    strip_start = call(strip_start_kernel, of((4 * rows, channels), jnp.float32), start_state, sides)
    flops = 18 * inner.size * half
    lhs, strip_start = lax.optimization_barrier((lhs, strip_start))
    first_sum, lhs = call(
        functools.partial(opening_kernel, parts[0], parts[0]),
        (inner, taps),
        lhs,
        swap_cores(give),
        output_weight,
        aliases={0: 1},
        flops=flops,
    )
    second_sum = call(
        functools.partial(further_kernel, parts[0], parts[1]),
        inner,
        lhs,
        output_weight,
        flops=flops,
    )
    *late, first_sum, second_sum = lax.optimization_barrier((*late, first_sum, second_sum))
    give = call(
        functools.partial(give_kernel, parts, rounds),
        of((count, 2 * cols, half), narrow),
        drive,
        beside,
        strips,
        start_state,
        strip_start,
        pole,
        scale,
        *early,
        *late,
    )
    beside, strips = call(
        functools.partial(late_kernel, parts, rounds),
        (of(beside.shape, narrow), of(strips.shape, narrow)),
        beside,
        strips,
        strip_start,
        pole,
        scale,
        *late,
    )
    taps = of((count * size + 2 * room, 3 * half), narrow)
    lhs = call(
        functools.partial(mixed_kernel, parts[1], rounds), taps, drive, *mixing, *early, *late
    )
    result, _ = call(
        functools.partial(result_kernel, parts),
        (of(frames.shape, narrow), taps),
        lhs,
        swap_cores(give),
        beside,
        strips,
        output_weight,
        first_sum,
        second_sum,
        out_specs=(HBM, WHOLE),
        aliases={0: 1},
        scratch=[
            pltpu.VMEM(frames.shape, narrow),
            pltpu.VMEM((4 * room, 3 * half), narrow),
            pltpu.SemaphoreType.DMA((count, len(parts))),
        ],
        flops=2 * flops,
    )
    return result


def solution(mesh):
    return jax.shard_map(
        on_device,
        mesh=mesh,
        in_specs=(P("tm", "sx", "sy", None), P(), P(), P(), P(), P("sx", "sy", None)),
        out_specs=P("tm", "sx", "sy", None),
        check_vma=False,
    )
```
